32 devices in a mesh: row: 4 (over z), col: 8 (over y, x, core).
Axes of the slice: x: 2, y: 2, z: 4, core: 2. Of those that a mesh axis runs over, the one named last changes fastest.
Arguments:
- image_embeds: float32 [8192, 512], P(('row', 'col')), may hold values from -60 to 60
- text_embeds: float32 [8192, 512], P(('col', 'row')), may hold values from -60 to 60
- logit_scale: float32 [], replicated, may hold values from 1 to 4
Outputs:
- grad_image: float32 [8192, 512], P(('row', 'col'))
- grad_text: float32 [8192, 512], P(('col', 'row'))
- grad_scale: float32 [], replicated
The draws below stay inside these ranges and needn't reach their ends.
All inputs are finite; a program needn't handle non-finite values.
Results may differ from the reference program's by a relative error of at most 0.0023.
The reference program's roundings to bfloat16 on the way (of `image_half`, `text_half` and `grad_half`) count: a program that leaves them out, or rounds other values in their place, can miss the bound.
Values may be sent and summed in bfloat16 or wider, within the bound.
No kernel may reach another device: no remote copies, remote signals or barrier semaphores. Data moves between devices by JAX's collectives and lax.ppermute only.
A program may use at most 128 MiB of HBM per device.

```python
import math
import jax
import jax.numpy as jnp
from jax import lax

E = 512
BATCH = 8192


def draw_image_embeds(key, part):
    key = jax.random.fold_in(key, 11)
    first_key, second_key = jax.random.split(key)
    noise = jax.random.normal(first_key, (BATCH, E), jnp.float32) * E ** (-0.25)
    factor = jnp.exp(jax.random.uniform(second_key, (BATCH, 1), jnp.float32, math.log(0.5), math.log(2.5)))
    values = factor * noise
    return jnp.clip(values, -60.0, 60.0)


def draw_text_embeds(key, part):
    key = jax.random.fold_in(key, 23)
    first_key, second_key = jax.random.split(key)
    noise = jax.random.normal(first_key, (BATCH, E), jnp.float32) * E ** (-0.25)
    factor = jnp.exp(jax.random.uniform(second_key, (BATCH, 1), jnp.float32, math.log(0.5), math.log(2.5)))
    values = factor * noise
    return jnp.clip(values, -60.0, 60.0)


def setup_inputs(seed: int = 0) -> dict:
    seeds = jax.random.split(jax.random.key(seed), 4)
    return {
        "image_embeds": draw_image_embeds(jax.random.fold_in(seeds[3], 71), 0),
        "text_embeds": draw_text_embeds(jax.random.fold_in(seeds[3], 71), 0),
        "logit_scale": jnp.clip(jnp.exp(jax.random.uniform(seeds[2], (), jnp.float32, math.log(1.0), math.log(4.0))), 1.0, 4.0),
    }


def reference(image_embeds, text_embeds, logit_scale):
    image_half = image_embeds.astype(jnp.bfloat16)
    text_half = text_embeds.astype(jnp.bfloat16)
    block_size = math.gcd(BATCH, 1024)
    blocks = BATCH // block_size
    image_blocks = image_half.reshape(blocks, block_size, E)

    def stats(state, block_rows):
        col_max, col_sum = state
        inner = jnp.dot(block_rows, text_half.T, preferred_element_type=jnp.float32)
        logits = logit_scale * inner
        row_max = jnp.max(logits, axis=1)
        row_lse = row_max + jnp.log(jnp.sum(jnp.exp(logits - row_max[:, None]), axis=1))
        merged = jnp.maximum(col_max, jnp.max(logits, axis=0))
        col_sum = col_sum * jnp.exp(col_max - merged) + jnp.sum(jnp.exp(logits - merged[None, :]), axis=0)
        return (merged, col_sum), row_lse

    start_state = (jnp.full((BATCH,), -1e30, jnp.float32), jnp.zeros((BATCH,), jnp.float32))
    (col_max, col_sum), row_lse = lax.scan(stats, start_state, image_blocks)
    row_lse = row_lse.reshape(blocks, block_size)
    col_lse = col_max + jnp.log(col_sum)
    starts = jnp.arange(blocks, dtype=jnp.int32) * block_size
    columns = jnp.arange(BATCH, dtype=jnp.int32)

    def grads(state, inputs):
        text_acc, scale_acc = state
        block_rows, lse_rows, start = inputs
        inner = jnp.dot(block_rows, text_half.T, preferred_element_type=jnp.float32)
        logits = logit_scale * inner
        matched = ((start + jnp.arange(block_size, dtype=jnp.int32))[:, None] == columns[None, :]).astype(jnp.float32)
        logit_grad = 0.5 * jnp.exp(logits - lse_rows[:, None]) + 0.5 * jnp.exp(logits - col_lse[None, :]) - matched
        scale_acc = scale_acc + jnp.sum(logit_grad * inner)
        grad_half = logit_grad.astype(jnp.bfloat16)
        image_part = logit_scale * jnp.dot(grad_half, text_half, preferred_element_type=jnp.float32)
        text_acc = text_acc + logit_scale * jnp.dot(grad_half.T, block_rows, preferred_element_type=jnp.float32)
        return (text_acc, scale_acc), image_part

    start_grads = (jnp.zeros((BATCH, E), jnp.float32), jnp.zeros((), jnp.float32))
    (grad_text, grad_scale), grad_image = lax.scan(grads, start_grads, (image_blocks, row_lse, starts))
    return grad_image.reshape(BATCH, E), grad_text, grad_scale
```

```python
import functools
import math

import jax
import jax.numpy as jnp
from jax import lax
from jax.experimental import pallas as pl
from jax.experimental.pallas import tpu as pltpu
from jax.sharding import PartitionSpec as P

LOG2E = 1.4426950408889634
LN2 = 0.6931471805599453
LANES = 128
VMEM = pltpu.VMEM
SMEM = pltpu.SMEM


def swap(x, axis, n, q):
    return lax.ppermute(x, axis, [(i, i ^ q) for i in range(n)])


def gather_hops(own, axis, n):
    half = own.shape[0] // 2
    blocks = {0: [own]}

    def top(pieces):
        return pieces[0][:half] if len(pieces) == 1 else pieces[0]

    def bottom(pieces):
        return pieces[0][half:] if len(pieces) == 1 else pieces[1]

    for q in sorted(range(1, n), key=lambda q: (bin(q).count("1"), q)):
        if q & 1:
            blocks[q] = [swap(p, axis, n, 1) for p in blocks[q ^ 1]]
        elif q & (q - 1) == 0:
            blocks[q] = [swap(own, axis, n, q)]
        else:
            high = 1 << (q.bit_length() - 1)
            low = q & -q
            blocks[q] = [
                swap(top(blocks[q ^ high]), axis, n, high),
                swap(bottom(blocks[q ^ low]), axis, n, low),
            ]
    return [blocks[q] for q in range(n)]


def nt_dot(a, b):
    return lax.dot_general(a, b, (((1,), (1,)), ((), ())), preferred_element_type=jnp.float32)


def stats_kernel(counts, block, coef_ref, *refs):
    n_image, n_text = counts
    pieces = refs[: n_image + n_text]
    row_ref, col_ref, images_out, texts_out = refs[n_image + n_text : n_image + n_text + 4]
    images, texts, tile, col_max, col_sum, sems, out_sems = refs[n_image + n_text + 4 :]
    copies = []
    for where, held in ((pieces[:n_image], images), (pieces[n_image:], texts)):
        at = 0
        for piece in where:
            rows = piece.shape[0]
            copies.append(
                pltpu.make_async_copy(piece, held.at[pl.ds(at, rows)], sems.at[len(copies)])
            )
            at += rows
    for copy in copies:
        copy.start()
    for copy in copies:
        copy.wait()
    keep = [
        pltpu.make_async_copy(images, images_out, out_sems.at[0]),
        pltpu.make_async_copy(texts, texts_out, out_sems.at[1]),
    ]
    for copy in keep:
        copy.start()

    coef = coef_ref[0, 0]
    cols, rows = tile.shape
    col_max[...] = jnp.full(col_max.shape, -jnp.inf, jnp.float32)

    def products(k, carry):
        at = pl.multiple_of(k * block, block)
        image = images[pl.ds(at, block), :]
        row_max = None
        for t in range(cols // block):
            part = pl.ds(t * block, block)
            x = nt_dot(texts[part, :], image) * coef
            tile[part, pl.ds(at, block)] = x
            top = jnp.max(x, axis=0, keepdims=True)
            row_max = top if row_max is None else jnp.maximum(row_max, top)
            held = col_max[part, :]
            for lane in range(0, block, LANES):
                held = jnp.maximum(held, x[:, lane : lane + LANES])
            col_max[part, :] = held
        row_ref[0:1, pl.ds(at, block)] = row_max
        return carry

    lax.fori_loop(0, rows // block, products, 0)

    def exponentials(i, acc):
        part = pl.ds(pl.multiple_of(i * 8, 8), 8)
        top = jnp.max(col_max[part, :], axis=1, keepdims=True)
        col_max[part, :] = jnp.broadcast_to(top, (8, LANES))
        x = tile[part, :]
        acc = acc + jnp.exp2(x - row_ref[0:1, :])
        e = jnp.exp2(x - top)
        total = e[:, :LANES]
        for lane in range(LANES, rows, LANES):
            total = total + e[:, lane : lane + LANES]
        col_sum[part, :] = total
        return acc

    acc = lax.fori_loop(0, cols // 8, exponentials, jnp.zeros((8, rows), jnp.float32), unroll=2)
    row_ref[1:2, :] = jnp.sum(acc, axis=0, keepdims=True)
    for t in range(cols // block):
        part = pl.ds(t * block, block)
        col_ref[0:1, part] = col_max[part, :].T[0:1, :]
        col_ref[1:2, part] = jnp.sum(col_sum[part, :].T, axis=0, keepdims=True)
    for copy in keep:
        copy.wait()


def stats(coef, image_pieces, text_pieces, block):
    rows = sum(p.shape[0] for p in image_pieces)
    cols = sum(p.shape[0] for p in text_pieces)
    width = image_pieces[0].shape[1]
    counts = (len(image_pieces), len(text_pieces))
    anywhere = pl.BlockSpec(memory_space=pl.ANY)
    return pl.pallas_call(
        functools.partial(stats_kernel, counts, block),
        out_shape=(
            jax.ShapeDtypeStruct((2, rows), jnp.float32),
            jax.ShapeDtypeStruct((2, cols), jnp.float32),
            jax.ShapeDtypeStruct((rows, width), jnp.bfloat16),
            jax.ShapeDtypeStruct((cols, width), jnp.bfloat16),
        ),
        in_specs=[pl.BlockSpec(memory_space=SMEM)] + [anywhere] * sum(counts),
        out_specs=(
            pl.BlockSpec(memory_space=VMEM),
            pl.BlockSpec(memory_space=VMEM),
            anywhere,
            anywhere,
        ),
        scratch_shapes=[
            VMEM((rows, width), jnp.bfloat16),
            VMEM((cols, width), jnp.bfloat16),
            VMEM((cols, rows), jnp.float32),
            VMEM((cols, LANES), jnp.float32),
            VMEM((cols, LANES), jnp.float32),
            pltpu.SemaphoreType.DMA((sum(counts),)),
            pltpu.SemaphoreType.DMA((2,)),
        ],
        compiler_params=pltpu.CompilerParams(vmem_limit_bytes=48 * 2**20),
        cost_estimate=pl.CostEstimate(
            flops=2 * rows * cols * width,
            bytes_accessed=4 * (rows + cols) * width,
            transcendentals=2 * rows * cols,
        ),
        name="stats",
    )(coef, *image_pieces, *text_pieces)


def lse_kernel(counts, block, *refs):
    outs = refs[sum(counts) :]
    for held, out in zip((refs[: counts[0]], refs[counts[0] : sum(counts)]), outs):
        n = len(held)
        for k in range(n):
            there = [pl.ds((k ^ q) * block, block) for q in range(n)]
            top = functools.reduce(
                jnp.maximum, [held[q][0:1, there[q]] for q in range(n)]
            )
            total = sum(
                held[q][1:2, there[q]] * jnp.exp2(held[q][0:1, there[q]] - top) for q in range(n)
            )
            out[0:1, pl.ds(k * block, block)] = top + jnp.log(total) * LOG2E


def lse(row_parts, col_parts, block):
    counts = (len(row_parts), len(col_parts))
    return pl.pallas_call(
        functools.partial(lse_kernel, counts, block),
        out_shape=(
            jax.ShapeDtypeStruct((1, row_parts[0].shape[1]), jnp.float32),
            jax.ShapeDtypeStruct((1, col_parts[0].shape[1]), jnp.float32),
        ),
        in_specs=[pl.BlockSpec(memory_space=VMEM)] * sum(counts),
        out_specs=(pl.BlockSpec(memory_space=VMEM),) * 2,
        name="lse",
    )(*row_parts, *col_parts)


def text_kernel(
    block, scale_ref, coef_ref, same_ref, images, text, row_lse, col_lse, grad_ref, out_ref, sum_ref
):
    coef = coef_ref[0, 0]
    rows = images.shape[0]
    size = text.shape[0]
    col_lse_down = jnp.broadcast_to(col_lse[...], (LANES, size)).T
    step = 32
    lane_ids = lax.broadcasted_iota(jnp.int32, (step, LANES), 1)
    row_ids = lax.broadcasted_iota(jnp.int32, (step, LANES), 0)

    def one(k, acc):
        at = pl.multiple_of(k * block, block)
        inner = nt_dot(text[...], images[pl.ds(at, block), :])
        same = same_ref[0, k]
        for r in range(0, size, step):
            for lane in range(0, block, LANES):
                v = inner[r : r + step, lane : lane + LANES]
                x = v * coef
                e = jnp.exp2(x - row_lse[0:1, pl.ds(at + lane, LANES)]) + jnp.exp2(
                    x - col_lse_down[r : r + step, :]
                )
                g = 0.5 * e
                if lane <= r < lane + LANES:
                    g = g - jnp.where(row_ids + (r - lane) == lane_ids, same, 0.0)
                acc = acc + g * v
                grad_ref[r : r + step, pl.ds(at + lane, LANES)] = g.astype(jnp.bfloat16)
        return acc

    acc = lax.fori_loop(0, rows // block, one, jnp.zeros((step, LANES), jnp.float32), unroll=2)
    sum_ref[...] = functools.reduce(jnp.add, [acc[i : i + 8] for i in range(0, step, 8)])
    out_ref[...] = scale_ref[0, 0] * jnp.dot(
        grad_ref[...], images[...], preferred_element_type=jnp.float32
    )


def text_grads(scale, coef, same, images, texts, row_lse, col_lse, t, block):
    rows, width = images.shape
    vmem = pl.BlockSpec(memory_space=VMEM)
    smem = pl.BlockSpec(memory_space=SMEM)
    return pl.pallas_call(
        functools.partial(text_kernel, block),
        grid=(1,),
        out_shape=(
            jax.ShapeDtypeStruct((block, rows), jnp.bfloat16),
            jax.ShapeDtypeStruct((block, width), jnp.float32),
            jax.ShapeDtypeStruct((8, LANES), jnp.float32),
        ),
        in_specs=[
            smem,
            smem,
            smem,
            vmem,
            pl.BlockSpec((block, width), lambda i: (t, 0)),
            vmem,
            pl.BlockSpec((1, block), lambda i: (0, t)),
        ],
        out_specs=(vmem, vmem, vmem),
        compiler_params=pltpu.CompilerParams(vmem_limit_bytes=32 * 2**20),
        cost_estimate=pl.CostEstimate(
            flops=4 * rows * block * width,
            bytes_accessed=2 * rows * (block + width) + 6 * block * width,
            transcendentals=2 * rows * block,
        ),
        name=f"text_grads_{t}",
    )(scale, coef, same, images, texts, row_lse, col_lse)


def image_kernel(n_text, block, scale_ref, *refs):
    grads, texts, out_ref = refs[:n_text], refs[n_text], refs[n_text + 1]
    total = None
    for t in range(n_text):
        part = lax.dot_general(
            grads[t][...],
            texts[pl.ds(t * block, block), :],
            (((0,), (0,)), ((), ())),
            preferred_element_type=jnp.float32,
        )
        total = part if total is None else total + part
    out_ref[0] = scale_ref[0, 0] * total


def image_grads(scale, grads, texts, odd, block):
    n_text = len(grads)
    rows = grads[0].shape[1]
    width = texts.shape[1]
    n = rows // block // 2
    return pl.pallas_call(
        functools.partial(image_kernel, n_text, block),
        grid=(n,),
        out_shape=jax.ShapeDtypeStruct((n, block, width), jnp.float32),
        in_specs=[pl.BlockSpec(memory_space=SMEM)]
        + [pl.BlockSpec((block, block), lambda j: (0, 2 * j + odd))] * n_text
        + [pl.BlockSpec(memory_space=VMEM)],
        out_specs=pl.BlockSpec((1, block, width), lambda j: (j, 0, 0)),
        compiler_params=pltpu.CompilerParams(vmem_limit_bytes=32 * 2**20),
        cost_estimate=pl.CostEstimate(
            flops=2 * n * block * n_text * block * width,
            bytes_accessed=2 * n * block * n_text * block + 4 * n * block * width,
            transcendentals=0,
        ),
        name=f"image_grads_{odd}",
    )(scale, *grads, texts)


def halve(blocks, axis, n, bits):
    for bit in bits:
        far = sorted(q for q in blocks if q & bit)
        sent = swap(jnp.stack([blocks[q] for q in far]), axis, n, bit)
        blocks = {q ^ bit: blocks[q ^ bit] + sent[i] for i, q in enumerate(far)}
    return blocks[0]


def scatter_images(scale, grads, texts, axis, n, block):
    far = image_grads(scale, grads, texts, 1, block)
    sent = swap(far, axis, n, 1)
    near = image_grads(scale, grads, texts, 0, block)
    half = block // 2
    bits = [1 << b for b in range(1, n.bit_length() - 1)]
    parts = []
    for piece, order in ((slice(0, half), bits), (slice(half, block), bits[::-1])):
        blocks = {2 * j: near[j, piece] + sent[j, piece] for j in range(n // 2)}
        parts.append(halve(blocks, axis, n, order))
    return jnp.concatenate(parts, axis=0)


def line_scatter(parts, axis):
    ends = [(0, 1), (3, 2)]
    middle = [(1, 2), (2, 1)]
    outward = [(1, 0), (2, 3)]
    first = lax.ppermute(parts[3], axis, ends)
    second = lax.ppermute(parts[2], axis, ends)
    second_middle = lax.ppermute(parts[2] + first, axis, middle)
    third = lax.ppermute(parts[1], axis, ends)
    third_middle = lax.ppermute(parts[3] + second, axis, middle)
    third_out = lax.ppermute(parts[1] + second_middle, axis, outward)
    return parts[0] + (third + third_middle + third_out)


def on_device(n_row, n_col, image_embeds, text_embeds, logit_scale):
    block = image_embeds.shape[0]
    r, c = lax.axis_index("row"), lax.axis_index("col")
    scale = logit_scale.reshape(1, 1)
    coef = scale * LOG2E
    image_half = image_embeds.astype(jnp.bfloat16)
    text_half = text_embeds.astype(jnp.bfloat16)
    text_blocks = [text_half] + [swap(text_half, "row", n_row, q) for q in range(1, n_row)]
    image_blocks = gather_hops(image_half, "col", n_col)
    image_pieces = [p for pieces in image_blocks for p in pieces]

    row_own, col_own, images, texts = stats(coef, image_pieces, text_blocks, block)
    row_parts = [row_own] + [swap(row_own, "col", n_col, q) for q in range(1, n_col)]
    col_parts = [col_own] + [swap(col_own, "row", n_row, q) for q in range(1, n_row)]
    row_lse, col_lse = lse(row_parts, col_parts, block)

    image_ids = r * n_col + (c ^ jnp.arange(n_col, dtype=jnp.int32))
    grads, parts, sums = {}, {}, []
    order = [3, 2, 1, 0] if n_row == 4 else list(range(n_row))[::-1]
    for t in order:
        same = (image_ids == c * n_row + (r ^ t)).astype(jnp.float32).reshape(1, n_col)
        grads[t], parts[t], partial = text_grads(
            scale, coef, same, images, texts, row_lse, col_lse, t, block
        )
        sums.append(partial)
    if n_row == 4:
        grad_text = line_scatter(parts, "row")
    else:
        grad_text = halve(parts, "row", n_row, [1 << b for b in range(n_row.bit_length() - 1)])

    total = functools.reduce(jnp.add, sums)
    for axis, n in (("col", n_col), ("row", n_row)):
        for b in range(n.bit_length() - 1):
            total = total + swap(total, axis, n, 1 << b)
    grad_scale = jnp.sum(total)

    grad_image = scatter_images(
        scale, [grads[t] for t in range(n_row)], texts, "col", n_col, block
    )
    return grad_image, grad_text, grad_scale


def solution(mesh):
    images = P(("row", "col"), None)
    texts = P(("col", "row"), None)
    return jax.shard_map(
        functools.partial(on_device, mesh.shape["row"], mesh.shape["col"]),
        mesh=mesh,
        in_specs=(images, texts, P()),
        out_specs=(images, texts, P()),
        check_vma=False,
    )
```

```python
import functools
import math

import jax
import jax.numpy as jnp
from jax import lax
from jax.experimental import pallas as pl
from jax.experimental.pallas import tpu as pltpu
from jax.sharding import PartitionSpec as P

LOG2E = 1.4426950408889634
LN2 = 0.6931471805599453
LANES = 128
VMEM = pltpu.VMEM
SMEM = pltpu.SMEM
FLOPS = 20


def swap(x, axis, n, q):
    return lax.ppermute(x, axis, [(i, i ^ q) for i in range(n)])


def gather_both(image, text, n_col, n_row):
    rounds = [1 << b for b in range(1, n_col.bit_length() - 1)][::-1]
    if n_row == 4 and n_col == 8:
        four = swap(image, "col", n_col, 4)
        two = swap(image, "col", n_col, 2)
        one = swap(text, "row", n_row, 1)
        middle = [(1, 2), (2, 1)]
        outward = [(1, 0), (2, 3)]
        mid_three = lax.ppermute(text, "row", middle)
        four, two, one, mid_three = lax.optimization_barrier((four, two, one, mid_three))
        six = swap(four, "col", n_col, 2)
        mid_two = lax.ppermute(one, "row", middle)
        end_two = lax.ppermute(mid_three, "row", outward)
        six, mid_two, end_two = lax.optimization_barrier((six, mid_two, end_two))
        even = jnp.concatenate([image, two, four, six], axis=0)
        odd = swap(even, "col", n_col, 1)
        end_three = lax.ppermute(mid_two, "row", outward)
        return even, odd, [text, one, mid_two + end_two, mid_three + end_three]
    blocks = {0: image}
    for bit in rounds:
        for q in sorted(blocks):
            blocks[q | bit] = swap(blocks[q], "col", n_col, bit)
    even = jnp.concatenate([blocks[q] for q in range(0, n_col, 2)], axis=0)
    texts = [text] + [swap(text, "row", n_row, q) for q in range(1, n_row)]
    return even, swap(even, "col", n_col, 1), texts


def cast_kernel(a_ref, b_ref, a_out, b_out):
    a_out[...] = a_ref[...].astype(jnp.bfloat16)
    b_out[...] = b_ref[...].astype(jnp.bfloat16)


def cast_both(a, b):
    vmem = pl.BlockSpec(memory_space=VMEM)
    return pl.pallas_call(
        cast_kernel,
        out_shape=tuple(jax.ShapeDtypeStruct(x.shape, jnp.bfloat16) for x in (a, b)),
        in_specs=[vmem] * 2,
        out_specs=(vmem,) * 2,
        name="cast_both",
    )(a, b)


def nt_dot(a, b):
    return lax.dot_general(a, b, (((1,), (1,)), ((), ())), preferred_element_type=jnp.float32)


def stats_kernel(n_text, first, block, coef_ref, place_ref, *refs):
    halves, texts = refs[:2], refs[2 : 2 + n_text]
    before = refs[2 + n_text : -6]
    row_ref, col_ref, tile, row_max, col_max, col_sum = refs[-6:]
    coef = coef_ref[0, 0]
    r_place, c_place = place_ref[0, 0], place_ref[0, 1]
    cols, rows = tile.shape
    half = rows // 2
    col_max[...] = jnp.full(col_max.shape, -jnp.inf, jnp.float32)

    for odd in range(2):

        def products(j, carry):
            image = halves[odd][pl.ds(pl.multiple_of(j * block, block), block), :]
            at = pl.multiple_of(j * block + odd * half, block)
            top = None
            for t in range(n_text):
                part = pl.ds(t * block, block)
                x = nt_dot(texts[t][...], image) * coef
                tile[part, pl.ds(at, block)] = x
                top_t = jnp.max(x, axis=0, keepdims=True)
                top = top_t if top is None else jnp.maximum(top, top_t)
                held = col_max[part, :]
                for lane in range(0, block, LANES):
                    held = jnp.maximum(held, x[:, lane : lane + LANES])
                col_max[part, :] = held
            row_max[0:1, pl.ds(at, block)] = top
            return carry

        lax.fori_loop(0, half // block, products, 0, unroll=2)

    col_max[...] = jnp.broadcast_to(
        jnp.max(col_max[...], axis=1, keepdims=True), col_max.shape
    )

    def exponentials(i, acc):
        part = pl.ds(pl.multiple_of(i * 8, 8), 8)
        top = col_max[part, :]
        total = None
        out = []
        for lane in range(0, rows, LANES):
            x = tile[part, lane : lane + LANES]
            out.append(acc[lane // LANES] + jnp.exp2(x - row_max[0:1, lane : lane + LANES]))
            e = jnp.exp2(x - top)
            total = e if total is None else total + e
        col_sum[part, :] = total
        return tuple(out)

    acc = lax.fori_loop(
        0,
        cols // 8,
        exponentials,
        tuple(jnp.zeros((8, LANES), jnp.float32) for _ in range(rows // LANES)),
        unroll=2,
    )
    n_col, n_row = row_ref.shape[1], col_ref.shape[1]
    row_ids = lax.broadcasted_iota(jnp.int32, (n_col, block), 0)
    top, total = jnp.zeros((n_col, block), jnp.float32), jnp.zeros((n_col, block), jnp.float32)
    for q in range(n_col):
        at = (q // 2) * block + (q % 2) * half
        sums = [
            jnp.sum(acc[(at + lane) // LANES], axis=0, keepdims=True)
            for lane in range(0, block, LANES)
        ]
        here = row_ids == (c_place ^ q)
        top = jnp.where(here, row_max[0:1, at : at + block], top)
        total = jnp.where(here, jnp.concatenate(sums, axis=1), total)
    if before:
        old_top, old_total = before[0][0], before[0][1]
        new_top = jnp.maximum(top, old_top)
        total = total * jnp.exp2(top - new_top) + old_total * jnp.exp2(old_top - new_top)
        top = new_top
    row_ref[0], row_ref[1] = top, total
    row_ids = lax.broadcasted_iota(jnp.int32, (n_row, block), 0)
    if before:
        top, total = before[1][0], before[1][1]
    else:
        top = total = jnp.zeros((n_row, block), jnp.float32)
    for t in range(n_text):
        part = pl.ds(t * block, block)
        here = row_ids == (r_place ^ (first + t))
        top = jnp.where(here, col_max[part, :].T[0:1, :], top)
        total = jnp.where(here, jnp.sum(col_sum[part, :].T, axis=0, keepdims=True), total)
    col_ref[0], col_ref[1] = top, total


def stats(coef, place, even, odd, texts, before, first, n_row):
    rows = 2 * even.shape[0]
    block, width = texts[0].shape
    cols = block * len(texts)
    vmem = pl.BlockSpec(memory_space=VMEM)
    smem = pl.BlockSpec(memory_space=SMEM)
    return pl.pallas_call(
        functools.partial(stats_kernel, len(texts), first, block),
        out_shape=(
            jax.ShapeDtypeStruct((2, rows // block, block), jnp.float32),
            jax.ShapeDtypeStruct((2, n_row, block), jnp.float32),
        ),
        in_specs=[smem, smem] + [vmem] * (2 + len(texts) + len(before)),
        out_specs=(vmem, vmem),
        scratch_shapes=[
            VMEM((cols, rows), jnp.float32),
            VMEM((8, rows), jnp.float32),
            VMEM((cols, LANES), jnp.float32),
            VMEM((cols, LANES), jnp.float32),
        ],
        compiler_params=pltpu.CompilerParams(vmem_limit_bytes=4 * rows * cols + 8 * 2**20),
        cost_estimate=pl.CostEstimate(
            flops=2 * rows * cols * width,
            bytes_accessed=2 * (rows + cols) * width,
            transcendentals=2 * rows * cols,
        ),
        name=f"stats_{first}",
    )(coef, place, even, odd, *texts, *before)


def merged(a, b):
    top = jnp.maximum(a[0], b[0])
    return jnp.stack([top, a[1] * jnp.exp2(a[0] - top) + b[1] * jnp.exp2(b[0] - top)])


def exchanged_lse(pairs, axis, n):
    for b in range(n.bit_length() - 1):
        pairs = merged(pairs, swap(pairs, axis, n, 1 << b))
    return pairs[0] + jnp.log(pairs[1]) * LOG2E


def text_block(text, t, halves, row_lse, col_lse, place_ref, scale_ref, coef_ref, grad_ref, out_ref, acc):
    coef = coef_ref[0, 0]
    r_place, c_place = place_ref[0, 0], place_ref[0, 1]
    half, width = halves[0].shape
    n_col, n_row = row_lse.shape[0], col_lse.shape[0]
    size = text.shape[0]
    block = size
    col_lse_down = jnp.broadcast_to(col_lse[pl.ds(r_place ^ t, 1), :], (LANES, size)).T
    text_id = c_place * n_row + (r_place ^ t)
    step = acc.shape[0]
    lane_ids = lax.broadcasted_iota(jnp.int32, (step, LANES), 1)
    row_ids = lax.broadcasted_iota(jnp.int32, (step, LANES), 0)

    for which, images in enumerate(halves):

        def one(j, acc):
            inner = nt_dot(text[...], images[pl.ds(pl.multiple_of(j * block, block), block), :])
            at = pl.multiple_of(j * block + which * half, block)
            column = c_place ^ (2 * j + which)
            same = jnp.where(r_place * n_col + column == text_id, 1.0, 0.0)
            lse = row_lse[pl.ds(column, 1), :]
            for r in range(0, size, step):
                for lane in range(0, block, LANES):
                    v = inner[r : r + step, lane : lane + LANES]
                    x = v * coef
                    e = jnp.exp2(x - lse[:, lane : lane + LANES]) + jnp.exp2(
                        x - col_lse_down[r : r + step, :]
                    )
                    g = 0.5 * e
                    if lane <= r < lane + LANES:
                        g = g - jnp.where(row_ids + (r - lane) == lane_ids, same, 0.0)
                    acc = acc + g * v
                    grad_ref[r : r + step, pl.ds(at + lane, LANES)] = g.astype(jnp.bfloat16)
            return acc

        acc = lax.fori_loop(0, half // block, one, acc, unroll=2)
    out_ref[...] = scale_ref[0, 0] * (
        jnp.dot(grad_ref[:, :half], halves[0][...], preferred_element_type=jnp.float32)
        + jnp.dot(grad_ref[:, half:], halves[1][...], preferred_element_type=jnp.float32)
    )
    return acc


def image_block(grads, texts, at, block, scale):
    total = None
    for grad, text in zip(grads, texts):
        part = lax.dot_general(
            grad[:, pl.ds(at, block)],
            text[...],
            (((0,), (0,)), ((), ())),
            preferred_element_type=jnp.float32,
        )
        total = part if total is None else total + part
    return scale * total


def text_kernel(order, n_done, block, scale_ref, coef_ref, place_ref, *refs):
    even, odd, row_lse, col_lse = refs[:4]
    n = len(order)
    texts = refs[4 : 4 + n]
    done_grads, done_texts = refs[4 + n : 4 + n + n_done], refs[4 + n + n_done : 4 + n + 2 * n_done]
    rest = refs[4 + n + 2 * n_done :]
    grads, outs, sum_ref = rest[:n], rest[n : 2 * n], rest[2 * n]
    acc = jnp.zeros((32, LANES), jnp.float32)
    for i, t in enumerate(order):
        acc = text_block(
            texts[i], t, (even, odd), row_lse, col_lse, place_ref, scale_ref, coef_ref, grads[i], outs[i], acc
        )
    sum_ref[...] = functools.reduce(jnp.add, [acc[i : i + 8] for i in range(0, 32, 8)])
    if n_done:
        far_ref = rest[2 * n + 1]
        half = even.shape[0]

        def one(j, carry):
            at = pl.multiple_of(j * block + half, block)
            far_ref[j] = image_block(
                [*done_grads, *grads], [*done_texts, *texts], at, block, scale_ref[0, 0]
            )
            return carry

        lax.fori_loop(0, half // block, one, 0)


def text_grads(scale, coef, place, even, odd, row_lse, col_lse, texts, order, done):
    half, width = even.shape
    block = texts[0].shape[0]
    n = len(order)
    vmem = pl.BlockSpec(memory_space=VMEM)
    smem = pl.BlockSpec(memory_space=SMEM)
    out_shape = (
        [jax.ShapeDtypeStruct((block, 2 * half), jnp.bfloat16)] * n
        + [jax.ShapeDtypeStruct((block, width), jnp.float32)] * n
        + [jax.ShapeDtypeStruct((8, LANES), jnp.float32)]
    )
    if done:
        out_shape.append(jax.ShapeDtypeStruct((half // block, block, width), jnp.float32))
    operands = [even, odd, row_lse, col_lse, *[texts[t] for t in order]]
    operands += [done[t] for t in done] + [texts[t] for t in done]
    outs = pl.pallas_call(
        functools.partial(text_kernel, tuple(order), len(done), block),
        out_shape=tuple(out_shape),
        in_specs=[smem] * 3 + [vmem] * len(operands),
        out_specs=(vmem,) * len(out_shape),
        compiler_params=pltpu.CompilerParams(vmem_limit_bytes=12 * 2**20),
        cost_estimate=pl.CostEstimate(
            flops=FLOPS * 4 * n * block * 2 * half * width, bytes_accessed=0, transcendentals=0
        ),
        name=f"text_grads_{n}",
    )(scale, coef, place, *operands)
    grads = {t: outs[i] for i, t in enumerate(order)}
    parts = {t: outs[n + i] for i, t in enumerate(order)}
    return grads, parts, outs[2 * n], outs[-1] if done else None


def image_kernel(n_text, block, scale_ref, *refs):
    grads, texts, out_ref = refs[:n_text], refs[n_text : 2 * n_text], refs[-1]

    def one(j, carry):
        out_ref[j] = image_block(
            grads, texts, pl.multiple_of(j * block, block), block, scale_ref[0, 0]
        )
        return carry

    lax.fori_loop(0, out_ref.shape[0], one, 0)


def image_grads(scale, grads, texts, after):
    n_text = len(grads)
    rows = grads[0].shape[1]
    block, width = texts[0].shape
    n = rows // block // 2
    vmem = pl.BlockSpec(memory_space=VMEM)
    return pl.pallas_call(
        functools.partial(image_kernel, n_text, block),
        out_shape=jax.ShapeDtypeStruct((n, block, width), jnp.float32),
        in_specs=[pl.BlockSpec(memory_space=SMEM)]
        + [vmem] * (2 * n_text)
        + [pl.BlockSpec(memory_space=pl.ANY)] * len(after),
        out_specs=vmem,
        compiler_params=pltpu.CompilerParams(vmem_limit_bytes=12 * 2**20),
        cost_estimate=pl.CostEstimate(
            flops=FLOPS * 2 * n * block * n_text * block * width, bytes_accessed=0, transcendentals=0
        ),
        name="image_grads",
    )(scale, *grads, *texts, *after)


def halve(blocks, axis, n, bits):
    for bit in bits:
        far = sorted(q for q in blocks if q & bit)
        sent = swap(jnp.stack([blocks[q] for q in far]), axis, n, bit)
        blocks = {q ^ bit: blocks[q ^ bit] + sent[i] for i, q in enumerate(far)}
    return blocks[0]


def scatter_images(near, far, axis, n):
    sent = swap(far, axis, n, 1)
    total = near[0] + sent[0]
    for j in range(1, n // 2):
        total = total + swap(near[j] + sent[j], axis, n, 2 * j)
    return total


def on_device(n_row, n_col, image_embeds, text_embeds, logit_scale):
    block = image_embeds.shape[0]
    r, c = lax.axis_index("row"), lax.axis_index("col")
    place = jnp.stack([r, c]).reshape(1, 2)
    scale = logit_scale.reshape(1, 1)
    coef = scale * LOG2E
    image_half, text_half = cast_both(image_embeds, text_embeds)
    even, odd, texts = gather_both(image_half, text_half, n_col, n_row)
    row_pairs, col_pairs = stats(coef, place, even, odd, texts, (), 0, n_row)
    row_lse = exchanged_lse(row_pairs, "col", n_col)
    col_lse = exchanged_lse(col_pairs, "row", n_row)

    held = (scale, coef, place, even, odd, row_lse, col_lse, texts)
    last = n_row - 1
    grads, parts, sum_first, _ = text_grads(*held, [last], {})
    received = swap(parts[last], "row", n_row, 1)
    more, more_parts, sum_rest, far = text_grads(*held, list(range(last))[::-1], grads)
    grads |= more
    parts |= more_parts
    sums = {last ^ 1: parts[last ^ 1] + received}
    near = image_grads(
        scale, [grads[t] for t in range(n_row)], texts, [sums[last ^ 1]]
    )
    for q in range(1, last, 2):
        sums[q ^ 1] = parts[q ^ 1] + swap(parts[q], "row", n_row, 1)
    grad_text = halve(sums, "row", n_row, [1 << b for b in range(1, n_row.bit_length() - 1)])
    grad_image = scatter_images(near, far, "col", n_col)
    total = lax.all_gather(sum_first + sum_rest, ("row", "col"))
    return grad_image, grad_text, jnp.sum(total)


def solution(mesh):
    images = P(("row", "col"), None)
    texts = P(("col", "row"), None)
    return jax.shard_map(
        functools.partial(on_device, mesh.shape["row"], mesh.shape["col"]),
        mesh=mesh,
        in_specs=(images, texts, P()),
        out_specs=(images, texts, P()),
        check_vma=False,
    )
```

```python
import functools
import math

import jax
import jax.numpy as jnp
from jax import lax
from jax.experimental import pallas as pl
from jax.experimental.pallas import tpu as pltpu
from jax.sharding import PartitionSpec as P

LOG2E = 1.4426950408889634
LN2 = 0.6931471805599453
LANES = 128
VMEM = pltpu.VMEM
SMEM = pltpu.SMEM
FLOPS = 20


def swap(x, axis, n, q):
    return lax.ppermute(x, axis, [(i, i ^ q) for i in range(n)])


def gather_both(image, text, n_col, n_row):
    images = [swap(image, "col", n_col, q) for q in range(2, n_col, 2)]
    texts = [swap(text, "row", n_row, q) for q in range(1, n_row)]
    odd = [swap(image, "col", n_col, 1)]
    texts, images = lax.optimization_barrier((texts, images))
    odd += [swap(i, "col", n_col, 1) for i in images]
    return [image, *images], odd, [text, *texts]


def cast_kernel(a_ref, b_ref, a_out, b_out):
    a_out[...] = a_ref[...].astype(jnp.bfloat16)
    b_out[...] = b_ref[...].astype(jnp.bfloat16)


def cast_both(a, b):
    vmem = pl.BlockSpec(memory_space=VMEM)
    return pl.pallas_call(
        cast_kernel,
        out_shape=tuple(jax.ShapeDtypeStruct(x.shape, jnp.bfloat16) for x in (a, b)),
        in_specs=[vmem] * 2,
        out_specs=(vmem,) * 2,
        name="cast_both",
    )(a, b)


def nt_dot(a, b):
    return lax.dot_general(a, b, (((1,), (1,)), ((), ())), preferred_element_type=jnp.float32)


def stats_kernel(n_text, n_image, odd, block, coef_ref, place_ref, *refs):
    pieces, refs = refs[:n_image], refs[n_image:]
    texts = refs[:n_text]
    before = refs[n_text:-9]
    row_ref, col_ref, images, tile, row_max, col_max, col_sum, col_dot, row_diag = refs[-9:]
    coef = coef_ref[0, 0]
    r_place, c_place = place_ref[0, 0], place_ref[0, 1]
    cols, rows = tile.shape
    col_max[...] = jnp.full(col_max.shape, -jnp.inf, jnp.float32)
    row_diag[...] = jnp.zeros(row_diag.shape, jnp.float32)
    n_col, n_row = row_ref.shape[1], col_ref.shape[1]
    for j, piece in enumerate(pieces):
        images[j * block : (j + 1) * block, :] = piece[...]

    def products(j, carry):
        at = pl.multiple_of(j * block, block)
        image = images[pl.ds(at, block), :]
        image_id = r_place * n_col + (c_place ^ (2 * j + odd))
        top = None
        for t in range(n_text):
            part = pl.ds(t * block, block)
            x = nt_dot(texts[t][...], image) * coef
            tile[part, pl.ds(at, block)] = x
            top_t = jnp.max(x, axis=0, keepdims=True)
            top = top_t if top is None else jnp.maximum(top, top_t)
            held = col_max[part, :]
            for lane in range(0, block, LANES):
                held = jnp.maximum(held, x[:, lane : lane + LANES])
            col_max[part, :] = held
        row_max[0:1, pl.ds(at, block)] = top
        for t in range(n_text):

            @pl.when(image_id == c_place * n_row + (r_place ^ t))
            def _():
                x = tile[pl.ds(t * block, block), pl.ds(at, block)]
                down = lax.broadcasted_iota(jnp.int32, x.shape, 0)
                across = lax.broadcasted_iota(jnp.int32, x.shape, 1)
                row_diag[0:1, pl.ds(at, block)] = jnp.sum(
                    jnp.where(down == across, x, 0.0), axis=0, keepdims=True
                )

        return carry

    lax.fori_loop(0, rows // block, products, 0, unroll=2)

    col_max[...] = jnp.broadcast_to(
        jnp.max(col_max[...], axis=1, keepdims=True), col_max.shape
    )

    lanes = range(0, rows, LANES)

    def exponentials(i, acc):
        part = pl.ds(pl.multiple_of(i * 8, 8), 8)
        top = col_max[part, :]
        total = dot = None
        sums, dots = [], []
        for n, lane in enumerate(lanes):
            x = tile[part, lane : lane + LANES]
            e = jnp.exp2(x - row_max[0:1, lane : lane + LANES])
            sums.append(acc[0][n] + e)
            dots.append(acc[1][n] + e * x)
            e = jnp.exp2(x - top)
            total = e if total is None else total + e
            dot = e * x if dot is None else dot + e * x
        col_sum[part, :] = total
        col_dot[part, :] = dot
        return tuple(sums), tuple(dots)

    zeros = tuple(jnp.zeros((8, LANES), jnp.float32) for _ in lanes)
    acc = lax.fori_loop(0, cols // 8, exponentials, (zeros, zeros), unroll=4)

    row_ids = lax.broadcasted_iota(jnp.int32, (n_col, block), 0)
    if before:
        placed = [before[0][i] for i in range(4)]
    else:
        placed = [jnp.zeros((n_col, block), jnp.float32)] * 4
    for j in range(rows // block):
        at = j * block
        here = row_ids == (c_place ^ (2 * j + odd))
        new = [row_max[0:1, at : at + block]]
        for which in acc:
            new.append(
                jnp.concatenate(
                    [
                        jnp.sum(which[(at + lane) // LANES], axis=0, keepdims=True)
                        for lane in range(0, block, LANES)
                    ],
                    axis=1,
                )
            )
        new.append(row_diag[0:1, at : at + block])
        placed = [jnp.where(here, n, p) for n, p in zip(new, placed)]
    for i in range(4):
        row_ref[i] = placed[i]
    row_ids = lax.broadcasted_iota(jnp.int32, (n_row, block), 0)
    placed = [jnp.zeros((n_row, block), jnp.float32)] * 3
    for t in range(n_text):
        part = pl.ds(t * block, block)
        here = row_ids == (r_place ^ t)
        new = [col_max[part, :].T[0:1, :]]
        for which in (col_sum, col_dot):
            new.append(jnp.sum(which[part, :].T, axis=0, keepdims=True))
        placed = [jnp.where(here, n, p) for n, p in zip(new, placed)]
    if before:
        placed = merged(placed, [before[1][i] for i in range(3)])
    for i in range(3):
        col_ref[i] = placed[i]


def merged(a, b):
    top = jnp.maximum(a[0], b[0])
    wa, wb = jnp.exp2(a[0] - top), jnp.exp2(b[0] - top)
    out = [top] + [a[i] * wa + b[i] * wb for i in (1, 2)]
    return out + [a[i] + b[i] for i in range(3, len(a))]


def stats(coef, place, images, texts, before, n_col):
    block, width = texts[0].shape
    rows, cols = block * len(images), block * len(texts)
    vmem = pl.BlockSpec(memory_space=VMEM)
    smem = pl.BlockSpec(memory_space=SMEM)
    return pl.pallas_call(
        functools.partial(stats_kernel, len(texts), len(images), 1 if before else 0, block),
        out_shape=(
            jax.ShapeDtypeStruct((4, n_col, block), jnp.float32),
            jax.ShapeDtypeStruct((3, len(texts), block), jnp.float32),
            jax.ShapeDtypeStruct((rows, width), jnp.bfloat16),
        ),
        in_specs=[smem, smem] + [vmem] * (len(images) + len(texts) + len(before)),
        out_specs=(vmem,) * 3,
        scratch_shapes=[
            VMEM((cols, rows), jnp.float32),
            VMEM((8, rows), jnp.float32),
            VMEM((cols, LANES), jnp.float32),
            VMEM((cols, LANES), jnp.float32),
            VMEM((cols, LANES), jnp.float32),
            VMEM((8, rows), jnp.float32),
        ],
        compiler_params=pltpu.CompilerParams(vmem_limit_bytes=4 * rows * cols + 8 * 2**20),
        cost_estimate=pl.CostEstimate(
            flops=FLOPS * 2 * rows * cols * width, bytes_accessed=0, transcendentals=0
        ),
        name="stats_odd" if before else "stats_even",
    )(coef, place, *images, *texts, *before)


def exchanged(parts, axis, n):
    parts = [parts[i] for i in range(parts.shape[0])]
    for b in range(n.bit_length() - 1):
        parts = merged(parts, swap(jnp.stack(parts), axis, n, 1 << b))
    mean = 0.5 * parts[2] / parts[1]
    return parts[0] + jnp.log(parts[1]) * LOG2E, mean - parts[3] if len(parts) > 3 else mean


def put_extra(out, extra_ref):
    n, width = extra_ref.shape
    rows = min(n, 8)
    out[...] = jnp.zeros(out.shape, out.dtype)
    out[:rows, :width] = sum(extra_ref[i : i + rows, :] for i in range(0, n, rows))


def text_block(text, t, halves, row_lse, col_lse, place_ref, scale_ref, coef_ref, extra, grad_ref, out_ref):
    coef = coef_ref[0, 0]
    r_place, c_place = place_ref[0, 0], place_ref[0, 1]
    half, width = halves[0].shape
    n_col, n_row = row_lse.shape[0], col_lse.shape[0]
    size = text.shape[0]
    block = size
    col_lse_down = jnp.broadcast_to(col_lse[pl.ds(r_place ^ t, 1), :], (LANES, size)).T
    text_id = c_place * n_row + (r_place ^ t)
    step = 32
    lane_ids = lax.broadcasted_iota(jnp.int32, (step, LANES), 1)
    row_ids = lax.broadcasted_iota(jnp.int32, (step, LANES), 0)

    for which, images in enumerate(halves):

        def one(j, carry):
            inner = nt_dot(text[...], images[pl.ds(pl.multiple_of(j * block, block), block), :])
            at = pl.multiple_of(j * block + which * half, block)
            column = c_place ^ (2 * j + which)
            same = jnp.where(r_place * n_col + column == text_id, 1.0, 0.0)
            lse = row_lse[pl.ds(column, 1), :]
            for r in range(0, size, step):
                for lane in range(0, block, LANES):
                    x = inner[r : r + step, lane : lane + LANES] * coef
                    e = jnp.exp2(x - lse[:, lane : lane + LANES]) + jnp.exp2(
                        x - col_lse_down[r : r + step, :]
                    )
                    g = 0.5 * e
                    if lane <= r < lane + LANES:
                        g = g - jnp.where(row_ids + (r - lane) == lane_ids, same, 0.0)
                    grad_ref[r : r + step, pl.ds(at + lane, LANES)] = g.astype(jnp.bfloat16)
            return carry

        lax.fori_loop(0, half // block, one, 0, unroll=2)
    out_ref[:size, :] = scale_ref[0, 0] * (
        jnp.dot(grad_ref[:, :half], halves[0][...], preferred_element_type=jnp.float32)
        + jnp.dot(grad_ref[:, half:], halves[1][...], preferred_element_type=jnp.float32)
    )
    put_extra(out_ref.at[size:, :], extra)


def image_block(grads, texts, at, block, scale):
    total = None
    for grad, text in zip(grads, texts):
        part = lax.dot_general(
            grad[:, pl.ds(at, block)],
            text[...],
            (((0,), (0,)), ((), ())),
            preferred_element_type=jnp.float32,
        )
        total = part if total is None else total + part
    return scale * total


def text_kernel(order, n_done, block, scale_ref, coef_ref, place_ref, *refs):
    even, odd, row_lse, col_lse, row_extra, col_extra = refs[:6]
    n = len(order)
    texts, rest = refs[6 : 6 + n], refs[6 + n :]
    done_grads, done_texts, rest = rest[:n_done], rest[n_done : 2 * n_done], rest[2 * n_done :]
    grads, outs = rest[:n], rest[n : 2 * n]
    for i, t in enumerate(order):
        text_block(
            texts[i], t, (even, odd), row_lse, col_lse, place_ref, scale_ref, coef_ref, row_extra, grads[i], outs[i]
        )
    if n_done:
        far_ref = rest[2 * n]
        half = even.shape[0]

        def one(j, carry):
            far_ref[j, :block, :] = image_block(
                [*done_grads, *grads],
                [*done_texts, *texts],
                pl.multiple_of(j * block + half, block),
                block,
                scale_ref[0, 0],
            )
            put_extra(far_ref.at[j, block:, :], col_extra)
            return carry

        lax.fori_loop(0, half // block, one, 0)


def text_grads(scale, coef, place, even, odd, row_lse, col_lse, row_extra, col_extra, texts, order, done):
    half, width = even.shape
    block = texts[0].shape[0]
    n = len(order)
    vmem = pl.BlockSpec(memory_space=VMEM)
    smem = pl.BlockSpec(memory_space=SMEM)
    out_shape = (
        [jax.ShapeDtypeStruct((block, 2 * half), jnp.bfloat16)] * n
        + [jax.ShapeDtypeStruct((block + 8, width), jnp.float32)] * n
    )
    if done:
        out_shape.append(jax.ShapeDtypeStruct((half // block, block + 8, width), jnp.float32))
    operands = [even, odd, row_lse, col_lse, row_extra, col_extra, *[texts[t] for t in order]]
    operands += [done[t] for t in done] + [texts[t] for t in done]
    outs = pl.pallas_call(
        functools.partial(text_kernel, tuple(order), len(done), block),
        out_shape=tuple(out_shape),
        in_specs=[smem] * 3 + [vmem] * len(operands),
        out_specs=(vmem,) * len(out_shape),
        compiler_params=pltpu.CompilerParams(vmem_limit_bytes=12 * 2**20),
        cost_estimate=pl.CostEstimate(
            flops=FLOPS * 4 * n * block * 2 * half * width, bytes_accessed=0, transcendentals=0
        ),
        name=f"text_grads_{n}",
    )(scale, coef, place, *operands)
    grads = {t: outs[i] for i, t in enumerate(order)}
    parts = {t: outs[n + i] for i, t in enumerate(order)}
    return grads, parts, outs[-1]


def image_kernel(n_text, block, scale_ref, extra, *refs):
    grads, texts, out_ref = refs[:n_text], refs[n_text : 2 * n_text], refs[-1]

    def one(j, carry):
        put_extra(out_ref.at[j, block:, :], extra)
        out_ref[j, :block, :] = image_block(
            grads, texts, pl.multiple_of(j * block, block), block, scale_ref[0, 0]
        )
        return carry

    lax.fori_loop(0, out_ref.shape[0], one, 0)


def image_grads(scale, extra, grads, texts, after):
    n_text = len(grads)
    rows = grads[0].shape[1]
    block, width = texts[0].shape
    n = rows // block // 2
    vmem = pl.BlockSpec(memory_space=VMEM)
    return pl.pallas_call(
        functools.partial(image_kernel, n_text, block),
        out_shape=jax.ShapeDtypeStruct((n, block + 8, width), jnp.float32),
        in_specs=[pl.BlockSpec(memory_space=SMEM)]
        + [vmem] * (2 * n_text + 1)
        + [pl.BlockSpec(memory_space=pl.ANY)] * len(after),
        out_specs=vmem,
        compiler_params=pltpu.CompilerParams(vmem_limit_bytes=12 * 2**20),
        cost_estimate=pl.CostEstimate(
            flops=FLOPS * 2 * n * block * n_text * block * width, bytes_accessed=0, transcendentals=0
        ),
        name="image_grads",
    )(scale, extra, *grads, *texts, *after)


def halve(blocks, axis, n, bits):
    for bit in bits:
        far = sorted(q for q in blocks if q & bit)
        sent = swap(jnp.stack([blocks[q] for q in far]), axis, n, bit)
        blocks = {q ^ bit: blocks[q ^ bit] + sent[i] for i, q in enumerate(far)}
    return blocks[0]


def scatter_images(near, far, axis, n):
    sent = swap(far, axis, n, 1)
    total = near[0] + sent[0]
    for j in range(1, n // 2):
        total = total + swap(near[j] + sent[j], axis, n, 2 * j)
    return total


def on_device(n_row, n_col, image_embeds, text_embeds, logit_scale):
    block = image_embeds.shape[0]
    r, c = lax.axis_index("row"), lax.axis_index("col")
    place = jnp.stack([r, c]).reshape(1, 2)
    scale = logit_scale.reshape(1, 1)
    coef = scale * LOG2E
    image_half, text_half = cast_both(image_embeds, text_embeds)
    even, odd, texts = gather_both(image_half, text_half, n_col, n_row)
    row_parts, col_parts, even = stats(coef, place, even, texts, (), n_col)
    row_parts, col_parts, odd = stats(coef, place, odd, texts, (row_parts, col_parts), n_col)
    row_lse, row_extra = exchanged(row_parts, "col", n_col)
    col_lse, col_extra = exchanged(col_parts, "row", n_row)

    held = (scale, coef, place, even, odd, row_lse, col_lse, row_extra, col_extra, texts)
    last = n_row - 1
    grads, parts, _ = text_grads(*held, [last], {})
    received = swap(parts[last], "row", n_row, 1)
    more, more_parts, far = text_grads(*held, list(range(last))[::-1], grads)
    grads |= more
    parts |= more_parts
    sums = {last ^ 1: parts[last ^ 1] + received}
    near = image_grads(
        scale, col_extra, [grads[t] for t in range(n_row)], texts, [sums[last ^ 1]]
    )
    for q in range(1, last, 2):
        sums[q ^ 1] = parts[q ^ 1] + swap(parts[q], "row", n_row, 1)
    text_sum = halve(sums, "row", n_row, [1 << b for b in range(1, n_row.bit_length() - 1)])
    image_sum = scatter_images(near, far, "col", n_col)
    grad_scale = (jnp.sum(text_sum[block:]) + jnp.sum(image_sum[block:])) / coef[0, 0]
    return image_sum[:block], text_sum[:block], grad_scale


def solution(mesh):
    images = P(("row", "col"), None)
    texts = P(("col", "row"), None)
    return jax.shard_map(
        functools.partial(on_device, mesh.shape["row"], mesh.shape["col"]),
        mesh=mesh,
        in_specs=(images, texts, P()),
        out_specs=(images, texts, P()),
        check_vma=False,
    )
```

```python
import functools
import math

import jax
import jax.numpy as jnp
from jax import lax
from jax.experimental import pallas as pl
from jax.experimental.pallas import tpu as pltpu
from jax.sharding import PartitionSpec as P

LOG2E = 1.4426950408889634
LN2 = 0.6931471805599453
LANES = 128
VMEM = pltpu.VMEM
SMEM = pltpu.SMEM
FLOPS = 20


def swap(x, axis, n, q):
    return lax.ppermute(x, axis, [(i, i ^ q) for i in range(n)])


def gather_both(image, text, n_col, n_row):
    images = [swap(image, "col", n_col, q) for q in range(2, n_col, 2)]
    texts = [swap(text, "row", n_row, q) for q in range(1, n_row)]
    odd = [swap(image, "col", n_col, 1)]
    texts, images = lax.optimization_barrier((texts, images))
    odd += [swap(i, "col", n_col, 1) for i in images]
    return [image, *images], odd, [text, *texts]


def nt_dot(a, b):
    return lax.dot_general(a, b, (((1,), (1,)), ((), ())), preferred_element_type=jnp.float32)


def stats_kernel(n_text, n_image, odd, block, coef_ref, place_ref, *refs):
    pieces, refs = refs[:n_image], refs[n_image:]
    texts = refs[:n_text]
    before = refs[n_text:-9]
    row_ref, col_ref, images, tile, row_max, col_max, col_sum, col_dot, row_diag = refs[-9:]
    coef = coef_ref[0, 0]
    r_place, c_place = place_ref[0, 0], place_ref[0, 1]
    cols, rows = tile.shape
    col_max[...] = jnp.full(col_max.shape, -jnp.inf, jnp.float32)
    row_diag[...] = jnp.zeros(row_diag.shape, jnp.float32)
    n_col, n_row = row_ref.shape[1], col_ref.shape[1]
    for j, piece in enumerate(pieces):
        images[j * block : (j + 1) * block, :] = piece[...]

    def products(j, carry):
        at = pl.multiple_of(j * block, block)
        image = images[pl.ds(at, block), :]
        image_id = r_place * n_col + (c_place ^ (2 * j + odd))
        top = None
        for t in range(n_text):
            part = pl.ds(t * block, block)
            x = nt_dot(texts[t][...], image) * coef
            tile[part, pl.ds(at, block)] = x
            top_t = jnp.max(x, axis=0, keepdims=True)
            top = top_t if top is None else jnp.maximum(top, top_t)
            held = col_max[part, :]
            for lane in range(0, block, LANES):
                held = jnp.maximum(held, x[:, lane : lane + LANES])
            col_max[part, :] = held
        row_max[0:1, pl.ds(at, block)] = top
        for t in range(n_text):

            @pl.when(image_id == c_place * n_row + (r_place ^ t))
            def _():
                x = tile[pl.ds(t * block, block), pl.ds(at, block)]
                down = lax.broadcasted_iota(jnp.int32, x.shape, 0)
                across = lax.broadcasted_iota(jnp.int32, x.shape, 1)
                row_diag[0:1, pl.ds(at, block)] = jnp.sum(
                    jnp.where(down == across, x, 0.0), axis=0, keepdims=True
                )

        return carry

    lax.fori_loop(0, rows // block, products, 0, unroll=4)

    col_max[...] = jnp.broadcast_to(
        jnp.max(col_max[...], axis=1, keepdims=True), col_max.shape
    )

    lanes = range(0, rows, LANES)

    def exponentials(i, acc):
        part = pl.ds(pl.multiple_of(i * 8, 8), 8)
        top = col_max[part, :]
        total = dot = None
        sums, dots = [], []
        for n, lane in enumerate(lanes):
            x = tile[part, lane : lane + LANES]
            e = jnp.exp2(x - row_max[0:1, lane : lane + LANES])
            sums.append(acc[0][n] + e)
            dots.append(acc[1][n] + e * x)
            e = jnp.exp2(x - top)
            total = e if total is None else total + e
            dot = e * x if dot is None else dot + e * x
        col_sum[part, :] = total
        col_dot[part, :] = dot
        return tuple(sums), tuple(dots)

    zeros = tuple(jnp.zeros((8, LANES), jnp.float32) for _ in lanes)
    acc = lax.fori_loop(0, cols // 8, exponentials, (zeros, zeros), unroll=4)

    row_ids = lax.broadcasted_iota(jnp.int32, (n_col, block), 0)
    if before:
        placed = [before[0][i] for i in range(4)]
    else:
        placed = [jnp.zeros((n_col, block), jnp.float32)] * 4
    for j in range(rows // block):
        at = j * block
        here = row_ids == (c_place ^ (2 * j + odd))
        new = [row_max[0:1, at : at + block]]
        for which in acc:
            new.append(
                jnp.concatenate(
                    [
                        jnp.sum(which[(at + lane) // LANES], axis=0, keepdims=True)
                        for lane in range(0, block, LANES)
                    ],
                    axis=1,
                )
            )
        new.append(row_diag[0:1, at : at + block])
        placed = [jnp.where(here, n, p) for n, p in zip(new, placed)]
    for i in range(4):
        row_ref[i] = placed[i]
    row_ids = lax.broadcasted_iota(jnp.int32, (n_row, block), 0)
    placed = [jnp.zeros((n_row, block), jnp.float32)] * 3
    for t in range(n_text):
        part = pl.ds(t * block, block)
        here = row_ids == (r_place ^ t)
        new = [col_max[part, :].T[0:1, :]]
        for which in (col_sum, col_dot):
            new.append(jnp.sum(which[part, :].T, axis=0, keepdims=True))
        placed = [jnp.where(here, n, p) for n, p in zip(new, placed)]
    if before:
        placed = merged(placed, [before[1][i] for i in range(3)])
    for i in range(3):
        col_ref[i] = placed[i]


def merged(a, b):
    top = jnp.maximum(a[0], b[0])
    wa, wb = jnp.exp2(a[0] - top), jnp.exp2(b[0] - top)
    out = [top] + [a[i] * wa + b[i] * wb for i in (1, 2)]
    return out + [a[i] + b[i] for i in range(3, len(a))]


def stats(coef, place, images, texts, before, n_col):
    block, width = texts[0].shape
    rows, cols = block * len(images), block * len(texts)
    vmem = pl.BlockSpec(memory_space=VMEM)
    smem = pl.BlockSpec(memory_space=SMEM)
    return pl.pallas_call(
        functools.partial(stats_kernel, len(texts), len(images), 1 if before else 0, block),
        out_shape=(
            jax.ShapeDtypeStruct((4, n_col, block), jnp.float32),
            jax.ShapeDtypeStruct((3, len(texts), block), jnp.float32),
            jax.ShapeDtypeStruct((rows, width), jnp.bfloat16),
        ),
        in_specs=[smem, smem] + [vmem] * (len(images) + len(texts) + len(before)),
        out_specs=(vmem,) * 3,
        scratch_shapes=[
            VMEM((cols, rows), jnp.float32),
            VMEM((8, rows), jnp.float32),
            VMEM((cols, LANES), jnp.float32),
            VMEM((cols, LANES), jnp.float32),
            VMEM((cols, LANES), jnp.float32),
            VMEM((8, rows), jnp.float32),
        ],
        compiler_params=pltpu.CompilerParams(vmem_limit_bytes=4 * rows * cols + 8 * 2**20),
        cost_estimate=pl.CostEstimate(
            flops=FLOPS * 2 * rows * cols * width, bytes_accessed=0, transcendentals=0
        ),
        name="stats_odd" if before else "stats_even",
    )(coef, place, *images, *texts, *before)


def by_pairs(blocks, add):
    while len(blocks) > 1:
        blocks = [add(blocks[i], blocks[i + 1]) for i in range(0, len(blocks), 2)]
    return blocks[0]


def lse_and_mean(parts):
    mean = 0.5 * parts[2] / parts[1]
    return parts[0] + jnp.log(parts[1]) * LOG2E, mean - parts[3] if len(parts) > 3 else mean


def exchanged(row_parts, col_parts, n_col, n_row):
    rows = [swap(row_parts, "col", n_col, q) for q in range(2, n_col, 2)]
    cols = [swap(col_parts, "row", n_row, q) for q in range(1, n_row)]
    rows, cols = lax.optimization_barrier((rows, cols))
    cols = by_pairs([list(x) for x in (col_parts, *cols)], merged)
    rows = by_pairs([list(x) for x in (row_parts, *rows)], merged)
    rows = merged(rows, list(swap(jnp.stack(rows), "col", n_col, 1)))
    return *lse_and_mean(rows), *lse_and_mean(cols)


def put_extra(out, extra_ref):
    n, width = extra_ref.shape
    rows = min(n, 8)
    out[...] = jnp.zeros(out.shape, out.dtype)
    out[:rows, :width] = sum(extra_ref[i : i + rows, :] for i in range(0, n, rows))


def text_block(text, t, halves, row_lse, col_lse, place_ref, scale_ref, coef_ref, extra, grad_ref, out_ref):
    coef = coef_ref[0, 0]
    r_place, c_place = place_ref[0, 0], place_ref[0, 1]
    half, width = halves[0].shape
    n_col, n_row = row_lse.shape[0], col_lse.shape[0]
    size = text.shape[0]
    block = size
    col_lse_down = jnp.broadcast_to(col_lse[pl.ds(r_place ^ t, 1), :], (LANES, size)).T
    text_id = c_place * n_row + (r_place ^ t)
    step = 32
    lane_ids = lax.broadcasted_iota(jnp.int32, (step, LANES), 1)
    row_ids = lax.broadcasted_iota(jnp.int32, (step, LANES), 0)

    for which, images in enumerate(halves):

        def one(j, carry):
            inner = nt_dot(text[...], images[pl.ds(pl.multiple_of(j * block, block), block), :])
            at = pl.multiple_of(j * block + which * half, block)
            column = c_place ^ (2 * j + which)
            same = jnp.where(r_place * n_col + column == text_id, 1.0, 0.0)
            lse = row_lse[pl.ds(column, 1), :]
            for r in range(0, size, step):
                for lane in range(0, block, LANES):
                    x = inner[r : r + step, lane : lane + LANES] * coef
                    e = jnp.exp2(x - lse[:, lane : lane + LANES]) + jnp.exp2(
                        x - col_lse_down[r : r + step, :]
                    )
                    g = 0.5 * e
                    if lane <= r < lane + LANES:
                        g = g - jnp.where(row_ids + (r - lane) == lane_ids, same, 0.0)
                    grad_ref[r : r + step, pl.ds(at + lane, LANES)] = g.astype(jnp.bfloat16)
            return carry

        lax.fori_loop(0, half // block, one, 0, unroll=4)
    out_ref[:size, :] = scale_ref[0, 0] * (
        jnp.dot(grad_ref[:, :half], halves[0][...], preferred_element_type=jnp.float32)
        + jnp.dot(grad_ref[:, half:], halves[1][...], preferred_element_type=jnp.float32)
    )
    put_extra(out_ref.at[size:, :], extra)


def image_block(grads, texts, at, block, scale):
    total = None
    for grad, text in zip(grads, texts):
        part = lax.dot_general(
            grad[:, pl.ds(at, block)],
            text[...],
            (((0,), (0,)), ((), ())),
            preferred_element_type=jnp.float32,
        )
        total = part if total is None else total + part
    return scale * total


def text_kernel(order, n_done, block, scale_ref, coef_ref, place_ref, *refs):
    even, odd, row_lse, col_lse, row_extra, col_extra = refs[:6]
    n = len(order)
    texts, rest = refs[6 : 6 + n], refs[6 + n :]
    done_grads, done_texts, rest = rest[:n_done], rest[n_done : 2 * n_done], rest[2 * n_done :]
    grads, outs = rest[:n], rest[n : 2 * n]
    for i, t in enumerate(order):
        text_block(
            texts[i], t, (even, odd), row_lse, col_lse, place_ref, scale_ref, coef_ref, row_extra, grads[i], outs[i]
        )
    if n_done:
        far_ref = rest[2 * n]
        half = even.shape[0]

        def one(j, carry):
            far_ref[j, :block, :] = image_block(
                [*done_grads, *grads],
                [*done_texts, *texts],
                pl.multiple_of(j * block + half, block),
                block,
                scale_ref[0, 0],
            )
            put_extra(far_ref.at[j, block:, :], col_extra)
            return carry

        lax.fori_loop(0, half // block, one, 0)


def text_grads(scale, coef, place, even, odd, row_lse, col_lse, row_extra, col_extra, texts, order, done):
    half, width = even.shape
    block = texts[0].shape[0]
    n = len(order)
    vmem = pl.BlockSpec(memory_space=VMEM)
    smem = pl.BlockSpec(memory_space=SMEM)
    out_shape = (
        [jax.ShapeDtypeStruct((block, 2 * half), jnp.bfloat16)] * n
        + [jax.ShapeDtypeStruct((block + 8, width), jnp.float32)] * n
    )
    if done:
        out_shape.append(jax.ShapeDtypeStruct((half // block, block + 8, width), jnp.float32))
    operands = [even, odd, row_lse, col_lse, row_extra, col_extra, *[texts[t] for t in order]]
    operands += [done[t] for t in done] + [texts[t] for t in done]
    outs = pl.pallas_call(
        functools.partial(text_kernel, tuple(order), len(done), block),
        out_shape=tuple(out_shape),
        in_specs=[smem] * 3 + [vmem] * len(operands),
        out_specs=(vmem,) * len(out_shape),
        compiler_params=pltpu.CompilerParams(vmem_limit_bytes=12 * 2**20),
        cost_estimate=pl.CostEstimate(
            flops=FLOPS * 4 * n * block * 2 * half * width, bytes_accessed=0, transcendentals=0
        ),
        name=f"text_grads_{n}",
    )(scale, coef, place, *operands)
    grads = {t: outs[i] for i, t in enumerate(order)}
    parts = {t: outs[n + i] for i, t in enumerate(order)}
    return grads, parts, outs[-1]


def image_kernel(n_text, block, scale_ref, extra, *refs):
    grads, texts, out_ref = refs[:n_text], refs[n_text : 2 * n_text], refs[-1]

    def one(j, carry):
        put_extra(out_ref.at[j, block:, :], extra)
        out_ref[j, :block, :] = image_block(
            grads, texts, pl.multiple_of(j * block, block), block, scale_ref[0, 0]
        )
        return carry

    lax.fori_loop(0, out_ref.shape[0], one, 0)


def image_grads(scale, extra, grads, texts, after):
    n_text = len(grads)
    rows = grads[0].shape[1]
    block, width = texts[0].shape
    n = rows // block // 2
    vmem = pl.BlockSpec(memory_space=VMEM)
    return pl.pallas_call(
        functools.partial(image_kernel, n_text, block),
        out_shape=jax.ShapeDtypeStruct((n, block + 8, width), jnp.float32),
        in_specs=[pl.BlockSpec(memory_space=SMEM)]
        + [vmem] * (2 * n_text + 1)
        + [pl.BlockSpec(memory_space=pl.ANY)] * len(after),
        out_specs=vmem,
        compiler_params=pltpu.CompilerParams(vmem_limit_bytes=12 * 2**20),
        cost_estimate=pl.CostEstimate(
            flops=FLOPS * 2 * n * block * n_text * block * width, bytes_accessed=0, transcendentals=0
        ),
        name="image_grads",
    )(scale, extra, *grads, *texts, *after)


def halve(blocks, axis, n, bits):
    for bit in bits:
        far = sorted(q for q in blocks if q & bit)
        sent = swap(jnp.stack([blocks[q] for q in far]), axis, n, bit)
        blocks = {q ^ bit: blocks[q ^ bit] + sent[i] for i, q in enumerate(far)}
    return blocks[0]


def scatter_images(near, far, axis, n):
    sent = swap(far, axis, n, 1)
    sums = [near[j] + sent[j] for j in range(n // 2)]
    return by_pairs([sums[0]] + [swap(sums[j], axis, n, 2 * j) for j in range(1, n // 2)], jnp.add)


def on_device(n_row, n_col, image_embeds, text_embeds, logit_scale):
    block = image_embeds.shape[0]
    r, c = lax.axis_index("row"), lax.axis_index("col")
    place = jnp.stack([r, c]).reshape(1, 2)
    scale = logit_scale.reshape(1, 1)
    coef = scale * LOG2E
    image_half, text_half = image_embeds.astype(jnp.bfloat16), text_embeds.astype(jnp.bfloat16)
    even, odd, texts = gather_both(image_half, text_half, n_col, n_row)
    row_parts, col_parts, even = stats(coef, place, even, texts, (), n_col)
    row_parts, col_parts, odd = stats(coef, place, odd, texts, (row_parts, col_parts), n_col)
    row_lse, row_extra, col_lse, col_extra = exchanged(row_parts, col_parts, n_col, n_row)

    held = (scale, coef, place, even, odd, row_lse, col_lse, row_extra, col_extra, texts)
    last = n_row - 1
    grads, parts, _ = text_grads(*held, [last], {})
    received = swap(parts[last], "row", n_row, 1)
    more, more_parts, far = text_grads(*held, list(range(last))[::-1], grads)
    grads |= more
    parts |= more_parts
    sums = {last ^ 1: parts[last ^ 1] + received}
    near = image_grads(
        scale, col_extra, [grads[t] for t in range(n_row)], texts, [sums[last ^ 1]]
    )
    for q in range(1, last, 2):
        sums[q ^ 1] = parts[q ^ 1] + swap(parts[q], "row", n_row, 1)
    text_sum = halve(sums, "row", n_row, [1 << b for b in range(1, n_row.bit_length() - 1)])
    image_sum = scatter_images(near, far, "col", n_col)
    grad_scale = (jnp.sum(text_sum[block:]) + jnp.sum(image_sum[block:])) / coef[0, 0]
    return image_sum[:block], text_sum[:block], grad_scale


def solution(mesh):
    images = P(("row", "col"), None)
    texts = P(("col", "row"), None)
    return jax.shard_map(
        functools.partial(on_device, mesh.shape["row"], mesh.shape["col"]),
        mesh=mesh,
        in_specs=(images, texts, P()),
        out_specs=(images, texts, P()),
        check_vma=False,
    )
```

```python
import functools
import math

import jax
import jax.numpy as jnp
from jax import lax
from jax.experimental import pallas as pl
from jax.experimental.pallas import tpu as pltpu
from jax.sharding import PartitionSpec as P

LOG2E = 1.4426950408889634
LN2 = 0.6931471805599453
LANES = 128
VMEM = pltpu.VMEM
SMEM = pltpu.SMEM
FLOPS = 20


def swap(x, axis, n, q):
    return lax.ppermute(x, axis, [(i, i ^ q) for i in range(n)])


def gather_both(image, text, n_col, n_row):
    images = [swap(image, "col", n_col, q) for q in range(2, n_col, 2)]
    texts = [swap(text, "row", n_row, q) for q in range(1, n_row)]
    odd = [swap(image, "col", n_col, 1)]
    texts, images = lax.optimization_barrier((texts, images))
    odd += [swap(i, "col", n_col, 1) for i in images]
    return [image, *images], odd, [text, *texts]


def nt_dot(a, b):
    return lax.dot_general(a, b, (((1,), (1,)), ((), ())), preferred_element_type=jnp.float32)


def stats_kernel(n_text, n_image, odd, block, coef_ref, place_ref, *refs):
    pieces, refs = refs[:n_image], refs[n_image:]
    texts = refs[:n_text]
    before = refs[n_text:-9]
    row_ref, col_ref, images, tile, row_max, col_max, col_sum, col_dot, row_diag = refs[-9:]
    coef = coef_ref[0, 0]
    r_place, c_place = place_ref[0, 0], place_ref[0, 1]
    cols, rows = tile.shape
    col_max[...] = jnp.full(col_max.shape, -jnp.inf, jnp.float32)
    row_diag[...] = jnp.zeros(row_diag.shape, jnp.float32)
    n_col, n_row = row_ref.shape[1], col_ref.shape[1]
    for j, piece in enumerate(pieces):
        images[j * block : (j + 1) * block, :] = piece[...]

    def products(j, carry):
        at = pl.multiple_of(j * block, block)
        image = images[pl.ds(at, block), :]
        image_id = r_place * n_col + (c_place ^ (2 * j + odd))
        top = None
        for t in range(n_text):
            part = pl.ds(t * block, block)
            x = nt_dot(texts[t][...], image) * coef
            tile[part, pl.ds(at, block)] = x
            top_t = jnp.max(x, axis=0, keepdims=True)
            top = top_t if top is None else jnp.maximum(top, top_t)
            held = col_max[part, :]
            for lane in range(0, block, LANES):
                held = jnp.maximum(held, x[:, lane : lane + LANES])
            col_max[part, :] = held
        row_max[0:1, pl.ds(at, block)] = top
        for t in range(n_text):

            @pl.when(image_id == c_place * n_row + (r_place ^ t))
            def _():
                x = tile[pl.ds(t * block, block), pl.ds(at, block)]
                down = lax.broadcasted_iota(jnp.int32, x.shape, 0)
                across = lax.broadcasted_iota(jnp.int32, x.shape, 1)
                row_diag[0:1, pl.ds(at, block)] = jnp.sum(
                    jnp.where(down == across, x, 0.0), axis=0, keepdims=True
                )

        return carry

    lax.fori_loop(0, rows // block, products, 0, unroll=4)

    col_max[...] = jnp.broadcast_to(
        jnp.max(col_max[...], axis=1, keepdims=True), col_max.shape
    )

    lanes = range(0, rows, LANES)

    def exponentials(i, acc):
        part = pl.ds(pl.multiple_of(i * 8, 8), 8)
        top = col_max[part, :]
        total = dot = None
        sums, dots = [], []
        for n, lane in enumerate(lanes):
            x = tile[part, lane : lane + LANES]
            e = jnp.exp2(x - row_max[0:1, lane : lane + LANES])
            sums.append(acc[0][n] + e)
            dots.append(acc[1][n] + e * x)
            e = jnp.exp2(x - top)
            total = e if total is None else total + e
            dot = e * x if dot is None else dot + e * x
        col_sum[part, :] = total
        col_dot[part, :] = dot
        return tuple(sums), tuple(dots)

    zeros = tuple(jnp.zeros((8, LANES), jnp.float32) for _ in lanes)
    acc = lax.fori_loop(0, cols // 8, exponentials, (zeros, zeros), unroll=4)

    row_ids = lax.broadcasted_iota(jnp.int32, (n_col, block), 0)
    if before:
        placed = [before[0][i] for i in range(4)]
    else:
        placed = [jnp.zeros((n_col, block), jnp.float32)] * 4
    for j in range(rows // block):
        at = j * block
        here = row_ids == (c_place ^ (2 * j + odd))
        new = [row_max[0:1, at : at + block]]
        for which in acc:
            new.append(
                jnp.concatenate(
                    [
                        jnp.sum(which[(at + lane) // LANES], axis=0, keepdims=True)
                        for lane in range(0, block, LANES)
                    ],
                    axis=1,
                )
            )
        new.append(row_diag[0:1, at : at + block])
        placed = [jnp.where(here, n, p) for n, p in zip(new, placed)]
    for i in range(4):
        row_ref[i] = placed[i]
    row_ids = lax.broadcasted_iota(jnp.int32, (n_row, block), 0)
    placed = [jnp.zeros((n_row, block), jnp.float32)] * 3
    for t in range(n_text):
        part = pl.ds(t * block, block)
        here = row_ids == (r_place ^ t)
        new = [col_max[part, :].T[0:1, :]]
        for which in (col_sum, col_dot):
            new.append(jnp.sum(which[part, :].T, axis=0, keepdims=True))
        placed = [jnp.where(here, n, p) for n, p in zip(new, placed)]
    if before:
        placed = merged(placed, [before[1][i] for i in range(3)])
    for i in range(3):
        col_ref[i] = placed[i]


def merged(a, b):
    top = jnp.maximum(a[0], b[0])
    wa, wb = jnp.exp2(a[0] - top), jnp.exp2(b[0] - top)
    out = [top] + [a[i] * wa + b[i] * wb for i in (1, 2)]
    return out + [a[i] + b[i] for i in range(3, len(a))]


def stats(coef, place, images, texts, before, n_col):
    block, width = texts[0].shape
    rows, cols = block * len(images), block * len(texts)
    vmem = pl.BlockSpec(memory_space=VMEM)
    smem = pl.BlockSpec(memory_space=SMEM)
    return pl.pallas_call(
        functools.partial(stats_kernel, len(texts), len(images), 1 if before else 0, block),
        out_shape=(
            jax.ShapeDtypeStruct((4, n_col, block), jnp.float32),
            jax.ShapeDtypeStruct((3, len(texts), block), jnp.float32),
            jax.ShapeDtypeStruct((rows, width), jnp.bfloat16),
        ),
        in_specs=[smem, smem] + [vmem] * (len(images) + len(texts) + len(before)),
        out_specs=(vmem,) * 3,
        scratch_shapes=[
            VMEM((cols, rows), jnp.float32),
            VMEM((8, rows), jnp.float32),
            VMEM((cols, LANES), jnp.float32),
            VMEM((cols, LANES), jnp.float32),
            VMEM((cols, LANES), jnp.float32),
            VMEM((8, rows), jnp.float32),
        ],
        compiler_params=pltpu.CompilerParams(vmem_limit_bytes=4 * rows * cols + 8 * 2**20),
        cost_estimate=pl.CostEstimate(
            flops=FLOPS * 2 * rows * cols * width, bytes_accessed=0, transcendentals=0
        ),
        name="stats_odd" if before else "stats_even",
    )(coef, place, *images, *texts, *before)


def by_pairs(blocks, add):
    while len(blocks) > 1:
        blocks = [add(blocks[i], blocks[i + 1]) for i in range(0, len(blocks), 2)]
    return blocks[0]


def lse_and_mean(parts):
    mean = 0.5 * parts[2] / parts[1]
    return parts[0] + jnp.log(parts[1]) * LOG2E, mean - parts[3] if len(parts) > 3 else mean


def exchanged(row_parts, col_parts, n_col, n_row):
    rows = [swap(row_parts, "col", n_col, q) for q in range(2, n_col, 2)]
    cols = swap(col_parts, "row", n_row, 1)
    rows, cols = lax.optimization_barrier((rows, cols))
    rows = by_pairs([list(x) for x in (row_parts, *rows)], merged)
    cols = merged(list(col_parts), list(cols))
    for b in range(1, n_row.bit_length() - 1):
        cols = merged(cols, list(swap(jnp.stack(cols), "row", n_row, 1 << b)))
    rows = merged(rows, list(swap(jnp.stack(rows), "col", n_col, 1)))
    return *lse_and_mean(rows), *lse_and_mean(cols)


LEVELS = 32000
LOW = 128
BIAS = 125
EXTRA = 8
MORE = 32


def put_extra(out, extra_ref):
    n, width = extra_ref.shape
    rows = min(n, EXTRA)
    out[...] = jnp.zeros(out.shape, out.dtype)
    out[:rows, :width] = sum(extra_ref[i : i + rows, :] for i in range(0, n, rows))


def power(k):
    return jnp.exp2(k).astype(jnp.bfloat16).astype(jnp.float32)


def encode(out, value, extra):
    size, width = value.shape
    top = jnp.maximum(jnp.max(jnp.abs(value), axis=1, keepdims=True), 1e-30)
    k = jnp.ceil(jnp.log2(top))
    whole = jnp.floor(jnp.abs(value) * (power(-k) * (LEVELS - 1)) + 0.5)
    high = jnp.floor(whole * (1 / LOW))
    code = (1.0 + (whole - LOW * high) * (1 / LOW)) * jnp.exp2(high - BIAS)
    out[:size, :] = jnp.where(value < 0, -code, code).astype(jnp.bfloat16)
    half = width // 2
    first = extra[:, :half].astype(jnp.bfloat16)
    rest = extra[:, :half] - first.astype(jnp.float32)
    second = rest.astype(jnp.bfloat16)
    third = (rest - second.astype(jnp.float32)).astype(jnp.bfloat16)
    zeros = jnp.zeros((EXTRA, half), jnp.bfloat16)
    out[size : size + 2 * EXTRA, :half] = jnp.concatenate([first, second], axis=0)
    out[size : size + 2 * EXTRA, half:] = jnp.concatenate([third, zeros], axis=0)
    powers = jnp.broadcast_to(power(k), (size, LANES)).T
    out[size + 2 * EXTRA :, :] = jnp.zeros((MORE - 2 * EXTRA, width), jnp.bfloat16)
    out[size + 2 * EXTRA :, :size] = powers[: MORE - 2 * EXTRA, :].astype(jnp.bfloat16)


def decode_powers(code, size):
    powers = code[size + 2 * EXTRA :, :size].astype(jnp.float32)
    return jnp.broadcast_to(powers[0:1, :], (LANES, size)).T * (1 / (LEVELS - 1))


def decode(code, powers):
    lanes = []
    for lane in range(0, code.shape[1], LANES):
        c = code[:, lane : lane + LANES].astype(jnp.float32)
        a = jnp.abs(c)
        high = jnp.floor(jnp.log2(a))
        whole = LOW * (high + (BIAS - 1) + a * jnp.exp2(-high))
        lanes.append(jnp.where(c < 0, -whole, whole) * powers)
    return jnp.concatenate(lanes, axis=1)


def decode_extra(code, size):
    half = code.shape[1] // 2
    left = code[size : size + 2 * EXTRA, :half].astype(jnp.float32)
    right = code[size : size + 2 * EXTRA, half:].astype(jnp.float32)
    return left[:EXTRA] + left[EXTRA:] + right[:EXTRA]


def pack_text_kernel(n, base, *refs):
    codes, out, total = refs[:n], refs[n], refs[n + 1]
    size = base.shape[0] - EXTRA
    total[...] = base[:size, :]
    extra = base[size:, :]
    half = base.shape[1] // 2
    more = extra[:, :half]
    for code in codes:
        total[...] += decode(code[:size, :], decode_powers(code, size))
        more = more + decode_extra(code, size)
    encode(out, total[...], more)


def pack_text(base, codes):
    size, width = base.shape[0] - EXTRA, base.shape[1]
    vmem = pl.BlockSpec(memory_space=VMEM)
    return pl.pallas_call(
        functools.partial(pack_text_kernel, len(codes)),
        out_shape=jax.ShapeDtypeStruct((size + MORE, width), jnp.bfloat16),
        in_specs=[vmem] * (1 + len(codes)),
        out_specs=vmem,
        scratch_shapes=[VMEM((size, width), jnp.float32)],
        name="pack_text",
    )(base, *codes)


def pack_images_kernel(near, far, own, *outs):
    size = near.shape[1] - EXTRA
    own[...] = near[0] + far[0]
    for j, out in enumerate(outs, 1):
        total = near[j] + far[j]
        encode(out, total[:size], total[size:])


def pack_images(near, far):
    n, rows, width = near.shape
    vmem = pl.BlockSpec(memory_space=VMEM)
    code = jax.ShapeDtypeStruct((rows - EXTRA + MORE, width), jnp.bfloat16)
    own, *codes = pl.pallas_call(
        pack_images_kernel,
        out_shape=(jax.ShapeDtypeStruct((rows, width), jnp.float32),) + (code,) * (n - 1),
        in_specs=[vmem] * 2,
        out_specs=(vmem,) * n,
        name="pack_images",
    )(near, far)
    return own, codes


def total_kernel(n, in_order, steps, base, *refs):
    codes, before, out, extra, powers = refs[:n], refs[n:-3], *refs[-3:]
    i = pl.program_id(0)
    size, width = base.shape[0] - EXTRA, base.shape[1]
    combine = functools.partial(functools.reduce, jnp.add) if in_order else by_pairs_added

    @pl.when(i == 0)
    def _():
        for c, code in enumerate(codes):
            powers[c] = decode_powers(code, size)
        more = combine([base[size:, : width // 2]] + [decode_extra(code, size) for code in codes])
        extra[...] = sum([b[...] for b in before], more)

    part = pl.ds(pl.multiple_of(i * (size // steps), size // steps), size // steps)
    out[...] = combine(
        [base[part, :]] + [decode(code[part, :], powers[c, part, :]) for c, code in enumerate(codes)]
    )


def by_pairs_added(blocks):
    return by_pairs(blocks, jnp.add)


def total_of(base, codes, in_order, before, name):
    size, width = base.shape[0] - EXTRA, base.shape[1]
    vmem = pl.BlockSpec(memory_space=VMEM)
    steps = 4
    return pl.pallas_call(
        functools.partial(total_kernel, len(codes), in_order, steps),
        grid=(steps,),
        out_shape=(
            jax.ShapeDtypeStruct((size, width), jnp.float32),
            jax.ShapeDtypeStruct((EXTRA, width // 2), jnp.float32),
        ),
        in_specs=[vmem] * (1 + len(codes) + len(before)),
        out_specs=(pl.BlockSpec((size // steps, width), lambda i: (i, 0)), vmem),
        scratch_shapes=[VMEM((len(codes), size, LANES), jnp.float32)],
        name=name,
    )(base, *codes, *before)


def text_block(text, t, halves, row_lse, col_lse, place_ref, scale_ref, coef_ref, extra, grad_ref, out_ref, total):
    coef = coef_ref[0, 0]
    r_place, c_place = place_ref[0, 0], place_ref[0, 1]
    half, width = halves[0].shape
    n_col, n_row = row_lse.shape[0], col_lse.shape[0]
    size = text.shape[0]
    block = size
    col_lse_down = jnp.broadcast_to(col_lse[pl.ds(r_place ^ t, 1), :], (LANES, size)).T
    text_id = c_place * n_row + (r_place ^ t)
    step = 32
    lane_ids = lax.broadcasted_iota(jnp.int32, (step, LANES), 1)
    row_ids = lax.broadcasted_iota(jnp.int32, (step, LANES), 0)

    for which, images in enumerate(halves):

        def one(j, carry):
            inner = nt_dot(text[...], images[pl.ds(pl.multiple_of(j * block, block), block), :])
            at = pl.multiple_of(j * block + which * half, block)
            column = c_place ^ (2 * j + which)
            same = jnp.where(r_place * n_col + column == text_id, 1.0, 0.0)
            lse = row_lse[pl.ds(column, 1), :]
            for r in range(0, size, step):
                for lane in range(0, block, LANES):
                    x = inner[r : r + step, lane : lane + LANES] * coef
                    e = jnp.exp2(x - lse[:, lane : lane + LANES]) + jnp.exp2(
                        x - col_lse_down[r : r + step, :]
                    )
                    g = 0.5 * e
                    if lane <= r < lane + LANES:
                        g = g - jnp.where(row_ids + (r - lane) == lane_ids, same, 0.0)
                    grad_ref[r : r + step, pl.ds(at + lane, LANES)] = g.astype(jnp.bfloat16)
            return carry

        lax.fori_loop(0, half // block, one, 0, unroll=4)
    total[:size, :] = scale_ref[0, 0] * (
        jnp.dot(grad_ref[:, :half], halves[0][...], preferred_element_type=jnp.float32)
        + jnp.dot(grad_ref[:, half:], halves[1][...], preferred_element_type=jnp.float32)
    )
    put_extra(total.at[size:, :], extra)
    if t & 1:
        encode(out_ref, total[:size, :], total[size:, :])
    else:
        out_ref[...] = total[...]


def image_block(grads, texts, at, block, scale):
    total = None
    for grad, text in zip(grads, texts):
        part = lax.dot_general(
            grad[:, pl.ds(at, block)],
            text[...],
            (((0,), (0,)), ((), ())),
            preferred_element_type=jnp.float32,
        )
        total = part if total is None else total + part
    return scale * total


def text_kernel(order, n_done, block, scale_ref, coef_ref, place_ref, *refs):
    even, odd, row_lse, col_lse, row_extra, col_extra = refs[:6]
    n = len(order)
    texts, rest = refs[6 : 6 + n], refs[6 + n :]
    done_grads, done_texts, rest = rest[:n_done], rest[n_done : 2 * n_done], rest[2 * n_done :]
    grads, outs = rest[:n], rest[n : 2 * n]
    for i, t in enumerate(order):
        text_block(
            texts[i], t, (even, odd), row_lse, col_lse, place_ref, scale_ref, coef_ref, row_extra, grads[i], outs[i], rest[-1]
        )
    if n_done:
        far_ref = rest[2 * n]
        half = even.shape[0]

        def one(j, carry):
            far_ref[j, :block, :] = image_block(
                [*done_grads, *grads],
                [*done_texts, *texts],
                pl.multiple_of(j * block + half, block),
                block,
                scale_ref[0, 0],
            )
            put_extra(far_ref.at[j, block:, :], col_extra)
            return carry

        lax.fori_loop(0, half // block, one, 0)


def text_grads(scale, coef, place, even, odd, row_lse, col_lse, row_extra, col_extra, texts, order, done):
    half, width = even.shape
    block = texts[0].shape[0]
    n = len(order)
    vmem = pl.BlockSpec(memory_space=VMEM)
    smem = pl.BlockSpec(memory_space=SMEM)
    out_shape = (
        [jax.ShapeDtypeStruct((block, 2 * half), jnp.bfloat16)] * n
        + [
            jax.ShapeDtypeStruct((block + MORE, width), jnp.bfloat16)
            if t & 1
            else jax.ShapeDtypeStruct((block + EXTRA, width), jnp.float32)
            for t in order
        ]
    )
    if done:
        out_shape.append(jax.ShapeDtypeStruct((half // block, block + EXTRA, width), jnp.float32))
    operands = [even, odd, row_lse, col_lse, row_extra, col_extra, *[texts[t] for t in order]]
    operands += [done[t] for t in done] + [texts[t] for t in done]
    outs = pl.pallas_call(
        functools.partial(text_kernel, tuple(order), len(done), block),
        out_shape=tuple(out_shape),
        in_specs=[smem] * 3 + [vmem] * len(operands),
        out_specs=(vmem,) * len(out_shape),
        scratch_shapes=[VMEM((block + EXTRA, width), jnp.float32)],
        compiler_params=pltpu.CompilerParams(vmem_limit_bytes=12 * 2**20),
        cost_estimate=pl.CostEstimate(
            flops=FLOPS * 4 * n * block * 2 * half * width, bytes_accessed=0, transcendentals=0
        ),
        name=f"text_grads_{n}",
    )(scale, coef, place, *operands)
    grads = {t: outs[i] for i, t in enumerate(order)}
    parts = {t: outs[n + i] for i, t in enumerate(order)}
    return grads, parts, outs[-1]


def image_kernel(n_text, block, scale_ref, extra, *refs):
    grads, texts, out_ref = refs[:n_text], refs[n_text : 2 * n_text], refs[-1]

    def one(j, carry):
        put_extra(out_ref.at[j, block:, :], extra)
        out_ref[j, :block, :] = image_block(
            grads, texts, pl.multiple_of(j * block, block), block, scale_ref[0, 0]
        )
        return carry

    lax.fori_loop(0, out_ref.shape[0], one, 0)


def image_grads(scale, extra, grads, texts, after):
    n_text = len(grads)
    rows = grads[0].shape[1]
    block, width = texts[0].shape
    n = rows // block // 2
    vmem = pl.BlockSpec(memory_space=VMEM)
    return pl.pallas_call(
        functools.partial(image_kernel, n_text, block),
        out_shape=jax.ShapeDtypeStruct((n, block + EXTRA, width), jnp.float32),
        in_specs=[pl.BlockSpec(memory_space=SMEM)]
        + [vmem] * (2 * n_text + 1)
        + [pl.BlockSpec(memory_space=pl.ANY)] * len(after),
        out_specs=vmem,
        compiler_params=pltpu.CompilerParams(vmem_limit_bytes=12 * 2**20),
        cost_estimate=pl.CostEstimate(
            flops=FLOPS * 2 * n * block * n_text * block * width, bytes_accessed=0, transcendentals=0
        ),
        name="image_grads",
    )(scale, extra, *grads, *texts, *after)


def on_device(n_row, n_col, image_embeds, text_embeds, logit_scale):
    block = image_embeds.shape[0]
    r, c = lax.axis_index("row"), lax.axis_index("col")
    place = jnp.stack([r, c]).reshape(1, 2)
    scale = logit_scale.reshape(1, 1)
    coef = scale * LOG2E
    image_half, text_half = image_embeds.astype(jnp.bfloat16), text_embeds.astype(jnp.bfloat16)
    even, odd, texts = gather_both(image_half, text_half, n_col, n_row)
    row_parts, col_parts, even = stats(coef, place, even, texts, (), n_col)
    row_parts, col_parts, odd = stats(coef, place, odd, texts, (row_parts, col_parts), n_col)
    row_lse, row_extra, col_lse, col_extra = exchanged(row_parts, col_parts, n_col, n_row)

    held = (scale, coef, place, even, odd, row_lse, col_lse, row_extra, col_extra, texts)
    last = n_row - 1
    grads, parts, _ = text_grads(*held, [last], {})
    received = swap(parts[last], "row", n_row, 1)
    more, more_parts, far = text_grads(*held, list(range(last))[::-1], grads)
    grads |= more
    parts |= more_parts
    codes = {q: [] for q in range(0, n_row, 2)}
    codes[last ^ 1].append(received)
    after = [pack_text(parts[last ^ 1], codes[last ^ 1])] if n_row > 2 else [received]
    near = image_grads(scale, col_extra, [grads[t] for t in range(n_row)], texts, after)
    for q in range(1, last, 2):
        codes[q ^ 1].append(swap(parts[q], "row", n_row, 1))
    for b in range(1, n_row.bit_length() - 1):
        for q in [q for q in codes if q & (1 << b)]:
            code = after[0] if (b, q) == (1, last ^ 1) else pack_text(parts[q], codes[q])
            codes[q ^ (1 << b)].append(swap(code, "row", n_row, 1 << b))
            del codes[q]
    grad_text, text_extra = total_of(parts[0], codes[0], True, [], "grad_text")

    own, others = pack_images(near, swap(far, "col", n_col, 1))
    others = [swap(code, "col", n_col, 2 * j) for j, code in enumerate(others, 1)]
    grad_image, extra = total_of(own, others, False, [text_extra], "grad_image")
    return grad_image, grad_text, jnp.sum(extra) / coef[0, 0]


def solution(mesh):
    images = P(("row", "col"), None)
    texts = P(("col", "row"), None)
    return jax.shard_map(
        functools.partial(on_device, mesh.shape["row"], mesh.shape["col"]),
        mesh=mesh,
        in_specs=(images, texts, P()),
        out_specs=(images, texts, P()),
        check_vma=False,
    )
```

```python
import functools
import math

import jax
import jax.numpy as jnp
from jax import lax
from jax.experimental import pallas as pl
from jax.experimental.pallas import tpu as pltpu
from jax.sharding import PartitionSpec as P

LOG2E = 1.4426950408889634
LN2 = 0.6931471805599453
LANES = 128
VMEM = pltpu.VMEM
SMEM = pltpu.SMEM
FLOPS = 20


def swap(x, axis, n, q):
    return lax.ppermute(x, axis, [(i, i ^ q) for i in range(n)])


def gather_both(image, text, n_col, n_row):
    images = [swap(image, "col", n_col, q) for q in range(2, n_col, 2)]
    texts = [swap(text, "row", n_row, q) for q in range(1, n_row)]
    odd = [swap(image, "col", n_col, 1)]
    texts, images = lax.optimization_barrier((texts, images))
    odd += [swap(i, "col", n_col, 1) for i in images]
    return [image, *images], odd, [text, *texts]


def nt_dot(a, b):
    return lax.dot_general(a, b, (((1,), (1,)), ((), ())), preferred_element_type=jnp.float32)


def stats_kernel(n_text, n_image, odd, block, coef_ref, place_ref, *refs):
    pieces, refs = refs[:n_image], refs[n_image:]
    texts = refs[:n_text]
    before = refs[n_text:-9]
    row_ref, col_ref, images, tile, row_max, col_max, col_sum, col_dot, row_diag = refs[-9:]
    coef = coef_ref[0, 0]
    r_place, c_place = place_ref[0, 0], place_ref[0, 1]
    cols, rows = tile.shape
    col_max[...] = jnp.full(col_max.shape, -jnp.inf, jnp.float32)
    row_diag[...] = jnp.zeros(row_diag.shape, jnp.float32)
    n_col, n_row = row_ref.shape[1], col_ref.shape[1]
    for j, piece in enumerate(pieces):
        images[j * block : (j + 1) * block, :] = piece[...]

    def products(j, carry):
        at = pl.multiple_of(j * block, block)
        image = images[pl.ds(at, block), :]
        image_id = r_place * n_col + (c_place ^ (2 * j + odd))
        top = None
        for t in range(n_text):
            part = pl.ds(t * block, block)
            x = nt_dot(texts[t][...], image) * coef
            tile[part, pl.ds(at, block)] = x
            top_t = jnp.max(x, axis=0, keepdims=True)
            top = top_t if top is None else jnp.maximum(top, top_t)
            held = col_max[part, :]
            for lane in range(0, block, LANES):
                held = jnp.maximum(held, x[:, lane : lane + LANES])
            col_max[part, :] = held
        row_max[0:1, pl.ds(at, block)] = top
        for t in range(n_text):

            @pl.when(image_id == c_place * n_row + (r_place ^ t))
            def _():
                x = tile[pl.ds(t * block, block), pl.ds(at, block)]
                down = lax.broadcasted_iota(jnp.int32, x.shape, 0)
                across = lax.broadcasted_iota(jnp.int32, x.shape, 1)
                row_diag[0:1, pl.ds(at, block)] = jnp.sum(
                    jnp.where(down == across, x, 0.0), axis=0, keepdims=True
                )

        return carry

    lax.fori_loop(0, rows // block, products, 0, unroll=4)

    col_max[...] = jnp.broadcast_to(
        jnp.max(col_max[...], axis=1, keepdims=True), col_max.shape
    )

    lanes = range(0, rows, LANES)

    def exponentials(i, acc):
        part = pl.ds(pl.multiple_of(i * 8, 8), 8)
        top = col_max[part, :]
        total = dot = None
        sums, dots = [], []
        for n, lane in enumerate(lanes):
            x = tile[part, lane : lane + LANES]
            e = jnp.exp2(x - row_max[0:1, lane : lane + LANES])
            sums.append(acc[0][n] + e)
            dots.append(acc[1][n] + e * x)
            e = jnp.exp2(x - top)
            total = e if total is None else total + e
            dot = e * x if dot is None else dot + e * x
        col_sum[part, :] = total
        col_dot[part, :] = dot
        return tuple(sums), tuple(dots)

    zeros = tuple(jnp.zeros((8, LANES), jnp.float32) for _ in lanes)
    acc = lax.fori_loop(0, cols // 8, exponentials, (zeros, zeros), unroll=4)

    row_ids = lax.broadcasted_iota(jnp.int32, (n_col, block), 0)
    if before:
        placed = [before[0][i] for i in range(4)]
    else:
        placed = [jnp.zeros((n_col, block), jnp.float32)] * 4
    for j in range(rows // block):
        at = j * block
        here = row_ids == (c_place ^ (2 * j + odd))
        new = [row_max[0:1, at : at + block]]
        for which in acc:
            new.append(
                jnp.concatenate(
                    [
                        jnp.sum(which[(at + lane) // LANES], axis=0, keepdims=True)
                        for lane in range(0, block, LANES)
                    ],
                    axis=1,
                )
            )
        new.append(row_diag[0:1, at : at + block])
        placed = [jnp.where(here, n, p) for n, p in zip(new, placed)]
    for i in range(4):
        row_ref[i] = placed[i]
    row_ids = lax.broadcasted_iota(jnp.int32, (n_row, block), 0)
    placed = [jnp.zeros((n_row, block), jnp.float32)] * 3
    for t in range(n_text):
        part = pl.ds(t * block, block)
        here = row_ids == (r_place ^ t)
        new = [col_max[part, :].T[0:1, :]]
        for which in (col_sum, col_dot):
            new.append(jnp.sum(which[part, :].T, axis=0, keepdims=True))
        placed = [jnp.where(here, n, p) for n, p in zip(new, placed)]
    if before:
        placed = merged(placed, [before[1][i] for i in range(3)])
    for i in range(3):
        col_ref[i] = placed[i]


def merged(a, b):
    top = jnp.maximum(a[0], b[0])
    wa, wb = jnp.exp2(a[0] - top), jnp.exp2(b[0] - top)
    out = [top] + [a[i] * wa + b[i] * wb for i in (1, 2)]
    return out + [a[i] + b[i] for i in range(3, len(a))]


def stats(coef, place, images, texts, before, n_col):
    block, width = texts[0].shape
    rows, cols = block * len(images), block * len(texts)
    vmem = pl.BlockSpec(memory_space=VMEM)
    smem = pl.BlockSpec(memory_space=SMEM)
    return pl.pallas_call(
        functools.partial(stats_kernel, len(texts), len(images), 1 if before else 0, block),
        out_shape=(
            jax.ShapeDtypeStruct((4, n_col, block), jnp.float32),
            jax.ShapeDtypeStruct((3, len(texts), block), jnp.float32),
            jax.ShapeDtypeStruct((rows, width), jnp.bfloat16),
        ),
        in_specs=[smem, smem] + [vmem] * (len(images) + len(texts) + len(before)),
        out_specs=(vmem,) * 3,
        scratch_shapes=[
            VMEM((cols, rows), jnp.float32),
            VMEM((8, rows), jnp.float32),
            VMEM((cols, LANES), jnp.float32),
            VMEM((cols, LANES), jnp.float32),
            VMEM((cols, LANES), jnp.float32),
            VMEM((8, rows), jnp.float32),
        ],
        compiler_params=pltpu.CompilerParams(vmem_limit_bytes=4 * rows * cols + 8 * 2**20),
        cost_estimate=pl.CostEstimate(
            flops=FLOPS * 2 * rows * cols * width, bytes_accessed=0, transcendentals=0
        ),
        name="stats_odd" if before else "stats_even",
    )(coef, place, *images, *texts, *before)


def by_pairs(blocks, add):
    while len(blocks) > 1:
        blocks = [add(blocks[i], blocks[i + 1]) for i in range(0, len(blocks), 2)]
    return blocks[0]


def lse_and_mean(parts):
    mean = 0.5 * parts[2] / parts[1]
    return parts[0] + jnp.log(parts[1]) * LOG2E, mean - parts[3] if len(parts) > 3 else mean


def exchanged(row_parts, col_parts, n_col, n_row):
    rows = [swap(row_parts, "col", n_col, q) for q in range(2, n_col, 2)]
    cols = swap(col_parts, "row", n_row, 1)
    rows, cols = lax.optimization_barrier((rows, cols))
    rows = by_pairs([list(x) for x in (row_parts, *rows)], merged)
    cols = merged(list(col_parts), list(cols))
    for b in range(1, n_row.bit_length() - 1):
        cols = merged(cols, list(swap(jnp.stack(cols), "row", n_row, 1 << b)))
    rows = merged(rows, list(swap(jnp.stack(rows), "col", n_col, 1)))
    return *lse_and_mean(rows), *lse_and_mean(cols)


LEVELS = 32000
LOW = 128
BIAS = 125
EXTRA = 8
MORE = 32
STEP = 32


def put_extra(out, extra_ref):
    n, width = extra_ref.shape
    rows = min(n, EXTRA)
    out[...] = jnp.zeros(out.shape, out.dtype)
    out[:rows, :width] = sum(extra_ref[i : i + rows, :] for i in range(0, n, rows))


def power(k):
    return jnp.exp2(k).astype(jnp.bfloat16).astype(jnp.float32)


def encode(out, powers, size, slab, extra):
    width = out.shape[1]
    for r in range(0, size, STEP):
        value = slab(r)
        top = jnp.maximum(jnp.max(jnp.abs(value), axis=1, keepdims=True), 1e-30)
        k = jnp.ceil(jnp.log(top) * LOG2E)
        powers[r : r + STEP, :] = jnp.broadcast_to(power(k), (STEP, LANES))
        whole = jnp.floor(jnp.abs(value) * (power(-k) * (LEVELS - 1)) + 0.5) * (1 / LOW)
        high = jnp.floor(whole)
        code = (1.0 + (whole - high)) * jnp.exp2(high - BIAS)
        out[r : r + STEP, :] = jnp.where(value < 0, -code, code).astype(jnp.bfloat16)
    half = width // 2
    first = extra[:, :half].astype(jnp.bfloat16)
    rest = extra[:, :half] - first.astype(jnp.float32)
    second = rest.astype(jnp.bfloat16)
    third = (rest - second.astype(jnp.float32)).astype(jnp.bfloat16)
    zeros = jnp.zeros((EXTRA, half), jnp.bfloat16)
    out[size : size + 2 * EXTRA, :half] = jnp.concatenate([first, second], axis=0)
    out[size : size + 2 * EXTRA, half:] = jnp.concatenate([third, zeros], axis=0)
    out[size + 2 * EXTRA :, :] = jnp.zeros((MORE - 2 * EXTRA, width), jnp.bfloat16)
    out[size + 2 * EXTRA :, :size] = powers[...].T[: MORE - 2 * EXTRA, :].astype(jnp.bfloat16)


def decode_powers(code, size):
    powers = code[size + 2 * EXTRA :, :size].astype(jnp.float32)
    return jnp.broadcast_to(powers[0:1, :], (LANES, size)).T * (LOW / (LEVELS - 1))


def decode(code, powers, r):
    lanes = []
    for lane in range(0, code.shape[1], LANES):
        c = code[r : r + STEP, lane : lane + LANES].astype(jnp.float32)
        a = jnp.abs(c)
        high = jnp.floor(jnp.log(a) * LOG2E)
        whole = (high + (BIAS - 1)) + a * jnp.exp2(-high)
        lanes.append(jnp.where(c < 0, -whole, whole) * powers[r : r + STEP, :])
    return jnp.concatenate(lanes, axis=1)


def decode_extra(code, size):
    half = code.shape[1] // 2
    left = code[size : size + 2 * EXTRA, :half].astype(jnp.float32)
    right = code[size : size + 2 * EXTRA, half:].astype(jnp.float32)
    return left[:EXTRA] + left[EXTRA:] + right[:EXTRA]


def pack_text_kernel(n, base, *refs):
    codes, out, powers, received = refs[:n], *refs[n:]
    size, half = base.shape[0] - EXTRA, base.shape[1] // 2
    more = base[size:, :half]
    for c, code in enumerate(codes):
        received[c] = decode_powers(code, size)
        more = more + decode_extra(code, size)

    def slab(r):
        value = base[r : r + STEP, :]
        for c, code in enumerate(codes):
            value = value + decode(code, received.at[c], r)
        return value

    encode(out, powers, size, slab, more)


def pack_text(base, codes):
    size, width = base.shape[0] - EXTRA, base.shape[1]
    vmem = pl.BlockSpec(memory_space=VMEM)
    return pl.pallas_call(
        functools.partial(pack_text_kernel, len(codes)),
        out_shape=jax.ShapeDtypeStruct((size + MORE, width), jnp.bfloat16),
        in_specs=[vmem] * (1 + len(codes)),
        out_specs=vmem,
        scratch_shapes=[VMEM((size, LANES), jnp.float32), VMEM((len(codes), size, LANES), jnp.float32)],
        compiler_params=pltpu.CompilerParams(vmem_limit_bytes=6 * 2**20),
        name="pack_text",
    )(base, *codes)


def pack_images_kernel(near, far, own, *refs):
    outs, powers = refs[:-1], refs[-1]
    size = near.shape[1] - EXTRA
    own[...] = near[0] + far[0]
    for j, out in enumerate(outs, 1):
        encode(
            out,
            powers.at[j - 1],
            size,
            lambda r, j=j: near[j, r : r + STEP, :] + far[j, r : r + STEP, :],
            near[j, size:, :] + far[j, size:, :],
        )


def pack_images(near, far):
    n, rows, width = near.shape
    size = rows - EXTRA
    vmem = pl.BlockSpec(memory_space=VMEM)
    code = jax.ShapeDtypeStruct((size + MORE, width), jnp.bfloat16)
    own, *codes = pl.pallas_call(
        pack_images_kernel,
        out_shape=(jax.ShapeDtypeStruct((rows, width), jnp.float32),) + (code,) * (n - 1),
        in_specs=[vmem] * 2,
        out_specs=(vmem,) * n,
        scratch_shapes=[VMEM((n - 1, size, LANES), jnp.float32)],
        compiler_params=pltpu.CompilerParams(vmem_limit_bytes=6 * 2**20),
        name="pack_images",
    )(near, far)
    return own, codes


def total_kernel(n, in_order, coef_ref, base, *refs):
    codes, before = refs[:n], refs[n:-6]
    out, extra, scalar, value, powers, sems = refs[-6:]
    size, width = base.shape[0] - EXTRA, base.shape[1]
    combine = functools.partial(functools.reduce, jnp.add) if in_order else by_pairs_added
    for c, code in enumerate(codes):
        powers[c] = decode_powers(code, size)
    copies = []
    steps = sems.shape[0]
    for i in range(steps):
        part = pl.ds(i * (size // steps), size // steps)
        for r in range(i * (size // steps), (i + 1) * (size // steps), STEP):
            value[r : r + STEP, :] = combine(
                [base[r : r + STEP, :]] + [decode(code, powers.at[c], r) for c, code in enumerate(codes)]
            )
        copies.append(pltpu.make_async_copy(value.at[part], out.at[part], sems.at[i]))
        copies[-1].start()
    more = combine([base[size:, : width // 2]] + [decode_extra(code, size) for code in codes])
    more = sum([b[...] for b in before], more)
    extra[...] = more
    scalar[0, 0] = jnp.sum(more) / coef_ref[0, 0]
    for copy in copies:
        copy.wait()


def by_pairs_added(blocks):
    return by_pairs(blocks, jnp.add)


def total_of(coef, base, codes, in_order, before, name):
    size, width = base.shape[0] - EXTRA, base.shape[1]
    vmem = pl.BlockSpec(memory_space=VMEM)
    smem = pl.BlockSpec(memory_space=SMEM)
    return pl.pallas_call(
        functools.partial(total_kernel, len(codes), in_order),
        out_shape=(
            jax.ShapeDtypeStruct((size, width), jnp.float32),
            jax.ShapeDtypeStruct((EXTRA, width // 2), jnp.float32),
            jax.ShapeDtypeStruct((1, 1), jnp.float32),
        ),
        in_specs=[smem] + [vmem] * (1 + len(codes) + len(before)),
        out_specs=(pl.BlockSpec(memory_space=pl.ANY), vmem, smem),
        scratch_shapes=[
            VMEM((size, width), jnp.float32),
            VMEM((len(codes), size, LANES), jnp.float32),
            pltpu.SemaphoreType.DMA((4,)),
        ],
        compiler_params=pltpu.CompilerParams(vmem_limit_bytes=8 * 2**20),
        name=name,
    )(coef, base, *codes, *before)


def text_block(text, t, halves, row_lse, col_lse, place_ref, scale_ref, coef_ref, extra, grad_ref, out_ref, total, powers):
    coef = coef_ref[0, 0]
    r_place, c_place = place_ref[0, 0], place_ref[0, 1]
    half, width = halves[0].shape
    n_col, n_row = row_lse.shape[0], col_lse.shape[0]
    size = text.shape[0]
    block = size
    col_lse_down = jnp.broadcast_to(col_lse[pl.ds(r_place ^ t, 1), :], (LANES, size)).T
    text_id = c_place * n_row + (r_place ^ t)
    step = 32
    lane_ids = lax.broadcasted_iota(jnp.int32, (step, LANES), 1)
    row_ids = lax.broadcasted_iota(jnp.int32, (step, LANES), 0)

    for which, images in enumerate(halves):

        def one(j, carry):
            inner = nt_dot(text[...], images[pl.ds(pl.multiple_of(j * block, block), block), :])
            at = pl.multiple_of(j * block + which * half, block)
            column = c_place ^ (2 * j + which)
            same = jnp.where(r_place * n_col + column == text_id, 1.0, 0.0)
            lse = row_lse[pl.ds(column, 1), :]
            for r in range(0, size, step):
                for lane in range(0, block, LANES):
                    x = inner[r : r + step, lane : lane + LANES] * coef
                    e = jnp.exp2(x - lse[:, lane : lane + LANES]) + jnp.exp2(
                        x - col_lse_down[r : r + step, :]
                    )
                    g = 0.5 * e
                    if lane <= r < lane + LANES:
                        g = g - jnp.where(row_ids + (r - lane) == lane_ids, same, 0.0)
                    grad_ref[r : r + step, pl.ds(at + lane, LANES)] = g.astype(jnp.bfloat16)
            return carry

        lax.fori_loop(0, half // block, one, 0, unroll=4)
    total[:size, :] = scale_ref[0, 0] * (
        jnp.dot(grad_ref[:, :half], halves[0][...], preferred_element_type=jnp.float32)
        + jnp.dot(grad_ref[:, half:], halves[1][...], preferred_element_type=jnp.float32)
    )
    put_extra(total.at[size:, :], extra)
    if t & 1:
        encode(out_ref, powers, size, lambda r: total[r : r + STEP, :], total[size:, :])
    else:
        out_ref[...] = total[...]


def image_block(grads, texts, at, block, scale):
    total = None
    for grad, text in zip(grads, texts):
        part = lax.dot_general(
            grad[:, pl.ds(at, block)],
            text[...],
            (((0,), (0,)), ((), ())),
            preferred_element_type=jnp.float32,
        )
        total = part if total is None else total + part
    return scale * total


def text_kernel(order, n_done, block, scale_ref, coef_ref, place_ref, *refs):
    even, odd, row_lse, col_lse, row_extra, col_extra = refs[:6]
    n = len(order)
    texts, rest = refs[6 : 6 + n], refs[6 + n :]
    done_grads, done_texts, rest = rest[:n_done], rest[n_done : 2 * n_done], rest[2 * n_done :]
    grads, outs = rest[:n], rest[n : 2 * n]
    for i, t in enumerate(order):
        text_block(
            texts[i], t, (even, odd), row_lse, col_lse, place_ref, scale_ref, coef_ref, row_extra, grads[i], outs[i], *rest[-2:]
        )
    if n_done:
        far_ref = rest[2 * n]
        half = even.shape[0]

        def one(j, carry):
            far_ref[j, :block, :] = image_block(
                [*done_grads, *grads],
                [*done_texts, *texts],
                pl.multiple_of(j * block + half, block),
                block,
                scale_ref[0, 0],
            )
            put_extra(far_ref.at[j, block:, :], col_extra)
            return carry

        lax.fori_loop(0, half // block, one, 0)


def text_grads(scale, coef, place, even, odd, row_lse, col_lse, row_extra, col_extra, texts, order, done):
    half, width = even.shape
    block = texts[0].shape[0]
    n = len(order)
    vmem = pl.BlockSpec(memory_space=VMEM)
    smem = pl.BlockSpec(memory_space=SMEM)
    out_shape = (
        [jax.ShapeDtypeStruct((block, 2 * half), jnp.bfloat16)] * n
        + [
            jax.ShapeDtypeStruct((block + MORE, width), jnp.bfloat16)
            if t & 1
            else jax.ShapeDtypeStruct((block + EXTRA, width), jnp.float32)
            for t in order
        ]
    )
    if done:
        out_shape.append(jax.ShapeDtypeStruct((half // block, block + EXTRA, width), jnp.float32))
    operands = [even, odd, row_lse, col_lse, row_extra, col_extra, *[texts[t] for t in order]]
    operands += [done[t] for t in done] + [texts[t] for t in done]
    outs = pl.pallas_call(
        functools.partial(text_kernel, tuple(order), len(done), block),
        out_shape=tuple(out_shape),
        in_specs=[smem] * 3 + [vmem] * len(operands),
        out_specs=(vmem,) * len(out_shape),
        scratch_shapes=[
            VMEM((block + EXTRA, width), jnp.float32),
            VMEM((block, LANES), jnp.float32),
        ],
        compiler_params=pltpu.CompilerParams(vmem_limit_bytes=12 * 2**20),
        cost_estimate=pl.CostEstimate(
            flops=FLOPS * 4 * n * block * 2 * half * width, bytes_accessed=0, transcendentals=0
        ),
        name=f"text_grads_{n}",
    )(scale, coef, place, *operands)
    grads = {t: outs[i] for i, t in enumerate(order)}
    parts = {t: outs[n + i] for i, t in enumerate(order)}
    return grads, parts, outs[-1]


def image_kernel(n_text, block, scale_ref, extra, *refs):
    grads, texts, out_ref = refs[:n_text], refs[n_text : 2 * n_text], refs[-1]

    def one(j, carry):
        put_extra(out_ref.at[j, block:, :], extra)
        out_ref[j, :block, :] = image_block(
            grads, texts, pl.multiple_of(j * block, block), block, scale_ref[0, 0]
        )
        return carry

    lax.fori_loop(0, out_ref.shape[0], one, 0)


def image_grads(scale, extra, grads, texts, after):
    n_text = len(grads)
    rows = grads[0].shape[1]
    block, width = texts[0].shape
    n = rows // block // 2
    vmem = pl.BlockSpec(memory_space=VMEM)
    return pl.pallas_call(
        functools.partial(image_kernel, n_text, block),
        out_shape=jax.ShapeDtypeStruct((n, block + EXTRA, width), jnp.float32),
        in_specs=[pl.BlockSpec(memory_space=SMEM)]
        + [vmem] * (2 * n_text + 1)
        + [pl.BlockSpec(memory_space=pl.ANY)] * len(after),
        out_specs=vmem,
        compiler_params=pltpu.CompilerParams(vmem_limit_bytes=12 * 2**20),
        cost_estimate=pl.CostEstimate(
            flops=FLOPS * 2 * n * block * n_text * block * width, bytes_accessed=0, transcendentals=0
        ),
        name="image_grads",
    )(scale, extra, *grads, *texts, *after)


def on_device(n_row, n_col, image_embeds, text_embeds, logit_scale):
    block = image_embeds.shape[0]
    r, c = lax.axis_index("row"), lax.axis_index("col")
    place = jnp.stack([r, c]).reshape(1, 2)
    scale = logit_scale.reshape(1, 1)
    coef = scale * LOG2E
    image_half, text_half = image_embeds.astype(jnp.bfloat16), text_embeds.astype(jnp.bfloat16)
    even, odd, texts = gather_both(image_half, text_half, n_col, n_row)
    row_parts, col_parts, even = stats(coef, place, even, texts, (), n_col)
    row_parts, col_parts, odd = stats(coef, place, odd, texts, (row_parts, col_parts), n_col)
    row_lse, row_extra, col_lse, col_extra = exchanged(row_parts, col_parts, n_col, n_row)

    held = (scale, coef, place, even, odd, row_lse, col_lse, row_extra, col_extra, texts)
    last = n_row - 1
    grads, parts, _ = text_grads(*held, [last], {})
    received = swap(parts[last], "row", n_row, 1)
    more, more_parts, far = text_grads(*held, list(range(last))[::-1], grads)
    grads |= more
    parts |= more_parts
    codes = {q: [] for q in range(0, n_row, 2)}
    codes[last ^ 1].append(received)
    after = [pack_text(parts[last ^ 1], codes[last ^ 1])] if n_row > 2 else [received]
    near = image_grads(scale, col_extra, [grads[t] for t in range(n_row)], texts, after)
    for q in range(1, last, 2):
        codes[q ^ 1].append(swap(parts[q], "row", n_row, 1))
    for b in range(1, n_row.bit_length() - 1):
        for q in [q for q in codes if q & (1 << b)]:
            code = after[0] if (b, q) == (1, last ^ 1) else pack_text(parts[q], codes[q])
            codes[q ^ (1 << b)].append(swap(code, "row", n_row, 1 << b))
            del codes[q]
    grad_text, text_extra, _ = total_of(coef, parts[0], codes[0], True, [], "grad_text")

    own, others = pack_images(near, swap(far, "col", n_col, 1))
    others = [swap(code, "col", n_col, 2 * j) for j, code in enumerate(others, 1)]
    grad_image, _, grad_scale = total_of(coef, own, others, False, [text_extra], "grad_image")
    return grad_image, grad_text, grad_scale.reshape(())


def solution(mesh):
    images = P(("row", "col"), None)
    texts = P(("col", "row"), None)
    return jax.shard_map(
        functools.partial(on_device, mesh.shape["row"], mesh.shape["col"]),
        mesh=mesh,
        in_specs=(images, texts, P()),
        out_specs=(images, texts, P()),
        check_vma=False,
    )
```

```python
import functools
import math

import jax
import jax.numpy as jnp
from jax import lax
from jax.experimental import pallas as pl
from jax.experimental.pallas import tpu as pltpu
from jax.sharding import PartitionSpec as P

LOG2E = 1.4426950408889634
LN2 = 0.6931471805599453
LANES = 128
VMEM = pltpu.VMEM
SMEM = pltpu.SMEM
FLOPS = 20


def swap(x, axis, n, q):
    return lax.ppermute(x, axis, [(i, i ^ q) for i in range(n)])


def gather_both(image, text, n_col, n_row):
    line = n_row == 4
    images = [swap(image, "col", n_col, q) for q in range(2, n_col, 2)]
    texts = [swap(text, "row", n_row, q) for q in range(1, 3 if line else n_row)]
    images, texts, text = lax.optimization_barrier((images, texts, text))
    odd = [swap(i, "col", n_col, 1) for i in (image, *images)]
    if line:
        middle = lax.ppermute(text, "row", [(1, 2), (2, 1)])
        return [image, *images], odd, [text, *texts], [middle, lax.ppermute(texts[1], "row", [(1, 0), (2, 3)])]
    return [image, *images], odd, [text, *texts[:-1]], texts[-1:]


def nt_dot(a, b):
    return lax.dot_general(a, b, (((1,), (1,)), ((), ())), preferred_element_type=jnp.float32)


def stats_kernel(first, n_text, block, coef_ref, place_ref, *refs):
    texts, refs = refs[:n_text], refs[n_text:]
    coef = coef_ref[0, 0]
    r_place, c_place = place_ref[0, 0], place_ref[0, 1]
    *refs, row_max, col_max, col_sum, col_dot, row_diag = refs
    if first:
        *refs, even, odd, row_ref, col_ref, tile = refs
        halves = (even, odd)
        each = len(refs) // 2
        for i, piece in enumerate(refs):
            at = (i % each) * block
            halves[i // each][at : at + block, :] = piece[...]
        before = None
    else:
        even, odd, *before, last, row_ref, col_ref, tile = refs
        halves = (even, odd)
        last[...] = functools.reduce(jnp.add, [text[...] for text in texts])
        texts, n_text = [last], 1
    cols, rows = tile.shape
    half = rows // 2
    lead = 0 if first else col_ref.shape[1] - n_text
    col_max[...] = jnp.full(col_max.shape, -jnp.inf, jnp.float32)
    row_diag[...] = jnp.zeros(row_diag.shape, jnp.float32)
    n_col, n_row = row_ref.shape[1], col_ref.shape[1]

    for which, images in enumerate(halves):

        def products(j, carry):
            image = images[pl.ds(pl.multiple_of(j * block, block), block), :]
            at = pl.multiple_of(j * block + which * half, block)
            image_id = r_place * n_col + (c_place ^ (2 * j + which))
            top = None
            for t in range(n_text):
                part = pl.ds(t * block, block)
                x = nt_dot(texts[t][...], image) * coef
                tile[part, pl.ds(at, block)] = x
                top_t = jnp.max(x, axis=0, keepdims=True)
                top = top_t if top is None else jnp.maximum(top, top_t)
                held = col_max[part, :]
                for lane in range(0, block, LANES):
                    held = jnp.maximum(held, x[:, lane : lane + LANES])
                col_max[part, :] = held
            row_max[0:1, pl.ds(at, block)] = top
            for t in range(n_text):

                @pl.when(image_id == c_place * n_row + (r_place ^ (lead + t)))
                def _():
                    x = tile[pl.ds(t * block, block), pl.ds(at, block)]
                    down = lax.broadcasted_iota(jnp.int32, x.shape, 0)
                    across = lax.broadcasted_iota(jnp.int32, x.shape, 1)
                    row_diag[0:1, pl.ds(at, block)] = jnp.sum(
                        jnp.where(down == across, x, 0.0), axis=0, keepdims=True
                    )

            return carry

        lax.fori_loop(0, half // block, products, 0, unroll=4)

    col_max[...] = jnp.broadcast_to(
        jnp.max(col_max[...], axis=1, keepdims=True), col_max.shape
    )
    sums = []
    for which in range(2):
        lanes = range(which * half, (which + 1) * half, LANES)

        def exponentials(i, acc):
            part = pl.ds(pl.multiple_of(i * 8, 8), 8)
            top = col_max[part, :]
            total = col_sum[part, :] if which else None
            dot = col_dot[part, :] if which else None
            new = [], []
            for n, lane in enumerate(lanes):
                x = tile[part, lane : lane + LANES]
                e = jnp.exp2(x - row_max[0:1, lane : lane + LANES])
                new[0].append(acc[0][n] + e)
                new[1].append(acc[1][n] + e * x)
                e = jnp.exp2(x - top)
                total = e if total is None else total + e
                dot = e * x if dot is None else dot + e * x
            col_sum[part, :] = total
            col_dot[part, :] = dot
            return tuple(new[0]), tuple(new[1])

        zeros = tuple(jnp.zeros((8, LANES), jnp.float32) for _ in lanes)
        sums.append(lax.fori_loop(0, cols // 8, exponentials, (zeros, zeros), unroll=4))

    row_ids = lax.broadcasted_iota(jnp.int32, (n_col, block), 0)
    placed = [jnp.zeros((n_col, block), jnp.float32)] * 4
    for q in range(n_col):
        at = (q // 2) * block
        here = row_ids == (c_place ^ q)
        new = [row_max[0:1, at + (q % 2) * half : at + (q % 2) * half + block]]
        for which in sums[q % 2]:
            new.append(
                jnp.concatenate(
                    [
                        jnp.sum(which[(at + lane) // LANES], axis=0, keepdims=True)
                        for lane in range(0, block, LANES)
                    ],
                    axis=1,
                )
            )
        new.append(row_diag[0:1, at + (q % 2) * half : at + (q % 2) * half + block])
        placed = [jnp.where(here, n, p) for n, p in zip(new, placed)]
    if before:
        placed = merged(placed, [before[0][i] for i in range(4)])
    for i in range(4):
        row_ref[i] = placed[i]
    row_ids = lax.broadcasted_iota(jnp.int32, (n_row, block), 0)
    placed = [before[1][i] if before else jnp.zeros((n_row, block), jnp.float32) for i in range(3)]
    for t in range(n_text):
        part = pl.ds(t * block, block)
        here = row_ids == (r_place ^ (lead + t))
        new = [col_max[part, :].T[0:1, :]]
        for which in (col_sum, col_dot):
            new.append(jnp.sum(which[part, :].T, axis=0, keepdims=True))
        placed = [jnp.where(here, n, p) for n, p in zip(new, placed)]
    for i in range(3):
        col_ref[i] = placed[i]


def stats(coef, place, texts, images, before, n_col, n_row, keep):
    block, width = texts[0].shape
    first = not before
    rows, cols = block * n_col, block * (len(texts) if first else 1)
    vmem = pl.BlockSpec(memory_space=VMEM)
    smem = pl.BlockSpec(memory_space=SMEM)
    half = jax.ShapeDtypeStruct((rows // 2, width), jnp.bfloat16)
    out_shape = [half, half] if first else [jax.ShapeDtypeStruct((block, width), jnp.bfloat16)]
    out_shape += [
        jax.ShapeDtypeStruct((4, n_col, block), jnp.float32),
        jax.ShapeDtypeStruct((3, n_row, block), jnp.float32),
    ]
    scratch = [
        VMEM((8, rows), jnp.float32),
        VMEM((cols, LANES), jnp.float32),
        VMEM((cols, LANES), jnp.float32),
        VMEM((cols, LANES), jnp.float32),
        VMEM((8, rows), jnp.float32),
    ]
    if keep:
        out_shape.append(jax.ShapeDtypeStruct((cols, rows), jnp.float32))
    else:
        scratch.insert(0, VMEM((cols, rows), jnp.float32))
    return pl.pallas_call(
        functools.partial(stats_kernel, first, len(texts), block),
        out_shape=tuple(out_shape),
        in_specs=[smem, smem] + [vmem] * (len(texts) + len(images) + len(before)),
        out_specs=(vmem,) * len(out_shape),
        scratch_shapes=scratch,
        compiler_params=pltpu.CompilerParams(
            vmem_limit_bytes=(0 if keep else 4 * rows * cols) + 8 * 2**20
        ),
        cost_estimate=pl.CostEstimate(
            flops=FLOPS * 2 * rows * cols * width, bytes_accessed=0, transcendentals=0
        ),
        name="stats" if first else "stats_last",
    )(coef, place, *texts, *images, *before)


def merged(a, b):
    top = jnp.maximum(a[0], b[0])
    wa, wb = jnp.exp2(a[0] - top), jnp.exp2(b[0] - top)
    out = [top] + [a[i] * wa + b[i] * wb for i in (1, 2)]
    return out + [a[i] + b[i] for i in range(3, len(a))]


def by_pairs(blocks, add):
    while len(blocks) > 1:
        blocks = [add(blocks[i], blocks[i + 1]) for i in range(0, len(blocks), 2)]
    return blocks[0]


def lse_and_mean(parts):
    mean = 0.5 * parts[2] / parts[1]
    return parts[0] + jnp.log(parts[1]) * LOG2E, mean - parts[3] if len(parts) > 3 else mean


def exchanged(row_parts, col_parts, n_col, n_row):
    rows = [swap(row_parts, "col", n_col, q) for q in range(2, n_col, 2)]
    cols = swap(col_parts, "row", n_row, 1)
    rows, cols = lax.optimization_barrier((rows, cols))
    rows = by_pairs([list(x) for x in (row_parts, *rows)], merged)
    cols = merged(list(col_parts), list(cols))
    for b in range(1, n_row.bit_length() - 1):
        cols = merged(cols, list(swap(jnp.stack(cols), "row", n_row, 1 << b)))
    rows = merged(rows, list(swap(jnp.stack(rows), "col", n_col, 1)))
    return *lse_and_mean(rows), *lse_and_mean(cols)


LEVELS = 32000
LOW = 128
BIAS = 125
EXTRA = 8
MORE = 32
STEP = 32


def put_extra(out, extra_ref):
    n, width = extra_ref.shape
    rows = min(n, EXTRA)
    out[...] = jnp.zeros(out.shape, out.dtype)
    out[:rows, :width] = sum(extra_ref[i : i + rows, :] for i in range(0, n, rows))


def power(k):
    return jnp.exp2(k).astype(jnp.bfloat16).astype(jnp.float32)


def encode(out, powers, size, slab, extra):
    width = out.shape[1]
    for r in range(0, size, STEP):
        value = slab(r)
        top = jnp.maximum(jnp.max(jnp.abs(value), axis=1, keepdims=True), 1e-30)
        k = jnp.ceil(jnp.log(top) * LOG2E)
        powers[r : r + STEP, :] = jnp.broadcast_to(power(k), (STEP, LANES))
        whole = jnp.floor(jnp.abs(value) * (power(-k) * (LEVELS - 1)) + 0.5) * (1 / LOW)
        high = jnp.floor(whole)
        code = (1.0 + (whole - high)) * jnp.exp2(high - BIAS)
        out[r : r + STEP, :] = jnp.where(value < 0, -code, code).astype(jnp.bfloat16)
    half = width // 2
    first = extra[:, :half].astype(jnp.bfloat16)
    rest = extra[:, :half] - first.astype(jnp.float32)
    second = rest.astype(jnp.bfloat16)
    third = (rest - second.astype(jnp.float32)).astype(jnp.bfloat16)
    zeros = jnp.zeros((EXTRA, half), jnp.bfloat16)
    out[size : size + 2 * EXTRA, :half] = jnp.concatenate([first, second], axis=0)
    out[size : size + 2 * EXTRA, half:] = jnp.concatenate([third, zeros], axis=0)
    out[size + 2 * EXTRA :, :] = jnp.zeros((MORE - 2 * EXTRA, width), jnp.bfloat16)
    out[size + 2 * EXTRA :, :size] = powers[...].T[: MORE - 2 * EXTRA, :].astype(jnp.bfloat16)


def decode_powers(code, size):
    powers = code[size + 2 * EXTRA :, :size].astype(jnp.float32)
    return jnp.broadcast_to(powers[0:1, :], (LANES, size)).T * (LOW / (LEVELS - 1))


def decode(code, powers, r):
    lanes = []
    for lane in range(0, code.shape[1], LANES):
        c = code[r : r + STEP, lane : lane + LANES].astype(jnp.float32)
        a = jnp.abs(c)
        high = jnp.floor(jnp.log(a) * LOG2E)
        whole = (high + (BIAS - 1)) + a * jnp.exp2(-high)
        lanes.append(jnp.where(c < 0, -whole, whole) * powers[r : r + STEP, :])
    return jnp.concatenate(lanes, axis=1)


def decode_extra(code, size):
    half = code.shape[1] // 2
    left = code[size : size + 2 * EXTRA, :half].astype(jnp.float32)
    right = code[size : size + 2 * EXTRA, half:].astype(jnp.float32)
    return left[:EXTRA] + left[EXTRA:] + right[:EXTRA]


def pack_text_kernel(n, base, *refs):
    codes, out, powers, received = refs[:n], *refs[n:]
    size, half = base.shape[0] - EXTRA, base.shape[1] // 2
    more = base[size:, :half]
    for c, code in enumerate(codes):
        received[c] = decode_powers(code, size)
        more = more + decode_extra(code, size)

    def slab(r):
        value = base[r : r + STEP, :]
        for c, code in enumerate(codes):
            value = value + decode(code, received.at[c], r)
        return value

    encode(out, powers, size, slab, more)


def pack_text(base, codes):
    size, width = base.shape[0] - EXTRA, base.shape[1]
    vmem = pl.BlockSpec(memory_space=VMEM)
    return pl.pallas_call(
        functools.partial(pack_text_kernel, len(codes)),
        out_shape=jax.ShapeDtypeStruct((size + MORE, width), jnp.bfloat16),
        in_specs=[vmem] * (1 + len(codes)),
        out_specs=vmem,
        scratch_shapes=[VMEM((size, LANES), jnp.float32), VMEM((len(codes), size, LANES), jnp.float32)],
        compiler_params=pltpu.CompilerParams(vmem_limit_bytes=6 * 2**20),
        name="pack_text",
    )(base, *codes)


def pack_images_kernel(near, far, own, *refs):
    outs, powers = refs[:-1], refs[-1]
    size = near.shape[1] - EXTRA
    own[...] = near[0] + far[0]
    for j, out in enumerate(outs, 1):
        encode(
            out,
            powers.at[j - 1],
            size,
            lambda r, j=j: near[j, r : r + STEP, :] + far[j, r : r + STEP, :],
            near[j, size:, :] + far[j, size:, :],
        )


def pack_images(near, far):
    n, rows, width = near.shape
    size = rows - EXTRA
    vmem = pl.BlockSpec(memory_space=VMEM)
    code = jax.ShapeDtypeStruct((size + MORE, width), jnp.bfloat16)
    own, *codes = pl.pallas_call(
        pack_images_kernel,
        out_shape=(jax.ShapeDtypeStruct((rows, width), jnp.float32),) + (code,) * (n - 1),
        in_specs=[vmem] * 2,
        out_specs=(vmem,) * n,
        scratch_shapes=[VMEM((n - 1, size, LANES), jnp.float32)],
        compiler_params=pltpu.CompilerParams(vmem_limit_bytes=6 * 2**20),
        name="pack_images",
    )(near, far)
    return own, codes


def total_kernel(n, in_order, coef_ref, base, *refs):
    codes, before = refs[:n], refs[n:-6]
    out, extra, scalar, value, powers, sems = refs[-6:]
    size, width = base.shape[0] - EXTRA, base.shape[1]
    combine = functools.partial(functools.reduce, jnp.add) if in_order else by_pairs_added
    for c, code in enumerate(codes):
        powers[c] = decode_powers(code, size)
    copies = []
    steps = sems.shape[0]
    for i in range(steps):
        part = pl.ds(i * (size // steps), size // steps)
        for r in range(i * (size // steps), (i + 1) * (size // steps), STEP):
            value[r : r + STEP, :] = combine(
                [base[r : r + STEP, :]] + [decode(code, powers.at[c], r) for c, code in enumerate(codes)]
            )
        copies.append(pltpu.make_async_copy(value.at[part], out.at[part], sems.at[i]))
        copies[-1].start()
    more = combine([base[size:, : width // 2]] + [decode_extra(code, size) for code in codes])
    more = sum([b[...] for b in before], more)
    extra[...] = more
    scalar[0, 0] = jnp.sum(more) / coef_ref[0, 0]
    for copy in copies:
        copy.wait()


def by_pairs_added(blocks):
    return by_pairs(blocks, jnp.add)


def total_of(coef, base, codes, in_order, before, name):
    size, width = base.shape[0] - EXTRA, base.shape[1]
    vmem = pl.BlockSpec(memory_space=VMEM)
    smem = pl.BlockSpec(memory_space=SMEM)
    return pl.pallas_call(
        functools.partial(total_kernel, len(codes), in_order),
        out_shape=(
            jax.ShapeDtypeStruct((size, width), jnp.float32),
            jax.ShapeDtypeStruct((EXTRA, width // 2), jnp.float32),
            jax.ShapeDtypeStruct((1, 1), jnp.float32),
        ),
        in_specs=[smem] + [vmem] * (1 + len(codes) + len(before)),
        out_specs=(pl.BlockSpec(memory_space=pl.ANY), vmem, smem),
        scratch_shapes=[
            VMEM((size, width), jnp.float32),
            VMEM((len(codes), size, LANES), jnp.float32),
            pltpu.SemaphoreType.DMA((4,)),
        ],
        compiler_params=pltpu.CompilerParams(vmem_limit_bytes=8 * 2**20),
        name=name,
    )(coef, base, *codes, *before)


def text_block(text, tile, t, halves, row_lse, col_lse, place_ref, scale_ref, coef_ref, extra, grad_ref, out_ref, total, powers):
    coef = coef_ref[0, 0]
    r_place, c_place = place_ref[0, 0], place_ref[0, 1]
    half, width = halves[0].shape
    n_col, n_row = row_lse.shape[0], col_lse.shape[0]
    size = text.shape[0]
    block = size
    col_lse_down = jnp.broadcast_to(col_lse[pl.ds(r_place ^ t, 1), :], (LANES, size)).T
    text_id = c_place * n_row + (r_place ^ t)
    step = 32
    lane_ids = lax.broadcasted_iota(jnp.int32, (step, LANES), 1)
    row_ids = lax.broadcasted_iota(jnp.int32, (step, LANES), 0)

    for which, images in enumerate(halves):

        def one(j, carry):
            at = pl.multiple_of(j * block + which * half, block)
            if tile is None:
                image = images[pl.ds(pl.multiple_of(j * block, block), block), :]
                xs = nt_dot(text[...], image) * coef
            column = c_place ^ (2 * j + which)
            same = jnp.where(r_place * n_col + column == text_id, 1.0, 0.0)
            lse = row_lse[pl.ds(column, 1), :]
            for r in range(0, size, step):
                for lane in range(0, block, LANES):
                    if tile is None:
                        x = xs[r : r + step, lane : lane + LANES]
                    else:
                        x = tile[r : r + step, pl.ds(at + lane, LANES)]
                    e = jnp.exp2(x - lse[:, lane : lane + LANES]) + jnp.exp2(
                        x - col_lse_down[r : r + step, :]
                    )
                    g = 0.5 * e
                    if lane <= r < lane + LANES:
                        g = g - jnp.where(row_ids + (r - lane) == lane_ids, same, 0.0)
                    grad_ref[r : r + step, pl.ds(at + lane, LANES)] = g.astype(jnp.bfloat16)
            return carry

        lax.fori_loop(0, half // block, one, 0, unroll=4)
    total[:size, :] = scale_ref[0, 0] * (
        jnp.dot(grad_ref[:, :half], halves[0][...], preferred_element_type=jnp.float32)
        + jnp.dot(grad_ref[:, half:], halves[1][...], preferred_element_type=jnp.float32)
    )
    put_extra(total.at[size:, :], extra)
    if t & 1:
        encode(out_ref, powers, size, lambda r: total[r : r + STEP, :], total[size:, :])
    else:
        out_ref[...] = total[...]


def image_block(grads, texts, at, block, scale):
    total = None
    for grad, text in zip(grads, texts):
        part = lax.dot_general(
            grad[:, pl.ds(at, block)],
            text[...],
            (((0,), (0,)), ((), ())),
            preferred_element_type=jnp.float32,
        )
        total = part if total is None else total + part
    return scale * total


def text_kernel(order, n_done, kept, block, scale_ref, coef_ref, place_ref, *refs):
    even, odd, row_lse, col_lse, row_extra, col_extra = refs[:6]
    n = len(order)
    texts, rest = refs[6 : 6 + n], refs[6 + n :]
    if kept:
        tile, rest = rest[0], rest[1:]
    done_grads, done_texts, rest = rest[:n_done], rest[n_done : 2 * n_done], rest[2 * n_done :]
    grads, outs = rest[:n], rest[n : 2 * n]
    for i, t in enumerate(order):
        text_block(
            texts[i],
            tile.at[pl.ds((t - min(order)) * block, block)] if kept else None,
            t, (even, odd), row_lse, col_lse, place_ref, scale_ref, coef_ref, row_extra, grads[i], outs[i], *rest[-2:]
        )
    if n_done:
        far_ref = rest[2 * n]
        half = even.shape[0]

        def one(j, carry):
            far_ref[j, :block, :] = image_block(
                [*done_grads, *grads],
                [*done_texts, *texts],
                pl.multiple_of(j * block + half, block),
                block,
                scale_ref[0, 0],
            )
            put_extra(far_ref.at[j, block:, :], col_extra)
            return carry

        lax.fori_loop(0, half // block, one, 0)


def text_grads(scale, coef, place, even, odd, row_lse, col_lse, row_extra, col_extra, texts, tile, order, done):
    half, width = even.shape
    block = texts[0].shape[0]
    n = len(order)
    vmem = pl.BlockSpec(memory_space=VMEM)
    smem = pl.BlockSpec(memory_space=SMEM)
    out_shape = (
        [jax.ShapeDtypeStruct((block, 2 * half), jnp.bfloat16)] * n
        + [
            jax.ShapeDtypeStruct((block + MORE, width), jnp.bfloat16)
            if t & 1
            else jax.ShapeDtypeStruct((block + EXTRA, width), jnp.float32)
            for t in order
        ]
    )
    if done:
        out_shape.append(jax.ShapeDtypeStruct((half // block, block + EXTRA, width), jnp.float32))
    operands = [even, odd, row_lse, col_lse, row_extra, col_extra, *[texts[t] for t in order]]
    operands += tile
    operands += [done[t] for t in done] + [texts[t] for t in done]
    outs = pl.pallas_call(
        functools.partial(text_kernel, tuple(order), len(done), len(tile), block),
        out_shape=tuple(out_shape),
        in_specs=[smem] * 3 + [vmem] * len(operands),
        out_specs=(vmem,) * len(out_shape),
        scratch_shapes=[
            VMEM((block + EXTRA, width), jnp.float32),
            VMEM((block, LANES), jnp.float32),
        ],
        compiler_params=pltpu.CompilerParams(vmem_limit_bytes=12 * 2**20),
        cost_estimate=pl.CostEstimate(
            flops=FLOPS * 4 * n * block * 2 * half * width, bytes_accessed=0, transcendentals=0
        ),
        name=f"text_grads_{n}",
    )(scale, coef, place, *operands)
    grads = {t: outs[i] for i, t in enumerate(order)}
    parts = {t: outs[n + i] for i, t in enumerate(order)}
    return grads, parts, outs[-1]


def image_kernel(n_text, block, scale_ref, extra, *refs):
    grads, texts, out_ref = refs[:n_text], refs[n_text : 2 * n_text], refs[-1]

    def one(j, carry):
        put_extra(out_ref.at[j, block:, :], extra)
        out_ref[j, :block, :] = image_block(
            grads, texts, pl.multiple_of(j * block, block), block, scale_ref[0, 0]
        )
        return carry

    lax.fori_loop(0, out_ref.shape[0], one, 0)


def image_grads(scale, extra, grads, texts, after):
    n_text = len(grads)
    rows = grads[0].shape[1]
    block, width = texts[0].shape
    n = rows // block // 2
    vmem = pl.BlockSpec(memory_space=VMEM)
    return pl.pallas_call(
        functools.partial(image_kernel, n_text, block),
        out_shape=jax.ShapeDtypeStruct((n, block + EXTRA, width), jnp.float32),
        in_specs=[pl.BlockSpec(memory_space=SMEM)]
        + [vmem] * (2 * n_text + 1)
        + [pl.BlockSpec(memory_space=pl.ANY)] * len(after),
        out_specs=vmem,
        compiler_params=pltpu.CompilerParams(vmem_limit_bytes=12 * 2**20),
        cost_estimate=pl.CostEstimate(
            flops=FLOPS * 2 * n * block * n_text * block * width, bytes_accessed=0, transcendentals=0
        ),
        name="image_grads",
    )(scale, extra, *grads, *texts, *after)


def on_device(n_row, n_col, image_embeds, text_embeds, logit_scale):
    block = image_embeds.shape[0]
    r, c = lax.axis_index("row"), lax.axis_index("col")
    place = jnp.stack([r, c]).reshape(1, 2)
    scale = logit_scale.reshape(1, 1)
    coef = scale * LOG2E
    image_half, text_half = image_embeds.astype(jnp.bfloat16), text_embeds.astype(jnp.bfloat16)
    even, odd, texts, text_last = gather_both(image_half, text_half, n_col, n_row)
    keep = 4 * n_row * n_col * block * block <= 16 * 2**20
    even, odd, *before = stats(
        coef, place, texts, (*even, *odd), (), n_col, n_row, keep
    )
    text_last, row_parts, col_parts, *tile_last = stats(
        coef, place, text_last, (even, odd), before[:2], n_col, n_row, keep
    )
    texts = [*texts, text_last]
    tile = before[2:]
    row_lse, row_extra, col_lse, col_extra = exchanged(row_parts, col_parts, n_col, n_row)

    held = (scale, coef, place, even, odd, row_lse, col_lse, row_extra, col_extra, texts)
    last = n_row - 1
    grads, parts, _ = text_grads(*held, tile_last, [last], {})
    received = swap(parts[last], "row", n_row, 1)
    more, more_parts, far = text_grads(*held, tile, list(range(last))[::-1], grads)
    grads |= more
    parts |= more_parts
    codes = {q: [] for q in range(0, n_row, 2)}
    codes[last ^ 1].append(received)
    after = [pack_text(parts[last ^ 1], codes[last ^ 1])] if n_row > 2 else [received]
    near = image_grads(scale, col_extra, [grads[t] for t in range(n_row)], texts, after)
    for q in range(1, last, 2):
        codes[q ^ 1].append(swap(parts[q], "row", n_row, 1))
    for b in range(1, n_row.bit_length() - 1):
        for q in [q for q in codes if q & (1 << b)]:
            code = after[0] if (b, q) == (1, last ^ 1) else pack_text(parts[q], codes[q])
            codes[q ^ (1 << b)].append(swap(code, "row", n_row, 1 << b))
            del codes[q]
    grad_text, text_extra, _ = total_of(coef, parts[0], codes[0], True, [], "grad_text")

    own, others = pack_images(near, swap(far, "col", n_col, 1))
    others = [swap(code, "col", n_col, 2 * j) for j, code in enumerate(others, 1)]
    grad_image, _, grad_scale = total_of(coef, own, others, False, [text_extra], "grad_image")
    return grad_image, grad_text, grad_scale.reshape(())


def solution(mesh):
    images = P(("row", "col"), None)
    texts = P(("col", "row"), None)
    return jax.shard_map(
        functools.partial(on_device, mesh.shape["row"], mesh.shape["col"]),
        mesh=mesh,
        in_specs=(images, texts, P()),
        out_specs=(images, texts, P()),
        check_vma=False,
    )
```

```python
import functools
import math

import jax
import jax.numpy as jnp
from jax import lax
from jax.experimental import pallas as pl
from jax.experimental.pallas import tpu as pltpu
from jax.sharding import PartitionSpec as P

LOG2E = 1.4426950408889634
LN2 = 0.6931471805599453
LANES = 128
VMEM = pltpu.VMEM
SMEM = pltpu.SMEM
FLOPS = 20


def swap(x, axis, n, q):
    return lax.ppermute(x, axis, [(i, i ^ q) for i in range(n)])


def gather_both(image, text, n_col, n_row):
    line = n_row == 4
    images = [swap(image, "col", n_col, q) for q in range(2, n_col, 2)]
    texts = [swap(text, "row", n_row, q) for q in range(1, 3 if line else n_row)]
    images, texts, text = lax.optimization_barrier((images, texts, text))
    odd = [swap(i, "col", n_col, 1) for i in (image, *images)]
    if line:
        middle = lax.ppermute(text, "row", [(1, 2), (2, 1)])
        return [image, *images], odd, [text, *texts], [middle, lax.ppermute(texts[1], "row", [(1, 0), (2, 3)])]
    return [image, *images], odd, [text, *texts[:-1]], texts[-1:]


def nt_dot(a, b):
    return lax.dot_general(a, b, (((1,), (1,)), ((), ())), preferred_element_type=jnp.float32)


def stats_kernel(first, n_text, block, coef_ref, place_ref, *refs):
    texts, refs = refs[:n_text], refs[n_text:]
    coef = coef_ref[0, 0]
    r_place, c_place = place_ref[0, 0], place_ref[0, 1]
    *refs, row_max, col_max, col_sum, col_dot, row_diag = refs
    if first:
        *refs, even, odd, row_ref, col_ref, tile = refs
        halves = (even, odd)
        each = len(refs) // 2
        for i, piece in enumerate(refs):
            at = (i % each) * block
            halves[i // each][at : at + block, :] = piece[...]
        before = None
    else:
        even, odd, *before, last, row_ref, col_ref, tile = refs
        halves = (even, odd)
        last[...] = functools.reduce(jnp.add, [text[...] for text in texts])
        texts, n_text = [last], 1
    cols, rows = tile.shape
    half = rows // 2
    lead = 0 if first else col_ref.shape[1] - n_text
    col_max[...] = jnp.full(col_max.shape, -jnp.inf, jnp.float32)
    row_diag[...] = jnp.zeros(row_diag.shape, jnp.float32)
    n_col, n_row = row_ref.shape[1], col_ref.shape[1]

    for which, images in enumerate(halves):

        def products(j, carry):
            image = images[pl.ds(pl.multiple_of(j * block, block), block), :]
            at = pl.multiple_of(j * block + which * half, block)
            top = None
            for t in range(n_text):
                part = pl.ds(t * block, block)
                x = nt_dot(texts[t][...], image) * coef
                tile[part, pl.ds(at, block)] = x
                top_t = jnp.max(x, axis=0, keepdims=True)
                top = top_t if top is None else jnp.maximum(top, top_t)
                held = col_max[part, :]
                for lane in range(0, block, LANES):
                    held = jnp.maximum(held, x[:, lane : lane + LANES])
                col_max[part, :] = held
            row_max[0:1, pl.ds(at, block)] = top
            return carry

        lax.fori_loop(0, half // block, products, 0, unroll=4)

    for t in range(n_text):
        among = c_place * n_row + (r_place ^ (lead + t)) - r_place * n_col

        @pl.when((among >= 0) & (among < n_col))
        def _():
            q = c_place ^ among
            at = pl.multiple_of((q // 2) * block + (q % 2) * half, block)
            x = tile[t * block : (t + 1) * block, pl.ds(at, block)]
            down = lax.broadcasted_iota(jnp.int32, x.shape, 0)
            across = lax.broadcasted_iota(jnp.int32, x.shape, 1)
            row_diag[0:1, pl.ds(at, block)] = jnp.sum(
                jnp.where(down == across, x, 0.0), axis=0, keepdims=True
            )

    col_max[...] = jnp.broadcast_to(
        jnp.max(col_max[...], axis=1, keepdims=True), col_max.shape
    )
    sums = []
    for which in range(2):
        lanes = range(which * half, (which + 1) * half, LANES)

        def exponentials(i, acc):
            part = pl.ds(pl.multiple_of(i * 8, 8), 8)
            top = col_max[part, :]
            total = col_sum[part, :] if which else None
            dot = col_dot[part, :] if which else None
            new = [], []
            for n, lane in enumerate(lanes):
                x = tile[part, lane : lane + LANES]
                e = jnp.exp2(x - row_max[0:1, lane : lane + LANES])
                new[0].append(acc[0][n] + e)
                new[1].append(acc[1][n] + e * x)
                e = jnp.exp2(x - top)
                total = e if total is None else total + e
                dot = e * x if dot is None else dot + e * x
            col_sum[part, :] = total
            col_dot[part, :] = dot
            return tuple(new[0]), tuple(new[1])

        zeros = tuple(jnp.zeros((8, LANES), jnp.float32) for _ in lanes)
        sums.append(lax.fori_loop(0, cols // 8, exponentials, (zeros, zeros), unroll=4))

    row_ids = lax.broadcasted_iota(jnp.int32, (n_col, block), 0)
    placed = [jnp.zeros((n_col, block), jnp.float32)] * 4
    for q in range(n_col):
        at = (q // 2) * block
        here = row_ids == (c_place ^ q)
        new = [row_max[0:1, at + (q % 2) * half : at + (q % 2) * half + block]]
        for which in sums[q % 2]:
            new.append(
                jnp.concatenate(
                    [
                        jnp.sum(which[(at + lane) // LANES], axis=0, keepdims=True)
                        for lane in range(0, block, LANES)
                    ],
                    axis=1,
                )
            )
        new.append(row_diag[0:1, at + (q % 2) * half : at + (q % 2) * half + block])
        placed = [jnp.where(here, n, p) for n, p in zip(new, placed)]
    if before:
        placed = merged(placed, [before[0][i] for i in range(4)])
    for i in range(4):
        row_ref[i] = placed[i]
    row_ids = lax.broadcasted_iota(jnp.int32, (n_row, block), 0)
    placed = [before[1][i] if before else jnp.zeros((n_row, block), jnp.float32) for i in range(3)]
    for t in range(n_text):
        part = pl.ds(t * block, block)
        here = row_ids == (r_place ^ (lead + t))
        new = [col_max[part, :].T[0:1, :]]
        for which in (col_sum, col_dot):
            new.append(jnp.sum(which[part, :].T, axis=0, keepdims=True))
        placed = [jnp.where(here, n, p) for n, p in zip(new, placed)]
    for i in range(3):
        col_ref[i] = placed[i]


def stats(coef, place, texts, images, before, n_col, n_row, keep):
    block, width = texts[0].shape
    first = not before
    rows, cols = block * n_col, block * (len(texts) if first else 1)
    vmem = pl.BlockSpec(memory_space=VMEM)
    smem = pl.BlockSpec(memory_space=SMEM)
    half = jax.ShapeDtypeStruct((rows // 2, width), jnp.bfloat16)
    out_shape = [half, half] if first else [jax.ShapeDtypeStruct((block, width), jnp.bfloat16)]
    out_shape += [
        jax.ShapeDtypeStruct((4, n_col, block), jnp.float32),
        jax.ShapeDtypeStruct((3, n_row, block), jnp.float32),
    ]
    scratch = [
        VMEM((8, rows), jnp.float32),
        VMEM((cols, LANES), jnp.float32),
        VMEM((cols, LANES), jnp.float32),
        VMEM((cols, LANES), jnp.float32),
        VMEM((8, rows), jnp.float32),
    ]
    if keep:
        out_shape.append(jax.ShapeDtypeStruct((cols, rows), jnp.float32))
    else:
        scratch.insert(0, VMEM((cols, rows), jnp.float32))
    return pl.pallas_call(
        functools.partial(stats_kernel, first, len(texts), block),
        out_shape=tuple(out_shape),
        in_specs=[smem, smem] + [vmem] * (len(texts) + len(images) + len(before)),
        out_specs=(vmem,) * len(out_shape),
        scratch_shapes=scratch,
        compiler_params=pltpu.CompilerParams(
            vmem_limit_bytes=(0 if keep else 4 * rows * cols) + 8 * 2**20
        ),
        cost_estimate=pl.CostEstimate(
            flops=FLOPS * 2 * rows * cols * width, bytes_accessed=0, transcendentals=0
        ),
        name="stats" if first else "stats_last",
    )(coef, place, *texts, *images, *before)


def merged(a, b):
    top = jnp.maximum(a[0], b[0])
    wa, wb = jnp.exp2(a[0] - top), jnp.exp2(b[0] - top)
    out = [top] + [a[i] * wa + b[i] * wb for i in (1, 2)]
    return out + [a[i] + b[i] for i in range(3, len(a))]


def by_pairs(blocks, add):
    while len(blocks) > 1:
        blocks = [add(blocks[i], blocks[i + 1]) for i in range(0, len(blocks), 2)]
    return blocks[0]


def lse_and_mean(parts):
    mean = 0.5 * parts[2] / parts[1]
    return parts[0] + jnp.log(parts[1]) * LOG2E, mean - parts[3] if len(parts) > 3 else mean


def exchanged(row_parts, col_parts, n_col, n_row):
    rows = [swap(row_parts, "col", n_col, q) for q in range(2, n_col, 2)]
    cols = swap(col_parts, "row", n_row, 1)
    rows, cols = lax.optimization_barrier((rows, cols))
    rows = by_pairs([list(x) for x in (row_parts, *rows)], merged)
    cols = merged(list(col_parts), list(cols))
    for b in range(1, n_row.bit_length() - 1):
        cols = merged(cols, list(swap(jnp.stack(cols), "row", n_row, 1 << b)))
    rows = merged(rows, list(swap(jnp.stack(rows), "col", n_col, 1)))
    return *lse_and_mean(rows), *lse_and_mean(cols)


LEVELS = 32000
LOW = 128
BIAS = 125
EXTRA = 8
MORE = 32
STEP = 32


def put_extra(out, extra_ref):
    n, width = extra_ref.shape
    rows = min(n, EXTRA)
    out[...] = jnp.zeros(out.shape, out.dtype)
    out[:rows, :width] = sum(extra_ref[i : i + rows, :] for i in range(0, n, rows))


def power(k):
    return jnp.exp2(k).astype(jnp.bfloat16).astype(jnp.float32)


def encode(out, powers, size, slab, extra):
    width = out.shape[1]
    for r in range(0, size, STEP):
        value = slab(r)
        top = jnp.maximum(jnp.max(jnp.abs(value), axis=1, keepdims=True), 1e-30)
        k = jnp.ceil(jnp.log(top) * LOG2E)
        powers[r : r + STEP, :] = jnp.broadcast_to(power(k), (STEP, LANES))
        whole = jnp.floor(jnp.abs(value) * (power(-k) * (LEVELS - 1)) + 0.5) * (1 / LOW)
        high = jnp.floor(whole)
        code = (1.0 + (whole - high)) * jnp.exp2(high - BIAS)
        out[r : r + STEP, :] = jnp.where(value < 0, -code, code).astype(jnp.bfloat16)
    half = width // 2
    first = extra[:, :half].astype(jnp.bfloat16)
    rest = extra[:, :half] - first.astype(jnp.float32)
    second = rest.astype(jnp.bfloat16)
    third = (rest - second.astype(jnp.float32)).astype(jnp.bfloat16)
    zeros = jnp.zeros((EXTRA, half), jnp.bfloat16)
    out[size : size + 2 * EXTRA, :half] = jnp.concatenate([first, second], axis=0)
    out[size : size + 2 * EXTRA, half:] = jnp.concatenate([third, zeros], axis=0)
    out[size + 2 * EXTRA :, :] = jnp.zeros((MORE - 2 * EXTRA, width), jnp.bfloat16)
    out[size + 2 * EXTRA :, :size] = powers[...].T[: MORE - 2 * EXTRA, :].astype(jnp.bfloat16)


def decode_powers(code, size):
    powers = code[size + 2 * EXTRA :, :size].astype(jnp.float32)
    return jnp.broadcast_to(powers[0:1, :], (LANES, size)).T * (LOW / (LEVELS - 1))


def decode(code, powers, r):
    lanes = []
    for lane in range(0, code.shape[1], LANES):
        c = code[r : r + STEP, lane : lane + LANES].astype(jnp.float32)
        a = jnp.abs(c)
        high = jnp.floor(jnp.log(a) * LOG2E)
        whole = (high + (BIAS - 1)) + a * jnp.exp2(-high)
        lanes.append(jnp.where(c < 0, -whole, whole) * powers[r : r + STEP, :])
    return jnp.concatenate(lanes, axis=1)


def decode_extra(code, size):
    half = code.shape[1] // 2
    left = code[size : size + 2 * EXTRA, :half].astype(jnp.float32)
    right = code[size : size + 2 * EXTRA, half:].astype(jnp.float32)
    return left[:EXTRA] + left[EXTRA:] + right[:EXTRA]


def pack_text_kernel(n, base, *refs):
    codes, out, powers, received = refs[:n], *refs[n:]
    size, half = base.shape[0] - EXTRA, base.shape[1] // 2
    more = base[size:, :half]
    for c, code in enumerate(codes):
        received[c] = decode_powers(code, size)
        more = more + decode_extra(code, size)

    def slab(r):
        value = base[r : r + STEP, :]
        for c, code in enumerate(codes):
            value = value + decode(code, received.at[c], r)
        return value

    encode(out, powers, size, slab, more)


def pack_text(base, codes):
    size, width = base.shape[0] - EXTRA, base.shape[1]
    vmem = pl.BlockSpec(memory_space=VMEM)
    return pl.pallas_call(
        functools.partial(pack_text_kernel, len(codes)),
        out_shape=jax.ShapeDtypeStruct((size + MORE, width), jnp.bfloat16),
        in_specs=[vmem] * (1 + len(codes)),
        out_specs=vmem,
        scratch_shapes=[VMEM((size, LANES), jnp.float32), VMEM((len(codes), size, LANES), jnp.float32)],
        compiler_params=pltpu.CompilerParams(vmem_limit_bytes=6 * 2**20),
        name="pack_text",
    )(base, *codes)


def pack_images_kernel(near, far, own, *refs):
    outs, powers = refs[:-1], refs[-1]
    size = near.shape[1] - EXTRA
    own[...] = near[0] + far[0]
    for j, out in enumerate(outs, 1):
        encode(
            out,
            powers.at[j - 1],
            size,
            lambda r, j=j: near[j, r : r + STEP, :] + far[j, r : r + STEP, :],
            near[j, size:, :] + far[j, size:, :],
        )


def pack_images(near, far):
    n, rows, width = near.shape
    size = rows - EXTRA
    vmem = pl.BlockSpec(memory_space=VMEM)
    code = jax.ShapeDtypeStruct((size + MORE, width), jnp.bfloat16)
    own, *codes = pl.pallas_call(
        pack_images_kernel,
        out_shape=(jax.ShapeDtypeStruct((rows, width), jnp.float32),) + (code,) * (n - 1),
        in_specs=[vmem] * 2,
        out_specs=(vmem,) * n,
        scratch_shapes=[VMEM((n - 1, size, LANES), jnp.float32)],
        compiler_params=pltpu.CompilerParams(vmem_limit_bytes=6 * 2**20),
        name="pack_images",
    )(near, far)
    return own, codes


def total_kernel(n, in_order, coef_ref, base, *refs):
    codes, before = refs[:n], refs[n:-6]
    out, extra, scalar, value, powers, sems = refs[-6:]
    size, width = base.shape[0] - EXTRA, base.shape[1]
    combine = functools.partial(functools.reduce, jnp.add) if in_order else by_pairs_added
    for c, code in enumerate(codes):
        powers[c] = decode_powers(code, size)
    copies = []
    steps = sems.shape[0]
    for i in range(steps):
        part = pl.ds(i * (size // steps), size // steps)
        for r in range(i * (size // steps), (i + 1) * (size // steps), STEP):
            value[r : r + STEP, :] = combine(
                [base[r : r + STEP, :]] + [decode(code, powers.at[c], r) for c, code in enumerate(codes)]
            )
        copies.append(pltpu.make_async_copy(value.at[part], out.at[part], sems.at[i]))
        copies[-1].start()
    more = combine([base[size:, : width // 2]] + [decode_extra(code, size) for code in codes])
    more = sum([b[...] for b in before], more)
    extra[...] = more
    scalar[0, 0] = jnp.sum(more) / coef_ref[0, 0]
    for copy in copies:
        copy.wait()


def by_pairs_added(blocks):
    return by_pairs(blocks, jnp.add)


def total_of(coef, base, codes, in_order, before, name):
    size, width = base.shape[0] - EXTRA, base.shape[1]
    vmem = pl.BlockSpec(memory_space=VMEM)
    smem = pl.BlockSpec(memory_space=SMEM)
    return pl.pallas_call(
        functools.partial(total_kernel, len(codes), in_order),
        out_shape=(
            jax.ShapeDtypeStruct((size, width), jnp.float32),
            jax.ShapeDtypeStruct((EXTRA, width // 2), jnp.float32),
            jax.ShapeDtypeStruct((1, 1), jnp.float32),
        ),
        in_specs=[smem] + [vmem] * (1 + len(codes) + len(before)),
        out_specs=(pl.BlockSpec(memory_space=pl.ANY), vmem, smem),
        scratch_shapes=[
            VMEM((size, width), jnp.float32),
            VMEM((len(codes), size, LANES), jnp.float32),
            pltpu.SemaphoreType.DMA((4,)),
        ],
        compiler_params=pltpu.CompilerParams(vmem_limit_bytes=8 * 2**20),
        name=name,
    )(coef, base, *codes, *before)


def text_block(text, tile, t, halves, row_lse, col_lse, place_ref, scale_ref, coef_ref, extra, grad_ref, out_ref, total, powers):
    coef = coef_ref[0, 0]
    r_place, c_place = place_ref[0, 0], place_ref[0, 1]
    half, width = halves[0].shape
    n_col, n_row = row_lse.shape[0], col_lse.shape[0]
    size = text.shape[0]
    block = size
    col_lse_down = jnp.broadcast_to(col_lse[pl.ds(r_place ^ t, 1), :], (LANES, size)).T
    text_id = c_place * n_row + (r_place ^ t)
    step = 32
    lane_ids = lax.broadcasted_iota(jnp.int32, (step, LANES), 1)
    row_ids = lax.broadcasted_iota(jnp.int32, (step, LANES), 0)

    for which, images in enumerate(halves):

        def one(j, carry):
            at = pl.multiple_of(j * block + which * half, block)
            if tile is None:
                image = images[pl.ds(pl.multiple_of(j * block, block), block), :]
                xs = nt_dot(text[...], image) * coef
            column = c_place ^ (2 * j + which)
            same = jnp.where(r_place * n_col + column == text_id, 1.0, 0.0)
            lse = row_lse[pl.ds(column, 1), :]
            for r in range(0, size, step):
                for lane in range(0, block, LANES):
                    if tile is None:
                        x = xs[r : r + step, lane : lane + LANES]
                    else:
                        x = tile[r : r + step, pl.ds(at + lane, LANES)]
                    e = jnp.exp2(x - lse[:, lane : lane + LANES]) + jnp.exp2(
                        x - col_lse_down[r : r + step, :]
                    )
                    g = 0.5 * e
                    if lane <= r < lane + LANES:
                        g = g - jnp.where(row_ids + (r - lane) == lane_ids, same, 0.0)
                    grad_ref[r : r + step, pl.ds(at + lane, LANES)] = g.astype(jnp.bfloat16)
            return carry

        lax.fori_loop(0, half // block, one, 0, unroll=4)
    total[:size, :] = scale_ref[0, 0] * (
        jnp.dot(grad_ref[:, :half], halves[0][...], preferred_element_type=jnp.float32)
        + jnp.dot(grad_ref[:, half:], halves[1][...], preferred_element_type=jnp.float32)
    )
    put_extra(total.at[size:, :], extra)
    if t & 1:
        encode(out_ref, powers, size, lambda r: total[r : r + STEP, :], total[size:, :])
    else:
        out_ref[...] = total[...]


def image_block(grads, texts, at, block, scale):
    total = None
    for grad, text in zip(grads, texts):
        part = lax.dot_general(
            grad[:, pl.ds(at, block)],
            text[...],
            (((0,), (0,)), ((), ())),
            preferred_element_type=jnp.float32,
        )
        total = part if total is None else total + part
    return scale * total


def text_kernel(order, n_done, kept, block, scale_ref, coef_ref, place_ref, *refs):
    even, odd, row_lse, col_lse, row_extra, col_extra = refs[:6]
    n = len(order)
    texts, rest = refs[6 : 6 + n], refs[6 + n :]
    if kept:
        tile, rest = rest[0], rest[1:]
    done_grads, done_texts, rest = rest[:n_done], rest[n_done : 2 * n_done], rest[2 * n_done :]
    grads, outs = rest[:n], rest[n : 2 * n]
    for i, t in enumerate(order):
        text_block(
            texts[i],
            tile.at[pl.ds((t - min(order)) * block, block)] if kept else None,
            t, (even, odd), row_lse, col_lse, place_ref, scale_ref, coef_ref, row_extra, grads[i], outs[i], *rest[-2:]
        )
    if n_done:
        far_ref = rest[2 * n]
        half = even.shape[0]

        def one(j, carry):
            far_ref[j, :block, :] = image_block(
                [*done_grads, *grads],
                [*done_texts, *texts],
                pl.multiple_of(j * block + half, block),
                block,
                scale_ref[0, 0],
            )
            put_extra(far_ref.at[j, block:, :], col_extra)
            return carry

        lax.fori_loop(0, half // block, one, 0)


def text_grads(scale, coef, place, even, odd, row_lse, col_lse, row_extra, col_extra, texts, tile, order, done):
    half, width = even.shape
    block = texts[0].shape[0]
    n = len(order)
    vmem = pl.BlockSpec(memory_space=VMEM)
    smem = pl.BlockSpec(memory_space=SMEM)
    out_shape = (
        [jax.ShapeDtypeStruct((block, 2 * half), jnp.bfloat16)] * n
        + [
            jax.ShapeDtypeStruct((block + MORE, width), jnp.bfloat16)
            if t & 1
            else jax.ShapeDtypeStruct((block + EXTRA, width), jnp.float32)
            for t in order
        ]
    )
    if done:
        out_shape.append(jax.ShapeDtypeStruct((half // block, block + EXTRA, width), jnp.float32))
    operands = [even, odd, row_lse, col_lse, row_extra, col_extra, *[texts[t] for t in order]]
    operands += tile
    operands += [done[t] for t in done] + [texts[t] for t in done]
    outs = pl.pallas_call(
        functools.partial(text_kernel, tuple(order), len(done), len(tile), block),
        out_shape=tuple(out_shape),
        in_specs=[smem] * 3 + [vmem] * len(operands),
        out_specs=(vmem,) * len(out_shape),
        scratch_shapes=[
            VMEM((block + EXTRA, width), jnp.float32),
            VMEM((block, LANES), jnp.float32),
        ],
        compiler_params=pltpu.CompilerParams(vmem_limit_bytes=12 * 2**20),
        cost_estimate=pl.CostEstimate(
            flops=FLOPS * 4 * n * block * 2 * half * width, bytes_accessed=0, transcendentals=0
        ),
        name=f"text_grads_{n}",
    )(scale, coef, place, *operands)
    grads = {t: outs[i] for i, t in enumerate(order)}
    parts = {t: outs[n + i] for i, t in enumerate(order)}
    return grads, parts, outs[-1]


def image_kernel(n_text, block, scale_ref, extra, *refs):
    grads, texts, out_ref = refs[:n_text], refs[n_text : 2 * n_text], refs[-1]

    def one(j, carry):
        put_extra(out_ref.at[j, block:, :], extra)
        out_ref[j, :block, :] = image_block(
            grads, texts, pl.multiple_of(j * block, block), block, scale_ref[0, 0]
        )
        return carry

    lax.fori_loop(0, out_ref.shape[0], one, 0)


def image_grads(scale, extra, grads, texts, after):
    n_text = len(grads)
    rows = grads[0].shape[1]
    block, width = texts[0].shape
    n = rows // block // 2
    vmem = pl.BlockSpec(memory_space=VMEM)
    return pl.pallas_call(
        functools.partial(image_kernel, n_text, block),
        out_shape=jax.ShapeDtypeStruct((n, block + EXTRA, width), jnp.float32),
        in_specs=[pl.BlockSpec(memory_space=SMEM)]
        + [vmem] * (2 * n_text + 1)
        + [pl.BlockSpec(memory_space=pl.ANY)] * len(after),
        out_specs=vmem,
        compiler_params=pltpu.CompilerParams(vmem_limit_bytes=12 * 2**20),
        cost_estimate=pl.CostEstimate(
            flops=FLOPS * 2 * n * block * n_text * block * width, bytes_accessed=0, transcendentals=0
        ),
        name="image_grads",
    )(scale, extra, *grads, *texts, *after)


def on_device(n_row, n_col, image_embeds, text_embeds, logit_scale):
    block = image_embeds.shape[0]
    r, c = lax.axis_index("row"), lax.axis_index("col")
    place = jnp.stack([r, c]).reshape(1, 2)
    scale = logit_scale.reshape(1, 1)
    coef = scale * LOG2E
    image_half, text_half = image_embeds.astype(jnp.bfloat16), text_embeds.astype(jnp.bfloat16)
    even, odd, texts, text_last = gather_both(image_half, text_half, n_col, n_row)
    keep = 4 * n_row * n_col * block * block <= 16 * 2**20
    even, odd, *before = stats(
        coef, place, texts, (*even, *odd), (), n_col, n_row, keep
    )
    text_last, row_parts, col_parts, *tile_last = stats(
        coef, place, text_last, (even, odd), before[:2], n_col, n_row, keep
    )
    texts = [*texts, text_last]
    tile = before[2:]
    row_lse, row_extra, col_lse, col_extra = exchanged(row_parts, col_parts, n_col, n_row)

    held = (scale, coef, place, even, odd, row_lse, col_lse, row_extra, col_extra, texts)
    last = n_row - 1
    grads, parts, _ = text_grads(*held, tile_last, [last], {})
    received = swap(parts[last], "row", n_row, 1)
    more, more_parts, far = text_grads(*held, tile, list(range(last))[::-1], grads)
    grads |= more
    parts |= more_parts
    codes = {q: [] for q in range(0, n_row, 2)}
    codes[last ^ 1].append(received)
    after = [pack_text(parts[last ^ 1], codes[last ^ 1])] if n_row > 2 else [received]
    near = image_grads(scale, col_extra, [grads[t] for t in range(n_row)], texts, after)
    for q in range(1, last, 2):
        codes[q ^ 1].append(swap(parts[q], "row", n_row, 1))
    for b in range(1, n_row.bit_length() - 1):
        for q in [q for q in codes if q & (1 << b)]:
            code = after[0] if (b, q) == (1, last ^ 1) else pack_text(parts[q], codes[q])
            codes[q ^ (1 << b)].append(swap(code, "row", n_row, 1 << b))
            del codes[q]
    grad_text, text_extra, _ = total_of(coef, parts[0], codes[0], True, [], "grad_text")

    own, others = pack_images(near, swap(far, "col", n_col, 1))
    others = [swap(code, "col", n_col, 2 * j) for j, code in enumerate(others, 1)]
    grad_image, _, grad_scale = total_of(coef, own, others, False, [text_extra], "grad_image")
    return grad_image, grad_text, grad_scale.reshape(())


def solution(mesh):
    images = P(("row", "col"), None)
    texts = P(("col", "row"), None)
    return jax.shard_map(
        functools.partial(on_device, mesh.shape["row"], mesh.shape["col"]),
        mesh=mesh,
        in_specs=(images, texts, P()),
        out_specs=(images, texts, P()),
        check_vma=False,
    )
```

```python
import functools
import math

import jax
import jax.numpy as jnp
from jax import lax
from jax.experimental import pallas as pl
from jax.experimental.pallas import tpu as pltpu
from jax.sharding import PartitionSpec as P

LOG2E = 1.4426950408889634
LN2 = 0.6931471805599453
LANES = 128
VMEM = pltpu.VMEM
SMEM = pltpu.SMEM
FLOPS = 20


def swap(x, axis, n, q):
    return lax.ppermute(x, axis, [(i, i ^ q) for i in range(n)])


def gather_both(image, text, n_col, n_row):
    images = [swap(image, "col", n_col, q) for q in range(2, n_col, 2)]
    if n_row == 4:
        ends = lax.ppermute(text, "row", [(0, 3), (3, 0)])
        texts = [swap(text, "row", n_row, q) for q in (1, 2)]
        images, texts, ends, text = lax.optimization_barrier((images, texts, ends, text))
        last = [ends, lax.ppermute(text, "row", [(1, 2), (2, 1)])]
    else:
        texts = [swap(text, "row", n_row, q) for q in range(1, n_row)]
        images, texts = lax.optimization_barrier((images, texts))
        *texts, last = texts
        last = [last]
    odd = [swap(i, "col", n_col, 1) for i in (image, *images)]
    return [image, *images], odd, [text, *texts], last


def nt_dot(a, b):
    return lax.dot_general(a, b, (((1,), (1,)), ((), ())), preferred_element_type=jnp.float32)


def stats_kernel(first, n_text, block, coef_ref, place_ref, *refs):
    texts, refs = refs[:n_text], refs[n_text:]
    coef = coef_ref[0, 0]
    r_place, c_place = place_ref[0, 0], place_ref[0, 1]
    *refs, row_max, col_max, col_sum, col_dot, row_diag = refs
    if first:
        *refs, even, odd, row_ref, col_ref, tile = refs
        halves = (even, odd)
        each = len(refs) // 2
        for i, piece in enumerate(refs):
            at = (i % each) * block
            halves[i // each][at : at + block, :] = piece[...]
        before = None
    else:
        even, odd, *before, last, row_ref, col_ref, tile = refs
        halves = (even, odd)
        last[...] = functools.reduce(jnp.add, [text[...] for text in texts])
        texts, n_text = [last], 1
    cols, rows = tile.shape
    half = rows // 2
    lead = 0 if first else col_ref.shape[1] - n_text
    col_max[...] = jnp.full(col_max.shape, -jnp.inf, jnp.float32)
    row_diag[...] = jnp.zeros(row_diag.shape, jnp.float32)
    n_col, n_row = row_ref.shape[1], col_ref.shape[1]

    for which, images in enumerate(halves):

        def products(j, carry):
            image = images[pl.ds(pl.multiple_of(j * block, block), block), :]
            at = pl.multiple_of(j * block + which * half, block)
            top = None
            for t in range(n_text):
                part = pl.ds(t * block, block)
                x = nt_dot(texts[t][...], image) * coef
                tile[part, pl.ds(at, block)] = x
                top_t = jnp.max(x, axis=0, keepdims=True)
                top = top_t if top is None else jnp.maximum(top, top_t)
                held = col_max[part, :]
                for lane in range(0, block, LANES):
                    held = jnp.maximum(held, x[:, lane : lane + LANES])
                col_max[part, :] = held
            row_max[0:1, pl.ds(at, block)] = top
            return carry

        lax.fori_loop(0, half // block, products, 0, unroll=4)

    for t in range(n_text):
        among = c_place * n_row + (r_place ^ (lead + t)) - r_place * n_col

        @pl.when((among >= 0) & (among < n_col))
        def _():
            q = c_place ^ among
            at = pl.multiple_of((q // 2) * block + (q % 2) * half, block)
            x = tile[t * block : (t + 1) * block, pl.ds(at, block)]
            down = lax.broadcasted_iota(jnp.int32, x.shape, 0)
            across = lax.broadcasted_iota(jnp.int32, x.shape, 1)
            row_diag[0:1, pl.ds(at, block)] = jnp.sum(
                jnp.where(down == across, x, 0.0), axis=0, keepdims=True
            )

    col_max[...] = jnp.broadcast_to(
        jnp.max(col_max[...], axis=1, keepdims=True), col_max.shape
    )
    sums = []
    for which in range(2):
        lanes = range(which * half, (which + 1) * half, LANES)

        def exponentials(i, acc):
            part = pl.ds(pl.multiple_of(i * 8, 8), 8)
            top = col_max[part, :]
            total = col_sum[part, :] if which else None
            dot = col_dot[part, :] if which else None
            new = [], []
            for n, lane in enumerate(lanes):
                x = tile[part, lane : lane + LANES]
                e = jnp.exp2(x - row_max[0:1, lane : lane + LANES])
                new[0].append(acc[0][n] + e)
                new[1].append(acc[1][n] + e * x)
                e = jnp.exp2(x - top)
                total = e if total is None else total + e
                dot = e * x if dot is None else dot + e * x
            col_sum[part, :] = total
            col_dot[part, :] = dot
            return tuple(new[0]), tuple(new[1])

        zeros = tuple(jnp.zeros((8, LANES), jnp.float32) for _ in lanes)
        sums.append(lax.fori_loop(0, cols // 8, exponentials, (zeros, zeros), unroll=4))

    row_ids = lax.broadcasted_iota(jnp.int32, (n_col, block), 0)
    placed = [jnp.zeros((n_col, block), jnp.float32)] * 4
    for q in range(n_col):
        at = (q // 2) * block
        here = row_ids == (c_place ^ q)
        new = [row_max[0:1, at + (q % 2) * half : at + (q % 2) * half + block]]
        for which in sums[q % 2]:
            new.append(
                jnp.concatenate(
                    [
                        jnp.sum(which[(at + lane) // LANES], axis=0, keepdims=True)
                        for lane in range(0, block, LANES)
                    ],
                    axis=1,
                )
            )
        new.append(row_diag[0:1, at + (q % 2) * half : at + (q % 2) * half + block])
        placed = [jnp.where(here, n, p) for n, p in zip(new, placed)]
    if before:
        placed = merged(placed, [before[0][i] for i in range(4)])
    for i in range(4):
        row_ref[i] = placed[i]
    row_ids = lax.broadcasted_iota(jnp.int32, (n_row, block), 0)
    placed = [before[1][i] if before else jnp.zeros((n_row, block), jnp.float32) for i in range(3)]
    for t in range(n_text):
        part = pl.ds(t * block, block)
        here = row_ids == (r_place ^ (lead + t))
        new = [col_max[part, :].T[0:1, :]]
        for which in (col_sum, col_dot):
            new.append(jnp.sum(which[part, :].T, axis=0, keepdims=True))
        placed = [jnp.where(here, n, p) for n, p in zip(new, placed)]
    for i in range(3):
        col_ref[i] = placed[i]


def stats(coef, place, texts, images, before, n_col, n_row, keep):
    block, width = texts[0].shape
    first = not before
    rows, cols = block * n_col, block * (len(texts) if first else 1)
    vmem = pl.BlockSpec(memory_space=VMEM)
    smem = pl.BlockSpec(memory_space=SMEM)
    half = jax.ShapeDtypeStruct((rows // 2, width), jnp.bfloat16)
    out_shape = [half, half] if first else [jax.ShapeDtypeStruct((block, width), jnp.bfloat16)]
    out_shape += [
        jax.ShapeDtypeStruct((4, n_col, block), jnp.float32),
        jax.ShapeDtypeStruct((3, n_row, block), jnp.float32),
    ]
    scratch = [
        VMEM((8, rows), jnp.float32),
        VMEM((cols, LANES), jnp.float32),
        VMEM((cols, LANES), jnp.float32),
        VMEM((cols, LANES), jnp.float32),
        VMEM((8, rows), jnp.float32),
    ]
    if keep:
        out_shape.append(jax.ShapeDtypeStruct((cols, rows), jnp.float32))
    else:
        scratch.insert(0, VMEM((cols, rows), jnp.float32))
    return pl.pallas_call(
        functools.partial(stats_kernel, first, len(texts), block),
        out_shape=tuple(out_shape),
        in_specs=[smem, smem] + [vmem] * (len(texts) + len(images) + len(before)),
        out_specs=(vmem,) * len(out_shape),
        scratch_shapes=scratch,
        compiler_params=pltpu.CompilerParams(
            vmem_limit_bytes=(0 if keep else 4 * rows * cols) + 8 * 2**20
        ),
        cost_estimate=pl.CostEstimate(
            flops=FLOPS * 2 * rows * cols * width, bytes_accessed=0, transcendentals=0
        ),
        name="stats" if first else "stats_last",
    )(coef, place, *texts, *images, *before)


def merged(a, b):
    top = jnp.maximum(a[0], b[0])
    wa, wb = jnp.exp2(a[0] - top), jnp.exp2(b[0] - top)
    out = [top] + [a[i] * wa + b[i] * wb for i in (1, 2)]
    return out + [a[i] + b[i] for i in range(3, len(a))]


def by_pairs(blocks, add):
    while len(blocks) > 1:
        blocks = [add(blocks[i], blocks[i + 1]) for i in range(0, len(blocks), 2)]
    return blocks[0]


def lse_and_mean(parts):
    mean = 0.5 * parts[2] / parts[1]
    return parts[0] + jnp.log(parts[1]) * LOG2E, mean - parts[3] if len(parts) > 3 else mean


def exchanged(row_parts, col_parts, n_col, n_row):
    rows, cols = list(row_parts), list(col_parts)
    row_bits = [1 << b for b in range(1, n_col.bit_length() - 1)] + [1]
    col_bits = [1 << b for b in range(n_row.bit_length() - 1)]
    for n, bit in enumerate(row_bits):
        received = swap(jnp.stack(rows), "col", n_col, bit)
        if n < len(col_bits):
            other = swap(jnp.stack(cols), "row", n_row, col_bits[n])
            received, other = lax.optimization_barrier((received, other))
            cols = merged(cols, list(other))
        rows = merged(rows, list(received))
    return *lse_and_mean(rows), *lse_and_mean(cols)


LEVELS = 32000
LOW = 128
BIAS = 125
EXTRA = 8
MORE = 32
STEP = 32


def put_extra(out, extra_ref):
    n, width = extra_ref.shape
    rows = min(n, EXTRA)
    out[...] = jnp.zeros(out.shape, out.dtype)
    out[:rows, :width] = sum(extra_ref[i : i + rows, :] for i in range(0, n, rows))


def power(k):
    return jnp.exp2(k).astype(jnp.bfloat16).astype(jnp.float32)


def encode(out, powers, size, slab, extra):
    width = out.shape[1]
    for r in range(0, size, STEP):
        value = slab(r)
        top = jnp.maximum(jnp.max(jnp.abs(value), axis=1, keepdims=True), 1e-30)
        k = jnp.ceil(jnp.log(top) * LOG2E)
        powers[r : r + STEP, :] = jnp.broadcast_to(power(k), (STEP, LANES))
        whole = jnp.floor(jnp.abs(value) * (power(-k) * (LEVELS - 1)) + 0.5) * (1 / LOW)
        high = jnp.floor(whole)
        code = (1.0 + (whole - high)) * jnp.exp2(high - BIAS)
        out[r : r + STEP, :] = jnp.where(value < 0, -code, code).astype(jnp.bfloat16)
    half = width // 2
    first = extra[:, :half].astype(jnp.bfloat16)
    rest = extra[:, :half] - first.astype(jnp.float32)
    second = rest.astype(jnp.bfloat16)
    third = (rest - second.astype(jnp.float32)).astype(jnp.bfloat16)
    zeros = jnp.zeros((EXTRA, half), jnp.bfloat16)
    out[size : size + 2 * EXTRA, :half] = jnp.concatenate([first, second], axis=0)
    out[size : size + 2 * EXTRA, half:] = jnp.concatenate([third, zeros], axis=0)
    out[size + 2 * EXTRA :, :] = jnp.zeros((MORE - 2 * EXTRA, width), jnp.bfloat16)
    out[size + 2 * EXTRA :, :size] = powers[...].T[: MORE - 2 * EXTRA, :].astype(jnp.bfloat16)


def decode_powers(code, size):
    powers = code[size + 2 * EXTRA :, :size].astype(jnp.float32)
    return jnp.broadcast_to(powers[0:1, :], (LANES, size)).T * (LOW / (LEVELS - 1))


def decode(code, powers, r):
    lanes = []
    for lane in range(0, code.shape[1], LANES):
        c = code[r : r + STEP, lane : lane + LANES].astype(jnp.float32)
        a = jnp.abs(c)
        high = jnp.floor(jnp.log(a) * LOG2E)
        whole = (high + (BIAS - 1)) + a * jnp.exp2(-high)
        lanes.append(jnp.where(c < 0, -whole, whole) * powers[r : r + STEP, :])
    return jnp.concatenate(lanes, axis=1)


def decode_extra(code, size):
    half = code.shape[1] // 2
    left = code[size : size + 2 * EXTRA, :half].astype(jnp.float32)
    right = code[size : size + 2 * EXTRA, half:].astype(jnp.float32)
    return left[:EXTRA] + left[EXTRA:] + right[:EXTRA]


def pack_text_kernel(n, base, *refs):
    codes, out, powers, received = refs[:n], *refs[n:]
    size, half = base.shape[0] - EXTRA, base.shape[1] // 2
    more = base[size:, :half]
    for c, code in enumerate(codes):
        received[c] = decode_powers(code, size)
        more = more + decode_extra(code, size)

    def slab(r):
        value = base[r : r + STEP, :]
        for c, code in enumerate(codes):
            value = value + decode(code, received.at[c], r)
        return value

    encode(out, powers, size, slab, more)


def pack_text(base, codes):
    size, width = base.shape[0] - EXTRA, base.shape[1]
    vmem = pl.BlockSpec(memory_space=VMEM)
    return pl.pallas_call(
        functools.partial(pack_text_kernel, len(codes)),
        out_shape=jax.ShapeDtypeStruct((size + MORE, width), jnp.bfloat16),
        in_specs=[vmem] * (1 + len(codes)),
        out_specs=vmem,
        scratch_shapes=[VMEM((size, LANES), jnp.float32), VMEM((len(codes), size, LANES), jnp.float32)],
        compiler_params=pltpu.CompilerParams(vmem_limit_bytes=6 * 2**20),
        name="pack_text",
    )(base, *codes)


def pack_images_kernel(near, far, own, *refs):
    outs, powers = refs[:-1], refs[-1]
    size = near.shape[1] - EXTRA
    own[...] = near[0] + far[0]
    for j, out in enumerate(outs, 1):
        encode(
            out,
            powers.at[j - 1],
            size,
            lambda r, j=j: near[j, r : r + STEP, :] + far[j, r : r + STEP, :],
            near[j, size:, :] + far[j, size:, :],
        )


def pack_images(near, far):
    n, rows, width = near.shape
    size = rows - EXTRA
    vmem = pl.BlockSpec(memory_space=VMEM)
    code = jax.ShapeDtypeStruct((size + MORE, width), jnp.bfloat16)
    own, *codes = pl.pallas_call(
        pack_images_kernel,
        out_shape=(jax.ShapeDtypeStruct((rows, width), jnp.float32),) + (code,) * (n - 1),
        in_specs=[vmem] * 2,
        out_specs=(vmem,) * n,
        scratch_shapes=[VMEM((n - 1, size, LANES), jnp.float32)],
        compiler_params=pltpu.CompilerParams(vmem_limit_bytes=(4 + 2 * n) * 2**20),
        name="pack_images",
    )(near, far)
    return own, codes


def total_kernel(n, in_order, coef_ref, base, *refs):
    codes, before = refs[:n], refs[n:-6]
    out, extra, scalar, value, powers, sems = refs[-6:]
    size, width = base.shape[0] - EXTRA, base.shape[1]
    combine = functools.partial(functools.reduce, jnp.add) if in_order else by_pairs_added
    for c, code in enumerate(codes):
        powers[c] = decode_powers(code, size)
    copies = []
    steps = sems.shape[0]
    for i in range(steps):
        part = pl.ds(i * (size // steps), size // steps)
        for r in range(i * (size // steps), (i + 1) * (size // steps), STEP):
            value[r : r + STEP, :] = combine(
                [base[r : r + STEP, :]] + [decode(code, powers.at[c], r) for c, code in enumerate(codes)]
            )
        copies.append(pltpu.make_async_copy(value.at[part], out.at[part], sems.at[i]))
        copies[-1].start()
    more = combine([base[size:, : width // 2]] + [decode_extra(code, size) for code in codes])
    more = sum([b[...] for b in before], more)
    extra[...] = more
    scalar[0, 0] = jnp.sum(more) / coef_ref[0, 0]
    for copy in copies:
        copy.wait()


def by_pairs_added(blocks):
    return by_pairs(blocks, jnp.add)


def total_of(coef, base, codes, in_order, before, name):
    size, width = base.shape[0] - EXTRA, base.shape[1]
    vmem = pl.BlockSpec(memory_space=VMEM)
    smem = pl.BlockSpec(memory_space=SMEM)
    return pl.pallas_call(
        functools.partial(total_kernel, len(codes), in_order),
        out_shape=(
            jax.ShapeDtypeStruct((size, width), jnp.float32),
            jax.ShapeDtypeStruct((EXTRA, width // 2), jnp.float32),
            jax.ShapeDtypeStruct((1, 1), jnp.float32),
        ),
        in_specs=[smem] + [vmem] * (1 + len(codes) + len(before)),
        out_specs=(pl.BlockSpec(memory_space=pl.ANY), vmem, smem),
        scratch_shapes=[
            VMEM((size, width), jnp.float32),
            VMEM((len(codes), size, LANES), jnp.float32),
            pltpu.SemaphoreType.DMA((4,)),
        ],
        compiler_params=pltpu.CompilerParams(vmem_limit_bytes=8 * 2**20),
        name=name,
    )(coef, base, *codes, *before)


def logit_block(text, tile, t, halves, row_lse, col_lse, place_ref, coef_ref, grad_ref):
    coef = coef_ref[0, 0]
    r_place, c_place = place_ref[0, 0], place_ref[0, 1]
    half = halves[0].shape[0]
    n_col, n_row = row_lse.shape[0], col_lse.shape[0]
    size = block = text.shape[0]
    col_lse_down = jnp.broadcast_to(col_lse[pl.ds(r_place ^ t, 1), :], (LANES, size)).T
    text_id = c_place * n_row + (r_place ^ t)
    lane_ids = lax.broadcasted_iota(jnp.int32, (STEP, LANES), 1)
    row_ids = lax.broadcasted_iota(jnp.int32, (STEP, LANES), 0)

    for which, images in enumerate(halves):

        def one(j, carry):
            at = pl.multiple_of(j * block + which * half, block)
            if tile is None:
                image = images[pl.ds(pl.multiple_of(j * block, block), block), :]
                xs = nt_dot(text[...], image) * coef
            column = c_place ^ (2 * j + which)
            same = jnp.where(r_place * n_col + column == text_id, 1.0, 0.0)
            lse = row_lse[pl.ds(column, 1), :]
            for r in range(0, size, STEP):
                for lane in range(0, block, LANES):
                    if tile is None:
                        x = xs[r : r + STEP, lane : lane + LANES]
                    else:
                        x = tile[r : r + STEP, pl.ds(at + lane, LANES)]
                    e = jnp.exp2(x - lse[:, lane : lane + LANES]) + jnp.exp2(
                        x - col_lse_down[r : r + STEP, :]
                    )
                    g = 0.5 * e
                    if lane <= r < lane + LANES:
                        g = g - jnp.where(row_ids + (r - lane) == lane_ids, same, 0.0)
                    grad_ref[r : r + STEP, pl.ds(at + lane, LANES)] = g.astype(jnp.bfloat16)
            return carry

        lax.fori_loop(0, half // block, one, 0, unroll=4)


def text_block(t, grad, halves, scale, extra, out, total, powers):
    half, size = halves[0].shape[0], grad.shape[0]
    total[:size, :] = scale * (
        jnp.dot(grad[:, :half], halves[0][...], preferred_element_type=jnp.float32)
        + jnp.dot(grad[:, half:], halves[1][...], preferred_element_type=jnp.float32)
    )
    put_extra(total.at[size:, :], extra)
    if t & 1:
        encode(out, powers, size, lambda r: total[r : r + STEP, :], total[size:, :])
    else:
        out[...] = total[...]


def image_blocks(out, first, grads, texts, scale, extra, block):
    def one(j, carry):
        total = None
        for grad, text in zip(grads, texts):
            part = lax.dot_general(
                grad[:, pl.ds(pl.multiple_of(j * block + first, block), block)],
                text[...],
                (((0,), (0,)), ((), ())),
                preferred_element_type=jnp.float32,
            )
            total = part if total is None else total + part
        out[j, :block, :] = scale * total
        put_extra(out.at[j, block:, :], extra)
        return carry

    lax.fori_loop(0, out.shape[0], one, 0)


def first_kernel(t, kept, scale_ref, coef_ref, place_ref, even, odd, row_lse, col_lse, row_extra, text, *refs):
    tile = refs[0] if kept else None
    grad, out, total, powers = refs[kept:]
    logit_block(text, tile, t, (even, odd), row_lse, col_lse, place_ref, coef_ref, grad)
    text_block(t, grad, (even, odd), scale_ref[0, 0], row_extra, out, total, powers)


def logits_kernel(n, kept, scale_ref, coef_ref, place_ref, even, odd, row_lse, col_lse, col_extra, *refs):
    texts, last, refs = refs[:n], refs[n], refs[n + 1 :]
    tile, last_grad, refs = refs[0] if kept else None, refs[kept], refs[kept + 1 :]
    grads, far = refs[:n], refs[n]
    block = last.shape[0]
    for t in range(n):
        part = tile.at[pl.ds(t * block, block)] if kept else None
        logit_block(texts[t], part, t, (even, odd), row_lse, col_lse, place_ref, coef_ref, grads[t])
    image_blocks(
        far, even.shape[0], (*grads, last_grad), (*texts, last), scale_ref[0, 0], col_extra, block
    )


def rest_kernel(n, scale_ref, even, odd, row_extra, col_extra, *refs):
    texts, grads, refs = refs[: n + 1], refs[n + 1 : 2 * n + 2], refs[2 * n + 2 :]
    outs, near, total, powers = refs[:n], refs[n], *refs[n + 1 :]
    for t in range(n)[::-1]:
        text_block(t, grads[t], (even, odd), scale_ref[0, 0], row_extra, outs[t], total, powers)
    image_blocks(near, 0, grads, texts, scale_ref[0, 0], col_extra, texts[0].shape[0])


def gradients(scale, coef, place, even, odd, texts, lses, extras, tile, tile_last):
    half, width = even.shape
    block = texts[0].shape[0]
    n = len(texts) - 1
    kept = len(tile)
    vmem = pl.BlockSpec(memory_space=VMEM)
    smem = pl.BlockSpec(memory_space=SMEM)
    grad = jax.ShapeDtypeStruct((block, 2 * half), jnp.bfloat16)
    images = jax.ShapeDtypeStruct((half // block, block + EXTRA, width), jnp.float32)
    row_extra, col_extra = extras

    def of_texts(t):
        if t & 1:
            return jax.ShapeDtypeStruct((block + MORE, width), jnp.bfloat16)
        return jax.ShapeDtypeStruct((block + EXTRA, width), jnp.float32)

    def call(kernel, name, out_shape, scalars, operands, blocks, scratch=True):
        return pl.pallas_call(
            kernel,
            out_shape=tuple(out_shape),
            in_specs=[smem] * len(scalars) + [vmem] * len(operands),
            out_specs=(vmem,) * len(out_shape),
            scratch_shapes=[
                VMEM((block + EXTRA, width), jnp.float32),
                VMEM((block, LANES), jnp.float32),
            ]
            if scratch
            else [],
            compiler_params=pltpu.CompilerParams(vmem_limit_bytes=(12 if kept else 20) * 2**20),
            cost_estimate=pl.CostEstimate(
                flops=FLOPS * 4 * blocks * block * 2 * half * width, bytes_accessed=0, transcendentals=0
            ),
            name=name,
        )(*scalars, *operands)

    grad_last, part_last = call(
        functools.partial(first_kernel, n, kept),
        "text_grads_last",
        [grad, of_texts(n)],
        (scale, coef, place),
        (even, odd, *lses, row_extra, texts[n], *tile_last),
        1,
    )

    def logits():
        *grads, far = call(
            functools.partial(logits_kernel, n, kept),
            "logit_and_image_grads",
            [grad] * n + [images],
            (scale, coef, place),
            (even, odd, *lses, col_extra, *texts, *tile, grad_last),
            n,
            False,
        )
        return grads, far

    def rest(grads):
        *parts, near = call(
            functools.partial(rest_kernel, n),
            "text_and_image_grads",
            [of_texts(t) for t in range(n)] + [images],
            (scale,),
            (even, odd, row_extra, col_extra, *texts, *grads, grad_last),
            n,
        )
        return parts, near

    return part_last, logits, rest


def on_device(n_row, n_col, image_embeds, text_embeds, logit_scale):
    block = image_embeds.shape[0]
    r, c = lax.axis_index("row"), lax.axis_index("col")
    place = jnp.stack([r, c]).reshape(1, 2)
    scale = logit_scale.reshape(1, 1)
    coef = scale * LOG2E
    image_half, text_half = image_embeds.astype(jnp.bfloat16), text_embeds.astype(jnp.bfloat16)
    even, odd, texts, text_last = gather_both(image_half, text_half, n_col, n_row)
    keep = 4 * n_row * n_col * block * block <= 16 * 2**20
    even, odd, *before = stats(
        coef, place, texts, (*even, *odd), (), n_col, n_row, keep
    )
    text_last, row_parts, col_parts, *tile_last = stats(
        coef, place, text_last, (even, odd), before[:2], n_col, n_row, keep
    )
    texts = [*texts, text_last]
    tile = before[2:]
    row_lse, row_extra, col_lse, col_extra = exchanged(row_parts, col_parts, n_col, n_row)

    last = n_row - 1
    part_last, logits, rest = gradients(
        scale, coef, place, even, odd, texts, (row_lse, col_lse), (row_extra, col_extra), tile, tile_last
    )
    received = swap(part_last, "row", n_row, 1)
    grads, far = logits()
    far = swap(far, "col", n_col, 1)
    parts, near = rest(grads)

    codes = {q: [] for q in range(0, n_row, 2)}
    codes[last ^ 1].append(received)
    if n_row > 2:
        leaving = pack_text(parts[last ^ 1], codes[last ^ 1])
        *odd_parts, far = lax.optimization_barrier((*parts[1:last:2], far))
        parts[1:last:2] = odd_parts
    for q in range(1, last, 2):
        codes[q ^ 1].append(swap(parts[q], "row", n_row, 1))
    for b in range(1, n_row.bit_length() - 1):
        for q in [q for q in codes if q & (1 << b)]:
            code = leaving if (b, q) == (1, last ^ 1) else pack_text(parts[q], codes[q])
            codes[q ^ (1 << b)].append(swap(code, "row", n_row, 1 << b))
            del codes[q]
    grad_text, text_extra, _ = total_of(coef, parts[0], codes[0], True, [], "grad_text")

    own, others = pack_images(near, far)
    others = [swap(code, "col", n_col, 2 * j) for j, code in enumerate(others, 1)]
    grad_image, _, grad_scale = total_of(coef, own, others, False, [text_extra], "grad_image")
    return grad_image, grad_text, grad_scale.reshape(())


def solution(mesh):
    images = P(("row", "col"), None)
    texts = P(("col", "row"), None)
    return jax.shard_map(
        functools.partial(on_device, mesh.shape["row"], mesh.shape["col"]),
        mesh=mesh,
        in_specs=(images, texts, P()),
        out_specs=(images, texts, P()),
        check_vma=False,
    )
```

```python
import functools
import math

import jax
import jax.numpy as jnp
from jax import lax
from jax.experimental import pallas as pl
from jax.experimental.pallas import tpu as pltpu
from jax.sharding import PartitionSpec as P

LOG2E = 1.4426950408889634
LN2 = 0.6931471805599453
LANES = 128
VMEM = pltpu.VMEM
SMEM = pltpu.SMEM
FLOPS = 20


def swap(x, axis, n, q):
    return lax.ppermute(x, axis, [(i, i ^ q) for i in range(n)])


def gather_both(image, text, n_col, n_row):
    images = [swap(image, "col", n_col, q) for q in range(2, n_col, 2)]
    texts = [swap(text, "row", n_row, q) for q in range(1, n_row - 1)]
    images, texts = lax.optimization_barrier((images, texts))
    odd = [swap(i, "col", n_col, 1) for i in (image, *images)]
    return [image, *images], odd, [text, *texts], [swap(texts[-1], "row", n_row, 1)]


def nt_dot(a, b):
    return lax.dot_general(a, b, (((1,), (1,)), ((), ())), preferred_element_type=jnp.float32)


def stats_kernel(first, n_text, block, coef_ref, place_ref, *refs):
    texts, refs = refs[:n_text], refs[n_text:]
    coef = coef_ref[0, 0]
    r_place, c_place = place_ref[0, 0], place_ref[0, 1]
    *refs, row_max, col_max, col_sum, col_dot, row_diag = refs
    if first:
        *refs, even, odd, row_ref, col_ref, tile = refs
        halves = (even, odd)
        each = len(refs) // 2
        for i, piece in enumerate(refs):
            at = (i % each) * block
            halves[i // each][at : at + block, :] = piece[...]
        before = None
    else:
        even, odd, *before, last, row_ref, col_ref, tile = refs
        halves = (even, odd)
        last[...] = functools.reduce(jnp.add, [text[...] for text in texts])
        texts, n_text = [last], 1
    cols, rows = tile.shape
    half = rows // 2
    lead = 0 if first else col_ref.shape[1] - n_text
    col_max[...] = jnp.full(col_max.shape, -jnp.inf, jnp.float32)
    row_diag[...] = jnp.zeros(row_diag.shape, jnp.float32)
    n_col, n_row = row_ref.shape[1], col_ref.shape[1]

    for which, images in enumerate(halves):

        def products(j, carry):
            image = images[pl.ds(pl.multiple_of(j * block, block), block), :]
            at = pl.multiple_of(j * block + which * half, block)
            top = None
            for t in range(n_text):
                part = pl.ds(t * block, block)
                x = nt_dot(texts[t][...], image) * coef
                tile[part, pl.ds(at, block)] = x
                top_t = jnp.max(x, axis=0, keepdims=True)
                top = top_t if top is None else jnp.maximum(top, top_t)
                held = col_max[part, :]
                for lane in range(0, block, LANES):
                    held = jnp.maximum(held, x[:, lane : lane + LANES])
                col_max[part, :] = held
            row_max[0:1, pl.ds(at, block)] = top
            return carry

        lax.fori_loop(0, half // block, products, 0, unroll=4)

    for t in range(n_text):
        among = c_place * n_row + (r_place ^ (lead + t)) - r_place * n_col

        @pl.when((among >= 0) & (among < n_col))
        def _():
            q = c_place ^ among
            at = pl.multiple_of((q // 2) * block + (q % 2) * half, block)
            x = tile[t * block : (t + 1) * block, pl.ds(at, block)]
            down = lax.broadcasted_iota(jnp.int32, x.shape, 0)
            across = lax.broadcasted_iota(jnp.int32, x.shape, 1)
            row_diag[0:1, pl.ds(at, block)] = jnp.sum(
                jnp.where(down == across, x, 0.0), axis=0, keepdims=True
            )

    col_max[...] = jnp.broadcast_to(
        jnp.max(col_max[...], axis=1, keepdims=True), col_max.shape
    )
    sums = []
    for which in range(2):
        lanes = range(which * half, (which + 1) * half, LANES)

        def exponentials(i, acc):
            part = pl.ds(pl.multiple_of(i * 8, 8), 8)
            top = col_max[part, :]
            total = col_sum[part, :] if which else None
            dot = col_dot[part, :] if which else None
            new = [], []
            for n, lane in enumerate(lanes):
                x = tile[part, lane : lane + LANES]
                e = jnp.exp2(x - row_max[0:1, lane : lane + LANES])
                new[0].append(acc[0][n] + e)
                new[1].append(acc[1][n] + e * x)
                e = jnp.exp2(x - top)
                total = e if total is None else total + e
                dot = e * x if dot is None else dot + e * x
            col_sum[part, :] = total
            col_dot[part, :] = dot
            return tuple(new[0]), tuple(new[1])

        zeros = tuple(jnp.zeros((8, LANES), jnp.float32) for _ in lanes)
        sums.append(lax.fori_loop(0, cols // 8, exponentials, (zeros, zeros), unroll=4))

    row_ids = lax.broadcasted_iota(jnp.int32, (n_col, block), 0)
    placed = [jnp.zeros((n_col, block), jnp.float32)] * 4
    for q in range(n_col):
        at = (q // 2) * block
        here = row_ids == (c_place ^ q)
        new = [row_max[0:1, at + (q % 2) * half : at + (q % 2) * half + block]]
        for which in sums[q % 2]:
            new.append(
                jnp.concatenate(
                    [
                        jnp.sum(which[(at + lane) // LANES], axis=0, keepdims=True)
                        for lane in range(0, block, LANES)
                    ],
                    axis=1,
                )
            )
        new.append(row_diag[0:1, at + (q % 2) * half : at + (q % 2) * half + block])
        placed = [jnp.where(here, n, p) for n, p in zip(new, placed)]
    if before:
        placed = merged(placed, [before[0][i] for i in range(4)])
    for i in range(4):
        row_ref[i] = placed[i]
    row_ids = lax.broadcasted_iota(jnp.int32, (n_row, block), 0)
    placed = [before[1][i] if before else jnp.zeros((n_row, block), jnp.float32) for i in range(3)]
    for t in range(n_text):
        part = pl.ds(t * block, block)
        here = row_ids == (r_place ^ (lead + t))
        new = [col_max[part, :].T[0:1, :]]
        for which in (col_sum, col_dot):
            new.append(jnp.sum(which[part, :].T, axis=0, keepdims=True))
        placed = [jnp.where(here, n, p) for n, p in zip(new, placed)]
    for i in range(3):
        col_ref[i] = placed[i]


def stats(coef, place, texts, images, before, n_col, n_row, keep):
    block, width = texts[0].shape
    first = not before
    rows, cols = block * n_col, block * (len(texts) if first else 1)
    vmem = pl.BlockSpec(memory_space=VMEM)
    smem = pl.BlockSpec(memory_space=SMEM)
    half = jax.ShapeDtypeStruct((rows // 2, width), jnp.bfloat16)
    out_shape = [half, half] if first else [jax.ShapeDtypeStruct((block, width), jnp.bfloat16)]
    out_shape += [
        jax.ShapeDtypeStruct((4, n_col, block), jnp.float32),
        jax.ShapeDtypeStruct((3, n_row, block), jnp.float32),
    ]
    scratch = [
        VMEM((8, rows), jnp.float32),
        VMEM((cols, LANES), jnp.float32),
        VMEM((cols, LANES), jnp.float32),
        VMEM((cols, LANES), jnp.float32),
        VMEM((8, rows), jnp.float32),
    ]
    if keep:
        out_shape.append(jax.ShapeDtypeStruct((cols, rows), jnp.float32))
    else:
        scratch.insert(0, VMEM((cols, rows), jnp.float32))
    return pl.pallas_call(
        functools.partial(stats_kernel, first, len(texts), block),
        out_shape=tuple(out_shape),
        in_specs=[smem, smem] + [vmem] * (len(texts) + len(images) + len(before)),
        out_specs=(vmem,) * len(out_shape),
        scratch_shapes=scratch,
        compiler_params=pltpu.CompilerParams(
            vmem_limit_bytes=(0 if keep else 4 * rows * cols) + 8 * 2**20
        ),
        cost_estimate=pl.CostEstimate(
            flops=FLOPS * 2 * rows * cols * width, bytes_accessed=0, transcendentals=0
        ),
        name="stats" if first else "stats_last",
    )(coef, place, *texts, *images, *before)


def merged(a, b):
    top = jnp.maximum(a[0], b[0])
    wa, wb = jnp.exp2(a[0] - top), jnp.exp2(b[0] - top)
    out = [top] + [a[i] * wa + b[i] * wb for i in (1, 2)]
    return out + [a[i] + b[i] for i in range(3, len(a))]


def by_pairs(blocks, add):
    while len(blocks) > 1:
        blocks = [add(blocks[i], blocks[i + 1]) for i in range(0, len(blocks), 2)]
    return blocks[0]


def lse_and_mean(parts):
    mean = 0.5 * parts[2] / parts[1]
    return parts[0] + jnp.log(parts[1]) * LOG2E, mean - parts[3] if len(parts) > 3 else mean


def exchanged(row_parts, col_parts, n_col, n_row):
    rows = [swap(row_parts, "col", n_col, q) for q in range(2, n_col, 2)]
    cols = swap(col_parts, "row", n_row, 1)
    rows, cols = lax.optimization_barrier((rows, cols))
    rows = by_pairs([list(x) for x in (row_parts, *rows)], merged)
    cols = merged(list(col_parts), list(cols))
    for b in range(1, n_row.bit_length() - 1):
        cols = merged(cols, list(swap(jnp.stack(cols), "row", n_row, 1 << b)))
    rows = merged(rows, list(swap(jnp.stack(rows), "col", n_col, 1)))
    return *lse_and_mean(rows), *lse_and_mean(cols)


LEVELS = 32000
LOW = 128
BIAS = 125
EXTRA = 8
MORE = 32
STEP = 32


def put_extra(out, extra_ref):
    n, width = extra_ref.shape
    rows = min(n, EXTRA)
    out[...] = jnp.zeros(out.shape, out.dtype)
    out[:rows, :width] = sum(extra_ref[i : i + rows, :] for i in range(0, n, rows))


def power(k):
    return jnp.exp2(k).astype(jnp.bfloat16).astype(jnp.float32)


def encode(out, powers, size, slab, extra):
    width = out.shape[1]
    for r in range(0, size, STEP):
        value = slab(r)
        top = jnp.maximum(jnp.max(jnp.abs(value), axis=1, keepdims=True), 1e-30)
        k = jnp.ceil(jnp.log(top) * LOG2E)
        powers[r : r + STEP, :] = jnp.broadcast_to(power(k), (STEP, LANES))
        whole = jnp.floor(jnp.abs(value) * (power(-k) * (LEVELS - 1)) + 0.5) * (1 / LOW)
        high = jnp.floor(whole)
        code = (1.0 + (whole - high)) * jnp.exp2(high - BIAS)
        out[r : r + STEP, :] = jnp.where(value < 0, -code, code).astype(jnp.bfloat16)
    half = width // 2
    first = extra[:, :half].astype(jnp.bfloat16)
    rest = extra[:, :half] - first.astype(jnp.float32)
    second = rest.astype(jnp.bfloat16)
    third = (rest - second.astype(jnp.float32)).astype(jnp.bfloat16)
    zeros = jnp.zeros((EXTRA, half), jnp.bfloat16)
    out[size : size + 2 * EXTRA, :half] = jnp.concatenate([first, second], axis=0)
    out[size : size + 2 * EXTRA, half:] = jnp.concatenate([third, zeros], axis=0)
    out[size + 2 * EXTRA :, :] = jnp.zeros((MORE - 2 * EXTRA, width), jnp.bfloat16)
    out[size + 2 * EXTRA :, :size] = powers[...].T[: MORE - 2 * EXTRA, :].astype(jnp.bfloat16)


def decode_powers(code, size):
    powers = code[size + 2 * EXTRA :, :size].astype(jnp.float32)
    return jnp.broadcast_to(powers[0:1, :], (LANES, size)).T * (LOW / (LEVELS - 1))


def decode(code, powers, r):
    lanes = []
    for lane in range(0, code.shape[1], LANES):
        c = code[r : r + STEP, lane : lane + LANES].astype(jnp.float32)
        a = jnp.abs(c)
        high = jnp.floor(jnp.log(a) * LOG2E)
        whole = (high + (BIAS - 1)) + a * jnp.exp2(-high)
        lanes.append(jnp.where(c < 0, -whole, whole) * powers[r : r + STEP, :])
    return jnp.concatenate(lanes, axis=1)


def decode_extra(code, size):
    half = code.shape[1] // 2
    left = code[size : size + 2 * EXTRA, :half].astype(jnp.float32)
    right = code[size : size + 2 * EXTRA, half:].astype(jnp.float32)
    return left[:EXTRA] + left[EXTRA:] + right[:EXTRA]


def pack_text_kernel(n, base, *refs):
    codes, out, powers, received = refs[:n], *refs[n:]
    size, half = base.shape[0] - EXTRA, base.shape[1] // 2
    more = base[size:, :half]
    for c, code in enumerate(codes):
        received[c] = decode_powers(code, size)
        more = more + decode_extra(code, size)

    def slab(r):
        value = base[r : r + STEP, :]
        for c, code in enumerate(codes):
            value = value + decode(code, received.at[c], r)
        return value

    encode(out, powers, size, slab, more)


def pack_text(base, codes):
    size, width = base.shape[0] - EXTRA, base.shape[1]
    vmem = pl.BlockSpec(memory_space=VMEM)
    return pl.pallas_call(
        functools.partial(pack_text_kernel, len(codes)),
        out_shape=jax.ShapeDtypeStruct((size + MORE, width), jnp.bfloat16),
        in_specs=[vmem] * (1 + len(codes)),
        out_specs=vmem,
        scratch_shapes=[VMEM((size, LANES), jnp.float32), VMEM((len(codes), size, LANES), jnp.float32)],
        compiler_params=pltpu.CompilerParams(vmem_limit_bytes=6 * 2**20),
        name="pack_text",
    )(base, *codes)


def pack_images_kernel(near, far, own, *refs):
    outs, powers = refs[:-1], refs[-1]
    size = near.shape[1] - EXTRA
    own[...] = near[0] + far[0]
    for j, out in enumerate(outs, 1):
        encode(
            out,
            powers.at[j - 1],
            size,
            lambda r, j=j: near[j, r : r + STEP, :] + far[j, r : r + STEP, :],
            near[j, size:, :] + far[j, size:, :],
        )


def pack_images(near, far):
    n, rows, width = near.shape
    size = rows - EXTRA
    vmem = pl.BlockSpec(memory_space=VMEM)
    code = jax.ShapeDtypeStruct((size + MORE, width), jnp.bfloat16)
    own, *codes = pl.pallas_call(
        pack_images_kernel,
        out_shape=(jax.ShapeDtypeStruct((rows, width), jnp.float32),) + (code,) * (n - 1),
        in_specs=[vmem] * 2,
        out_specs=(vmem,) * n,
        scratch_shapes=[VMEM((n - 1, size, LANES), jnp.float32)],
        compiler_params=pltpu.CompilerParams(vmem_limit_bytes=(4 + 2 * n) * 2**20),
        name="pack_images",
    )(near, far)
    return own, codes


def total_kernel(n, in_order, coef_ref, base, *refs):
    codes, before = refs[:n], refs[n:-6]
    out, extra, scalar, value, powers, sems = refs[-6:]
    size, width = base.shape[0] - EXTRA, base.shape[1]
    combine = functools.partial(functools.reduce, jnp.add) if in_order else by_pairs_added
    for c, code in enumerate(codes):
        powers[c] = decode_powers(code, size)
    copies = []
    steps = sems.shape[0]
    for i in range(steps):
        part = pl.ds(i * (size // steps), size // steps)
        for r in range(i * (size // steps), (i + 1) * (size // steps), STEP):
            value[r : r + STEP, :] = combine(
                [base[r : r + STEP, :]] + [decode(code, powers.at[c], r) for c, code in enumerate(codes)]
            )
        copies.append(pltpu.make_async_copy(value.at[part], out.at[part], sems.at[i]))
        copies[-1].start()
    more = combine([base[size:, : width // 2]] + [decode_extra(code, size) for code in codes])
    more = sum([b[...] for b in before], more)
    extra[...] = more
    scalar[0, 0] = jnp.sum(more) / coef_ref[0, 0]
    for copy in copies:
        copy.wait()


def by_pairs_added(blocks):
    return by_pairs(blocks, jnp.add)


def total_of(coef, base, codes, in_order, before, name):
    size, width = base.shape[0] - EXTRA, base.shape[1]
    vmem = pl.BlockSpec(memory_space=VMEM)
    smem = pl.BlockSpec(memory_space=SMEM)
    return pl.pallas_call(
        functools.partial(total_kernel, len(codes), in_order),
        out_shape=(
            jax.ShapeDtypeStruct((size, width), jnp.float32),
            jax.ShapeDtypeStruct((EXTRA, width // 2), jnp.float32),
            jax.ShapeDtypeStruct((1, 1), jnp.float32),
        ),
        in_specs=[smem] + [vmem] * (1 + len(codes) + len(before)),
        out_specs=(pl.BlockSpec(memory_space=pl.ANY), vmem, smem),
        scratch_shapes=[
            VMEM((size, width), jnp.float32),
            VMEM((len(codes), size, LANES), jnp.float32),
            pltpu.SemaphoreType.DMA((4,)),
        ],
        compiler_params=pltpu.CompilerParams(vmem_limit_bytes=8 * 2**20),
        name=name,
    )(coef, base, *codes, *before)


def text_block(text, tile, t, halves, row_lse, col_lse, place_ref, scale_ref, coef_ref, extra, grad_ref, out_ref, total, powers):
    coef = coef_ref[0, 0]
    r_place, c_place = place_ref[0, 0], place_ref[0, 1]
    half, width = halves[0].shape
    n_col, n_row = row_lse.shape[0], col_lse.shape[0]
    size = text.shape[0]
    block = size
    col_lse_down = jnp.broadcast_to(col_lse[pl.ds(r_place ^ t, 1), :], (LANES, size)).T
    text_id = c_place * n_row + (r_place ^ t)
    step = 32
    lane_ids = lax.broadcasted_iota(jnp.int32, (step, LANES), 1)
    row_ids = lax.broadcasted_iota(jnp.int32, (step, LANES), 0)

    for which, images in enumerate(halves):

        def one(j, carry):
            at = pl.multiple_of(j * block + which * half, block)
            if tile is None:
                image = images[pl.ds(pl.multiple_of(j * block, block), block), :]
                xs = nt_dot(text[...], image) * coef
            column = c_place ^ (2 * j + which)
            same = jnp.where(r_place * n_col + column == text_id, 1.0, 0.0)
            lse = row_lse[pl.ds(column, 1), :]
            for r in range(0, size, step):
                for lane in range(0, block, LANES):
                    if tile is None:
                        x = xs[r : r + step, lane : lane + LANES]
                    else:
                        x = tile[r : r + step, pl.ds(at + lane, LANES)]
                    e = jnp.exp2(x - lse[:, lane : lane + LANES]) + jnp.exp2(
                        x - col_lse_down[r : r + step, :]
                    )
                    g = 0.5 * e
                    if lane <= r < lane + LANES:
                        g = g - jnp.where(row_ids + (r - lane) == lane_ids, same, 0.0)
                    grad_ref[r : r + step, pl.ds(at + lane, LANES)] = g.astype(jnp.bfloat16)
            return carry

        lax.fori_loop(0, half // block, one, 0, unroll=4)
    total[:size, :] = scale_ref[0, 0] * (
        jnp.dot(grad_ref[:, :half], halves[0][...], preferred_element_type=jnp.float32)
        + jnp.dot(grad_ref[:, half:], halves[1][...], preferred_element_type=jnp.float32)
    )
    put_extra(total.at[size:, :], extra)
    if t & 1:
        encode(out_ref, powers, size, lambda r: total[r : r + STEP, :], total[size:, :])
    else:
        out_ref[...] = total[...]


def image_block(grads, texts, at, block, scale):
    total = None
    for grad, text in zip(grads, texts):
        part = lax.dot_general(
            grad[:, pl.ds(at, block)],
            text[...],
            (((0,), (0,)), ((), ())),
            preferred_element_type=jnp.float32,
        )
        total = part if total is None else total + part
    return scale * total


def text_kernel(order, n_done, kept, block, scale_ref, coef_ref, place_ref, *refs):
    even, odd, row_lse, col_lse, row_extra, col_extra = refs[:6]
    n = len(order)
    texts, rest = refs[6 : 6 + n], refs[6 + n :]
    if kept:
        tile, rest = rest[0], rest[1:]
    done_grads, done_texts, rest = rest[:n_done], rest[n_done : 2 * n_done], rest[2 * n_done :]
    grads, outs = rest[:n], rest[n : 2 * n]
    for i, t in enumerate(order):
        text_block(
            texts[i],
            tile.at[pl.ds((t - min(order)) * block, block)] if kept else None,
            t, (even, odd), row_lse, col_lse, place_ref, scale_ref, coef_ref, row_extra, grads[i], outs[i], *rest[-2:]
        )
    if n_done:
        far_ref = rest[2 * n]
        half = even.shape[0]

        def one(j, carry):
            far_ref[j, :block, :] = image_block(
                [*done_grads, *grads],
                [*done_texts, *texts],
                pl.multiple_of(j * block + half, block),
                block,
                scale_ref[0, 0],
            )
            put_extra(far_ref.at[j, block:, :], col_extra)
            return carry

        lax.fori_loop(0, half // block, one, 0)


def text_grads(scale, coef, place, even, odd, row_lse, col_lse, row_extra, col_extra, texts, tile, order, done):
    half, width = even.shape
    block = texts[0].shape[0]
    n = len(order)
    vmem = pl.BlockSpec(memory_space=VMEM)
    smem = pl.BlockSpec(memory_space=SMEM)
    out_shape = (
        [jax.ShapeDtypeStruct((block, 2 * half), jnp.bfloat16)] * n
        + [
            jax.ShapeDtypeStruct((block + MORE, width), jnp.bfloat16)
            if t & 1
            else jax.ShapeDtypeStruct((block + EXTRA, width), jnp.float32)
            for t in order
        ]
    )
    if done:
        out_shape.append(jax.ShapeDtypeStruct((half // block, block + EXTRA, width), jnp.float32))
    operands = [even, odd, row_lse, col_lse, row_extra, col_extra, *[texts[t] for t in order]]
    operands += tile
    operands += [done[t] for t in done] + [texts[t] for t in done]
    outs = pl.pallas_call(
        functools.partial(text_kernel, tuple(order), len(done), len(tile), block),
        out_shape=tuple(out_shape),
        in_specs=[smem] * 3 + [vmem] * len(operands),
        out_specs=(vmem,) * len(out_shape),
        scratch_shapes=[
            VMEM((block + EXTRA, width), jnp.float32),
            VMEM((block, LANES), jnp.float32),
        ],
        compiler_params=pltpu.CompilerParams(vmem_limit_bytes=12 * 2**20),
        cost_estimate=pl.CostEstimate(
            flops=FLOPS * 4 * n * block * 2 * half * width, bytes_accessed=0, transcendentals=0
        ),
        name=f"text_grads_{n}",
    )(scale, coef, place, *operands)
    grads = {t: outs[i] for i, t in enumerate(order)}
    parts = {t: outs[n + i] for i, t in enumerate(order)}
    return grads, parts, outs[-1]


def image_kernel(n_text, block, scale_ref, extra, *refs):
    grads, texts, out_ref = refs[:n_text], refs[n_text : 2 * n_text], refs[-1]

    def one(j, carry):
        put_extra(out_ref.at[j, block:, :], extra)
        out_ref[j, :block, :] = image_block(
            grads, texts, pl.multiple_of(j * block, block), block, scale_ref[0, 0]
        )
        return carry

    lax.fori_loop(0, out_ref.shape[0], one, 0)


def image_grads(scale, extra, grads, texts, after):
    n_text = len(grads)
    rows = grads[0].shape[1]
    block, width = texts[0].shape
    n = rows // block // 2
    vmem = pl.BlockSpec(memory_space=VMEM)
    return pl.pallas_call(
        functools.partial(image_kernel, n_text, block),
        out_shape=jax.ShapeDtypeStruct((n, block + EXTRA, width), jnp.float32),
        in_specs=[pl.BlockSpec(memory_space=SMEM)]
        + [vmem] * (2 * n_text + 1)
        + [pl.BlockSpec(memory_space=pl.ANY)] * len(after),
        out_specs=vmem,
        compiler_params=pltpu.CompilerParams(vmem_limit_bytes=12 * 2**20),
        cost_estimate=pl.CostEstimate(
            flops=FLOPS * 2 * n * block * n_text * block * width, bytes_accessed=0, transcendentals=0
        ),
        name="image_grads",
    )(scale, extra, *grads, *texts, *after)


def on_device(n_row, n_col, image_embeds, text_embeds, logit_scale):
    block = image_embeds.shape[0]
    r, c = lax.axis_index("row"), lax.axis_index("col")
    place = jnp.stack([r, c]).reshape(1, 2)
    scale = logit_scale.reshape(1, 1)
    coef = scale * LOG2E
    image_half, text_half = image_embeds.astype(jnp.bfloat16), text_embeds.astype(jnp.bfloat16)
    even, odd, texts, text_last = gather_both(image_half, text_half, n_col, n_row)
    keep = 4 * n_row * n_col * block * block <= 16 * 2**20
    even, odd, *before = stats(
        coef, place, texts, (*even, *odd), (), n_col, n_row, keep
    )
    text_last, row_parts, col_parts, *tile_last = stats(
        coef, place, text_last, (even, odd), before[:2], n_col, n_row, keep
    )
    texts = [*texts, text_last]
    tile = before[2:]
    row_lse, row_extra, col_lse, col_extra = exchanged(row_parts, col_parts, n_col, n_row)

    held = (scale, coef, place, even, odd, row_lse, col_lse, row_extra, col_extra, texts)
    last = n_row - 1
    grads, parts, _ = text_grads(*held, tile_last, [last], {})
    received = swap(parts[last], "row", n_row, 1)
    more, more_parts, far = text_grads(*held, tile, list(range(last))[::-1], grads)
    grads |= more
    parts |= more_parts
    codes = {q: [] for q in range(0, n_row, 2)}
    codes[last ^ 1].append(received)
    after = [pack_text(parts[last ^ 1], codes[last ^ 1])] if n_row > 2 else [received]
    near = image_grads(scale, col_extra, [grads[t] for t in range(n_row)], texts, after)
    far = swap(far, "col", n_col, 1)
    odd_parts, far = lax.optimization_barrier(([parts[q] for q in range(1, last, 2)], far))
    for q, part in zip(range(1, last, 2), odd_parts):
        codes[q ^ 1].append(swap(part, "row", n_row, 1))
    for b in range(1, n_row.bit_length() - 1):
        for q in [q for q in codes if q & (1 << b)]:
            code = after[0] if (b, q) == (1, last ^ 1) else pack_text(parts[q], codes[q])
            codes[q ^ (1 << b)].append(swap(code, "row", n_row, 1 << b))
            del codes[q]
    grad_text, text_extra, _ = total_of(coef, parts[0], codes[0], True, [], "grad_text")

    own, others = pack_images(near, far)
    others = [swap(code, "col", n_col, 2 * j) for j, code in enumerate(others, 1)]
    grad_image, _, grad_scale = total_of(coef, own, others, False, [text_extra], "grad_image")
    return grad_image, grad_text, grad_scale.reshape(())


def solution(mesh):
    images = P(("row", "col"), None)
    texts = P(("col", "row"), None)
    return jax.shard_map(
        functools.partial(on_device, mesh.shape["row"], mesh.shape["col"]),
        mesh=mesh,
        in_specs=(images, texts, P()),
        out_specs=(images, texts, P()),
        check_vma=False,
    )
```

```python
import functools
import math

import jax
import jax.numpy as jnp
from jax import lax
from jax.experimental import pallas as pl
from jax.experimental.pallas import tpu as pltpu
from jax.sharding import PartitionSpec as P

LOG2E = 1.4426950408889634
LN2 = 0.6931471805599453
LANES = 128
VMEM = pltpu.VMEM
SMEM = pltpu.SMEM
FLOPS = 20


def swap(x, axis, n, q):
    return lax.ppermute(x, axis, [(i, i ^ q) for i in range(n)])


def gather_both(image, text, n_col, n_row):
    images = [swap(image, "col", n_col, q) for q in range(2, n_col, 2)]
    texts = [swap(text, "row", n_row, q) for q in range(1, n_row - 1)]
    images, texts = lax.optimization_barrier((images, texts))
    odd = [swap(i, "col", n_col, 1) for i in (image, *images)]
    return [image, *images], odd, [text, *texts], [swap(texts[-1], "row", n_row, 1)]


def nt_dot(a, b):
    return lax.dot_general(a, b, (((1,), (1,)), ((), ())), preferred_element_type=jnp.float32)


def stats_kernel(first, n_text, block, coef_ref, place_ref, *refs):
    texts, refs = refs[:n_text], refs[n_text:]
    coef = coef_ref[0, 0]
    r_place, c_place = place_ref[0, 0], place_ref[0, 1]
    *refs, row_max, col_max, col_sum, col_dot, row_diag = refs
    if first:
        *refs, even, odd, row_ref, col_ref, tile = refs
        halves = (even, odd)
        each = len(refs) // 2
        for i, piece in enumerate(refs):
            at = (i % each) * block
            halves[i // each][at : at + block, :] = piece[...]
        before = None
    else:
        even, odd, *before, last, row_ref, col_ref, tile = refs
        halves = (even, odd)
        last[...] = functools.reduce(jnp.add, [text[...] for text in texts])
        texts, n_text = [last], 1
    cols, rows = tile.shape
    half = rows // 2
    lead = 0 if first else col_ref.shape[1] - n_text
    col_max[...] = jnp.full(col_max.shape, -jnp.inf, jnp.float32)
    row_diag[...] = jnp.zeros(row_diag.shape, jnp.float32)
    n_col, n_row = row_ref.shape[1], col_ref.shape[1]

    for which, images in enumerate(halves):

        def products(j, carry):
            image = images[pl.ds(pl.multiple_of(j * block, block), block), :]
            at = pl.multiple_of(j * block + which * half, block)
            top = None
            for t in range(n_text):
                part = pl.ds(t * block, block)
                x = nt_dot(texts[t][...], image) * coef
                tile[part, pl.ds(at, block)] = x
                top_t = jnp.max(x, axis=0, keepdims=True)
                top = top_t if top is None else jnp.maximum(top, top_t)
                held = col_max[part, :]
                for lane in range(0, block, LANES):
                    held = jnp.maximum(held, x[:, lane : lane + LANES])
                col_max[part, :] = held
            row_max[0:1, pl.ds(at, block)] = top
            return carry

        lax.fori_loop(0, half // block, products, 0, unroll=4)

    for t in range(n_text):
        among = c_place * n_row + (r_place ^ (lead + t)) - r_place * n_col

        @pl.when((among >= 0) & (among < n_col))
        def _():
            q = c_place ^ among
            at = pl.multiple_of((q // 2) * block + (q % 2) * half, block)
            x = tile[t * block : (t + 1) * block, pl.ds(at, block)]
            down = lax.broadcasted_iota(jnp.int32, x.shape, 0)
            across = lax.broadcasted_iota(jnp.int32, x.shape, 1)
            row_diag[0:1, pl.ds(at, block)] = jnp.sum(
                jnp.where(down == across, x, 0.0), axis=0, keepdims=True
            )

    col_max[...] = jnp.broadcast_to(
        jnp.max(col_max[...], axis=1, keepdims=True), col_max.shape
    )
    sums = []
    for which in range(2):
        lanes = range(which * half, (which + 1) * half, LANES)

        def exponentials(i, acc):
            part = pl.ds(pl.multiple_of(i * 8, 8), 8)
            top = col_max[part, :]
            total = col_sum[part, :] if which else None
            dot = col_dot[part, :] if which else None
            new = [], []
            for n, lane in enumerate(lanes):
                x = tile[part, lane : lane + LANES]
                e = jnp.exp2(x - row_max[0:1, lane : lane + LANES])
                new[0].append(acc[0][n] + e)
                new[1].append(acc[1][n] + e * x)
                e = jnp.exp2(x - top)
                total = e if total is None else total + e
                dot = e * x if dot is None else dot + e * x
            col_sum[part, :] = total
            col_dot[part, :] = dot
            return tuple(new[0]), tuple(new[1])

        zeros = tuple(jnp.zeros((8, LANES), jnp.float32) for _ in lanes)
        sums.append(lax.fori_loop(0, cols // 8, exponentials, (zeros, zeros), unroll=8))

    row_ids = lax.broadcasted_iota(jnp.int32, (n_col, block), 0)
    placed = [jnp.zeros((n_col, block), jnp.float32)] * 4
    for q in range(n_col):
        at = (q // 2) * block
        here = row_ids == (c_place ^ q)
        new = [row_max[0:1, at + (q % 2) * half : at + (q % 2) * half + block]]
        for which in sums[q % 2]:
            new.append(
                jnp.concatenate(
                    [
                        jnp.sum(which[(at + lane) // LANES], axis=0, keepdims=True)
                        for lane in range(0, block, LANES)
                    ],
                    axis=1,
                )
            )
        new.append(row_diag[0:1, at + (q % 2) * half : at + (q % 2) * half + block])
        placed = [jnp.where(here, n, p) for n, p in zip(new, placed)]
    if before:
        placed = merged(placed, [before[0][i] for i in range(4)])
    for i in range(4):
        row_ref[i] = placed[i]
    row_ids = lax.broadcasted_iota(jnp.int32, (n_row, block), 0)
    placed = [before[1][i] if before else jnp.zeros((n_row, block), jnp.float32) for i in range(3)]
    for t in range(n_text):
        part = pl.ds(t * block, block)
        here = row_ids == (r_place ^ (lead + t))
        new = [col_max[part, :].T[0:1, :]]
        for which in (col_sum, col_dot):
            new.append(jnp.sum(which[part, :].T, axis=0, keepdims=True))
        placed = [jnp.where(here, n, p) for n, p in zip(new, placed)]
    for i in range(3):
        col_ref[i] = placed[i]


def stats(coef, place, texts, images, before, n_col, n_row, keep):
    block, width = texts[0].shape
    first = not before
    rows, cols = block * n_col, block * (len(texts) if first else 1)
    vmem = pl.BlockSpec(memory_space=VMEM)
    smem = pl.BlockSpec(memory_space=SMEM)
    half = jax.ShapeDtypeStruct((rows // 2, width), jnp.bfloat16)
    out_shape = [half, half] if first else [jax.ShapeDtypeStruct((block, width), jnp.bfloat16)]
    out_shape += [
        jax.ShapeDtypeStruct((4, n_col, block), jnp.float32),
        jax.ShapeDtypeStruct((3, n_row, block), jnp.float32),
    ]
    scratch = [
        VMEM((8, rows), jnp.float32),
        VMEM((cols, LANES), jnp.float32),
        VMEM((cols, LANES), jnp.float32),
        VMEM((cols, LANES), jnp.float32),
        VMEM((8, rows), jnp.float32),
    ]
    if keep:
        out_shape.append(jax.ShapeDtypeStruct((cols, rows), jnp.float32))
    else:
        scratch.insert(0, VMEM((cols, rows), jnp.float32))
    return pl.pallas_call(
        functools.partial(stats_kernel, first, len(texts), block),
        out_shape=tuple(out_shape),
        in_specs=[smem, smem] + [vmem] * (len(texts) + len(images) + len(before)),
        out_specs=(vmem,) * len(out_shape),
        scratch_shapes=scratch,
        compiler_params=pltpu.CompilerParams(
            vmem_limit_bytes=(0 if keep else 4 * rows * cols) + 8 * 2**20
        ),
        cost_estimate=pl.CostEstimate(
            flops=FLOPS * 2 * rows * cols * width, bytes_accessed=0, transcendentals=0
        ),
        name="stats" if first else "stats_last",
    )(coef, place, *texts, *images, *before)


def merged(a, b):
    top = jnp.maximum(a[0], b[0])
    wa, wb = jnp.exp2(a[0] - top), jnp.exp2(b[0] - top)
    out = [top] + [a[i] * wa + b[i] * wb for i in (1, 2)]
    return out + [a[i] + b[i] for i in range(3, len(a))]


def by_pairs(blocks, add):
    while len(blocks) > 1:
        blocks = [add(blocks[i], blocks[i + 1]) for i in range(0, len(blocks), 2)]
    return blocks[0]


def lse_and_mean(parts):
    mean = 0.5 * parts[2] / parts[1]
    return parts[0] + jnp.log(parts[1]) * LOG2E, mean - parts[3] if len(parts) > 3 else mean


def exchanged(row_parts, col_parts, n_col, n_row):
    rows = [swap(row_parts, "col", n_col, q) for q in range(2, n_col, 2)]
    cols = swap(col_parts, "row", n_row, 1)
    rows, cols = lax.optimization_barrier((rows, cols))
    rows = by_pairs([list(x) for x in (row_parts, *rows)], merged)
    cols = merged(list(col_parts), list(cols))
    for b in range(1, n_row.bit_length() - 1):
        cols = merged(cols, list(swap(jnp.stack(cols), "row", n_row, 1 << b)))
    rows = merged(rows, list(swap(jnp.stack(rows), "col", n_col, 1)))
    return *lse_and_mean(rows), *lse_and_mean(cols)


LEVELS = 32000
LOW = 128
BIAS = 125
EXTRA = 8
MORE = 2 * EXTRA
STEP = 32


def put_extra(out, extra_ref):
    n, width = extra_ref.shape
    rows = min(n, EXTRA)
    out[...] = jnp.zeros(out.shape, out.dtype)
    out[:rows, :width] = sum(extra_ref[i : i + rows, :] for i in range(0, n, rows))


def power(k):
    return jnp.exp2(k).astype(jnp.bfloat16).astype(jnp.float32)


def encode(out, powers, size, slab, extra):
    width = out.shape[1]
    for r in range(0, size, STEP):
        value = slab(r)
        top = jnp.maximum(jnp.max(jnp.abs(value), axis=1, keepdims=True), 1e-30)
        k = jnp.ceil(jnp.log(top) * LOG2E)
        powers[r : r + STEP, :] = jnp.broadcast_to(power(k), (STEP, LANES))
        whole = jnp.floor(jnp.abs(value) * (power(-k) * (LEVELS - 1)) + 0.5) * (1 / LOW)
        high = jnp.floor(whole)
        code = (1.0 + (whole - high)) * jnp.exp2(high - BIAS)
        out[r : r + STEP, :] = jnp.where(value < 0, -code, code).astype(jnp.bfloat16)
    half = width // 2
    first = extra[:, :half].astype(jnp.bfloat16)
    rest = extra[:, :half] - first.astype(jnp.float32)
    second = rest.astype(jnp.bfloat16)
    third = (rest - second.astype(jnp.float32)).astype(jnp.bfloat16)
    fourth = powers[...].T[:EXTRA, :].astype(jnp.bfloat16)
    if size < half:
        fourth = jnp.concatenate([fourth, jnp.zeros((EXTRA, half - size), jnp.bfloat16)], axis=1)
    out[size:, :half] = jnp.concatenate([first, second], axis=0)
    out[size:, half:] = jnp.concatenate([third, fourth], axis=0)


def decode_powers(code, size):
    half = code.shape[1] // 2
    powers = code[size:, half : half + size].astype(jnp.float32)
    return jnp.broadcast_to(powers[EXTRA : EXTRA + 1, :], (LANES, size)).T * (LOW / (LEVELS - 1))


def decode(code, powers, r):
    lanes = []
    for lane in range(0, code.shape[1], LANES):
        c = code[r : r + STEP, lane : lane + LANES].astype(jnp.float32)
        a = jnp.abs(c)
        high = jnp.floor(jnp.log(a) * LOG2E)
        whole = (high + (BIAS - 1)) + a * jnp.exp2(-high)
        lanes.append(jnp.where(c < 0, -whole, whole) * powers[r : r + STEP, :])
    return jnp.concatenate(lanes, axis=1)


def decode_extra(code, size):
    half = code.shape[1] // 2
    left = code[size:, :half].astype(jnp.float32)
    right = code[size:, half:].astype(jnp.float32)
    return left[:EXTRA] + left[EXTRA:] + right[:EXTRA]


def pack_text_kernel(n, base, *refs):
    codes, out, powers, received = refs[:n], *refs[n:]
    size, half = base.shape[0] - EXTRA, base.shape[1] // 2
    more = base[size:, :half]
    for c, code in enumerate(codes):
        received[c] = decode_powers(code, size)
        more = more + decode_extra(code, size)

    def slab(r):
        value = base[r : r + STEP, :]
        for c, code in enumerate(codes):
            value = value + decode(code, received.at[c], r)
        return value

    encode(out, powers, size, slab, more)


def pack_text(base, codes):
    size, width = base.shape[0] - EXTRA, base.shape[1]
    vmem = pl.BlockSpec(memory_space=VMEM)
    return pl.pallas_call(
        functools.partial(pack_text_kernel, len(codes)),
        out_shape=jax.ShapeDtypeStruct((size + MORE, width), jnp.bfloat16),
        in_specs=[vmem] * (1 + len(codes)),
        out_specs=vmem,
        scratch_shapes=[VMEM((size, LANES), jnp.float32), VMEM((len(codes), size, LANES), jnp.float32)],
        compiler_params=pltpu.CompilerParams(vmem_limit_bytes=6 * 2**20),
        name="pack_text",
    )(base, *codes)


def pack_images_kernel(near, far, own, *refs):
    outs, powers = refs[:-1], refs[-1]
    size = near.shape[1] - EXTRA
    own[...] = near[0] + far[0]
    for j, out in enumerate(outs, 1):
        encode(
            out,
            powers.at[j - 1],
            size,
            lambda r, j=j: near[j, r : r + STEP, :] + far[j, r : r + STEP, :],
            near[j, size:, :] + far[j, size:, :],
        )


def pack_images(near, far):
    n, rows, width = near.shape
    size = rows - EXTRA
    vmem = pl.BlockSpec(memory_space=VMEM)
    code = jax.ShapeDtypeStruct((size + MORE, width), jnp.bfloat16)
    own, *codes = pl.pallas_call(
        pack_images_kernel,
        out_shape=(jax.ShapeDtypeStruct((rows, width), jnp.float32),) + (code,) * (n - 1),
        in_specs=[vmem] * 2,
        out_specs=(vmem,) * n,
        scratch_shapes=[VMEM((n - 1, size, LANES), jnp.float32)],
        compiler_params=pltpu.CompilerParams(vmem_limit_bytes=(4 + 2 * n) * 2**20),
        name="pack_images",
    )(near, far)
    return own, codes


def total_kernel(n, in_order, coef_ref, base, *refs):
    codes, before = refs[:n], refs[n:-6]
    out, extra, scalar, value, powers, sems = refs[-6:]
    size, width = base.shape[0] - EXTRA, base.shape[1]
    combine = functools.partial(functools.reduce, jnp.add) if in_order else first_and_pairs
    for c, code in enumerate(codes):
        powers[c] = decode_powers(code, size)
    copies = []
    steps = sems.shape[0]
    for i in range(steps):
        part = pl.ds(i * (size // steps), size // steps)
        for r in range(i * (size // steps), (i + 1) * (size // steps), STEP):
            value[r : r + STEP, :] = combine(
                [base[r : r + STEP, :]] + [decode(code, powers.at[c], r) for c, code in enumerate(codes)]
            )
        copies.append(pltpu.make_async_copy(value.at[part], out.at[part], sems.at[i]))
        copies[-1].start()
    more = combine([base[size:, : width // 2]] + [decode_extra(code, size) for code in codes])
    more = sum([b[...] for b in before], more)
    extra[...] = more
    scalar[0, 0] = jnp.sum(more) / coef_ref[0, 0]
    for copy in copies:
        copy.wait()


def add_kernel(base, code, out, powers):
    size, half = base.shape[0] - EXTRA, base.shape[1] // 2
    powers[...] = decode_powers(code, size)
    for r in range(0, size, STEP):
        out[r : r + STEP, :] = base[r : r + STEP, :] + decode(code, powers, r)
    out[size:, :half] = base[size:, :half] + decode_extra(code, size)
    out[size:, half:] = jnp.zeros((EXTRA, half), jnp.float32)


def added(base, code):
    vmem = pl.BlockSpec(memory_space=VMEM)
    return pl.pallas_call(
        add_kernel,
        out_shape=jax.ShapeDtypeStruct(base.shape, jnp.float32),
        in_specs=[vmem] * 2,
        out_specs=vmem,
        scratch_shapes=[VMEM((base.shape[0] - EXTRA, LANES), jnp.float32)],
        compiler_params=pltpu.CompilerParams(vmem_limit_bytes=6 * 2**20),
        name="added",
    )(base, code)


def first_and_pairs(blocks):
    if len(blocks) == 1:
        return blocks[0]
    pairs = [blocks[0]] + [blocks[i] + blocks[i + 1] for i in range(1, len(blocks), 2)]
    return by_pairs(pairs, jnp.add)


def total_of(coef, base, codes, in_order, before, name):
    size, width = base.shape[0] - EXTRA, base.shape[1]
    vmem = pl.BlockSpec(memory_space=VMEM)
    smem = pl.BlockSpec(memory_space=SMEM)
    return pl.pallas_call(
        functools.partial(total_kernel, len(codes), in_order),
        out_shape=(
            jax.ShapeDtypeStruct((size, width), jnp.float32),
            jax.ShapeDtypeStruct((EXTRA, width // 2), jnp.float32),
            jax.ShapeDtypeStruct((1, 1), jnp.float32),
        ),
        in_specs=[smem] + [vmem] * (1 + len(codes) + len(before)),
        out_specs=(pl.BlockSpec(memory_space=pl.ANY), vmem, smem),
        scratch_shapes=[
            VMEM((size, width), jnp.float32),
            VMEM((len(codes), size, LANES), jnp.float32),
            pltpu.SemaphoreType.DMA((4,)),
        ],
        compiler_params=pltpu.CompilerParams(vmem_limit_bytes=8 * 2**20),
        name=name,
    )(coef, base, *codes, *before)


def text_block(text, tile, t, halves, row_lse, col_lse, place_ref, scale_ref, coef_ref, extra, grad_ref, out_ref, total, powers):
    coef = coef_ref[0, 0]
    r_place, c_place = place_ref[0, 0], place_ref[0, 1]
    half, width = halves[0].shape
    n_col, n_row = row_lse.shape[0], col_lse.shape[0]
    size = text.shape[0]
    block = size
    col_lse_down = jnp.broadcast_to(col_lse[pl.ds(r_place ^ t, 1), :], (LANES, size)).T
    text_id = c_place * n_row + (r_place ^ t)
    step = 32
    lane_ids = lax.broadcasted_iota(jnp.int32, (step, LANES), 1)
    row_ids = lax.broadcasted_iota(jnp.int32, (step, LANES), 0)

    for which, images in enumerate(halves):

        def one(j, carry):
            at = pl.multiple_of(j * block + which * half, block)
            if tile is None:
                image = images[pl.ds(pl.multiple_of(j * block, block), block), :]
                xs = nt_dot(text[...], image) * coef
            column = c_place ^ (2 * j + which)
            same = jnp.where(r_place * n_col + column == text_id, 1.0, 0.0)
            lse = row_lse[pl.ds(column, 1), :]
            for r in range(0, size, step):
                for lane in range(0, block, LANES):
                    if tile is None:
                        x = xs[r : r + step, lane : lane + LANES]
                    else:
                        x = tile[r : r + step, pl.ds(at + lane, LANES)]
                    e = jnp.exp2(x - lse[:, lane : lane + LANES]) + jnp.exp2(
                        x - col_lse_down[r : r + step, :]
                    )
                    g = 0.5 * e
                    if lane <= r < lane + LANES:
                        g = g - jnp.where(row_ids + (r - lane) == lane_ids, same, 0.0)
                    grad_ref[r : r + step, pl.ds(at + lane, LANES)] = g.astype(jnp.bfloat16)
            return carry

        lax.fori_loop(0, half // block, one, 0, unroll=4)
    total[:size, :] = scale_ref[0, 0] * (
        jnp.dot(grad_ref[:, :half], halves[0][...], preferred_element_type=jnp.float32)
        + jnp.dot(grad_ref[:, half:], halves[1][...], preferred_element_type=jnp.float32)
    )
    put_extra(total.at[size:, :], extra)
    if t & 1:
        encode(out_ref, powers, size, lambda r: total[r : r + STEP, :], total[size:, :])
    else:
        out_ref[...] = total[...]


def image_block(grads, texts, at, block, scale):
    total = None
    for grad, text in zip(grads, texts):
        part = lax.dot_general(
            grad[:, pl.ds(at, block)],
            text[...],
            (((0,), (0,)), ((), ())),
            preferred_element_type=jnp.float32,
        )
        total = part if total is None else total + part
    return scale * total


def text_kernel(order, n_done, kept, block, scale_ref, coef_ref, place_ref, *refs):
    even, odd, row_lse, col_lse, row_extra, col_extra = refs[:6]
    n = len(order)
    texts, rest = refs[6 : 6 + n], refs[6 + n :]
    if kept:
        tile, rest = rest[0], rest[1:]
    done_grads, done_texts, rest = rest[:n_done], rest[n_done : 2 * n_done], rest[2 * n_done :]
    grads, outs = rest[:n], rest[n : 2 * n]
    for i, t in enumerate(order):
        text_block(
            texts[i],
            tile.at[pl.ds((t - min(order)) * block, block)] if kept else None,
            t, (even, odd), row_lse, col_lse, place_ref, scale_ref, coef_ref, row_extra, grads[i], outs[i], *rest[-2:]
        )
    if n_done:
        far_ref = rest[2 * n]
        half = even.shape[0]

        def one(j, carry):
            far_ref[j, :block, :] = image_block(
                [*done_grads, *grads],
                [*done_texts, *texts],
                pl.multiple_of(j * block + half, block),
                block,
                scale_ref[0, 0],
            )
            put_extra(far_ref.at[j, block:, :], col_extra)
            return carry

        lax.fori_loop(0, half // block, one, 0, unroll=4)


def text_grads(scale, coef, place, even, odd, row_lse, col_lse, row_extra, col_extra, texts, tile, order, done):
    half, width = even.shape
    block = texts[0].shape[0]
    n = len(order)
    vmem = pl.BlockSpec(memory_space=VMEM)
    smem = pl.BlockSpec(memory_space=SMEM)
    out_shape = (
        [jax.ShapeDtypeStruct((block, 2 * half), jnp.bfloat16)] * n
        + [
            jax.ShapeDtypeStruct((block + MORE, width), jnp.bfloat16)
            if t & 1
            else jax.ShapeDtypeStruct((block + EXTRA, width), jnp.float32)
            for t in order
        ]
    )
    if done:
        out_shape.append(jax.ShapeDtypeStruct((half // block, block + EXTRA, width), jnp.float32))
    operands = [even, odd, row_lse, col_lse, row_extra, col_extra, *[texts[t] for t in order]]
    operands += tile
    operands += [done[t] for t in done] + [texts[t] for t in done]
    outs = pl.pallas_call(
        functools.partial(text_kernel, tuple(order), len(done), len(tile), block),
        out_shape=tuple(out_shape),
        in_specs=[smem] * 3 + [vmem] * len(operands),
        out_specs=(vmem,) * len(out_shape),
        scratch_shapes=[
            VMEM((block + EXTRA, width), jnp.float32),
            VMEM((block, LANES), jnp.float32),
        ],
        compiler_params=pltpu.CompilerParams(vmem_limit_bytes=12 * 2**20),
        cost_estimate=pl.CostEstimate(
            flops=FLOPS * 4 * n * block * 2 * half * width, bytes_accessed=0, transcendentals=0
        ),
        name=f"text_grads_{n}",
    )(scale, coef, place, *operands)
    grads = {t: outs[i] for i, t in enumerate(order)}
    parts = {t: outs[n + i] for i, t in enumerate(order)}
    return grads, parts, outs[-1]


def image_kernel(n_text, block, scale_ref, extra, *refs):
    grads, texts, out_ref = refs[:n_text], refs[n_text : 2 * n_text], refs[-1]

    def one(j, carry):
        put_extra(out_ref.at[j, block:, :], extra)
        out_ref[j, :block, :] = image_block(
            grads, texts, pl.multiple_of(j * block, block), block, scale_ref[0, 0]
        )
        return carry

    lax.fori_loop(0, out_ref.shape[0], one, 0, unroll=4)


def image_grads(scale, extra, grads, texts, after):
    n_text = len(grads)
    rows = grads[0].shape[1]
    block, width = texts[0].shape
    n = rows // block // 2
    vmem = pl.BlockSpec(memory_space=VMEM)
    return pl.pallas_call(
        functools.partial(image_kernel, n_text, block),
        out_shape=jax.ShapeDtypeStruct((n, block + EXTRA, width), jnp.float32),
        in_specs=[pl.BlockSpec(memory_space=SMEM)]
        + [vmem] * (2 * n_text + 1)
        + [pl.BlockSpec(memory_space=pl.ANY)] * len(after),
        out_specs=vmem,
        compiler_params=pltpu.CompilerParams(vmem_limit_bytes=12 * 2**20),
        cost_estimate=pl.CostEstimate(
            flops=FLOPS * 2 * n * block * n_text * block * width, bytes_accessed=0, transcendentals=0
        ),
        name="image_grads",
    )(scale, extra, *grads, *texts, *after)


def on_device(n_row, n_col, image_embeds, text_embeds, logit_scale):
    block = image_embeds.shape[0]
    r, c = lax.axis_index("row"), lax.axis_index("col")
    place = jnp.stack([r, c]).reshape(1, 2)
    scale = logit_scale.reshape(1, 1)
    coef = scale * LOG2E
    image_half, text_half = image_embeds.astype(jnp.bfloat16), text_embeds.astype(jnp.bfloat16)
    even, odd, texts, text_last = gather_both(image_half, text_half, n_col, n_row)
    keep = 4 * n_row * n_col * block * block <= 16 * 2**20
    even, odd, *before = stats(
        coef, place, texts, (*even, *odd), (), n_col, n_row, keep
    )
    text_last, row_parts, col_parts, *tile_last = stats(
        coef, place, text_last, (even, odd), before[:2], n_col, n_row, keep
    )
    texts = [*texts, text_last]
    tile = before[2:]
    row_lse, row_extra, col_lse, col_extra = exchanged(row_parts, col_parts, n_col, n_row)

    held = (scale, coef, place, even, odd, row_lse, col_lse, row_extra, col_extra, texts)
    last = n_row - 1
    grads, parts, _ = text_grads(*held, tile_last, [last], {})
    received = swap(parts[last], "row", n_row, 1)
    more, more_parts, far = text_grads(*held, tile, list(range(last))[::-1], grads)
    grads |= more
    parts |= more_parts
    codes = {q: [] for q in range(0, n_row, 2)}
    codes[last ^ 1].append(received)
    after = [pack_text(parts[last ^ 1], codes[last ^ 1])] if n_row > 2 else [received]
    near = image_grads(scale, col_extra, [grads[t] for t in range(n_row)], texts, after)
    far = swap(far, "col", n_col, 1)
    odd_parts, far = lax.optimization_barrier(([parts[q] for q in range(1, last, 2)], far))
    for q, part in zip(range(1, last, 2), odd_parts):
        codes[q ^ 1].append(swap(part, "row", n_row, 1))
    for b in range(1, n_row.bit_length() - 1):
        for q in [q for q in codes if q & (1 << b)]:
            code = after[0] if (b, q) == (1, last ^ 1) else pack_text(parts[q], codes[q])
            codes[q ^ (1 << b)].append(swap(code, "row", n_row, 1 << b))
            del codes[q]
    grad_text, text_extra, _ = total_of(coef, parts[0], codes[0], True, [], "grad_text")

    own, others = pack_images(near, far)
    others = [swap(code, "col", n_col, 2 * j) for j, code in enumerate(others, 1)]
    first, text_extra = lax.optimization_barrier((others[0], text_extra))
    grad_image, _, grad_scale = total_of(
        coef, added(own, first), others[1:], False, [text_extra], "grad_image"
    )
    return grad_image, grad_text, grad_scale.reshape(())


def solution(mesh):
    images = P(("row", "col"), None)
    texts = P(("col", "row"), None)
    return jax.shard_map(
        functools.partial(on_device, mesh.shape["row"], mesh.shape["col"]),
        mesh=mesh,
        in_specs=(images, texts, P()),
        out_specs=(images, texts, P()),
        check_vma=False,
    )
```

```python
import functools
import math

import jax
import jax.numpy as jnp
from jax import lax
from jax.experimental import pallas as pl
from jax.experimental.pallas import tpu as pltpu
from jax.sharding import PartitionSpec as P

LOG2E = 1.4426950408889634
LN2 = 0.6931471805599453
LANES = 128
VMEM = pltpu.VMEM
SMEM = pltpu.SMEM
FLOPS = 20


def swap(x, axis, n, q):
    return lax.ppermute(x, axis, [(i, i ^ q) for i in range(n)])


def gather_both(image, text, n_col, n_row):
    images = [swap(image, "col", n_col, q) for q in range(2, n_col, 2)]
    texts = [swap(text, "row", n_row, q) for q in range(1, n_row - 1)]
    images, texts = lax.optimization_barrier((images, texts))
    odd = [swap(i, "col", n_col, 1) for i in (image, *images)]
    return [image, *images], odd, [text, *texts], [swap(texts[-1], "row", n_row, 1)]


def nt_dot(a, b):
    return lax.dot_general(a, b, (((1,), (1,)), ((), ())), preferred_element_type=jnp.float32)


def stats_kernel(first, keep, n_text, block, coef_ref, place_ref, *refs):
    coef = coef_ref[0, 0]
    r_place, c_place = place_ref[0, 0], place_ref[0, 1]
    texts, refs = refs[:n_text], refs[n_text:]
    *refs, col_sum, col_dot, row_diag = refs
    if keep:
        *refs, tile, other, row_max, col_max = refs
    else:
        *refs, tile, row_max, col_max = refs
    if first:
        *refs, even, odd, row_ref, col_ref = refs
        halves = (even, odd)
        each = len(refs) // 2
        for i, piece in enumerate(refs):
            at = (i % each) * block
            halves[i // each][at : at + block, :] = piece[...]
        before = None
    else:
        even, odd, *before, last, row_ref, col_ref = refs
        halves = (even, odd)
        last[...] = functools.reduce(jnp.add, [text[...] for text in texts])
        texts, n_text = [last], 1
    cols, rows = tile.shape
    half = rows // 2
    lead = 0 if first else col_ref.shape[1] - n_text
    col_max[...] = jnp.full(col_max.shape, -jnp.inf, jnp.float32)
    row_diag[...] = jnp.zeros(row_diag.shape, jnp.float32)
    n_col, n_row = row_ref.shape[1], col_ref.shape[1]

    for which, images in enumerate(halves):

        def products(j, carry):
            image = images[pl.ds(pl.multiple_of(j * block, block), block), :]
            at = pl.multiple_of(j * block + which * half, block)
            top = None
            for t in range(n_text):
                part = pl.ds(t * block, block)
                x = nt_dot(texts[t][...], image) * coef
                tile[part, pl.ds(at, block)] = x
                top_t = jnp.max(x, axis=0, keepdims=True)
                top = top_t if top is None else jnp.maximum(top, top_t)
                held = col_max[part, :]
                for lane in range(0, block, LANES):
                    held = jnp.maximum(held, x[:, lane : lane + LANES])
                col_max[part, :] = held
            row_max[0:1, pl.ds(at, block)] = top
            return carry

        lax.fori_loop(0, half // block, products, 0, unroll=4)

    for t in range(n_text):
        among = c_place * n_row + (r_place ^ (lead + t)) - r_place * n_col

        @pl.when((among >= 0) & (among < n_col))
        def _():
            q = c_place ^ among
            at = pl.multiple_of((q // 2) * block + (q % 2) * half, block)
            x = tile[t * block : (t + 1) * block, pl.ds(at, block)]
            down = lax.broadcasted_iota(jnp.int32, x.shape, 0)
            across = lax.broadcasted_iota(jnp.int32, x.shape, 1)
            row_diag[0:1, pl.ds(at, block)] = jnp.sum(
                jnp.where(down == across, x, 0.0), axis=0, keepdims=True
            )

    col_max[...] = jnp.broadcast_to(
        jnp.max(col_max[...], axis=1, keepdims=True), col_max.shape
    )
    sums = []
    for which in range(2):
        lanes = range(which * half, (which + 1) * half, LANES)

        def exponentials(i, acc):
            part = pl.ds(pl.multiple_of(i * 8, 8), 8)
            top = col_max[part, :]
            total = col_sum[part, :] if which else None
            dot = col_dot[part, :] if which else None
            new = [], []
            for n, lane in enumerate(lanes):
                x = tile[part, lane : lane + LANES]
                e = jnp.exp2(x - row_max[0:1, lane : lane + LANES])
                new[0].append(acc[0][n] + e)
                new[1].append(acc[1][n] + e * x)
                if keep:
                    tile[part, lane : lane + LANES] = e
                e = jnp.exp2(x - top)
                if keep:
                    other[part, lane : lane + LANES] = e
                total = e if total is None else total + e
                dot = e * x if dot is None else dot + e * x
            col_sum[part, :] = total
            col_dot[part, :] = dot
            return tuple(new[0]), tuple(new[1])

        zeros = tuple(jnp.zeros((8, LANES), jnp.float32) for _ in lanes)
        sums.append(lax.fori_loop(0, cols // 8, exponentials, (zeros, zeros), unroll=8))

    row_ids = lax.broadcasted_iota(jnp.int32, (n_col, block), 0)
    placed = [jnp.zeros((n_col, block), jnp.float32)] * 4
    for q in range(n_col):
        at = (q // 2) * block
        here = row_ids == (c_place ^ q)
        new = [row_max[0:1, at + (q % 2) * half : at + (q % 2) * half + block]]
        for which in sums[q % 2]:
            new.append(
                jnp.concatenate(
                    [
                        jnp.sum(which[(at + lane) // LANES], axis=0, keepdims=True)
                        for lane in range(0, block, LANES)
                    ],
                    axis=1,
                )
            )
        new.append(row_diag[0:1, at + (q % 2) * half : at + (q % 2) * half + block])
        placed = [jnp.where(here, n, p) for n, p in zip(new, placed)]
    if before:
        placed = merged(placed, [before[0][i] for i in range(4)])
    for i in range(4):
        row_ref[i] = placed[i]
    row_ids = lax.broadcasted_iota(jnp.int32, (n_row, block), 0)
    placed = [before[1][i] if before else jnp.zeros((n_row, block), jnp.float32) for i in range(3)]
    for t in range(n_text):
        part = pl.ds(t * block, block)
        here = row_ids == (r_place ^ (lead + t))
        new = [col_max[part, :].T[0:1, :]]
        for which in (col_sum, col_dot):
            new.append(jnp.sum(which[part, :].T, axis=0, keepdims=True))
        placed = [jnp.where(here, n, p) for n, p in zip(new, placed)]
    for i in range(3):
        col_ref[i] = placed[i]


def stats(coef, place, texts, images, before, n_col, n_row, keep):
    block, width = texts[0].shape
    first = not before
    rows, cols = block * n_col, block * (len(texts) if first else 1)
    vmem = pl.BlockSpec(memory_space=VMEM)
    smem = pl.BlockSpec(memory_space=SMEM)
    half = jax.ShapeDtypeStruct((rows // 2, width), jnp.bfloat16)
    out_shape = [half, half] if first else [jax.ShapeDtypeStruct((block, width), jnp.bfloat16)]
    out_shape += [
        jax.ShapeDtypeStruct((4, n_col, block), jnp.float32),
        jax.ShapeDtypeStruct((3, n_row, block), jnp.float32),
    ]
    held = [(cols, rows), (cols, rows), (8, rows), (cols, LANES)]
    scratch = [VMEM((cols, LANES), jnp.float32)] * 2 + [VMEM((8, rows), jnp.float32)]
    if keep:
        out_shape += [jax.ShapeDtypeStruct(shape, jnp.float32) for shape in held]
    else:
        scratch = [VMEM(shape, jnp.float32) for shape in held[1:]] + scratch
    return pl.pallas_call(
        functools.partial(stats_kernel, first, keep, len(texts) if first else 1, block),
        out_shape=tuple(out_shape),
        in_specs=[smem, smem] + [vmem] * (len(texts) + len(images) + len(before)),
        out_specs=(vmem,) * len(out_shape),
        scratch_shapes=scratch,
        compiler_params=pltpu.CompilerParams(
            vmem_limit_bytes=(0 if keep else 4 * rows * cols) + 8 * 2**20
        ),
        cost_estimate=pl.CostEstimate(
            flops=FLOPS * 2 * rows * cols * width, bytes_accessed=0, transcendentals=0
        ),
        name="stats" if first else "stats_last",
    )(coef, place, *texts, *images, *before)


def merged(a, b):
    top = jnp.maximum(a[0], b[0])
    wa, wb = jnp.exp2(a[0] - top), jnp.exp2(b[0] - top)
    out = [top] + [a[i] * wa + b[i] * wb for i in (1, 2)]
    return out + [a[i] + b[i] for i in range(3, len(a))]


def by_pairs(blocks, add):
    while len(blocks) > 1:
        blocks = [add(blocks[i], blocks[i + 1]) for i in range(0, len(blocks), 2)]
    return blocks[0]


def lse_and_mean(parts):
    mean = 0.5 * parts[2] / parts[1]
    return parts[0] + jnp.log(parts[1]) * LOG2E, mean - parts[3] if len(parts) > 3 else mean


def exchanged(row_parts, col_parts, n_col, n_row):
    rows = [swap(row_parts, "col", n_col, q) for q in range(2, n_col, 2)]
    count = col_parts.shape[0]
    fill = row_parts.size // col_parts.size + 1
    cols = swap(jnp.concatenate([col_parts] * fill), "row", n_row, 1)[:count]
    rows, cols = lax.optimization_barrier((rows, cols))
    rows = by_pairs([list(x) for x in (row_parts, *rows)], merged)
    cols = merged(list(col_parts), list(cols))
    for b in range(1, n_row.bit_length() - 1):
        cols = merged(cols, list(swap(jnp.stack(cols), "row", n_row, 1 << b)))
    rows = merged(rows, list(swap(jnp.stack(rows), "col", n_col, 1)))
    return *lse_and_mean(rows), *lse_and_mean(cols)


LEVELS = 32000
LOW = 128
BIAS = 125
EXTRA = 8
MORE = 2 * EXTRA
STEP = 32


def put_extra(out, extra_ref):
    n, width = extra_ref.shape
    rows = min(n, EXTRA)
    out[...] = jnp.zeros(out.shape, out.dtype)
    out[:rows, :width] = sum(extra_ref[i : i + rows, :] for i in range(0, n, rows))


def power(k):
    return jnp.exp2(k).astype(jnp.bfloat16).astype(jnp.float32)


def encode(out, powers, size, slab, extra):
    width = out.shape[1]
    for r in range(0, size, STEP):
        value = slab(r)
        top = jnp.maximum(jnp.max(jnp.abs(value), axis=1, keepdims=True), 1e-30)
        k = jnp.ceil(jnp.log(top) * LOG2E)
        powers[r : r + STEP, :] = jnp.broadcast_to(power(k), (STEP, LANES))
        whole = jnp.floor(jnp.abs(value) * (power(-k) * (LEVELS - 1)) + 0.5) * (1 / LOW)
        high = jnp.floor(whole)
        code = (1.0 + (whole - high)) * jnp.exp2(high - BIAS)
        out[r : r + STEP, :] = jnp.where(value < 0, -code, code).astype(jnp.bfloat16)
    half = width // 2
    first = extra[:, :half].astype(jnp.bfloat16)
    rest = extra[:, :half] - first.astype(jnp.float32)
    second = rest.astype(jnp.bfloat16)
    third = (rest - second.astype(jnp.float32)).astype(jnp.bfloat16)
    fourth = powers[...].T[:EXTRA, :].astype(jnp.bfloat16)
    if size < half:
        fourth = jnp.concatenate([fourth, jnp.zeros((EXTRA, half - size), jnp.bfloat16)], axis=1)
    out[size:, :half] = jnp.concatenate([first, second], axis=0)
    out[size:, half:] = jnp.concatenate([third, fourth], axis=0)


def decode_powers(code, size):
    half = code.shape[1] // 2
    powers = code[size:, half : half + size].astype(jnp.float32)
    return jnp.broadcast_to(powers[EXTRA : EXTRA + 1, :], (LANES, size)).T * (LOW / (LEVELS - 1))


def decode(code, powers, r):
    lanes = []
    for lane in range(0, code.shape[1], LANES):
        c = code[r : r + STEP, lane : lane + LANES].astype(jnp.float32)
        a = jnp.abs(c)
        high = jnp.floor(jnp.log(a) * LOG2E)
        whole = (high + (BIAS - 1)) + a * jnp.exp2(-high)
        lanes.append(jnp.where(c < 0, -whole, whole) * powers[r : r + STEP, :])
    return jnp.concatenate(lanes, axis=1)


def decode_extra(code, size):
    half = code.shape[1] // 2
    left = code[size:, :half].astype(jnp.float32)
    right = code[size:, half:].astype(jnp.float32)
    return left[:EXTRA] + left[EXTRA:] + right[:EXTRA]


def pack_text_kernel(n, base, *refs):
    codes, out, powers, received = refs[:n], *refs[n:]
    size, half = base.shape[0] - EXTRA, base.shape[1] // 2
    more = base[size:, :half]
    for c, code in enumerate(codes):
        received[c] = decode_powers(code, size)
        more = more + decode_extra(code, size)

    def slab(r):
        value = base[r : r + STEP, :]
        for c, code in enumerate(codes):
            value = value + decode(code, received.at[c], r)
        return value

    encode(out, powers, size, slab, more)


def pack_text(base, codes):
    size, width = base.shape[0] - EXTRA, base.shape[1]
    vmem = pl.BlockSpec(memory_space=VMEM)
    return pl.pallas_call(
        functools.partial(pack_text_kernel, len(codes)),
        out_shape=jax.ShapeDtypeStruct((size + MORE, width), jnp.bfloat16),
        in_specs=[vmem] * (1 + len(codes)),
        out_specs=vmem,
        scratch_shapes=[VMEM((size, LANES), jnp.float32), VMEM((len(codes), size, LANES), jnp.float32)],
        compiler_params=pltpu.CompilerParams(vmem_limit_bytes=6 * 2**20),
        name="pack_text",
    )(base, *codes)


def pack_images_kernel(near, far, own, *refs):
    outs, powers = refs[:-1], refs[-1]
    size = near.shape[1] - EXTRA
    own[...] = near[0] + far[0]
    for j, out in enumerate(outs, 1):
        encode(
            out,
            powers.at[j - 1],
            size,
            lambda r, j=j: near[j, r : r + STEP, :] + far[j, r : r + STEP, :],
            near[j, size:, :] + far[j, size:, :],
        )


def pack_images(near, far):
    n, rows, width = near.shape
    size = rows - EXTRA
    vmem = pl.BlockSpec(memory_space=VMEM)
    code = jax.ShapeDtypeStruct((size + MORE, width), jnp.bfloat16)
    own, *codes = pl.pallas_call(
        pack_images_kernel,
        out_shape=(jax.ShapeDtypeStruct((rows, width), jnp.float32),) + (code,) * (n - 1),
        in_specs=[vmem] * 2,
        out_specs=(vmem,) * n,
        scratch_shapes=[VMEM((n - 1, size, LANES), jnp.float32)],
        compiler_params=pltpu.CompilerParams(vmem_limit_bytes=(4 + 2 * n) * 2**20),
        name="pack_images",
    )(near, far)
    return own, codes


def total_kernel(n, in_order, coef_ref, base, *refs):
    codes, before = refs[:n], refs[n:-6]
    out, extra, scalar, value, powers, sems = refs[-6:]
    size, width = base.shape[0] - EXTRA, base.shape[1]
    combine = functools.partial(functools.reduce, jnp.add) if in_order else first_and_pairs
    more = combine([base[size:, : width // 2]] + [decode_extra(code, size) for code in codes])
    more = sum([b[...] for b in before], more)
    extra[...] = more
    scalar[0, 0] = jnp.sum(more) / coef_ref[0, 0]
    for c, code in enumerate(codes):
        powers[c] = decode_powers(code, size)
    copies = []
    steps = sems.shape[0]
    for i in range(steps):
        part = pl.ds(i * (size // steps), size // steps)
        for r in range(i * (size // steps), (i + 1) * (size // steps), STEP):
            value[r : r + STEP, :] = combine(
                [base[r : r + STEP, :]] + [decode(code, powers.at[c], r) for c, code in enumerate(codes)]
            )
        copies.append(pltpu.make_async_copy(value.at[part], out.at[part], sems.at[i]))
        copies[-1].start()
    for copy in copies:
        copy.wait()


def add_kernel(base, code, out, powers):
    size, half = base.shape[0] - EXTRA, base.shape[1] // 2
    powers[...] = decode_powers(code, size)
    for r in range(0, size, STEP):
        out[r : r + STEP, :] = base[r : r + STEP, :] + decode(code, powers, r)
    out[size:, :half] = base[size:, :half] + decode_extra(code, size)
    out[size:, half:] = jnp.zeros((EXTRA, half), jnp.float32)


def added(base, code):
    vmem = pl.BlockSpec(memory_space=VMEM)
    return pl.pallas_call(
        add_kernel,
        out_shape=jax.ShapeDtypeStruct(base.shape, jnp.float32),
        in_specs=[vmem] * 2,
        out_specs=vmem,
        scratch_shapes=[VMEM((base.shape[0] - EXTRA, LANES), jnp.float32)],
        compiler_params=pltpu.CompilerParams(vmem_limit_bytes=6 * 2**20),
        name="added",
    )(base, code)


def first_and_pairs(blocks):
    if len(blocks) == 1:
        return blocks[0]
    pairs = [blocks[0]] + [blocks[i] + blocks[i + 1] for i in range(1, len(blocks), 2)]
    return by_pairs(pairs, jnp.add)


def total_of(coef, base, codes, in_order, before, name):
    size, width = base.shape[0] - EXTRA, base.shape[1]
    vmem = pl.BlockSpec(memory_space=VMEM)
    smem = pl.BlockSpec(memory_space=SMEM)
    return pl.pallas_call(
        functools.partial(total_kernel, len(codes), in_order),
        out_shape=(
            jax.ShapeDtypeStruct((size, width), jnp.float32),
            jax.ShapeDtypeStruct((EXTRA, width // 2), jnp.float32),
            jax.ShapeDtypeStruct((1, 1), jnp.float32),
        ),
        in_specs=[smem] + [vmem] * (1 + len(codes) + len(before)),
        out_specs=(pl.BlockSpec(memory_space=pl.ANY), vmem, smem),
        scratch_shapes=[
            VMEM((size, width), jnp.float32),
            VMEM((len(codes), size, LANES), jnp.float32),
            pltpu.SemaphoreType.DMA((8,)),
        ],
        compiler_params=pltpu.CompilerParams(vmem_limit_bytes=8 * 2**20),
        name=name,
    )(coef, base, *codes, *before)


def text_block(text, tile, t, halves, row_lse, col_lse, place_ref, scale_ref, coef_ref, extra, grad_ref, out_ref, total, powers):
    coef = coef_ref[0, 0]
    r_place, c_place = place_ref[0, 0], place_ref[0, 1]
    half, width = halves[0].shape
    n_col, n_row = row_lse.shape[0], col_lse.shape[0]
    size = text.shape[0]
    block = size
    col_lse_down = jnp.broadcast_to(col_lse[pl.ds(r_place ^ t, 1), :], (LANES, size)).T
    if tile:
        col_scale = 0.5 * jnp.exp2(tile[3][...] - col_lse_down)
    text_id = c_place * n_row + (r_place ^ t)
    step = 32
    lane_ids = lax.broadcasted_iota(jnp.int32, (step, LANES), 1)
    row_ids = lax.broadcasted_iota(jnp.int32, (step, LANES), 0)

    for which, images in enumerate(halves):

        def one(j, carry):
            at = pl.multiple_of(j * block + which * half, block)
            column = c_place ^ (2 * j + which)
            lse = row_lse[pl.ds(column, 1), :]
            if tile:
                row_scale = 0.5 * jnp.exp2(tile[2][0:1, pl.ds(at, block)] - lse)
            else:
                image = images[pl.ds(pl.multiple_of(j * block, block), block), :]
                xs = nt_dot(text[...], image) * coef
            same = jnp.where(r_place * n_col + column == text_id, 1.0, 0.0)
            for r in range(0, size, step):
                for lane in range(0, block, LANES):
                    if tile:
                        g = (
                            tile[0][r : r + step, pl.ds(at + lane, LANES)]
                            * row_scale[:, lane : lane + LANES]
                            + tile[1][r : r + step, pl.ds(at + lane, LANES)]
                            * col_scale[r : r + step, :]
                        )
                    else:
                        x = xs[r : r + step, lane : lane + LANES]
                        g = 0.5 * (
                            jnp.exp2(x - lse[:, lane : lane + LANES])
                            + jnp.exp2(x - col_lse_down[r : r + step, :])
                        )
                    if lane <= r < lane + LANES:
                        g = g - jnp.where(row_ids + (r - lane) == lane_ids, same, 0.0)
                    grad_ref[r : r + step, pl.ds(at + lane, LANES)] = g.astype(jnp.bfloat16)
            return carry

        lax.fori_loop(0, half // block, one, 0, unroll=4)
    total[:size, :] = scale_ref[0, 0] * (
        jnp.dot(grad_ref[:, :half], halves[0][...], preferred_element_type=jnp.float32)
        + jnp.dot(grad_ref[:, half:], halves[1][...], preferred_element_type=jnp.float32)
    )
    put_extra(total.at[size:, :], extra)
    if t & 1:
        encode(out_ref, powers, size, lambda r: total[r : r + STEP, :], total[size:, :])
    else:
        out_ref[...] = total[...]


def image_block(grads, texts, at, block, scale):
    total = None
    for grad, text in zip(grads, texts):
        part = lax.dot_general(
            grad[:, pl.ds(at, block)],
            text[...],
            (((0,), (0,)), ((), ())),
            preferred_element_type=jnp.float32,
        )
        total = part if total is None else total + part
    return scale * total


def text_kernel(order, n_done, kept, block, scale_ref, coef_ref, place_ref, *refs):
    even, odd, row_lse, col_lse, row_extra, col_extra = refs[:6]
    n = len(order)
    texts, rest = refs[6 : 6 + n], refs[6 + n :]
    tile, rest = rest[:kept], rest[kept:]
    done_grads, done_texts, rest = rest[:n_done], rest[n_done : 2 * n_done], rest[2 * n_done :]
    grads, outs = rest[:n], rest[n : 2 * n]
    for i, t in enumerate(order):
        text_block(
            texts[i],
            [
                held if i == 2 else held.at[pl.ds((t - min(order)) * block, block)]
                for i, held in enumerate(tile)
            ],
            t, (even, odd), row_lse, col_lse, place_ref, scale_ref, coef_ref, row_extra, grads[i], outs[i], *rest[-2:]
        )
    if n_done:
        far_ref = rest[2 * n]
        half = even.shape[0]

        def one(j, carry):
            far_ref[j, :block, :] = image_block(
                [*done_grads, *grads],
                [*done_texts, *texts],
                pl.multiple_of(j * block + half, block),
                block,
                scale_ref[0, 0],
            )
            put_extra(far_ref.at[j, block:, :], col_extra)
            return carry

        lax.fori_loop(0, half // block, one, 0, unroll=4)


def text_grads(scale, coef, place, even, odd, row_lse, col_lse, row_extra, col_extra, texts, tile, order, done):
    half, width = even.shape
    block = texts[0].shape[0]
    n = len(order)
    vmem = pl.BlockSpec(memory_space=VMEM)
    smem = pl.BlockSpec(memory_space=SMEM)
    out_shape = (
        [jax.ShapeDtypeStruct((block, 2 * half), jnp.bfloat16)] * n
        + [
            jax.ShapeDtypeStruct((block + MORE, width), jnp.bfloat16)
            if t & 1
            else jax.ShapeDtypeStruct((block + EXTRA, width), jnp.float32)
            for t in order
        ]
    )
    if done:
        out_shape.append(jax.ShapeDtypeStruct((half // block, block + EXTRA, width), jnp.float32))
    operands = [even, odd, row_lse, col_lse, row_extra, col_extra, *[texts[t] for t in order]]
    operands += tile
    operands += [done[t] for t in done] + [texts[t] for t in done]
    outs = pl.pallas_call(
        functools.partial(text_kernel, tuple(order), len(done), len(tile), block),
        out_shape=tuple(out_shape),
        in_specs=[smem] * 3 + [vmem] * len(operands),
        out_specs=(vmem,) * len(out_shape),
        scratch_shapes=[
            VMEM((block + EXTRA, width), jnp.float32),
            VMEM((block, LANES), jnp.float32),
        ],
        compiler_params=pltpu.CompilerParams(vmem_limit_bytes=12 * 2**20),
        cost_estimate=pl.CostEstimate(
            flops=FLOPS * 4 * n * block * 2 * half * width, bytes_accessed=0, transcendentals=0
        ),
        name=f"text_grads_{n}",
    )(scale, coef, place, *operands)
    grads = {t: outs[i] for i, t in enumerate(order)}
    parts = {t: outs[n + i] for i, t in enumerate(order)}
    return grads, parts, outs[-1]


def image_kernel(n_text, block, scale_ref, extra, *refs):
    grads, texts, out_ref = refs[:n_text], refs[n_text : 2 * n_text], refs[-1]

    def one(j, carry):
        put_extra(out_ref.at[j, block:, :], extra)
        out_ref[j, :block, :] = image_block(
            grads, texts, pl.multiple_of(j * block, block), block, scale_ref[0, 0]
        )
        return carry

    lax.fori_loop(0, out_ref.shape[0], one, 0, unroll=4)


def image_grads(scale, extra, grads, texts, after):
    n_text = len(grads)
    rows = grads[0].shape[1]
    block, width = texts[0].shape
    n = rows // block // 2
    vmem = pl.BlockSpec(memory_space=VMEM)
    return pl.pallas_call(
        functools.partial(image_kernel, n_text, block),
        out_shape=jax.ShapeDtypeStruct((n, block + EXTRA, width), jnp.float32),
        in_specs=[pl.BlockSpec(memory_space=SMEM)]
        + [vmem] * (2 * n_text + 1)
        + [pl.BlockSpec(memory_space=pl.ANY)] * len(after),
        out_specs=vmem,
        compiler_params=pltpu.CompilerParams(vmem_limit_bytes=12 * 2**20),
        cost_estimate=pl.CostEstimate(
            flops=FLOPS * 2 * n * block * n_text * block * width, bytes_accessed=0, transcendentals=0
        ),
        name="image_grads",
    )(scale, extra, *grads, *texts, *after)


def on_device(n_row, n_col, image_embeds, text_embeds, logit_scale):
    block = image_embeds.shape[0]
    r, c = lax.axis_index("row"), lax.axis_index("col")
    place = jnp.stack([r, c]).reshape(1, 2)
    scale = logit_scale.reshape(1, 1)
    coef = scale * LOG2E
    image_half, text_half = image_embeds.astype(jnp.bfloat16), text_embeds.astype(jnp.bfloat16)
    even, odd, texts, text_last = gather_both(image_half, text_half, n_col, n_row)
    keep = 4 * n_row * n_col * block * block <= 16 * 2**20
    even, odd, *before = stats(
        coef, place, texts, (*even, *odd), (), n_col, n_row, keep
    )
    text_last, row_parts, col_parts, *tile_last = stats(
        coef, place, text_last, (even, odd), before[:2], n_col, n_row, keep
    )
    texts = [*texts, text_last]
    tile = before[2:]
    row_lse, row_extra, col_lse, col_extra = exchanged(row_parts, col_parts, n_col, n_row)

    held = (scale, coef, place, even, odd, row_lse, col_lse, row_extra, col_extra, texts)
    last = n_row - 1
    grads, parts, _ = text_grads(*held, tile_last, [last], {})
    received = swap(parts[last], "row", n_row, 1)
    more, more_parts, far = text_grads(*held, tile, list(range(last))[::-1], grads)
    grads |= more
    parts |= more_parts
    codes = {q: [] for q in range(0, n_row, 2)}
    codes[last ^ 1].append(received)
    after = [pack_text(parts[last ^ 1], codes[last ^ 1])] if n_row > 2 else [received]
    near = image_grads(scale, col_extra, [grads[t] for t in range(n_row)], texts, after)
    far = swap(far, "col", n_col, 1)
    odd_parts, far = lax.optimization_barrier(([parts[q] for q in range(1, last, 2)], far))
    for q, part in zip(range(1, last, 2), odd_parts):
        codes[q ^ 1].append(swap(part, "row", n_row, 1))
    for b in range(1, n_row.bit_length() - 1):
        for q in [q for q in codes if q & (1 << b)]:
            code = after[0] if (b, q) == (1, last ^ 1) else pack_text(parts[q], codes[q])
            codes[q ^ (1 << b)].append(swap(code, "row", n_row, 1 << b))
            del codes[q]
    grad_text, text_extra, _ = total_of(coef, parts[0], codes[0], True, [], "grad_text")

    own, others = pack_images(near, far)
    others = [swap(code, "col", n_col, 2 * j) for j, code in enumerate(others, 1)]
    first, text_extra = lax.optimization_barrier((others[0], text_extra))
    grad_image, _, grad_scale = total_of(
        coef, added(own, first), others[1:], False, [text_extra], "grad_image"
    )
    return grad_image, grad_text, grad_scale.reshape(())


def solution(mesh):
    images = P(("row", "col"), None)
    texts = P(("col", "row"), None)
    return jax.shard_map(
        functools.partial(on_device, mesh.shape["row"], mesh.shape["col"]),
        mesh=mesh,
        in_specs=(images, texts, P()),
        out_specs=(images, texts, P()),
        check_vma=False,
    )
```

```python
import functools
import math

import jax
import jax.numpy as jnp
from jax import lax
from jax.experimental import pallas as pl
from jax.experimental.pallas import tpu as pltpu
from jax.sharding import PartitionSpec as P

LOG2E = 1.4426950408889634
LN2 = 0.6931471805599453
LANES = 128
VMEM = pltpu.VMEM
SMEM = pltpu.SMEM
FLOPS = 20


def swap(x, axis, n, q):
    return lax.ppermute(x, axis, [(i, i ^ q) for i in range(n)])


def gather_both(image, text, n_col, n_row):
    images = [swap(image, "col", n_col, q) for q in range(2, n_col, 2)]
    texts = [swap(text, "row", n_row, q) for q in range(1, n_row - 1)]
    images, texts = lax.optimization_barrier((images, texts))
    odd = [swap(i, "col", n_col, 1) for i in (image, *images)]
    return [image, *images], odd, [text, *texts], [swap(texts[-1], "row", n_row, 1)]


def nt_dot(a, b):
    return lax.dot_general(a, b, (((1,), (1,)), ((), ())), preferred_element_type=jnp.float32)


def stats_kernel(first, n_text, block, coef_ref, place_ref, *refs):
    texts, refs = refs[:n_text], refs[n_text:]
    coef = coef_ref[0, 0]
    r_place, c_place = place_ref[0, 0], place_ref[0, 1]
    *refs, row_max, col_max, col_sum, col_dot, row_diag = refs
    if first:
        *refs, even, odd, row_ref, col_ref, tile = refs
        halves = (even, odd)
        each = len(refs) // 2
        for i, piece in enumerate(refs):
            at = (i % each) * block
            halves[i // each][at : at + block, :] = piece[...]
        before = None
    else:
        even, odd, *before, last, row_ref, col_ref, tile = refs
        halves = (even, odd)
        last[...] = functools.reduce(jnp.add, [text[...] for text in texts])
        texts, n_text = [last], 1
    cols, rows = tile.shape
    half = rows // 2
    lead = 0 if first else col_ref.shape[1] - n_text
    col_max[...] = jnp.full(col_max.shape, -jnp.inf, jnp.float32)
    row_diag[...] = jnp.zeros(row_diag.shape, jnp.float32)
    n_col, n_row = row_ref.shape[1], col_ref.shape[1]

    for which, images in enumerate(halves):

        def products(j, carry):
            image = images[pl.ds(pl.multiple_of(j * block, block), block), :]
            at = pl.multiple_of(j * block + which * half, block)
            top = None
            for t in range(n_text):
                part = pl.ds(t * block, block)
                x = nt_dot(texts[t][...], image) * coef
                tile[part, pl.ds(at, block)] = x
                top_t = jnp.max(x, axis=0, keepdims=True)
                top = top_t if top is None else jnp.maximum(top, top_t)
                held = col_max[part, :]
                for lane in range(0, block, LANES):
                    held = jnp.maximum(held, x[:, lane : lane + LANES])
                col_max[part, :] = held
            row_max[0:1, pl.ds(at, block)] = top
            return carry

        lax.fori_loop(0, half // block, products, 0, unroll=4)

    for t in range(n_text):
        among = c_place * n_row + (r_place ^ (lead + t)) - r_place * n_col

        @pl.when((among >= 0) & (among < n_col))
        def _():
            q = c_place ^ among
            at = pl.multiple_of((q // 2) * block + (q % 2) * half, block)
            x = tile[t * block : (t + 1) * block, pl.ds(at, block)]
            down = lax.broadcasted_iota(jnp.int32, x.shape, 0)
            across = lax.broadcasted_iota(jnp.int32, x.shape, 1)
            row_diag[0:1, pl.ds(at, block)] = jnp.sum(
                jnp.where(down == across, x, 0.0), axis=0, keepdims=True
            )

    col_max[...] = jnp.broadcast_to(
        jnp.max(col_max[...], axis=1, keepdims=True), col_max.shape
    )
    sums = []
    for which in range(2):
        lanes = range(which * half, (which + 1) * half, LANES)

        def exponentials(i, acc):
            part = pl.ds(pl.multiple_of(i * 8, 8), 8)
            top = col_max[part, :]
            total = col_sum[part, :] if which else None
            dot = col_dot[part, :] if which else None
            new = [], []
            for n, lane in enumerate(lanes):
                x = tile[part, lane : lane + LANES]
                e = jnp.exp2(x - row_max[0:1, lane : lane + LANES])
                new[0].append(acc[0][n] + e)
                new[1].append(acc[1][n] + e * x)
                e = jnp.exp2(x - top)
                total = e if total is None else total + e
                dot = e * x if dot is None else dot + e * x
            col_sum[part, :] = total
            col_dot[part, :] = dot
            return tuple(new[0]), tuple(new[1])

        zeros = tuple(jnp.zeros((8, LANES), jnp.float32) for _ in lanes)
        sums.append(lax.fori_loop(0, cols // 8, exponentials, (zeros, zeros), unroll=8))

    row_ids = lax.broadcasted_iota(jnp.int32, (n_col, block), 0)
    placed = [jnp.zeros((n_col, block), jnp.float32)] * 4
    for q in range(n_col):
        at = (q // 2) * block
        here = row_ids == (c_place ^ q)
        new = [row_max[0:1, at + (q % 2) * half : at + (q % 2) * half + block]]
        for which in sums[q % 2]:
            new.append(
                jnp.concatenate(
                    [
                        jnp.sum(which[(at + lane) // LANES], axis=0, keepdims=True)
                        for lane in range(0, block, LANES)
                    ],
                    axis=1,
                )
            )
        new.append(row_diag[0:1, at + (q % 2) * half : at + (q % 2) * half + block])
        placed = [jnp.where(here, n, p) for n, p in zip(new, placed)]
    if before:
        placed = merged(placed, [before[0][i] for i in range(4)])
    for i in range(4):
        row_ref[i] = placed[i]
    row_ids = lax.broadcasted_iota(jnp.int32, (n_row, block), 0)
    placed = [before[1][i] if before else jnp.zeros((n_row, block), jnp.float32) for i in range(3)]
    for t in range(n_text):
        part = pl.ds(t * block, block)
        here = row_ids == (r_place ^ (lead + t))
        new = [col_max[part, :].T[0:1, :]]
        for which in (col_sum, col_dot):
            new.append(jnp.sum(which[part, :].T, axis=0, keepdims=True))
        placed = [jnp.where(here, n, p) for n, p in zip(new, placed)]
    for i in range(3):
        col_ref[i] = placed[i]


def stats(coef, place, texts, images, before, n_col, n_row, keep):
    block, width = texts[0].shape
    first = not before
    rows, cols = block * n_col, block * (len(texts) if first else 1)
    vmem = pl.BlockSpec(memory_space=VMEM)
    smem = pl.BlockSpec(memory_space=SMEM)
    half = jax.ShapeDtypeStruct((rows // 2, width), jnp.bfloat16)
    out_shape = [half, half] if first else [jax.ShapeDtypeStruct((block, width), jnp.bfloat16)]
    out_shape += [
        jax.ShapeDtypeStruct((4, n_col, block), jnp.float32),
        jax.ShapeDtypeStruct((3, n_row, block), jnp.float32),
    ]
    scratch = [
        VMEM((8, rows), jnp.float32),
        VMEM((cols, LANES), jnp.float32),
        VMEM((cols, LANES), jnp.float32),
        VMEM((cols, LANES), jnp.float32),
        VMEM((8, rows), jnp.float32),
    ]
    if keep:
        out_shape.append(jax.ShapeDtypeStruct((cols, rows), jnp.float32))
    else:
        scratch.insert(0, VMEM((cols, rows), jnp.float32))
    return pl.pallas_call(
        functools.partial(stats_kernel, first, len(texts), block),
        out_shape=tuple(out_shape),
        in_specs=[smem, smem] + [vmem] * (len(texts) + len(images) + len(before)),
        out_specs=(vmem,) * len(out_shape),
        scratch_shapes=scratch,
        compiler_params=pltpu.CompilerParams(
            vmem_limit_bytes=(0 if keep else 4 * rows * cols) + 8 * 2**20
        ),
        cost_estimate=pl.CostEstimate(
            flops=FLOPS * 2 * rows * cols * width, bytes_accessed=0, transcendentals=0
        ),
        name="stats" if first else "stats_last",
    )(coef, place, *texts, *images, *before)


def merged(a, b):
    top = jnp.maximum(a[0], b[0])
    wa, wb = jnp.exp2(a[0] - top), jnp.exp2(b[0] - top)
    out = [top] + [a[i] * wa + b[i] * wb for i in (1, 2)]
    return out + [a[i] + b[i] for i in range(3, len(a))]


def by_pairs(blocks, add):
    while len(blocks) > 1:
        blocks = [add(blocks[i], blocks[i + 1]) for i in range(0, len(blocks), 2)]
    return blocks[0]


def lse_and_mean(parts):
    mean = 0.5 * parts[2] / parts[1]
    return parts[0] + jnp.log(parts[1]) * LOG2E, mean - parts[3] if len(parts) > 3 else mean


def exchanged(row_parts, col_parts, n_col, n_row):
    rows, cols = list(row_parts), list(col_parts)
    count = len(cols)
    fill = row_parts.size // col_parts.size + 1
    row_bits = [1 << b for b in range(1, n_col.bit_length() - 1)] + [1]
    col_bits = [1 << b for b in range(n_row.bit_length() - 1)]
    for n, bit in enumerate(row_bits):
        received = swap(jnp.stack(rows), "col", n_col, bit)
        if n < len(col_bits):
            other = swap(jnp.stack(cols * fill), "row", n_row, col_bits[n])
            received, other = lax.optimization_barrier((received, other))
            cols = merged(cols, list(other[:count]))
        rows = merged(rows, list(received))
    return *lse_and_mean(rows), *lse_and_mean(cols)


LEVELS = 32000
LOW = 128
BIAS = 125
EXTRA = 8
MORE = 2 * EXTRA
STEP = 32


def put_extra(out, extra_ref):
    n, width = extra_ref.shape
    rows = min(n, EXTRA)
    out[...] = jnp.zeros(out.shape, out.dtype)
    out[:rows, :width] = sum(extra_ref[i : i + rows, :] for i in range(0, n, rows))


def power(k):
    return jnp.exp2(k).astype(jnp.bfloat16).astype(jnp.float32)


def encode(out, powers, size, slab, extra):
    width = out.shape[1]
    for r in range(0, size, STEP):
        value = slab(r)
        top = jnp.maximum(jnp.max(jnp.abs(value), axis=1, keepdims=True), 1e-30)
        k = jnp.ceil(jnp.log(top) * LOG2E)
        powers[r : r + STEP, :] = jnp.broadcast_to(power(k), (STEP, LANES))
        whole = jnp.floor(jnp.abs(value) * (power(-k) * (LEVELS - 1)) + 0.5) * (1 / LOW)
        high = jnp.floor(whole)
        code = (1.0 + (whole - high)) * jnp.exp2(high - BIAS)
        out[r : r + STEP, :] = jnp.where(value < 0, -code, code).astype(jnp.bfloat16)
    half = width // 2
    first = extra[:, :half].astype(jnp.bfloat16)
    rest = extra[:, :half] - first.astype(jnp.float32)
    second = rest.astype(jnp.bfloat16)
    third = (rest - second.astype(jnp.float32)).astype(jnp.bfloat16)
    fourth = powers[...].T[:EXTRA, :].astype(jnp.bfloat16)
    if size < half:
        fourth = jnp.concatenate([fourth, jnp.zeros((EXTRA, half - size), jnp.bfloat16)], axis=1)
    out[size:, :half] = jnp.concatenate([first, second], axis=0)
    out[size:, half:] = jnp.concatenate([third, fourth], axis=0)


def decode_powers(code, size):
    half = code.shape[1] // 2
    powers = code[size:, half : half + size].astype(jnp.float32)
    return jnp.broadcast_to(powers[EXTRA : EXTRA + 1, :], (LANES, size)).T * (LOW / (LEVELS - 1))


def decode(code, powers, r):
    lanes = []
    for lane in range(0, code.shape[1], LANES):
        c = code[r : r + STEP, lane : lane + LANES].astype(jnp.float32)
        a = jnp.abs(c)
        high = jnp.floor(jnp.log(a) * LOG2E)
        whole = (high + (BIAS - 1)) + a * jnp.exp2(-high)
        lanes.append(jnp.where(c < 0, -whole, whole) * powers[r : r + STEP, :])
    return jnp.concatenate(lanes, axis=1)


def decode_extra(code, size):
    half = code.shape[1] // 2
    left = code[size:, :half].astype(jnp.float32)
    right = code[size:, half:].astype(jnp.float32)
    return left[:EXTRA] + left[EXTRA:] + right[:EXTRA]


def pack_text_kernel(n, base, *refs):
    codes, out, powers, received = refs[:n], *refs[n:]
    size, half = base.shape[0] - EXTRA, base.shape[1] // 2
    more = base[size:, :half]
    for c, code in enumerate(codes):
        received[c] = decode_powers(code, size)
        more = more + decode_extra(code, size)

    def slab(r):
        value = base[r : r + STEP, :]
        for c, code in enumerate(codes):
            value = value + decode(code, received.at[c], r)
        return value

    encode(out, powers, size, slab, more)


def pack_text(base, codes):
    size, width = base.shape[0] - EXTRA, base.shape[1]
    vmem = pl.BlockSpec(memory_space=VMEM)
    return pl.pallas_call(
        functools.partial(pack_text_kernel, len(codes)),
        out_shape=jax.ShapeDtypeStruct((size + MORE, width), jnp.bfloat16),
        in_specs=[vmem] * (1 + len(codes)),
        out_specs=vmem,
        scratch_shapes=[VMEM((size, LANES), jnp.float32), VMEM((len(codes), size, LANES), jnp.float32)],
        compiler_params=pltpu.CompilerParams(vmem_limit_bytes=6 * 2**20),
        name="pack_text",
    )(base, *codes)


def pack_images_kernel(near, far, own, *refs):
    outs, powers = refs[:-1], refs[-1]
    size = near.shape[1] - EXTRA
    own[...] = near[0] + far[0]
    for j, out in enumerate(outs, 1):
        encode(
            out,
            powers.at[j - 1],
            size,
            lambda r, j=j: near[j, r : r + STEP, :] + far[j, r : r + STEP, :],
            near[j, size:, :] + far[j, size:, :],
        )


def pack_images(near, far):
    n, rows, width = near.shape
    size = rows - EXTRA
    vmem = pl.BlockSpec(memory_space=VMEM)
    code = jax.ShapeDtypeStruct((size + MORE, width), jnp.bfloat16)
    own, *codes = pl.pallas_call(
        pack_images_kernel,
        out_shape=(jax.ShapeDtypeStruct((rows, width), jnp.float32),) + (code,) * (n - 1),
        in_specs=[vmem] * 2,
        out_specs=(vmem,) * n,
        scratch_shapes=[VMEM((n - 1, size, LANES), jnp.float32)],
        compiler_params=pltpu.CompilerParams(vmem_limit_bytes=(4 + 2 * n) * 2**20),
        name="pack_images",
    )(near, far)
    return own, codes


def total_kernel(n, in_order, coef_ref, base, *refs):
    codes, before = refs[:n], refs[n:-6]
    out, extra, scalar, value, powers, sems = refs[-6:]
    size, width = base.shape[0] - EXTRA, base.shape[1]
    combine = functools.partial(functools.reduce, jnp.add) if in_order else first_and_pairs
    for c, code in enumerate(codes):
        powers[c] = decode_powers(code, size)
    copies = []
    steps = sems.shape[0]
    for i in range(steps):
        part = pl.ds(i * (size // steps), size // steps)
        for r in range(i * (size // steps), (i + 1) * (size // steps), STEP):
            value[r : r + STEP, :] = combine(
                [base[r : r + STEP, :]] + [decode(code, powers.at[c], r) for c, code in enumerate(codes)]
            )
        copies.append(pltpu.make_async_copy(value.at[part], out.at[part], sems.at[i]))
        copies[-1].start()
    more = combine([base[size:, : width // 2]] + [decode_extra(code, size) for code in codes])
    more = sum([b[...] for b in before], more)
    extra[...] = more
    scalar[0, 0] = jnp.sum(more) / coef_ref[0, 0]
    for copy in copies:
        copy.wait()


def add_kernel(base, code, out, powers):
    size, half = base.shape[0] - EXTRA, base.shape[1] // 2
    powers[...] = decode_powers(code, size)
    for r in range(0, size, STEP):
        out[r : r + STEP, :] = base[r : r + STEP, :] + decode(code, powers, r)
    out[size:, :half] = base[size:, :half] + decode_extra(code, size)
    out[size:, half:] = jnp.zeros((EXTRA, half), jnp.float32)


def added(base, code):
    vmem = pl.BlockSpec(memory_space=VMEM)
    return pl.pallas_call(
        add_kernel,
        out_shape=jax.ShapeDtypeStruct(base.shape, jnp.float32),
        in_specs=[vmem] * 2,
        out_specs=vmem,
        scratch_shapes=[VMEM((base.shape[0] - EXTRA, LANES), jnp.float32)],
        compiler_params=pltpu.CompilerParams(vmem_limit_bytes=6 * 2**20),
        name="added",
    )(base, code)


def first_and_pairs(blocks):
    if len(blocks) == 1:
        return blocks[0]
    pairs = [blocks[0]] + [blocks[i] + blocks[i + 1] for i in range(1, len(blocks), 2)]
    return by_pairs(pairs, jnp.add)


def total_of(coef, base, codes, in_order, before, name):
    size, width = base.shape[0] - EXTRA, base.shape[1]
    vmem = pl.BlockSpec(memory_space=VMEM)
    smem = pl.BlockSpec(memory_space=SMEM)
    return pl.pallas_call(
        functools.partial(total_kernel, len(codes), in_order),
        out_shape=(
            jax.ShapeDtypeStruct((size, width), jnp.float32),
            jax.ShapeDtypeStruct((EXTRA, width // 2), jnp.float32),
            jax.ShapeDtypeStruct((1, 1), jnp.float32),
        ),
        in_specs=[smem] + [vmem] * (1 + len(codes) + len(before)),
        out_specs=(pl.BlockSpec(memory_space=pl.ANY), vmem, smem),
        scratch_shapes=[
            VMEM((size, width), jnp.float32),
            VMEM((len(codes), size, LANES), jnp.float32),
            pltpu.SemaphoreType.DMA((4,)),
        ],
        compiler_params=pltpu.CompilerParams(vmem_limit_bytes=8 * 2**20),
        name=name,
    )(coef, base, *codes, *before)


def text_block(text, tile, t, halves, row_lse, col_lse, place_ref, coef_ref, grad_ref):
    coef = coef_ref[0, 0]
    r_place, c_place = place_ref[0, 0], place_ref[0, 1]
    half, width = halves[0].shape
    n_col, n_row = row_lse.shape[0], col_lse.shape[0]
    size = text.shape[0]
    block = size
    col_lse_down = jnp.broadcast_to(col_lse[pl.ds(r_place ^ t, 1), :], (LANES, size)).T
    text_id = c_place * n_row + (r_place ^ t)
    step = 32
    lane_ids = lax.broadcasted_iota(jnp.int32, (step, LANES), 1)
    row_ids = lax.broadcasted_iota(jnp.int32, (step, LANES), 0)

    for which, images in enumerate(halves):

        def one(j, carry):
            at = pl.multiple_of(j * block + which * half, block)
            if tile is None:
                image = images[pl.ds(pl.multiple_of(j * block, block), block), :]
                xs = nt_dot(text[...], image) * coef
            column = c_place ^ (2 * j + which)
            same = jnp.where(r_place * n_col + column == text_id, 1.0, 0.0)
            lse = row_lse[pl.ds(column, 1), :]
            for r in range(0, size, step):
                for lane in range(0, block, LANES):
                    if tile is None:
                        x = xs[r : r + step, lane : lane + LANES]
                    else:
                        x = tile[r : r + step, pl.ds(at + lane, LANES)]
                    e = jnp.exp2(x - lse[:, lane : lane + LANES]) + jnp.exp2(
                        x - col_lse_down[r : r + step, :]
                    )
                    g = 0.5 * e
                    if lane <= r < lane + LANES:
                        g = g - jnp.where(row_ids + (r - lane) == lane_ids, same, 0.0)
                    grad_ref[r : r + step, pl.ds(at + lane, LANES)] = g.astype(jnp.bfloat16)
            return carry

        lax.fori_loop(0, half // block, one, 0, unroll=4)


def image_block(grads, texts, at, block, scale):
    total = None
    for grad, text in zip(grads, texts):
        part = lax.dot_general(
            grad[:, pl.ds(at, block)],
            text[...],
            (((0,), (0,)), ((), ())),
            preferred_element_type=jnp.float32,
        )
        total = part if total is None else total + part
    return scale * total


def text_kernel(order, n_done, kept, block, scale_ref, coef_ref, place_ref, *refs):
    even, odd, row_lse, col_lse, row_extra, col_extra = refs[:6]
    n = len(order)
    texts, rest = refs[6 : 6 + n], refs[6 + n :]
    if kept:
        tile, rest = rest[0], rest[1:]
    done_grads, done_texts, rest = rest[:n_done], rest[n_done : 2 * n_done], rest[2 * n_done :]
    grads, outs, rest = rest[0], rest[1 : 1 + n], rest[1 + n :]
    total, powers = rest[-2:]
    lowest = min(order)
    for i, t in enumerate(order):
        text_block(
            texts[i],
            tile.at[pl.ds((t - lowest) * block, block)] if kept else None,
            t,
            (even, odd),
            row_lse,
            col_lse,
            place_ref,
            coef_ref,
            grads.at[pl.ds((t - lowest) * block, block)],
        )
    half = even.shape[0]
    scale = scale_ref[0, 0]
    total[...] = scale * (
        jnp.dot(grads[:, :half], even[...], preferred_element_type=jnp.float32)
        + jnp.dot(grads[:, half:], odd[...], preferred_element_type=jnp.float32)
    )
    for i, t in enumerate(order):
        at = (t - lowest) * block
        if t & 1:
            extra_rows = rest[-3]
            put_extra(extra_rows, row_extra)
            encode(outs[i], powers, block, lambda r, at=at: total[at + r : at + r + STEP, :], extra_rows[...])
        else:
            outs[i][:block, :] = total[at : at + block, :]
            put_extra(outs[i].at[block:, :], row_extra)
    if n_done:
        far_ref = rest[0]
        by_text = {t: (grads.at[pl.ds((t - lowest) * block, block)], texts[i]) for i, t in enumerate(order)}

        def one(j, carry):
            far_ref[j, :block, :] = image_block(
                [*done_grads, *[by_text[t][0] for t in order]],
                [*done_texts, *[by_text[t][1] for t in order]],
                pl.multiple_of(j * block + half, block),
                block,
                scale,
            )
            put_extra(far_ref.at[j, block:, :], col_extra)
            return carry

        lax.fori_loop(0, half // block, one, 0, unroll=4)


def text_grads(scale, coef, place, even, odd, row_lse, col_lse, row_extra, col_extra, texts, tile, order, done):
    half, width = even.shape
    block = texts[0].shape[0]
    n = len(order)
    vmem = pl.BlockSpec(memory_space=VMEM)
    smem = pl.BlockSpec(memory_space=SMEM)
    out_shape = (
        [jax.ShapeDtypeStruct((n * block, 2 * half), jnp.bfloat16)]
        + [
            jax.ShapeDtypeStruct((block + MORE, width), jnp.bfloat16)
            if t & 1
            else jax.ShapeDtypeStruct((block + EXTRA, width), jnp.float32)
            for t in order
        ]
    )
    if done:
        out_shape.append(jax.ShapeDtypeStruct((half // block, block + EXTRA, width), jnp.float32))
    operands = [even, odd, row_lse, col_lse, row_extra, col_extra, *[texts[t] for t in order]]
    operands += tile
    operands += [grad for _, grad in done] + [texts[t] for t, _ in done]
    outs = pl.pallas_call(
        functools.partial(text_kernel, tuple(order), len(done), len(tile), block),
        out_shape=tuple(out_shape),
        in_specs=[smem] * 3 + [vmem] * len(operands),
        out_specs=(vmem,) * len(out_shape),
        scratch_shapes=[
            VMEM((EXTRA, width), jnp.float32),
            VMEM((n * block, width), jnp.float32),
            VMEM((block, LANES), jnp.float32),
        ],
        compiler_params=pltpu.CompilerParams(vmem_limit_bytes=(10 + 2 * n) * 2**20),
        cost_estimate=pl.CostEstimate(
            flops=FLOPS * 4 * n * block * 2 * half * width, bytes_accessed=0, transcendentals=0
        ),
        name=f"text_grads_{n}",
    )(scale, coef, place, *operands)
    parts = {t: outs[1 + i] for i, t in enumerate(order)}
    return outs[0], parts, outs[-1]


def image_kernel(n_text, block, scale_ref, extra, near_grads, last_grad, *refs):
    texts, out_ref = refs[:n_text], refs[-1]
    grads = [near_grads.at[pl.ds(t * block, block)] for t in range(n_text - 1)] + [last_grad]

    def one(j, carry):
        put_extra(out_ref.at[j, block:, :], extra)
        out_ref[j, :block, :] = image_block(
            grads, texts, pl.multiple_of(j * block, block), block, scale_ref[0, 0]
        )
        return carry

    lax.fori_loop(0, out_ref.shape[0], one, 0, unroll=4)


def image_grads(scale, extra, grads, texts, after):
    n_text = len(texts)
    rows = grads[0].shape[1]
    block, width = texts[0].shape
    n = rows // block // 2
    vmem = pl.BlockSpec(memory_space=VMEM)
    return pl.pallas_call(
        functools.partial(image_kernel, n_text, block),
        out_shape=jax.ShapeDtypeStruct((n, block + EXTRA, width), jnp.float32),
        in_specs=[pl.BlockSpec(memory_space=SMEM)]
        + [vmem] * (n_text + 3)
        + [pl.BlockSpec(memory_space=pl.ANY)] * len(after),
        out_specs=vmem,
        compiler_params=pltpu.CompilerParams(vmem_limit_bytes=12 * 2**20),
        cost_estimate=pl.CostEstimate(
            flops=FLOPS * 2 * n * block * n_text * block * width, bytes_accessed=0, transcendentals=0
        ),
        name="image_grads",
    )(scale, extra, *grads, *texts, *after)


def on_device(n_row, n_col, image_embeds, text_embeds, logit_scale):
    block = image_embeds.shape[0]
    r, c = lax.axis_index("row"), lax.axis_index("col")
    place = jnp.stack([r, c]).reshape(1, 2)
    scale = logit_scale.reshape(1, 1)
    coef = scale * LOG2E
    image_half, text_half = image_embeds.astype(jnp.bfloat16), text_embeds.astype(jnp.bfloat16)
    even, odd, texts, text_last = gather_both(image_half, text_half, n_col, n_row)
    keep = 4 * n_row * n_col * block * block <= 16 * 2**20
    even, odd, *before = stats(
        coef, place, texts, (*even, *odd), (), n_col, n_row, keep
    )
    text_last, row_parts, col_parts, *tile_last = stats(
        coef, place, text_last, (even, odd), before[:2], n_col, n_row, keep
    )
    texts = [*texts, text_last]
    tile = before[2:]
    row_lse, row_extra, col_lse, col_extra = exchanged(row_parts, col_parts, n_col, n_row)

    held = (scale, coef, place, even, odd, row_lse, col_lse, row_extra, col_extra, texts)
    last = n_row - 1
    last_grad, parts, _ = text_grads(*held, tile_last, [last], [])
    received = swap(parts[last], "row", n_row, 1)
    near_grads, more_parts, far = text_grads(*held, tile, list(range(last))[::-1], [(last, last_grad)])
    parts |= more_parts
    codes = {q: [] for q in range(0, n_row, 2)}
    codes[last ^ 1].append(received)
    after = [pack_text(parts[last ^ 1], codes[last ^ 1])] if n_row > 2 else [received]
    near = image_grads(scale, col_extra, [near_grads, last_grad], texts, after)
    far = swap(far, "col", n_col, 1)
    odd_parts, far = lax.optimization_barrier(([parts[q] for q in range(1, last, 2)], far))
    for q, part in zip(range(1, last, 2), odd_parts):
        codes[q ^ 1].append(swap(part, "row", n_row, 1))
    for b in range(1, n_row.bit_length() - 1):
        for q in [q for q in codes if q & (1 << b)]:
            code = after[0] if (b, q) == (1, last ^ 1) else pack_text(parts[q], codes[q])
            codes[q ^ (1 << b)].append(swap(code, "row", n_row, 1 << b))
            del codes[q]
    grad_text, text_extra, _ = total_of(coef, parts[0], codes[0], True, [], "grad_text")

    own, others = pack_images(near, far)
    others = [swap(code, "col", n_col, 2 * j) for j, code in enumerate(others, 1)]
    first, text_extra = lax.optimization_barrier((others[0], text_extra))
    grad_image, _, grad_scale = total_of(
        coef, added(own, first), others[1:], False, [text_extra], "grad_image"
    )
    return grad_image, grad_text, grad_scale.reshape(())


def solution(mesh):
    images = P(("row", "col"), None)
    texts = P(("col", "row"), None)
    return jax.shard_map(
        functools.partial(on_device, mesh.shape["row"], mesh.shape["col"]),
        mesh=mesh,
        in_specs=(images, texts, P()),
        out_specs=(images, texts, P()),
        check_vma=False,
    )
```

```python
import functools
import math

import jax
import jax.numpy as jnp
from jax import lax
from jax.experimental import pallas as pl
from jax.experimental.pallas import tpu as pltpu
from jax.sharding import PartitionSpec as P

LOG2E = 1.4426950408889634
LN2 = 0.6931471805599453
LANES = 128
VMEM = pltpu.VMEM
SMEM = pltpu.SMEM
FLOPS = 20


def swap(x, axis, n, q):
    return lax.ppermute(x, axis, [(i, i ^ q) for i in range(n)])


def gather_both(image, text, n_col, n_row):
    images = [swap(image, "col", n_col, q) for q in range(2, n_col, 2)]
    texts = [swap(text, "row", n_row, q) for q in range(1, n_row - 1)]
    texts.append(swap(texts[-1], "row", n_row, 1))
    images, texts[:-1] = lax.optimization_barrier((images, texts[:-1]))
    odd = [swap(i, "col", n_col, 1) for i in (image, *images)]
    return [image, *images], odd, [text, *texts]


def nt_dot(a, b):
    return lax.dot_general(a, b, (((1,), (1,)), ((), ())), preferred_element_type=jnp.float32)


def stats_kernel(n_text, block, coef_ref, place_ref, *refs):
    received, refs = refs[:n_text], refs[n_text:]
    coef = coef_ref[0, 0]
    r_place, c_place = place_ref[0, 0], place_ref[0, 1]
    *refs, row_ref, col_ref, tile, row_max, col_max, col_sum, col_dot, row_diag = refs
    *refs, even, odd = refs
    pieces, texts = refs[:-n_text], refs[-n_text:]
    for text, whole in zip(texts, received):
        text[...] = whole[:block, :]
    halves = (even, odd)
    each = len(pieces) // 2
    for i, piece in enumerate(pieces):
        at = (i % each) * block
        halves[i // each][at : at + block, :] = piece[...]
    cols, rows = tile.shape
    half = rows // 2
    col_max[...] = jnp.full(col_max.shape, -jnp.inf, jnp.float32)
    row_diag[...] = jnp.zeros(row_diag.shape, jnp.float32)
    n_col, n_row = row_ref.shape[1], col_ref.shape[1]

    for which, images in enumerate(halves):

        def products(j, carry):
            image = images[pl.ds(pl.multiple_of(j * block, block), block), :]
            at = pl.multiple_of(j * block + which * half, block)
            top = None
            for t in range(n_text):
                part = pl.ds(t * block, block)
                x = nt_dot(texts[t][...], image) * coef
                tile[part, pl.ds(at, block)] = x
                top_t = jnp.max(x, axis=0, keepdims=True)
                top = top_t if top is None else jnp.maximum(top, top_t)
                held = col_max[part, :]
                for lane in range(0, block, LANES):
                    held = jnp.maximum(held, x[:, lane : lane + LANES])
                col_max[part, :] = held
            row_max[0:1, pl.ds(at, block)] = top
            return carry

        lax.fori_loop(0, half // block, products, 0, unroll=4)

    for t in range(n_text):
        among = c_place * n_row + (r_place ^ t) - r_place * n_col

        @pl.when((among >= 0) & (among < n_col))
        def _():
            q = c_place ^ among
            at = pl.multiple_of((q // 2) * block + (q % 2) * half, block)
            x = tile[t * block : (t + 1) * block, pl.ds(at, block)]
            down = lax.broadcasted_iota(jnp.int32, x.shape, 0)
            across = lax.broadcasted_iota(jnp.int32, x.shape, 1)
            row_diag[0:1, pl.ds(at, block)] = jnp.sum(
                jnp.where(down == across, x, 0.0), axis=0, keepdims=True
            )

    col_max[...] = jnp.broadcast_to(
        jnp.max(col_max[...], axis=1, keepdims=True), col_max.shape
    )
    sums = []
    for which in range(2):
        lanes = range(which * half, (which + 1) * half, LANES)

        def exponentials(i, acc):
            part = pl.ds(pl.multiple_of(i * 8, 8), 8)
            top = col_max[part, :]
            total = col_sum[part, :] if which else None
            dot = col_dot[part, :] if which else None
            new = [], []
            for n, lane in enumerate(lanes):
                x = tile[part, lane : lane + LANES]
                e = jnp.exp2(x - row_max[0:1, lane : lane + LANES])
                new[0].append(acc[0][n] + e)
                new[1].append(acc[1][n] + e * x)
                e = jnp.exp2(x - top)
                total = e if total is None else total + e
                dot = e * x if dot is None else dot + e * x
            col_sum[part, :] = total
            col_dot[part, :] = dot
            return tuple(new[0]), tuple(new[1])

        zeros = tuple(jnp.zeros((8, LANES), jnp.float32) for _ in lanes)
        sums.append(lax.fori_loop(0, cols // 8, exponentials, (zeros, zeros), unroll=8))

    row_ids = lax.broadcasted_iota(jnp.int32, (n_col, block), 0)
    placed = [jnp.zeros((n_col, block), jnp.float32)] * 4
    for q in range(n_col):
        at = (q // 2) * block
        here = row_ids == (c_place ^ q)
        new = [row_max[0:1, at + (q % 2) * half : at + (q % 2) * half + block]]
        for which in sums[q % 2]:
            new.append(
                jnp.concatenate(
                    [
                        jnp.sum(which[(at + lane) // LANES], axis=0, keepdims=True)
                        for lane in range(0, block, LANES)
                    ],
                    axis=1,
                )
            )
        new.append(row_diag[0:1, at + (q % 2) * half : at + (q % 2) * half + block])
        placed = [jnp.where(here, n, p) for n, p in zip(new, placed)]
    for i in range(4):
        row_ref[i] = placed[i]
    row_ids = lax.broadcasted_iota(jnp.int32, (n_row, block), 0)
    placed = [jnp.zeros((n_row, block), jnp.float32)] * 3
    for t in range(n_text):
        part = pl.ds(t * block, block)
        here = row_ids == (r_place ^ t)
        new = [col_max[part, :].T[0:1, :]]
        for which in (col_sum, col_dot):
            new.append(jnp.sum(which[part, :].T, axis=0, keepdims=True))
        placed = [jnp.where(here, n, p) for n, p in zip(new, placed)]
    for i in range(3):
        col_ref[i] = placed[i]


def stats(coef, place, texts, images, keep):
    block, width = images[0].shape
    rows, cols = block * len(images), block * len(texts)
    vmem = pl.BlockSpec(memory_space=VMEM)
    smem = pl.BlockSpec(memory_space=SMEM)
    out_shape = [jax.ShapeDtypeStruct((block, width), jnp.bfloat16)] * len(texts)
    out_shape += [jax.ShapeDtypeStruct((rows // 2, width), jnp.bfloat16)] * 2
    out_shape += [
        jax.ShapeDtypeStruct((4, len(images), block), jnp.float32),
        jax.ShapeDtypeStruct((3, len(texts), block), jnp.float32),
    ]
    scratch = [
        VMEM((8, rows), jnp.float32),
        VMEM((cols, LANES), jnp.float32),
        VMEM((cols, LANES), jnp.float32),
        VMEM((cols, LANES), jnp.float32),
        VMEM((8, rows), jnp.float32),
    ]
    if keep:
        out_shape.append(jax.ShapeDtypeStruct((cols, rows), jnp.float32))
    else:
        scratch.insert(0, VMEM((cols, rows), jnp.float32))
    outs = pl.pallas_call(
        functools.partial(stats_kernel, len(texts), block),
        out_shape=tuple(out_shape),
        in_specs=[smem, smem] + [vmem] * (len(texts) + len(images)),
        out_specs=(vmem,) * len(out_shape),
        scratch_shapes=scratch,
        compiler_params=pltpu.CompilerParams(
            vmem_limit_bytes=(0 if keep else 4 * rows * cols) + 8 * 2**20
        ),
        cost_estimate=pl.CostEstimate(
            flops=FLOPS * 2 * rows * cols * width, bytes_accessed=0, transcendentals=0
        ),
        name="stats",
    )(coef, place, *texts, *images)
    return outs[: len(texts)], *outs[len(texts) : len(texts) + 4], outs[len(texts) + 4 :]


def merged(a, b):
    top = jnp.maximum(a[0], b[0])
    wa, wb = jnp.exp2(a[0] - top), jnp.exp2(b[0] - top)
    out = [top] + [a[i] * wa + b[i] * wb for i in (1, 2)]
    return out + [a[i] + b[i] for i in range(3, len(a))]


def by_pairs(blocks, add):
    while len(blocks) > 1:
        blocks = [add(blocks[i], blocks[i + 1]) for i in range(0, len(blocks), 2)]
    return blocks[0]


def lse_and_mean(parts):
    mean = 0.5 * parts[2] / parts[1]
    return parts[0] + jnp.log(parts[1]) * LOG2E, mean - parts[3] if len(parts) > 3 else mean


def exchanged(row_parts, col_parts, n_col, n_row):
    rows, cols = list(row_parts), list(col_parts)
    count = len(cols)
    fill = row_parts.size // col_parts.size + 1
    row_bits = [1 << b for b in range(1, n_col.bit_length() - 1)] + [1]
    col_bits = [1 << b for b in range(n_row.bit_length() - 1)]
    for n, bit in enumerate(row_bits):
        received = swap(jnp.stack(rows), "col", n_col, bit)
        if n < len(col_bits):
            other = swap(jnp.stack(cols * fill), "row", n_row, col_bits[n])
            received, other = lax.optimization_barrier((received, other))
            cols = merged(cols, list(other[:count]))
        rows = merged(rows, list(received))
    return *lse_and_mean(rows), *lse_and_mean(cols)


LEVELS = 32000
LOW = 128
BIAS = 125
EXTRA = 8
MORE = 2 * EXTRA
STEP = 32


def put_extra(out, extra_ref):
    n, width = extra_ref.shape
    rows = min(n, EXTRA)
    out[...] = jnp.zeros(out.shape, out.dtype)
    out[:rows, :width] = sum(extra_ref[i : i + rows, :] for i in range(0, n, rows))


def power(k):
    return jnp.exp2(k).astype(jnp.bfloat16).astype(jnp.float32)


def encode(out, powers, size, slab, extra):
    width = out.shape[1]
    for r in range(0, size, STEP):
        value = slab(r)
        top = jnp.maximum(jnp.max(jnp.abs(value), axis=1, keepdims=True), 1e-30)
        k = jnp.ceil(jnp.log(top) * LOG2E)
        powers[r : r + STEP, :] = jnp.broadcast_to(power(k), (STEP, LANES))
        whole = jnp.floor(jnp.abs(value) * (power(-k) * (LEVELS - 1)) + 0.5) * (1 / LOW)
        high = jnp.floor(whole)
        code = (1.0 + (whole - high)) * jnp.exp2(high - BIAS)
        out[r : r + STEP, :] = jnp.where(value < 0, -code, code).astype(jnp.bfloat16)
    half = width // 2
    first = extra[:, :half].astype(jnp.bfloat16)
    rest = extra[:, :half] - first.astype(jnp.float32)
    second = rest.astype(jnp.bfloat16)
    third = (rest - second.astype(jnp.float32)).astype(jnp.bfloat16)
    fourth = powers[...].T[:EXTRA, :].astype(jnp.bfloat16)
    if size < half:
        fourth = jnp.concatenate([fourth, jnp.zeros((EXTRA, half - size), jnp.bfloat16)], axis=1)
    out[size:, :half] = jnp.concatenate([first, second], axis=0)
    out[size:, half:] = jnp.concatenate([third, fourth], axis=0)


def decode_powers(code, size):
    half = code.shape[1] // 2
    powers = code[size:, half : half + size].astype(jnp.float32)
    return jnp.broadcast_to(powers[EXTRA : EXTRA + 1, :], (LANES, size)).T * (LOW / (LEVELS - 1))


def decode(code, powers, r):
    lanes = []
    for lane in range(0, code.shape[1], LANES):
        c = code[r : r + STEP, lane : lane + LANES].astype(jnp.float32)
        a = jnp.abs(c)
        high = jnp.floor(jnp.log(a) * LOG2E)
        whole = (high + (BIAS - 1)) + a * jnp.exp2(-high)
        lanes.append(jnp.where(c < 0, -whole, whole) * powers[r : r + STEP, :])
    return jnp.concatenate(lanes, axis=1)


def decode_extra(code, size):
    half = code.shape[1] // 2
    left = code[size:, :half].astype(jnp.float32)
    right = code[size:, half:].astype(jnp.float32)
    return left[:EXTRA] + left[EXTRA:] + right[:EXTRA]


def pack_text_kernel(n, base, *refs):
    codes, out, powers, received = refs[:n], *refs[n:]
    size, half = base.shape[0] - EXTRA, base.shape[1] // 2
    more = base[size:, :half]
    for c, code in enumerate(codes):
        received[c] = decode_powers(code, size)
        more = more + decode_extra(code, size)

    def slab(r):
        value = base[r : r + STEP, :]
        for c, code in enumerate(codes):
            value = value + decode(code, received.at[c], r)
        return value

    encode(out, powers, size, slab, more)


def pack_text(base, codes):
    size, width = base.shape[0] - EXTRA, base.shape[1]
    vmem = pl.BlockSpec(memory_space=VMEM)
    return pl.pallas_call(
        functools.partial(pack_text_kernel, len(codes)),
        out_shape=jax.ShapeDtypeStruct((size + MORE, width), jnp.bfloat16),
        in_specs=[vmem] * (1 + len(codes)),
        out_specs=vmem,
        scratch_shapes=[VMEM((size, LANES), jnp.float32), VMEM((len(codes), size, LANES), jnp.float32)],
        compiler_params=pltpu.CompilerParams(vmem_limit_bytes=6 * 2**20),
        cost_estimate=pl.CostEstimate(
            flops=FLOPS * 32 * size * size * width, bytes_accessed=0, transcendentals=0
        ),
        name="pack_text",
    )(base, *codes)


def pack_images_kernel(n, near, far, *refs):
    own, *outs, powers = refs[-n - 1 :]
    size = near.shape[1] - EXTRA
    own[...] = near[0] + far[0]
    for j, out in enumerate(outs, 1):
        encode(
            out,
            powers.at[j - 1],
            size,
            lambda r, j=j: near[j, r : r + STEP, :] + far[j, r : r + STEP, :],
            near[j, size:, :] + far[j, size:, :],
        )


def pack_images(near, far, after):
    n, rows, width = near.shape
    size = rows - EXTRA
    vmem = pl.BlockSpec(memory_space=VMEM)
    code = jax.ShapeDtypeStruct((size + MORE, width), jnp.bfloat16)
    own, *codes = pl.pallas_call(
        functools.partial(pack_images_kernel, n),
        out_shape=(jax.ShapeDtypeStruct((rows, width), jnp.float32),) + (code,) * (n - 1),
        in_specs=[vmem] * 2 + [pl.BlockSpec(memory_space=pl.ANY)] * len(after),
        out_specs=(vmem,) * n,
        scratch_shapes=[VMEM((n - 1, size, LANES), jnp.float32)],
        compiler_params=pltpu.CompilerParams(vmem_limit_bytes=(4 + 2 * n) * 2**20),
        cost_estimate=pl.CostEstimate(
            flops=FLOPS * 8 * n * size * size * width, bytes_accessed=0, transcendentals=0
        ),
        name="pack_images",
    )(near, far, *after)
    return own, codes


def total_kernel(n, in_order, coef_ref, base, *refs):
    codes, before = refs[:n], refs[n:-6]
    out, extra, scalar, value, powers, sems = refs[-6:]
    size, width = base.shape[0] - EXTRA, base.shape[1]
    combine = functools.partial(functools.reduce, jnp.add) if in_order else first_and_pairs
    for c, code in enumerate(codes):
        powers[c] = decode_powers(code, size)
    copies = []
    steps = sems.shape[0]
    for i in range(steps):
        part = pl.ds(i * (size // steps), size // steps)
        for r in range(i * (size // steps), (i + 1) * (size // steps), STEP):
            value[r : r + STEP, :] = combine(
                [base[r : r + STEP, :]] + [decode(code, powers.at[c], r) for c, code in enumerate(codes)]
            )
        copies.append(pltpu.make_async_copy(value.at[part], out.at[part], sems.at[i]))
        copies[-1].start()
    more = combine([base[size:, : width // 2]] + [decode_extra(code, size) for code in codes])
    more = sum([b[...] for b in before], more)
    extra[...] = more
    scalar[0, 0] = jnp.sum(more) / coef_ref[0, 0]
    for copy in copies:
        copy.wait()


def add_kernel(base, code, out, powers):
    size, half = base.shape[0] - EXTRA, base.shape[1] // 2
    powers[...] = decode_powers(code, size)
    for r in range(0, size, STEP):
        out[r : r + STEP, :] = base[r : r + STEP, :] + decode(code, powers, r)
    out[size:, :half] = base[size:, :half] + decode_extra(code, size)
    out[size:, half:] = jnp.zeros((EXTRA, half), jnp.float32)


def added(base, code):
    vmem = pl.BlockSpec(memory_space=VMEM)
    return pl.pallas_call(
        add_kernel,
        out_shape=jax.ShapeDtypeStruct(base.shape, jnp.float32),
        in_specs=[vmem] * 2,
        out_specs=vmem,
        scratch_shapes=[VMEM((base.shape[0] - EXTRA, LANES), jnp.float32)],
        compiler_params=pltpu.CompilerParams(vmem_limit_bytes=6 * 2**20),
        name="added",
    )(base, code)


def first_and_pairs(blocks):
    if len(blocks) == 1:
        return blocks[0]
    pairs = [blocks[0]] + [blocks[i] + blocks[i + 1] for i in range(1, len(blocks), 2)]
    return by_pairs(pairs, jnp.add)


def total_of(coef, base, codes, in_order, before, name):
    size, width = base.shape[0] - EXTRA, base.shape[1]
    vmem = pl.BlockSpec(memory_space=VMEM)
    smem = pl.BlockSpec(memory_space=SMEM)
    return pl.pallas_call(
        functools.partial(total_kernel, len(codes), in_order),
        out_shape=(
            jax.ShapeDtypeStruct((size, width), jnp.float32),
            jax.ShapeDtypeStruct((EXTRA, width // 2), jnp.float32),
            jax.ShapeDtypeStruct((1, 1), jnp.float32),
        ),
        in_specs=[smem] + [vmem] * (1 + len(codes) + len(before)),
        out_specs=(pl.BlockSpec(memory_space=pl.ANY), vmem, smem),
        scratch_shapes=[
            VMEM((size, width), jnp.float32),
            VMEM((len(codes), size, LANES), jnp.float32),
            pltpu.SemaphoreType.DMA((4,)),
        ],
        compiler_params=pltpu.CompilerParams(vmem_limit_bytes=8 * 2**20),
        name=name,
    )(coef, base, *codes, *before)


def text_block(text, tile, t, halves, row_lse, col_lse, place_ref, coef_ref, grad_ref):
    coef = coef_ref[0, 0]
    r_place, c_place = place_ref[0, 0], place_ref[0, 1]
    half, width = halves[0].shape
    n_col, n_row = row_lse.shape[0], col_lse.shape[0]
    size = text.shape[0]
    block = size
    col_lse_down = jnp.broadcast_to(col_lse[pl.ds(r_place ^ t, 1), :], (LANES, size)).T
    text_id = c_place * n_row + (r_place ^ t)
    step = 32
    lane_ids = lax.broadcasted_iota(jnp.int32, (step, LANES), 1)
    row_ids = lax.broadcasted_iota(jnp.int32, (step, LANES), 0)

    for which, images in enumerate(halves):

        def one(j, carry):
            at = pl.multiple_of(j * block + which * half, block)
            if tile is None:
                image = images[pl.ds(pl.multiple_of(j * block, block), block), :]
                xs = nt_dot(text[...], image) * coef
            column = c_place ^ (2 * j + which)
            same = jnp.where(r_place * n_col + column == text_id, 1.0, 0.0)
            lse = row_lse[pl.ds(column, 1), :]
            for r in range(0, size, step):
                for lane in range(0, block, LANES):
                    if tile is None:
                        x = xs[r : r + step, lane : lane + LANES]
                    else:
                        x = tile[r : r + step, pl.ds(at + lane, LANES)]
                    e = jnp.exp2(x - lse[:, lane : lane + LANES]) + jnp.exp2(
                        x - col_lse_down[r : r + step, :]
                    )
                    g = 0.5 * e
                    if lane <= r < lane + LANES:
                        g = g - jnp.where(row_ids + (r - lane) == lane_ids, same, 0.0)
                    grad_ref[r : r + step, pl.ds(at + lane, LANES)] = g.astype(jnp.bfloat16)
            return carry

        lax.fori_loop(0, half // block, one, 0, unroll=4)


def image_block(grads, texts, at, block, scale):
    total = None
    for grad, text in zip(grads, texts):
        part = lax.dot_general(
            grad[:, pl.ds(at, block)],
            text[...],
            (((0,), (0,)), ((), ())),
            preferred_element_type=jnp.float32,
        )
        total = part if total is None else total + part
    return scale * total


def text_kernel(order, n_done, kept, block, scale_ref, coef_ref, place_ref, *refs):
    even, odd, row_lse, col_lse, row_extra, col_extra = refs[:6]
    n = len(order)
    texts, rest = refs[6 : 6 + n], refs[6 + n :]
    if kept:
        tile, rest = rest[0], rest[1:]
    done_grads, done_texts, rest = rest[:n_done], rest[n_done : 2 * n_done], rest[2 * n_done :]
    grads, outs, rest = rest[0], rest[1 : 1 + n], rest[1 + n :]
    total, powers = rest[-2:]
    lowest = min(order)
    for i, t in enumerate(order):
        text_block(
            texts[i],
            tile.at[pl.ds(t * block, block)] if kept else None,
            t,
            (even, odd),
            row_lse,
            col_lse,
            place_ref,
            coef_ref,
            grads.at[pl.ds((t - lowest) * block, block)],
        )
    half = even.shape[0]
    scale = scale_ref[0, 0]
    total[...] = scale * (
        jnp.dot(grads[:, :half], even[...], preferred_element_type=jnp.float32)
        + jnp.dot(grads[:, half:], odd[...], preferred_element_type=jnp.float32)
    )
    for i, t in enumerate(order):
        at = (t - lowest) * block
        if t & 1:
            extra_rows = rest[-3]
            put_extra(extra_rows, row_extra)
            encode(outs[i], powers, block, lambda r, at=at: total[at + r : at + r + STEP, :], extra_rows[...])
        else:
            outs[i][:block, :] = total[at : at + block, :]
            put_extra(outs[i].at[block:, :], row_extra)
    if n_done:
        far_ref, near_ref = rest[:2]
        by_text = {t: (grads.at[pl.ds((t - lowest) * block, block)], texts[i]) for i, t in enumerate(order)}

        for images_ref, first in ((far_ref, half), (near_ref, 0)):

            def one(j, carry):
                images_ref[j, :block, :] = image_block(
                    [*done_grads, *[by_text[t][0] for t in order]],
                    [*done_texts, *[by_text[t][1] for t in order]],
                    pl.multiple_of(j * block + first, block),
                    block,
                    scale,
                )
                put_extra(images_ref.at[j, block:, :], col_extra)
                return carry

            lax.fori_loop(0, half // block, one, 0, unroll=4)


def text_grads(scale, coef, place, even, odd, row_lse, col_lse, row_extra, col_extra, texts, tile, order, done):
    half, width = even.shape
    block = texts[0].shape[0]
    n = len(order)
    vmem = pl.BlockSpec(memory_space=VMEM)
    smem = pl.BlockSpec(memory_space=SMEM)
    out_shape = (
        [jax.ShapeDtypeStruct((n * block, 2 * half), jnp.bfloat16)]
        + [
            jax.ShapeDtypeStruct((block + MORE, width), jnp.bfloat16)
            if t & 1
            else jax.ShapeDtypeStruct((block + EXTRA, width), jnp.float32)
            for t in order
        ]
    )
    if done:
        out_shape += [jax.ShapeDtypeStruct((half // block, block + EXTRA, width), jnp.float32)] * 2
    operands = [even, odd, row_lse, col_lse, row_extra, col_extra, *[texts[t] for t in order]]
    operands += tile
    operands += [grad for _, grad in done] + [texts[t] for t, _ in done]
    outs = pl.pallas_call(
        functools.partial(text_kernel, tuple(order), len(done), len(tile), block),
        out_shape=tuple(out_shape),
        in_specs=[smem] * 3 + [vmem] * len(operands),
        out_specs=(vmem,) * len(out_shape),
        scratch_shapes=[
            VMEM((EXTRA, width), jnp.float32),
            VMEM((n * block, width), jnp.float32),
            VMEM((block, LANES), jnp.float32),
        ],
        compiler_params=pltpu.CompilerParams(vmem_limit_bytes=(10 + 2 * n) * 2**20),
        cost_estimate=pl.CostEstimate(
            flops=FLOPS * 4 * n * block * 2 * half * width, bytes_accessed=0, transcendentals=0
        ),
        name=f"text_grads_{n}",
    )(scale, coef, place, *operands)
    parts = {t: outs[1 + i] for i, t in enumerate(order)}
    return outs[0], parts, outs[1 + n :]


def on_device(n_row, n_col, image_embeds, text_embeds, logit_scale):
    block = image_embeds.shape[0]
    r, c = lax.axis_index("row"), lax.axis_index("col")
    place = jnp.stack([r, c]).reshape(1, 2)
    scale = logit_scale.reshape(1, 1)
    coef = scale * LOG2E
    image_half = image_embeds.astype(jnp.bfloat16)
    text_half = jnp.pad(text_embeds.astype(jnp.bfloat16), ((0, 16), (0, 0)))
    even, odd, texts = gather_both(image_half, text_half, n_col, n_row)
    keep = 4 * n_row * n_col * block * block <= 16 * 2**20
    texts, even, odd, row_parts, col_parts, tile = stats(coef, place, texts, (*even, *odd), keep)
    row_lse, row_extra, col_lse, col_extra = exchanged(row_parts, col_parts, n_col, n_row)

    held = (scale, coef, place, even, odd, row_lse, col_lse, row_extra, col_extra, texts)
    last = n_row - 1
    last_grad, parts, _ = text_grads(*held, tile, [last], [])
    received = swap(parts[last], "row", n_row, 1)
    _, more_parts, (far, near) = text_grads(*held, tile, list(range(last))[::-1], [(last, last_grad)])
    parts |= more_parts
    codes = {q: [] for q in range(0, n_row, 2)}
    codes[last ^ 1].append(received)
    after = [pack_text(parts[last ^ 1], codes[last ^ 1])] if n_row > 2 else [received]
    far = swap(far, "col", n_col, 1)
    odd_parts, far = lax.optimization_barrier(([parts[q] for q in range(1, last, 2)], far))
    for q, part in zip(range(1, last, 2), odd_parts):
        codes[q ^ 1].append(swap(part, "row", n_row, 1))
    for b in range(1, n_row.bit_length() - 1):
        for q in [q for q in codes if q & (1 << b)]:
            code = after[0] if (b, q) == (1, last ^ 1) else pack_text(parts[q], codes[q])
            codes[q ^ (1 << b)].append(swap(code, "row", n_row, 1 << b))
            del codes[q]
    grad_text, text_extra, _ = total_of(coef, parts[0], codes[0], True, [], "grad_text")

    own, others = pack_images(near, far, after)
    others = [swap(code, "col", n_col, 2 * j) for j, code in enumerate(others, 1)]
    first, text_extra = lax.optimization_barrier((others[0], text_extra))
    grad_image, _, grad_scale = total_of(
        coef, added(own, first), others[1:], False, [text_extra], "grad_image"
    )
    return grad_image, grad_text, grad_scale.reshape(())


def solution(mesh):
    images = P(("row", "col"), None)
    texts = P(("col", "row"), None)
    return jax.shard_map(
        functools.partial(on_device, mesh.shape["row"], mesh.shape["col"]),
        mesh=mesh,
        in_specs=(images, texts, P()),
        out_specs=(images, texts, P()),
        check_vma=False,
    )
```

```python
import functools
import math

import jax
import jax.numpy as jnp
from jax import lax
from jax.experimental import pallas as pl
from jax.experimental.pallas import tpu as pltpu
from jax.sharding import PartitionSpec as P

LOG2E = 1.4426950408889634
LN2 = 0.6931471805599453
LANES = 128
VMEM = pltpu.VMEM
SMEM = pltpu.SMEM
FLOPS = 20


def swap(x, axis, n, q):
    return lax.ppermute(x, axis, [(i, i ^ q) for i in range(n)])


def gather_both(image, text, n_col, n_row):
    images = [swap(image, "col", n_col, q) for q in range(2, n_col, 2)]
    texts = [swap(text, "row", n_row, q) for q in range(1, n_row - 1)]
    last = swap(texts[-1], "row", n_row, 1)
    images, texts = lax.optimization_barrier((images, texts))
    odd = [swap(i, "col", n_col, 1) for i in (image, *images)]
    return [image, *images], odd, [text, *texts], last


def nt_dot(a, b):
    return lax.dot_general(a, b, (((1,), (1,)), ((), ())), preferred_element_type=jnp.float32)


def stats_kernel(first, n_text, block, coef_ref, place_ref, *refs):
    texts, refs = refs[:n_text], refs[n_text:]
    coef = coef_ref[0, 0]
    r_place, c_place = place_ref[0, 0], place_ref[0, 1]
    *refs, row_max, col_max, col_sum, col_dot, row_diag = refs
    if first:
        *refs, even, odd, row_ref, col_ref, tile = refs
        halves = (even, odd)
        each = len(refs) // 2
        for i, piece in enumerate(refs):
            at = (i % each) * block
            halves[i // each][at : at + block, :] = piece[...]
        before = None
    else:
        even, odd, *before, row_ref, col_ref, tile = refs
        halves = (even, odd)
    cols, rows = tile.shape
    half = rows // 2
    lead = 0 if first else col_ref.shape[1] - n_text
    col_max[...] = jnp.full(col_max.shape, -jnp.inf, jnp.float32)
    row_diag[...] = jnp.zeros(row_diag.shape, jnp.float32)
    n_col, n_row = row_ref.shape[1], col_ref.shape[1]

    for which, images in enumerate(halves):

        def products(j, carry):
            image = images[pl.ds(pl.multiple_of(j * block, block), block), :]
            at = pl.multiple_of(j * block + which * half, block)
            top = None
            for t in range(n_text):
                part = pl.ds(t * block, block)
                x = nt_dot(texts[t][:block, :], image) * coef
                tile[part, pl.ds(at, block)] = x
                top_t = jnp.max(x, axis=0, keepdims=True)
                top = top_t if top is None else jnp.maximum(top, top_t)
                held = col_max[part, :]
                for lane in range(0, block, LANES):
                    held = jnp.maximum(held, x[:, lane : lane + LANES])
                col_max[part, :] = held
            row_max[0:1, pl.ds(at, block)] = top
            return carry

        lax.fori_loop(0, half // block, products, 0, unroll=4)

    for t in range(n_text):
        among = c_place * n_row + (r_place ^ (lead + t)) - r_place * n_col

        @pl.when((among >= 0) & (among < n_col))
        def _():
            q = c_place ^ among
            at = pl.multiple_of((q // 2) * block + (q % 2) * half, block)
            x = tile[t * block : (t + 1) * block, pl.ds(at, block)]
            down = lax.broadcasted_iota(jnp.int32, x.shape, 0)
            across = lax.broadcasted_iota(jnp.int32, x.shape, 1)
            row_diag[0:1, pl.ds(at, block)] = jnp.sum(
                jnp.where(down == across, x, 0.0), axis=0, keepdims=True
            )

    col_max[...] = jnp.broadcast_to(
        jnp.max(col_max[...], axis=1, keepdims=True), col_max.shape
    )
    sums = []
    for which in range(2):
        lanes = range(which * half, (which + 1) * half, LANES)

        def exponentials(i, acc):
            part = pl.ds(pl.multiple_of(i * 8, 8), 8)
            top = col_max[part, :]
            total = col_sum[part, :] if which else None
            dot = col_dot[part, :] if which else None
            new = [], []
            for n, lane in enumerate(lanes):
                x = tile[part, lane : lane + LANES]
                e = jnp.exp2(x - row_max[0:1, lane : lane + LANES])
                new[0].append(acc[0][n] + e)
                new[1].append(acc[1][n] + e * x)
                e = jnp.exp2(x - top)
                total = e if total is None else total + e
                dot = e * x if dot is None else dot + e * x
            col_sum[part, :] = total
            col_dot[part, :] = dot
            return tuple(new[0]), tuple(new[1])

        zeros = tuple(jnp.zeros((8, LANES), jnp.float32) for _ in lanes)
        sums.append(lax.fori_loop(0, cols // 8, exponentials, (zeros, zeros), unroll=8))

    row_ids = lax.broadcasted_iota(jnp.int32, (n_col, block), 0)
    placed = [jnp.zeros((n_col, block), jnp.float32)] * 4
    for q in range(n_col):
        at = (q // 2) * block
        here = row_ids == (c_place ^ q)
        new = [row_max[0:1, at + (q % 2) * half : at + (q % 2) * half + block]]
        for which in sums[q % 2]:
            new.append(
                jnp.concatenate(
                    [
                        jnp.sum(which[(at + lane) // LANES], axis=0, keepdims=True)
                        for lane in range(0, block, LANES)
                    ],
                    axis=1,
                )
            )
        new.append(row_diag[0:1, at + (q % 2) * half : at + (q % 2) * half + block])
        placed = [jnp.where(here, n, p) for n, p in zip(new, placed)]
    if before:
        placed = merged(placed, [before[0][i] for i in range(4)])
    for i in range(4):
        row_ref[i] = placed[i]
    row_ids = lax.broadcasted_iota(jnp.int32, (n_row, block), 0)
    placed = [before[1][i] if before else jnp.zeros((n_row, block), jnp.float32) for i in range(3)]
    for t in range(n_text):
        part = pl.ds(t * block, block)
        here = row_ids == (r_place ^ (lead + t))
        new = [col_max[part, :].T[0:1, :]]
        for which in (col_sum, col_dot):
            new.append(jnp.sum(which[part, :].T, axis=0, keepdims=True))
        placed = [jnp.where(here, n, p) for n, p in zip(new, placed)]
    for i in range(3):
        col_ref[i] = placed[i]


def stats(coef, place, texts, images, before, n_col, n_row, block, keep):
    width = texts[0].shape[1]
    first = not before
    rows, cols = block * n_col, block * len(texts)
    vmem = pl.BlockSpec(memory_space=VMEM)
    smem = pl.BlockSpec(memory_space=SMEM)
    half = jax.ShapeDtypeStruct((rows // 2, width), jnp.bfloat16)
    out_shape = [half, half] if first else []
    out_shape += [
        jax.ShapeDtypeStruct((4, n_col, block), jnp.float32),
        jax.ShapeDtypeStruct((3, n_row, block), jnp.float32),
    ]
    scratch = [
        VMEM((8, rows), jnp.float32),
        VMEM((cols, LANES), jnp.float32),
        VMEM((cols, LANES), jnp.float32),
        VMEM((cols, LANES), jnp.float32),
        VMEM((8, rows), jnp.float32),
    ]
    if keep:
        out_shape.append(jax.ShapeDtypeStruct((cols, rows), jnp.float32))
    else:
        scratch.insert(0, VMEM((cols, rows), jnp.float32))
    return pl.pallas_call(
        functools.partial(stats_kernel, first, len(texts), block),
        out_shape=tuple(out_shape),
        in_specs=[smem, smem] + [vmem] * (len(texts) + len(images) + len(before)),
        out_specs=(vmem,) * len(out_shape),
        scratch_shapes=scratch,
        compiler_params=pltpu.CompilerParams(
            vmem_limit_bytes=(0 if keep else 4 * rows * cols) + 8 * 2**20
        ),
        cost_estimate=pl.CostEstimate(
            flops=2 * rows * width, bytes_accessed=0, transcendentals=0
        ),
        name="stats" if first else "stats_last",
    )(coef, place, *texts, *images, *before)


def merged(a, b):
    top = jnp.maximum(a[0], b[0])
    wa, wb = jnp.exp2(a[0] - top), jnp.exp2(b[0] - top)
    out = [top] + [a[i] * wa + b[i] * wb for i in (1, 2)]
    return out + [a[i] + b[i] for i in range(3, len(a))]


def by_pairs(blocks, add):
    while len(blocks) > 1:
        blocks = [add(blocks[i], blocks[i + 1]) for i in range(0, len(blocks), 2)]
    return blocks[0]


def lse_and_mean(parts):
    mean = 0.5 * parts[2] / parts[1]
    return parts[0] + jnp.log(parts[1]) * LOG2E, mean - parts[3] if len(parts) > 3 else mean


def exchanged(row_parts, col_parts, n_col, n_row):
    rows, cols = list(row_parts), list(col_parts)
    count = len(cols)
    fill = row_parts.size // col_parts.size + 1
    row_bits = [1 << b for b in range(1, n_col.bit_length() - 1)] + [1]
    col_bits = [1 << b for b in range(n_row.bit_length() - 1)]
    for n, bit in enumerate(row_bits):
        received = swap(jnp.stack(rows), "col", n_col, bit)
        if n < len(col_bits):
            other = swap(jnp.stack(cols * fill), "row", n_row, col_bits[n])
            received, other = lax.optimization_barrier((received, other))
            cols = merged(cols, list(other[:count]))
        rows = merged(rows, list(received))
    return *lse_and_mean(rows), *lse_and_mean(cols)


LEVELS = 32000
LOW = 128
BIAS = 125
EXTRA = 8
MORE = 2 * EXTRA
STEP = 32


def put_extra(out, extra_ref):
    n, width = extra_ref.shape
    rows = min(n, EXTRA)
    out[...] = jnp.zeros(out.shape, out.dtype)
    out[:rows, :width] = sum(extra_ref[i : i + rows, :] for i in range(0, n, rows))


def power(k):
    return jnp.exp2(k).astype(jnp.bfloat16).astype(jnp.float32)


def encode(out, powers, size, slab, extra):
    width = out.shape[1]
    for r in range(0, size, STEP):
        value = slab(r)
        top = jnp.maximum(jnp.max(jnp.abs(value), axis=1, keepdims=True), 1e-30)
        k = jnp.ceil(jnp.log(top) * LOG2E)
        powers[r : r + STEP, :] = jnp.broadcast_to(power(k), (STEP, LANES))
        whole = jnp.floor(jnp.abs(value) * (power(-k) * (LEVELS - 1)) + 0.5) * (1 / LOW)
        high = jnp.floor(whole)
        code = (1.0 + (whole - high)) * jnp.exp2(high - BIAS)
        out[r : r + STEP, :] = jnp.where(value < 0, -code, code).astype(jnp.bfloat16)
    half = width // 2
    first = extra[:, :half].astype(jnp.bfloat16)
    rest = extra[:, :half] - first.astype(jnp.float32)
    second = rest.astype(jnp.bfloat16)
    third = (rest - second.astype(jnp.float32)).astype(jnp.bfloat16)
    fourth = powers[...].T[:EXTRA, :].astype(jnp.bfloat16)
    if size < half:
        fourth = jnp.concatenate([fourth, jnp.zeros((EXTRA, half - size), jnp.bfloat16)], axis=1)
    out[size:, :half] = jnp.concatenate([first, second], axis=0)
    out[size:, half:] = jnp.concatenate([third, fourth], axis=0)


def decode_powers(code, size):
    half = code.shape[1] // 2
    powers = code[size:, half : half + size].astype(jnp.float32)
    return jnp.broadcast_to(powers[EXTRA : EXTRA + 1, :], (LANES, size)).T * (LOW / (LEVELS - 1))


def decode(code, powers, r):
    lanes = []
    for lane in range(0, code.shape[1], LANES):
        c = code[r : r + STEP, lane : lane + LANES].astype(jnp.float32)
        a = jnp.abs(c)
        high = jnp.floor(jnp.log(a) * LOG2E)
        whole = (high + (BIAS - 1)) + a * jnp.exp2(-high)
        lanes.append(jnp.where(c < 0, -whole, whole) * powers[r : r + STEP, :])
    return jnp.concatenate(lanes, axis=1)


def decode_extra(code, size):
    half = code.shape[1] // 2
    left = code[size:, :half].astype(jnp.float32)
    right = code[size:, half:].astype(jnp.float32)
    return left[:EXTRA] + left[EXTRA:] + right[:EXTRA]


def pack_text_kernel(n, base, *refs):
    codes, out, powers, received = refs[:n], *refs[n:]
    size, half = base.shape[0] - EXTRA, base.shape[1] // 2
    more = base[size:, :half]
    for c, code in enumerate(codes):
        received[c] = decode_powers(code, size)
        more = more + decode_extra(code, size)

    def slab(r):
        value = base[r : r + STEP, :]
        for c, code in enumerate(codes):
            value = value + decode(code, received.at[c], r)
        return value

    encode(out, powers, size, slab, more)


def pack_text(base, codes):
    size, width = base.shape[0] - EXTRA, base.shape[1]
    vmem = pl.BlockSpec(memory_space=VMEM)
    return pl.pallas_call(
        functools.partial(pack_text_kernel, len(codes)),
        out_shape=jax.ShapeDtypeStruct((size + MORE, width), jnp.bfloat16),
        in_specs=[vmem] * (1 + len(codes)),
        out_specs=vmem,
        scratch_shapes=[VMEM((size, LANES), jnp.float32), VMEM((len(codes), size, LANES), jnp.float32)],
        compiler_params=pltpu.CompilerParams(vmem_limit_bytes=6 * 2**20),
        cost_estimate=pl.CostEstimate(
            flops=FLOPS * 32 * size * size * width, bytes_accessed=0, transcendentals=0
        ),
        name="pack_text",
    )(base, *codes)


def pack_images_kernel(n, near, far, *refs):
    own, *outs, powers = refs[-n - 1 :]
    size = near.shape[1] - EXTRA
    own[...] = near[0] + far[0]
    for j, out in enumerate(outs, 1):
        encode(
            out,
            powers.at[j - 1],
            size,
            lambda r, j=j: near[j, r : r + STEP, :] + far[j, r : r + STEP, :],
            near[j, size:, :] + far[j, size:, :],
        )


def pack_images(near, far, after):
    n, rows, width = near.shape
    size = rows - EXTRA
    vmem = pl.BlockSpec(memory_space=VMEM)
    code = jax.ShapeDtypeStruct((size + MORE, width), jnp.bfloat16)
    own, *codes = pl.pallas_call(
        functools.partial(pack_images_kernel, n),
        out_shape=(jax.ShapeDtypeStruct((rows, width), jnp.float32),) + (code,) * (n - 1),
        in_specs=[vmem] * 2 + [pl.BlockSpec(memory_space=pl.ANY)] * len(after),
        out_specs=(vmem,) * n,
        scratch_shapes=[VMEM((n - 1, size, LANES), jnp.float32)],
        compiler_params=pltpu.CompilerParams(vmem_limit_bytes=(4 + 2 * n) * 2**20),
        cost_estimate=pl.CostEstimate(
            flops=FLOPS * 8 * n * size * size * width, bytes_accessed=0, transcendentals=0
        ),
        name="pack_images",
    )(near, far, *after)
    return own, codes


def total_kernel(n, in_order, coef_ref, base, *refs):
    codes, before = refs[:n], refs[n:-6]
    out, extra, scalar, value, powers, sems = refs[-6:]
    size, width = base.shape[0] - EXTRA, base.shape[1]
    combine = functools.partial(functools.reduce, jnp.add) if in_order else first_and_pairs
    for c, code in enumerate(codes):
        powers[c] = decode_powers(code, size)
    copies = []
    steps = sems.shape[0]
    for i in range(steps):
        part = pl.ds(i * (size // steps), size // steps)
        for r in range(i * (size // steps), (i + 1) * (size // steps), STEP):
            value[r : r + STEP, :] = combine(
                [base[r : r + STEP, :]] + [decode(code, powers.at[c], r) for c, code in enumerate(codes)]
            )
        copies.append(pltpu.make_async_copy(value.at[part], out.at[part], sems.at[i]))
        copies[-1].start()
    more = combine([base[size:, : width // 2]] + [decode_extra(code, size) for code in codes])
    more = sum([b[...] for b in before], more)
    extra[...] = more
    scalar[0, 0] = jnp.sum(more) / coef_ref[0, 0]
    for copy in copies:
        copy.wait()


def add_kernel(base, code, out, powers):
    size, half = base.shape[0] - EXTRA, base.shape[1] // 2
    powers[...] = decode_powers(code, size)
    for r in range(0, size, STEP):
        out[r : r + STEP, :] = base[r : r + STEP, :] + decode(code, powers, r)
    out[size:, :half] = base[size:, :half] + decode_extra(code, size)
    out[size:, half:] = jnp.zeros((EXTRA, half), jnp.float32)


def added(base, code):
    vmem = pl.BlockSpec(memory_space=VMEM)
    return pl.pallas_call(
        add_kernel,
        out_shape=jax.ShapeDtypeStruct(base.shape, jnp.float32),
        in_specs=[vmem] * 2,
        out_specs=vmem,
        scratch_shapes=[VMEM((base.shape[0] - EXTRA, LANES), jnp.float32)],
        compiler_params=pltpu.CompilerParams(vmem_limit_bytes=6 * 2**20),
        name="added",
    )(base, code)


def first_and_pairs(blocks):
    if len(blocks) == 1:
        return blocks[0]
    pairs = [blocks[0]] + [blocks[i] + blocks[i + 1] for i in range(1, len(blocks), 2)]
    return by_pairs(pairs, jnp.add)


def total_of(coef, base, codes, in_order, before, name):
    size, width = base.shape[0] - EXTRA, base.shape[1]
    vmem = pl.BlockSpec(memory_space=VMEM)
    smem = pl.BlockSpec(memory_space=SMEM)
    return pl.pallas_call(
        functools.partial(total_kernel, len(codes), in_order),
        out_shape=(
            jax.ShapeDtypeStruct((size, width), jnp.float32),
            jax.ShapeDtypeStruct((EXTRA, width // 2), jnp.float32),
            jax.ShapeDtypeStruct((1, 1), jnp.float32),
        ),
        in_specs=[smem] + [vmem] * (1 + len(codes) + len(before)),
        out_specs=(pl.BlockSpec(memory_space=pl.ANY), vmem, smem),
        scratch_shapes=[
            VMEM((size, width), jnp.float32),
            VMEM((len(codes), size, LANES), jnp.float32),
            pltpu.SemaphoreType.DMA((4,)),
        ],
        compiler_params=pltpu.CompilerParams(vmem_limit_bytes=8 * 2**20),
        name=name,
    )(coef, base, *codes, *before)


def text_block(block, text, tile, t, halves, row_lse, col_lse, place_ref, coef_ref, grad_ref):
    coef = coef_ref[0, 0]
    r_place, c_place = place_ref[0, 0], place_ref[0, 1]
    half, width = halves[0].shape
    n_col, n_row = row_lse.shape[0], col_lse.shape[0]
    size = block
    col_lse_down = jnp.broadcast_to(col_lse[pl.ds(r_place ^ t, 1), :], (LANES, size)).T
    text_id = c_place * n_row + (r_place ^ t)
    step = 32
    lane_ids = lax.broadcasted_iota(jnp.int32, (step, LANES), 1)
    row_ids = lax.broadcasted_iota(jnp.int32, (step, LANES), 0)

    for which, images in enumerate(halves):

        def one(j, carry):
            at = pl.multiple_of(j * block + which * half, block)
            if tile is None:
                image = images[pl.ds(pl.multiple_of(j * block, block), block), :]
                xs = nt_dot(text[:block, :], image) * coef
            column = c_place ^ (2 * j + which)
            same = jnp.where(r_place * n_col + column == text_id, 1.0, 0.0)
            lse = row_lse[pl.ds(column, 1), :]
            for r in range(0, size, step):
                for lane in range(0, block, LANES):
                    if tile is None:
                        x = xs[r : r + step, lane : lane + LANES]
                    else:
                        x = tile[r : r + step, pl.ds(at + lane, LANES)]
                    e = jnp.exp2(x - lse[:, lane : lane + LANES]) + jnp.exp2(
                        x - col_lse_down[r : r + step, :]
                    )
                    g = 0.5 * e
                    if lane <= r < lane + LANES:
                        g = g - jnp.where(row_ids + (r - lane) == lane_ids, same, 0.0)
                    grad_ref[r : r + step, pl.ds(at + lane, LANES)] = g.astype(jnp.bfloat16)
            return carry

        lax.fori_loop(0, half // block, one, 0, unroll=4)


def image_block(grads, texts, at, block, scale):
    total = None
    for grad, text in zip(grads, texts):
        part = lax.dot_general(
            grad[:, pl.ds(at, block)],
            text[:block, :],
            (((0,), (0,)), ((), ())),
            preferred_element_type=jnp.float32,
        )
        total = part if total is None else total + part
    return scale * total


def text_kernel(order, n_done, kept, block, scale_ref, coef_ref, place_ref, *refs):
    even, odd, row_lse, col_lse, row_extra, col_extra = refs[:6]
    n = len(order)
    texts, rest = refs[6 : 6 + n], refs[6 + n :]
    if kept:
        tile, rest = rest[0], rest[1:]
    done_grads, done_texts, rest = rest[:n_done], rest[n_done : 2 * n_done], rest[2 * n_done :]
    grads, outs, rest = rest[0], rest[1 : 1 + n], rest[1 + n :]
    total, powers = rest[-2:]
    lowest = min(order)
    for i, t in enumerate(order):
        text_block(
            block,
            texts[i],
            tile.at[pl.ds((t - lowest) * block, block)] if kept else None,
            t,
            (even, odd),
            row_lse,
            col_lse,
            place_ref,
            coef_ref,
            grads.at[pl.ds((t - lowest) * block, block)],
        )
    half = even.shape[0]
    scale = scale_ref[0, 0]
    total[...] = scale * (
        jnp.dot(grads[:, :half], even[...], preferred_element_type=jnp.float32)
        + jnp.dot(grads[:, half:], odd[...], preferred_element_type=jnp.float32)
    )
    for i, t in enumerate(order):
        at = (t - lowest) * block
        if t & 1:
            extra_rows = rest[-3]
            put_extra(extra_rows, row_extra)
            encode(outs[i], powers, block, lambda r, at=at: total[at + r : at + r + STEP, :], extra_rows[...])
        else:
            outs[i][:block, :] = total[at : at + block, :]
            put_extra(outs[i].at[block:, :], row_extra)
    if n_done:
        far_ref, near_ref = rest[:2]
        by_text = {t: (grads.at[pl.ds((t - lowest) * block, block)], texts[i]) for i, t in enumerate(order)}

        for images_ref, first in ((far_ref, half), (near_ref, 0)):

            def one(j, carry):
                images_ref[j, :block, :] = image_block(
                    [*done_grads, *[by_text[t][0] for t in order]],
                    [*done_texts, *[by_text[t][1] for t in order]],
                    pl.multiple_of(j * block + first, block),
                    block,
                    scale,
                )
                put_extra(images_ref.at[j, block:, :], col_extra)
                return carry

            lax.fori_loop(0, half // block, one, 0, unroll=4)


def text_grads(scale, coef, place, even, odd, row_lse, col_lse, row_extra, col_extra, texts, tile, order, done):
    half, width = even.shape
    block = row_lse.shape[1]
    n = len(order)
    vmem = pl.BlockSpec(memory_space=VMEM)
    smem = pl.BlockSpec(memory_space=SMEM)
    out_shape = (
        [jax.ShapeDtypeStruct((n * block, 2 * half), jnp.bfloat16)]
        + [
            jax.ShapeDtypeStruct((block + MORE, width), jnp.bfloat16)
            if t & 1
            else jax.ShapeDtypeStruct((block + EXTRA, width), jnp.float32)
            for t in order
        ]
    )
    if done:
        out_shape += [jax.ShapeDtypeStruct((half // block, block + EXTRA, width), jnp.float32)] * 2
    operands = [even, odd, row_lse, col_lse, row_extra, col_extra, *[texts[t] for t in order]]
    operands += tile
    operands += [grad for _, grad in done] + [texts[t] for t, _ in done]
    outs = pl.pallas_call(
        functools.partial(text_kernel, tuple(order), len(done), len(tile), block),
        out_shape=tuple(out_shape),
        in_specs=[smem] * 3 + [vmem] * len(operands),
        out_specs=(vmem,) * len(out_shape),
        scratch_shapes=[
            VMEM((EXTRA, width), jnp.float32),
            VMEM((n * block, width), jnp.float32),
            VMEM((block, LANES), jnp.float32),
        ],
        compiler_params=pltpu.CompilerParams(vmem_limit_bytes=(10 + 2 * n) * 2**20),
        cost_estimate=pl.CostEstimate(
            flops=FLOPS * 4 * n * block * 2 * half * width, bytes_accessed=0, transcendentals=0
        ),
        name=f"text_grads_{n}",
    )(scale, coef, place, *operands)
    parts = {t: outs[1 + i] for i, t in enumerate(order)}
    return outs[0], parts, outs[1 + n :]


def on_device(n_row, n_col, image_embeds, text_embeds, logit_scale):
    block = image_embeds.shape[0]
    r, c = lax.axis_index("row"), lax.axis_index("col")
    place = jnp.stack([r, c]).reshape(1, 2)
    scale = logit_scale.reshape(1, 1)
    coef = scale * LOG2E
    image_half = image_embeds.astype(jnp.bfloat16)
    text_half = jnp.pad(text_embeds.astype(jnp.bfloat16), ((0, 16), (0, 0)))
    even, odd, texts, text_last = gather_both(image_half, text_half, n_col, n_row)
    keep = 4 * n_row * n_col * block * block <= 16 * 2**20
    even, odd, *before = stats(
        coef, place, texts, (*even, *odd), (), n_col, n_row, block, keep
    )
    row_parts, col_parts, *tile_last = stats(
        coef, place, [text_last], (even, odd), before[:2], n_col, n_row, block, keep
    )
    texts = [*texts, text_last]
    tile = before[2:]
    row_lse, row_extra, col_lse, col_extra = exchanged(row_parts, col_parts, n_col, n_row)

    held = (scale, coef, place, even, odd, row_lse, col_lse, row_extra, col_extra, texts)
    last = n_row - 1
    last_grad, parts, _ = text_grads(*held, tile_last, [last], [])
    received = swap(parts[last], "row", n_row, 1)
    _, more_parts, (far, near) = text_grads(*held, tile, list(range(last))[::-1], [(last, last_grad)])
    parts |= more_parts
    codes = {q: [] for q in range(0, n_row, 2)}
    codes[last ^ 1].append(received)
    after = [pack_text(parts[last ^ 1], codes[last ^ 1])] if n_row > 2 else [received]
    far = swap(far, "col", n_col, 1)
    odd_parts, far = lax.optimization_barrier(([parts[q] for q in range(1, last, 2)], far))
    for q, part in zip(range(1, last, 2), odd_parts):
        codes[q ^ 1].append(swap(part, "row", n_row, 1))
    for b in range(1, n_row.bit_length() - 1):
        for q in [q for q in codes if q & (1 << b)]:
            code = after[0] if (b, q) == (1, last ^ 1) else pack_text(parts[q], codes[q])
            codes[q ^ (1 << b)].append(swap(code, "row", n_row, 1 << b))
            del codes[q]
    grad_text, text_extra, _ = total_of(coef, parts[0], codes[0], True, [], "grad_text")

    own, others = pack_images(near, far, after)
    others = [swap(code, "col", n_col, 2 * j) for j, code in enumerate(others, 1)]
    first, text_extra = lax.optimization_barrier((others[0], text_extra))
    grad_image, _, grad_scale = total_of(
        coef, added(own, first), others[1:], False, [text_extra], "grad_image"
    )
    return grad_image, grad_text, grad_scale.reshape(())


def solution(mesh):
    images = P(("row", "col"), None)
    texts = P(("col", "row"), None)
    return jax.shard_map(
        functools.partial(on_device, mesh.shape["row"], mesh.shape["col"]),
        mesh=mesh,
        in_specs=(images, texts, P()),
        out_specs=(images, texts, P()),
        check_vma=False,
    )
```

```python
import functools
import math

import jax
import jax.numpy as jnp
from jax import lax
from jax.experimental import pallas as pl
from jax.experimental.pallas import tpu as pltpu
from jax.sharding import PartitionSpec as P

LOG2E = 1.4426950408889634
LN2 = 0.6931471805599453
LANES = 128
VMEM = pltpu.VMEM
SMEM = pltpu.SMEM
FLOPS = 20


def swap(x, axis, n, q):
    return lax.ppermute(x, axis, [(i, i ^ q) for i in range(n)])


def gather_both(image, text, n_col, n_row):
    images = [swap(image, "col", n_col, q) for q in range(2, n_col, 2)]
    texts = [swap(text, "row", n_row, q) for q in range(1, n_row - 1)]
    last = swap(texts[-1], "row", n_row, 1)
    images, texts = lax.optimization_barrier((images, texts))
    odd = [swap(i, "col", n_col, 1) for i in (image, *images)]
    return [image, *images], odd, [text, *texts], last


def nt_dot(a, b):
    return lax.dot_general(a, b, (((1,), (1,)), ((), ())), preferred_element_type=jnp.float32)


def stats_kernel(first, n_text, block, coef_ref, place_ref, *refs):
    texts, refs = refs[:n_text], refs[n_text:]
    coef = coef_ref[0, 0]
    r_place, c_place = place_ref[0, 0], place_ref[0, 1]
    *refs, row_max, col_max, col_sum, col_dot, row_diag = refs
    if first:
        *refs, even, odd, row_ref, col_ref, tile = refs
        halves = (even, odd)
        each = len(refs) // 2
        for i, piece in enumerate(refs):
            at = (i % each) * block
            halves[i // each][at : at + block, :] = piece[...]
        before = None
    else:
        even, odd, *before, row_ref, col_ref, tile = refs
        halves = (even, odd)
    cols, rows = tile.shape
    half = rows // 2
    lead = 0 if first else col_ref.shape[1] - n_text
    col_max[...] = jnp.full(col_max.shape, -jnp.inf, jnp.float32)
    row_diag[...] = jnp.zeros(row_diag.shape, jnp.float32)
    n_col, n_row = row_ref.shape[1], col_ref.shape[1]

    for which, images in enumerate(halves):

        def products(j, carry):
            image = images[pl.ds(pl.multiple_of(j * block, block), block), :]
            at = pl.multiple_of(j * block + which * half, block)
            top = None
            for t in range(n_text):
                part = pl.ds(t * block, block)
                x = nt_dot(texts[t][:block, :], image) * coef
                tile[part, pl.ds(at, block)] = x
                top_t = jnp.max(x, axis=0, keepdims=True)
                top = top_t if top is None else jnp.maximum(top, top_t)
                held = col_max[part, :]
                for lane in range(0, block, LANES):
                    held = jnp.maximum(held, x[:, lane : lane + LANES])
                col_max[part, :] = held
            row_max[0:1, pl.ds(at, block)] = top
            return carry

        lax.fori_loop(0, half // block, products, 0, unroll=4)

    for t in range(n_text):
        among = c_place * n_row + (r_place ^ (lead + t)) - r_place * n_col

        @pl.when((among >= 0) & (among < n_col))
        def _():
            q = c_place ^ among
            at = pl.multiple_of((q // 2) * block + (q % 2) * half, block)
            x = tile[t * block : (t + 1) * block, pl.ds(at, block)]
            down = lax.broadcasted_iota(jnp.int32, x.shape, 0)
            across = lax.broadcasted_iota(jnp.int32, x.shape, 1)
            row_diag[0:1, pl.ds(at, block)] = jnp.sum(
                jnp.where(down == across, x, 0.0), axis=0, keepdims=True
            )

    col_max[...] = jnp.broadcast_to(
        jnp.max(col_max[...], axis=1, keepdims=True), col_max.shape
    )
    sums = []
    for which in range(2):
        lanes = range(which * half, (which + 1) * half, LANES)

        def exponentials(i, acc):
            part = pl.ds(pl.multiple_of(i * 8, 8), 8)
            top = col_max[part, :]
            total = col_sum[part, :] if which else None
            dot = col_dot[part, :] if which else None
            new = [], []
            for n, lane in enumerate(lanes):
                x = tile[part, lane : lane + LANES]
                e = jnp.exp2(x - row_max[0:1, lane : lane + LANES])
                new[0].append(acc[0][n] + e)
                new[1].append(acc[1][n] + e * x)
                e = jnp.exp2(x - top)
                total = e if total is None else total + e
                dot = e * x if dot is None else dot + e * x
            col_sum[part, :] = total
            col_dot[part, :] = dot
            return tuple(new[0]), tuple(new[1])

        zeros = tuple(jnp.zeros((8, LANES), jnp.float32) for _ in lanes)
        sums.append(lax.fori_loop(0, cols // 8, exponentials, (zeros, zeros), unroll=8))

    row_ids = lax.broadcasted_iota(jnp.int32, (n_col, block), 0)
    placed = [jnp.zeros((n_col, block), jnp.float32)] * 4
    for q in range(n_col):
        at = (q // 2) * block
        here = row_ids == (c_place ^ q)
        new = [row_max[0:1, at + (q % 2) * half : at + (q % 2) * half + block]]
        for which in sums[q % 2]:
            new.append(
                jnp.concatenate(
                    [
                        jnp.sum(which[(at + lane) // LANES], axis=0, keepdims=True)
                        for lane in range(0, block, LANES)
                    ],
                    axis=1,
                )
            )
        new.append(row_diag[0:1, at + (q % 2) * half : at + (q % 2) * half + block])
        placed = [jnp.where(here, n, p) for n, p in zip(new, placed)]
    if before:
        placed = merged(placed, [before[0][i] for i in range(4)])
    for i in range(4):
        row_ref[i] = placed[i]
    row_ids = lax.broadcasted_iota(jnp.int32, (n_row, block), 0)
    placed = [before[1][i] if before else jnp.zeros((n_row, block), jnp.float32) for i in range(3)]
    for t in range(n_text):
        part = pl.ds(t * block, block)
        here = row_ids == (r_place ^ (lead + t))
        new = [col_max[part, :].T[0:1, :]]
        for which in (col_sum, col_dot):
            new.append(jnp.sum(which[part, :].T, axis=0, keepdims=True))
        placed = [jnp.where(here, n, p) for n, p in zip(new, placed)]
    for i in range(3):
        col_ref[i] = placed[i]


def stats(coef, place, texts, images, before, n_col, n_row, block, keep):
    width = texts[0].shape[1]
    first = not before
    rows, cols = block * n_col, block * len(texts)
    vmem = pl.BlockSpec(memory_space=VMEM)
    smem = pl.BlockSpec(memory_space=SMEM)
    half = jax.ShapeDtypeStruct((rows // 2, width), jnp.bfloat16)
    out_shape = [half, half] if first else []
    out_shape += [
        jax.ShapeDtypeStruct((4, n_col, block), jnp.float32),
        jax.ShapeDtypeStruct((3, n_row, block), jnp.float32),
    ]
    scratch = [
        VMEM((8, rows), jnp.float32),
        VMEM((cols, LANES), jnp.float32),
        VMEM((cols, LANES), jnp.float32),
        VMEM((cols, LANES), jnp.float32),
        VMEM((8, rows), jnp.float32),
    ]
    if keep:
        out_shape.append(jax.ShapeDtypeStruct((cols, rows), jnp.float32))
    else:
        scratch.insert(0, VMEM((cols, rows), jnp.float32))
    return pl.pallas_call(
        functools.partial(stats_kernel, first, len(texts), block),
        out_shape=tuple(out_shape),
        in_specs=[smem, smem] + [vmem] * (len(texts) + len(images) + len(before)),
        out_specs=(vmem,) * len(out_shape),
        scratch_shapes=scratch,
        compiler_params=pltpu.CompilerParams(
            vmem_limit_bytes=(0 if keep else 4 * rows * cols) + 8 * 2**20
        ),
        cost_estimate=pl.CostEstimate(
            flops=2 * rows * width, bytes_accessed=0, transcendentals=0
        ),
        name="stats" if first else "stats_last",
    )(coef, place, *texts, *images, *before)


def merged(a, b):
    top = jnp.maximum(a[0], b[0])
    wa, wb = jnp.exp2(a[0] - top), jnp.exp2(b[0] - top)
    out = [top] + [a[i] * wa + b[i] * wb for i in (1, 2)]
    return out + [a[i] + b[i] for i in range(3, len(a))]


def by_pairs(blocks, add):
    while len(blocks) > 1:
        blocks = [add(blocks[i], blocks[i + 1]) for i in range(0, len(blocks), 2)]
    return blocks[0]


def lse_and_mean(parts):
    mean = 0.5 * parts[2] / parts[1]
    return parts[0] + jnp.log(parts[1]) * LOG2E, mean - parts[3] if len(parts) > 3 else mean


def exchanged(row_parts, col_parts, n_col, n_row):
    rows, cols = list(row_parts), list(col_parts)
    count = len(cols)
    fill = row_parts.size // col_parts.size + 1
    row_bits = [1 << b for b in range(1, n_col.bit_length() - 1)] + [1]
    col_bits = [1 << b for b in range(n_row.bit_length() - 1)]
    for n, bit in enumerate(row_bits):
        received = swap(jnp.stack(rows), "col", n_col, bit)
        if n < len(col_bits):
            other = swap(jnp.stack(cols * fill), "row", n_row, col_bits[n])
            received, other = lax.optimization_barrier((received, other))
            cols = merged(cols, list(other[:count]))
        rows = merged(rows, list(received))
    return *lse_and_mean(rows), *lse_and_mean(cols)


LEVELS = 32000
LOW = 128
BIAS = 125
EXTRA = 8
MORE = 2 * EXTRA
STEP = 32


def put_extra(out, extra_ref):
    n, width = extra_ref.shape
    rows = min(n, EXTRA)
    out[...] = jnp.zeros(out.shape, out.dtype)
    out[:rows, :width] = sum(extra_ref[i : i + rows, :] for i in range(0, n, rows))


def power(k):
    return jnp.exp2(k).astype(jnp.bfloat16).astype(jnp.float32)


def encode(out, powers, size, slab, extra):
    width = out.shape[1]
    for r in range(0, size, STEP):
        value = slab(r)
        top = jnp.maximum(jnp.max(jnp.abs(value), axis=1, keepdims=True), 1e-30)
        k = jnp.ceil(jnp.log(top) * LOG2E)
        powers[r : r + STEP, :] = jnp.broadcast_to(power(k), (STEP, LANES))
        whole = jnp.floor(jnp.abs(value) * (power(-k) * (LEVELS - 1)) + 0.5) * (1 / LOW)
        high = jnp.floor(whole)
        code = (1.0 + (whole - high)) * jnp.exp2(high - BIAS)
        out[r : r + STEP, :] = jnp.where(value < 0, -code, code).astype(jnp.bfloat16)
    half = width // 2
    first = extra[:, :half].astype(jnp.bfloat16)
    rest = extra[:, :half] - first.astype(jnp.float32)
    second = rest.astype(jnp.bfloat16)
    third = (rest - second.astype(jnp.float32)).astype(jnp.bfloat16)
    fourth = powers[...].T[:EXTRA, :].astype(jnp.bfloat16)
    if size < half:
        fourth = jnp.concatenate([fourth, jnp.zeros((EXTRA, half - size), jnp.bfloat16)], axis=1)
    out[size:, :half] = jnp.concatenate([first, second], axis=0)
    out[size:, half:] = jnp.concatenate([third, fourth], axis=0)


def decode_powers(code, size):
    half = code.shape[1] // 2
    powers = code[size:, half : half + size].astype(jnp.float32)
    return jnp.broadcast_to(powers[EXTRA : EXTRA + 1, :], (LANES, size)).T * (LOW / (LEVELS - 1))


def decode(code, powers, r):
    lanes = []
    for lane in range(0, code.shape[1], LANES):
        c = code[r : r + STEP, lane : lane + LANES].astype(jnp.float32)
        a = jnp.abs(c)
        high = jnp.floor(jnp.log(a) * LOG2E)
        whole = (high + (BIAS - 1)) + a * jnp.exp2(-high)
        lanes.append(jnp.where(c < 0, -whole, whole) * powers[r : r + STEP, :])
    return jnp.concatenate(lanes, axis=1)


def decode_extra(code, size):
    half = code.shape[1] // 2
    left = code[size:, :half].astype(jnp.float32)
    right = code[size:, half:].astype(jnp.float32)
    return left[:EXTRA] + left[EXTRA:] + right[:EXTRA]


def pack_text_kernel(n, base, *refs):
    codes, out, powers, received = refs[:n], *refs[n:]
    size, half = base.shape[0] - EXTRA, base.shape[1] // 2
    more = base[size:, :half]
    for c, code in enumerate(codes):
        received[c] = decode_powers(code, size)
        more = more + decode_extra(code, size)

    def slab(r):
        value = base[r : r + STEP, :]
        for c, code in enumerate(codes):
            value = value + decode(code, received.at[c], r)
        return value

    encode(out, powers, size, slab, more)


def pack_text(base, codes):
    size, width = base.shape[0] - EXTRA, base.shape[1]
    vmem = pl.BlockSpec(memory_space=VMEM)
    return pl.pallas_call(
        functools.partial(pack_text_kernel, len(codes)),
        out_shape=jax.ShapeDtypeStruct((size + MORE, width), jnp.bfloat16),
        in_specs=[vmem] * (1 + len(codes)),
        out_specs=vmem,
        scratch_shapes=[VMEM((size, LANES), jnp.float32), VMEM((len(codes), size, LANES), jnp.float32)],
        compiler_params=pltpu.CompilerParams(vmem_limit_bytes=6 * 2**20),
        cost_estimate=pl.CostEstimate(
            flops=FLOPS * 32 * size * size * width, bytes_accessed=0, transcendentals=0
        ),
        name="pack_text",
    )(base, *codes)


def pack_images_kernel(n, near, far, *refs):
    own, *outs, powers = refs[-n - 1 :]
    size = near.shape[1] - EXTRA
    own[...] = near[0] + far[0]
    for j, out in enumerate(outs, 1):
        encode(
            out,
            powers.at[j - 1],
            size,
            lambda r, j=j: near[j, r : r + STEP, :] + far[j, r : r + STEP, :],
            near[j, size:, :] + far[j, size:, :],
        )


def pack_images(near, far, after):
    n, rows, width = near.shape
    size = rows - EXTRA
    vmem = pl.BlockSpec(memory_space=VMEM)
    code = jax.ShapeDtypeStruct((size + MORE, width), jnp.bfloat16)
    own, *codes = pl.pallas_call(
        functools.partial(pack_images_kernel, n),
        out_shape=(jax.ShapeDtypeStruct((rows, width), jnp.float32),) + (code,) * (n - 1),
        in_specs=[vmem] * 2 + [pl.BlockSpec(memory_space=pl.ANY)] * len(after),
        out_specs=(vmem,) * n,
        scratch_shapes=[VMEM((n - 1, size, LANES), jnp.float32)],
        compiler_params=pltpu.CompilerParams(vmem_limit_bytes=(4 + 2 * n) * 2**20),
        cost_estimate=pl.CostEstimate(
            flops=FLOPS * 8 * n * size * size * width, bytes_accessed=0, transcendentals=0
        ),
        name="pack_images",
    )(near, far, *after)
    return own, codes


def total_kernel(n, in_order, coef_ref, base, *refs):
    codes, before = refs[:n], refs[n:-6]
    out, extra, scalar, value, powers, sems = refs[-6:]
    size, width = base.shape[0] - EXTRA, base.shape[1]
    combine = functools.partial(functools.reduce, jnp.add) if in_order else first_and_pairs
    for c, code in enumerate(codes):
        powers[c] = decode_powers(code, size)
    copies = []
    steps = sems.shape[0]
    for i in range(steps):
        part = pl.ds(i * (size // steps), size // steps)
        for r in range(i * (size // steps), (i + 1) * (size // steps), STEP):
            value[r : r + STEP, :] = combine(
                [base[r : r + STEP, :]] + [decode(code, powers.at[c], r) for c, code in enumerate(codes)]
            )
        copies.append(pltpu.make_async_copy(value.at[part], out.at[part], sems.at[i]))
        copies[-1].start()
    more = combine([base[size:, : width // 2]] + [decode_extra(code, size) for code in codes])
    more = sum([b[...] for b in before], more)
    extra[...] = more
    scalar[0, 0] = jnp.sum(more) / coef_ref[0, 0]
    for copy in copies:
        copy.wait()


def add_kernel(base, code, out, powers):
    size, half = base.shape[0] - EXTRA, base.shape[1] // 2
    powers[...] = decode_powers(code, size)
    for r in range(0, size, STEP):
        out[r : r + STEP, :] = base[r : r + STEP, :] + decode(code, powers, r)
    out[size:, :half] = base[size:, :half] + decode_extra(code, size)
    out[size:, half:] = jnp.zeros((EXTRA, half), jnp.float32)


def added(base, code):
    vmem = pl.BlockSpec(memory_space=VMEM)
    return pl.pallas_call(
        add_kernel,
        out_shape=jax.ShapeDtypeStruct(base.shape, jnp.float32),
        in_specs=[vmem] * 2,
        out_specs=vmem,
        scratch_shapes=[VMEM((base.shape[0] - EXTRA, LANES), jnp.float32)],
        compiler_params=pltpu.CompilerParams(vmem_limit_bytes=6 * 2**20),
        name="added",
    )(base, code)


def first_and_pairs(blocks):
    if len(blocks) == 1:
        return blocks[0]
    pairs = [blocks[0]] + [blocks[i] + blocks[i + 1] for i in range(1, len(blocks), 2)]
    return by_pairs(pairs, jnp.add)


def total_of(coef, base, codes, in_order, before, name):
    size, width = base.shape[0] - EXTRA, base.shape[1]
    vmem = pl.BlockSpec(memory_space=VMEM)
    smem = pl.BlockSpec(memory_space=SMEM)
    return pl.pallas_call(
        functools.partial(total_kernel, len(codes), in_order),
        out_shape=(
            jax.ShapeDtypeStruct((size, width), jnp.float32),
            jax.ShapeDtypeStruct((EXTRA, width // 2), jnp.float32),
            jax.ShapeDtypeStruct((1, 1), jnp.float32),
        ),
        in_specs=[smem] + [vmem] * (1 + len(codes) + len(before)),
        out_specs=(pl.BlockSpec(memory_space=pl.ANY), vmem, smem),
        scratch_shapes=[
            VMEM((size, width), jnp.float32),
            VMEM((len(codes), size, LANES), jnp.float32),
            pltpu.SemaphoreType.DMA((4,)),
        ],
        compiler_params=pltpu.CompilerParams(vmem_limit_bytes=8 * 2**20),
        name=name,
    )(coef, base, *codes, *before)


def text_block(block, text, tile, t, halves, row_lse, col_lse, place_ref, coef_ref, grad_ref):
    coef = coef_ref[0, 0]
    r_place, c_place = place_ref[0, 0], place_ref[0, 1]
    half, width = halves[0].shape
    n_col, n_row = row_lse.shape[0], col_lse.shape[0]
    size = block
    col_lse_down = jnp.broadcast_to(col_lse[pl.ds(r_place ^ t, 1), :], (LANES, size)).T
    text_id = c_place * n_row + (r_place ^ t)
    step = 32
    lane_ids = lax.broadcasted_iota(jnp.int32, (step, LANES), 1)
    row_ids = lax.broadcasted_iota(jnp.int32, (step, LANES), 0)

    for which, images in enumerate(halves):

        def one(j, carry):
            at = pl.multiple_of(j * block + which * half, block)
            if tile is None:
                image = images[pl.ds(pl.multiple_of(j * block, block), block), :]
                xs = nt_dot(text[:block, :], image) * coef
            column = c_place ^ (2 * j + which)
            same = jnp.where(r_place * n_col + column == text_id, 1.0, 0.0)
            lse = row_lse[pl.ds(column, 1), :]
            for r in range(0, size, step):
                for lane in range(0, block, LANES):
                    if tile is None:
                        x = xs[r : r + step, lane : lane + LANES]
                    else:
                        x = tile[r : r + step, pl.ds(at + lane, LANES)]
                    e = jnp.exp2(x - lse[:, lane : lane + LANES]) + jnp.exp2(
                        x - col_lse_down[r : r + step, :]
                    )
                    g = 0.5 * e
                    if lane <= r < lane + LANES:
                        g = g - jnp.where(row_ids + (r - lane) == lane_ids, same, 0.0)
                    grad_ref[r : r + step, pl.ds(at + lane, LANES)] = g.astype(jnp.bfloat16)
            return carry

        lax.fori_loop(0, half // block, one, 0, unroll=4)


def over_texts(grad, text):
    return lax.dot_general(grad, text, (((0,), (0,)), ((), ())), preferred_element_type=jnp.float32)


def text_kernel(order, n_done, kept, block, scale_ref, coef_ref, place_ref, *refs):
    even, odd, row_lse, col_lse, row_extra, col_extra = refs[:6]
    n = len(order)
    texts, rest = refs[6 : 6 + n], refs[6 + n :]
    if kept:
        tile, rest = rest[0], rest[1:]
    done_grads, done_texts, rest = rest[:n_done], rest[n_done : 2 * n_done], rest[2 * n_done :]
    grads, outs, rest = rest[0], rest[1 : 1 + n], rest[1 + n :]
    total, powers = rest[-2:]
    lowest = min(order)
    for i, t in enumerate(order):
        text_block(
            block,
            texts[i],
            tile.at[pl.ds((t - lowest) * block, block)] if kept else None,
            t,
            (even, odd),
            row_lse,
            col_lse,
            place_ref,
            coef_ref,
            grads.at[pl.ds((t - lowest) * block, block)],
        )
    half = even.shape[0]
    scale = scale_ref[0, 0]
    total[...] = scale * (
        jnp.dot(grads[:, :half], even[...], preferred_element_type=jnp.float32)
        + jnp.dot(grads[:, half:], odd[...], preferred_element_type=jnp.float32)
    )
    for i, t in enumerate(order):
        at = (t - lowest) * block
        if t & 1:
            extra_rows = rest[-3]
            put_extra(extra_rows, row_extra)
            encode(outs[i], powers, block, lambda r, at=at: total[at + r : at + r + STEP, :], extra_rows[...])
        else:
            outs[i][:block, :] = total[at : at + block, :]
            put_extra(outs[i].at[block:, :], row_extra)
    if n_done:
        far_ref, near_ref = rest[:2]
        stacked = rest[-4]
        for i, t in enumerate(order):
            stacked[(t - lowest) * block : (t - lowest + 1) * block, :] = texts[i][:block, :]

        for images_ref, first in ((far_ref, half), (near_ref, 0)):

            def one(j, carry):
                part = pl.ds(pl.multiple_of(j * block + first, block), block)
                total = over_texts(grads[:, part], stacked[...])
                for grad, text in zip(done_grads, done_texts):
                    total = total + over_texts(grad[:, part], text[:block, :])
                images_ref[j, :block, :] = scale * total
                put_extra(images_ref.at[j, block:, :], col_extra)
                return carry

            lax.fori_loop(0, half // block, one, 0, unroll=4)


def text_grads(scale, coef, place, even, odd, row_lse, col_lse, row_extra, col_extra, texts, tile, order, done):
    half, width = even.shape
    block = row_lse.shape[1]
    n = len(order)
    vmem = pl.BlockSpec(memory_space=VMEM)
    smem = pl.BlockSpec(memory_space=SMEM)
    out_shape = (
        [jax.ShapeDtypeStruct((n * block, 2 * half), jnp.bfloat16)]
        + [
            jax.ShapeDtypeStruct((block + MORE, width), jnp.bfloat16)
            if t & 1
            else jax.ShapeDtypeStruct((block + EXTRA, width), jnp.float32)
            for t in order
        ]
    )
    if done:
        out_shape += [jax.ShapeDtypeStruct((half // block, block + EXTRA, width), jnp.float32)] * 2
    operands = [even, odd, row_lse, col_lse, row_extra, col_extra, *[texts[t] for t in order]]
    operands += tile
    operands += [grad for _, grad in done] + [texts[t] for t, _ in done]
    outs = pl.pallas_call(
        functools.partial(text_kernel, tuple(order), len(done), len(tile), block),
        out_shape=tuple(out_shape),
        in_specs=[smem] * 3 + [vmem] * len(operands),
        out_specs=(vmem,) * len(out_shape),
        scratch_shapes=[
            VMEM((n * block, width), jnp.bfloat16),
            VMEM((EXTRA, width), jnp.float32),
            VMEM((n * block, width), jnp.float32),
            VMEM((block, LANES), jnp.float32),
        ],
        compiler_params=pltpu.CompilerParams(vmem_limit_bytes=(10 + 2 * n) * 2**20),
        cost_estimate=pl.CostEstimate(
            flops=FLOPS * 4 * n * block * 2 * half * width, bytes_accessed=0, transcendentals=0
        ),
        name=f"text_grads_{n}",
    )(scale, coef, place, *operands)
    parts = {t: outs[1 + i] for i, t in enumerate(order)}
    return outs[0], parts, outs[1 + n :]


def on_device(n_row, n_col, image_embeds, text_embeds, logit_scale):
    block = image_embeds.shape[0]
    r, c = lax.axis_index("row"), lax.axis_index("col")
    place = jnp.stack([r, c]).reshape(1, 2)
    scale = logit_scale.reshape(1, 1)
    coef = scale * LOG2E
    image_half = image_embeds.astype(jnp.bfloat16)
    text_half = jnp.pad(text_embeds.astype(jnp.bfloat16), ((0, 16), (0, 0)))
    even, odd, texts, text_last = gather_both(image_half, text_half, n_col, n_row)
    keep = 4 * n_row * n_col * block * block <= 16 * 2**20
    even, odd, *before = stats(
        coef, place, texts, (*even, *odd), (), n_col, n_row, block, keep
    )
    row_parts, col_parts, *tile_last = stats(
        coef, place, [text_last], (even, odd), before[:2], n_col, n_row, block, keep
    )
    texts = [*texts, text_last]
    tile = before[2:]
    row_lse, row_extra, col_lse, col_extra = exchanged(row_parts, col_parts, n_col, n_row)

    held = (scale, coef, place, even, odd, row_lse, col_lse, row_extra, col_extra, texts)
    last = n_row - 1
    last_grad, parts, _ = text_grads(*held, tile_last, [last], [])
    received = swap(parts[last], "row", n_row, 1)
    _, more_parts, (far, near) = text_grads(*held, tile, list(range(last))[::-1], [(last, last_grad)])
    parts |= more_parts
    codes = {q: [] for q in range(0, n_row, 2)}
    codes[last ^ 1].append(received)
    after = [pack_text(parts[last ^ 1], codes[last ^ 1])] if n_row > 2 else [received]
    far = swap(far, "col", n_col, 1)
    odd_parts, far = lax.optimization_barrier(([parts[q] for q in range(1, last, 2)], far))
    for q, part in zip(range(1, last, 2), odd_parts):
        codes[q ^ 1].append(swap(part, "row", n_row, 1))
    for b in range(1, n_row.bit_length() - 1):
        for q in [q for q in codes if q & (1 << b)]:
            code = after[0] if (b, q) == (1, last ^ 1) else pack_text(parts[q], codes[q])
            codes[q ^ (1 << b)].append(swap(code, "row", n_row, 1 << b))
            del codes[q]
    grad_text, text_extra, _ = total_of(coef, parts[0], codes[0], True, [], "grad_text")

    own, others = pack_images(near, far, after)
    others = [swap(code, "col", n_col, 2 * j) for j, code in enumerate(others, 1)]
    first, text_extra = lax.optimization_barrier((others[0], text_extra))
    grad_image, _, grad_scale = total_of(
        coef, added(own, first), others[1:], False, [text_extra], "grad_image"
    )
    return grad_image, grad_text, grad_scale.reshape(())


def solution(mesh):
    images = P(("row", "col"), None)
    texts = P(("col", "row"), None)
    return jax.shard_map(
        functools.partial(on_device, mesh.shape["row"], mesh.shape["col"]),
        mesh=mesh,
        in_specs=(images, texts, P()),
        out_specs=(images, texts, P()),
        check_vma=False,
    )
```

```python
import functools
import math

import jax
import jax.numpy as jnp
from jax import lax
from jax.experimental import pallas as pl
from jax.experimental.pallas import tpu as pltpu
from jax.sharding import PartitionSpec as P

LOG2E = 1.4426950408889634
LN2 = 0.6931471805599453
LANES = 128
VMEM = pltpu.VMEM
SMEM = pltpu.SMEM
FLOPS = 20


def swap(x, axis, n, q):
    return lax.ppermute(x, axis, [(i, i ^ q) for i in range(n)])


def gather_both(image, text, n_col, n_row):
    images = [swap(image, "col", n_col, q) for q in range(2, n_col, 2)]
    texts = [swap(text, "row", n_row, q) for q in range(1, n_row - 1)]
    last = swap(texts[-1], "row", n_row, 1)
    images, texts = lax.optimization_barrier((images, texts))
    odd = [swap(i, "col", n_col, 1) for i in (image, *images)]
    return [image, *images], odd, [text, *texts], last


def cast_kernel(image_ref, text_ref, image_out, text_out, image, text, sems):
    copies = [
        pltpu.make_async_copy(text_ref, text, sems.at[0]),
        pltpu.make_async_copy(image_ref, image, sems.at[1]),
    ]
    for copy in copies:
        copy.start()
    block, width = text.shape
    text_out[block:, :] = jnp.zeros((text_out.shape[0] - block, width), jnp.bfloat16)
    copies[0].wait()
    text_out[:block, :] = text[...].astype(jnp.bfloat16)
    copies[1].wait()
    image_out[...] = image[...].astype(jnp.bfloat16)


def cast(image, text, more):
    block, width = text.shape
    vmem = pl.BlockSpec(memory_space=VMEM)
    return pl.pallas_call(
        cast_kernel,
        out_shape=(
            jax.ShapeDtypeStruct(image.shape, jnp.bfloat16),
            jax.ShapeDtypeStruct((block + more, width), jnp.bfloat16),
        ),
        in_specs=[pl.BlockSpec(memory_space=pl.ANY)] * 2,
        out_specs=(vmem, vmem),
        scratch_shapes=[
            VMEM(image.shape, jnp.float32),
            VMEM(text.shape, jnp.float32),
            pltpu.SemaphoreType.DMA((2,)),
        ],
        compiler_params=pltpu.CompilerParams(vmem_limit_bytes=4 * 2**20),
        name="cast",
    )(image, text)


def nt_dot(a, b):
    return lax.dot_general(a, b, (((1,), (1,)), ((), ())), preferred_element_type=jnp.float32)


def stats_kernel(first, n_text, block, coef_ref, place_ref, *refs):
    texts, refs = refs[:n_text], refs[n_text:]
    coef = coef_ref[0, 0]
    r_place, c_place = place_ref[0, 0], place_ref[0, 1]
    *refs, row_max, col_max, col_sum, col_dot, row_diag = refs
    if first:
        *refs, even, odd, row_ref, col_ref, tile = refs
        halves = (even, odd)
        each = len(refs) // 2
        for i, piece in enumerate(refs):
            at = (i % each) * block
            halves[i // each][at : at + block, :] = piece[...]
        before = None
    else:
        even, odd, *before, row_ref, col_ref, tile = refs
        halves = (even, odd)
    cols, rows = tile.shape
    half = rows // 2
    lead = 0 if first else col_ref.shape[1] - n_text
    col_max[...] = jnp.full(col_max.shape, -jnp.inf, jnp.float32)
    row_diag[...] = jnp.zeros(row_diag.shape, jnp.float32)
    n_col, n_row = row_ref.shape[1], col_ref.shape[1]

    for which, images in enumerate(halves):

        def products(j, carry):
            image = images[pl.ds(pl.multiple_of(j * block, block), block), :]
            at = pl.multiple_of(j * block + which * half, block)
            top = None
            for t in range(n_text):
                part = pl.ds(t * block, block)
                x = nt_dot(texts[t][:block, :], image) * coef
                tile[part, pl.ds(at, block)] = x
                top_t = jnp.max(x, axis=0, keepdims=True)
                top = top_t if top is None else jnp.maximum(top, top_t)
                held = col_max[part, :]
                for lane in range(0, block, LANES):
                    held = jnp.maximum(held, x[:, lane : lane + LANES])
                col_max[part, :] = held
            row_max[0:1, pl.ds(at, block)] = top
            return carry

        lax.fori_loop(0, half // block, products, 0, unroll=4)

    for t in range(n_text):
        among = c_place * n_row + (r_place ^ (lead + t)) - r_place * n_col

        @pl.when((among >= 0) & (among < n_col))
        def _():
            q = c_place ^ among
            at = pl.multiple_of((q // 2) * block + (q % 2) * half, block)
            x = tile[t * block : (t + 1) * block, pl.ds(at, block)]
            down = lax.broadcasted_iota(jnp.int32, x.shape, 0)
            across = lax.broadcasted_iota(jnp.int32, x.shape, 1)
            row_diag[0:1, pl.ds(at, block)] = jnp.sum(
                jnp.where(down == across, x, 0.0), axis=0, keepdims=True
            )

    col_max[...] = jnp.broadcast_to(
        jnp.max(col_max[...], axis=1, keepdims=True), col_max.shape
    )
    sums = []
    for which in range(2):
        lanes = range(which * half, (which + 1) * half, LANES)

        def exponentials(i, acc):
            part = pl.ds(pl.multiple_of(i * 8, 8), 8)
            top = col_max[part, :]
            total = col_sum[part, :] if which else None
            dot = col_dot[part, :] if which else None
            new = [], []
            for n, lane in enumerate(lanes):
                x = tile[part, lane : lane + LANES]
                e = jnp.exp2(x - row_max[0:1, lane : lane + LANES])
                new[0].append(acc[0][n] + e)
                new[1].append(acc[1][n] + e * x)
                e = jnp.exp2(x - top)
                total = e if total is None else total + e
                dot = e * x if dot is None else dot + e * x
            col_sum[part, :] = total
            col_dot[part, :] = dot
            return tuple(new[0]), tuple(new[1])

        zeros = tuple(jnp.zeros((8, LANES), jnp.float32) for _ in lanes)
        sums.append(lax.fori_loop(0, cols // 8, exponentials, (zeros, zeros), unroll=8))

    row_ids = lax.broadcasted_iota(jnp.int32, (n_col, block), 0)
    placed = [jnp.zeros((n_col, block), jnp.float32)] * 4
    for q in range(n_col):
        at = (q // 2) * block
        here = row_ids == (c_place ^ q)
        new = [row_max[0:1, at + (q % 2) * half : at + (q % 2) * half + block]]
        for which in sums[q % 2]:
            new.append(
                jnp.concatenate(
                    [
                        jnp.sum(which[(at + lane) // LANES], axis=0, keepdims=True)
                        for lane in range(0, block, LANES)
                    ],
                    axis=1,
                )
            )
        new.append(row_diag[0:1, at + (q % 2) * half : at + (q % 2) * half + block])
        placed = [jnp.where(here, n, p) for n, p in zip(new, placed)]
    if before:
        placed = merged(placed, [before[0][i] for i in range(4)])
    for i in range(4):
        row_ref[i] = placed[i]
    row_ids = lax.broadcasted_iota(jnp.int32, (n_row, block), 0)
    placed = [before[1][i] if before else jnp.zeros((n_row, block), jnp.float32) for i in range(3)]
    for t in range(n_text):
        part = pl.ds(t * block, block)
        here = row_ids == (r_place ^ (lead + t))
        new = [col_max[part, :].T[0:1, :]]
        for which in (col_sum, col_dot):
            new.append(jnp.sum(which[part, :].T, axis=0, keepdims=True))
        placed = [jnp.where(here, n, p) for n, p in zip(new, placed)]
    for i in range(3):
        col_ref[i] = placed[i]


def stats(coef, place, texts, images, before, n_col, n_row, block, keep):
    width = texts[0].shape[1]
    first = not before
    rows, cols = block * n_col, block * len(texts)
    vmem = pl.BlockSpec(memory_space=VMEM)
    smem = pl.BlockSpec(memory_space=SMEM)
    half = jax.ShapeDtypeStruct((rows // 2, width), jnp.bfloat16)
    out_shape = [half, half] if first else []
    out_shape += [
        jax.ShapeDtypeStruct((4, n_col, block), jnp.float32),
        jax.ShapeDtypeStruct((3, n_row, block), jnp.float32),
    ]
    scratch = [
        VMEM((8, rows), jnp.float32),
        VMEM((cols, LANES), jnp.float32),
        VMEM((cols, LANES), jnp.float32),
        VMEM((cols, LANES), jnp.float32),
        VMEM((8, rows), jnp.float32),
    ]
    if keep:
        out_shape.append(jax.ShapeDtypeStruct((cols, rows), jnp.float32))
    else:
        scratch.insert(0, VMEM((cols, rows), jnp.float32))
    return pl.pallas_call(
        functools.partial(stats_kernel, first, len(texts), block),
        out_shape=tuple(out_shape),
        in_specs=[smem, smem] + [vmem] * (len(texts) + len(images) + len(before)),
        out_specs=(vmem,) * len(out_shape),
        scratch_shapes=scratch,
        compiler_params=pltpu.CompilerParams(
            vmem_limit_bytes=(0 if keep else 4 * rows * cols) + 8 * 2**20
        ),
        cost_estimate=pl.CostEstimate(
            flops=2 * rows * width, bytes_accessed=0, transcendentals=0
        ),
        name="stats" if first else "stats_last",
    )(coef, place, *texts, *images, *before)


def merged(a, b):
    top = jnp.maximum(a[0], b[0])
    wa, wb = jnp.exp2(a[0] - top), jnp.exp2(b[0] - top)
    out = [top] + [a[i] * wa + b[i] * wb for i in (1, 2)]
    return out + [a[i] + b[i] for i in range(3, len(a))]


def by_pairs(blocks, add):
    while len(blocks) > 1:
        blocks = [add(blocks[i], blocks[i + 1]) for i in range(0, len(blocks), 2)]
    return blocks[0]


def lse_and_mean(parts):
    mean = 0.5 * parts[2] / parts[1]
    return parts[0] + jnp.log(parts[1]) * LOG2E, mean - parts[3] if len(parts) > 3 else mean


def exchanged(row_parts, col_parts, n_col, n_row):
    rows, cols = list(row_parts), list(col_parts)
    count = len(cols)
    fill = row_parts.size // col_parts.size + 1
    row_bits = [1 << b for b in range(1, n_col.bit_length() - 1)] + [1]
    col_bits = [1 << b for b in range(n_row.bit_length() - 1)]
    for n, bit in enumerate(row_bits):
        received = swap(jnp.stack(rows), "col", n_col, bit)
        if n < len(col_bits):
            other = swap(jnp.stack(cols * fill), "row", n_row, col_bits[n])
            received, other = lax.optimization_barrier((received, other))
            cols = merged(cols, list(other[:count]))
        rows = merged(rows, list(received))
    return *lse_and_mean(rows), *lse_and_mean(cols)


LEVELS = 32000
LOW = 128
BIAS = 125
EXTRA = 8
MORE = 2 * EXTRA
STEP = 32


def put_extra(out, extra_ref):
    n, width = extra_ref.shape
    rows = min(n, EXTRA)
    out[...] = jnp.zeros(out.shape, out.dtype)
    out[:rows, :width] = sum(extra_ref[i : i + rows, :] for i in range(0, n, rows))


def power(k):
    return jnp.exp2(k).astype(jnp.bfloat16).astype(jnp.float32)


def encode(out, powers, size, slab, extra):
    width = out.shape[1]
    for r in range(0, size, STEP):
        value = slab(r)
        top = jnp.maximum(jnp.max(jnp.abs(value), axis=1, keepdims=True), 1e-30)
        k = jnp.ceil(jnp.log(top) * LOG2E)
        powers[r : r + STEP, :] = jnp.broadcast_to(power(k), (STEP, LANES))
        whole = jnp.floor(jnp.abs(value) * (power(-k) * (LEVELS - 1)) + 0.5) * (1 / LOW)
        high = jnp.floor(whole)
        code = (1.0 + (whole - high)) * jnp.exp2(high - BIAS)
        out[r : r + STEP, :] = jnp.where(value < 0, -code, code).astype(jnp.bfloat16)
    half = width // 2
    first = extra[:, :half].astype(jnp.bfloat16)
    rest = extra[:, :half] - first.astype(jnp.float32)
    second = rest.astype(jnp.bfloat16)
    third = (rest - second.astype(jnp.float32)).astype(jnp.bfloat16)
    fourth = powers[...].T[:EXTRA, :].astype(jnp.bfloat16)
    if size < half:
        fourth = jnp.concatenate([fourth, jnp.zeros((EXTRA, half - size), jnp.bfloat16)], axis=1)
    out[size:, :half] = jnp.concatenate([first, second], axis=0)
    out[size:, half:] = jnp.concatenate([third, fourth], axis=0)


def decode_powers(code, size):
    half = code.shape[1] // 2
    powers = code[size:, half : half + size].astype(jnp.float32)
    return jnp.broadcast_to(powers[EXTRA : EXTRA + 1, :], (LANES, size)).T * (LOW / (LEVELS - 1))


def decode(code, powers, r):
    lanes = []
    for lane in range(0, code.shape[1], LANES):
        c = code[r : r + STEP, lane : lane + LANES].astype(jnp.float32)
        a = jnp.abs(c)
        high = jnp.floor(jnp.log(a) * LOG2E)
        whole = (high + (BIAS - 1)) + a * jnp.exp2(-high)
        lanes.append(jnp.where(c < 0, -whole, whole) * powers[r : r + STEP, :])
    return jnp.concatenate(lanes, axis=1)


def decode_extra(code, size):
    half = code.shape[1] // 2
    left = code[size:, :half].astype(jnp.float32)
    right = code[size:, half:].astype(jnp.float32)
    return left[:EXTRA] + left[EXTRA:] + right[:EXTRA]


def pack_text_kernel(n, base, *refs):
    codes, out, powers, received = refs[:n], *refs[n:]
    size, half = base.shape[0] - EXTRA, base.shape[1] // 2
    more = base[size:, :half]
    for c, code in enumerate(codes):
        received[c] = decode_powers(code, size)
        more = more + decode_extra(code, size)

    def slab(r):
        value = base[r : r + STEP, :]
        for c, code in enumerate(codes):
            value = value + decode(code, received.at[c], r)
        return value

    encode(out, powers, size, slab, more)


def pack_text(base, codes):
    size, width = base.shape[0] - EXTRA, base.shape[1]
    vmem = pl.BlockSpec(memory_space=VMEM)
    return pl.pallas_call(
        functools.partial(pack_text_kernel, len(codes)),
        out_shape=jax.ShapeDtypeStruct((size + MORE, width), jnp.bfloat16),
        in_specs=[vmem] * (1 + len(codes)),
        out_specs=vmem,
        scratch_shapes=[VMEM((size, LANES), jnp.float32), VMEM((len(codes), size, LANES), jnp.float32)],
        compiler_params=pltpu.CompilerParams(vmem_limit_bytes=6 * 2**20),
        cost_estimate=pl.CostEstimate(
            flops=FLOPS * 32 * size * size * width, bytes_accessed=0, transcendentals=0
        ),
        name="pack_text",
    )(base, *codes)


def pack_images_kernel(n, near, far, *refs):
    own, *outs, powers = refs[-n - 1 :]
    size = near.shape[1] - EXTRA
    own[...] = near[0] + far[0]
    for j, out in enumerate(outs, 1):
        encode(
            out,
            powers.at[j - 1],
            size,
            lambda r, j=j: near[j, r : r + STEP, :] + far[j, r : r + STEP, :],
            near[j, size:, :] + far[j, size:, :],
        )


def pack_images(near, far, after):
    n, rows, width = near.shape
    size = rows - EXTRA
    vmem = pl.BlockSpec(memory_space=VMEM)
    code = jax.ShapeDtypeStruct((size + MORE, width), jnp.bfloat16)
    own, *codes = pl.pallas_call(
        functools.partial(pack_images_kernel, n),
        out_shape=(jax.ShapeDtypeStruct((rows, width), jnp.float32),) + (code,) * (n - 1),
        in_specs=[vmem] * 2 + [pl.BlockSpec(memory_space=pl.ANY)] * len(after),
        out_specs=(vmem,) * n,
        scratch_shapes=[VMEM((n - 1, size, LANES), jnp.float32)],
        compiler_params=pltpu.CompilerParams(vmem_limit_bytes=(4 + 2 * n) * 2**20),
        cost_estimate=pl.CostEstimate(
            flops=FLOPS * 8 * n * size * size * width, bytes_accessed=0, transcendentals=0
        ),
        name="pack_images",
    )(near, far, *after)
    return own, codes


def total_kernel(n, in_order, coef_ref, base, *refs):
    codes, before = refs[:n], refs[n:-6]
    out, extra, scalar, value, powers, sems = refs[-6:]
    size, width = base.shape[0] - EXTRA, base.shape[1]
    combine = functools.partial(functools.reduce, jnp.add) if in_order else first_and_pairs
    for c, code in enumerate(codes):
        powers[c] = decode_powers(code, size)
    copies = []
    steps = sems.shape[0]
    for i in range(steps):
        part = pl.ds(i * (size // steps), size // steps)
        for r in range(i * (size // steps), (i + 1) * (size // steps), STEP):
            value[r : r + STEP, :] = combine(
                [base[r : r + STEP, :]] + [decode(code, powers.at[c], r) for c, code in enumerate(codes)]
            )
        copies.append(pltpu.make_async_copy(value.at[part], out.at[part], sems.at[i]))
        copies[-1].start()
    more = combine([base[size:, : width // 2]] + [decode_extra(code, size) for code in codes])
    more = sum([b[...] for b in before], more)
    extra[...] = more
    scalar[0, 0] = jnp.sum(more) / coef_ref[0, 0]
    for copy in copies:
        copy.wait()


def add_kernel(base, code, out, powers):
    size, half = base.shape[0] - EXTRA, base.shape[1] // 2
    powers[...] = decode_powers(code, size)
    for r in range(0, size, STEP):
        out[r : r + STEP, :] = base[r : r + STEP, :] + decode(code, powers, r)
    out[size:, :half] = base[size:, :half] + decode_extra(code, size)
    out[size:, half:] = jnp.zeros((EXTRA, half), jnp.float32)


def added(base, code):
    vmem = pl.BlockSpec(memory_space=VMEM)
    return pl.pallas_call(
        add_kernel,
        out_shape=jax.ShapeDtypeStruct(base.shape, jnp.float32),
        in_specs=[vmem] * 2,
        out_specs=vmem,
        scratch_shapes=[VMEM((base.shape[0] - EXTRA, LANES), jnp.float32)],
        compiler_params=pltpu.CompilerParams(vmem_limit_bytes=6 * 2**20),
        name="added",
    )(base, code)


def first_and_pairs(blocks):
    if len(blocks) == 1:
        return blocks[0]
    pairs = [blocks[0]] + [blocks[i] + blocks[i + 1] for i in range(1, len(blocks), 2)]
    return by_pairs(pairs, jnp.add)


def total_of(coef, base, codes, in_order, before, name):
    size, width = base.shape[0] - EXTRA, base.shape[1]
    vmem = pl.BlockSpec(memory_space=VMEM)
    smem = pl.BlockSpec(memory_space=SMEM)
    return pl.pallas_call(
        functools.partial(total_kernel, len(codes), in_order),
        out_shape=(
            jax.ShapeDtypeStruct((size, width), jnp.float32),
            jax.ShapeDtypeStruct((EXTRA, width // 2), jnp.float32),
            jax.ShapeDtypeStruct((1, 1), jnp.float32),
        ),
        in_specs=[smem] + [vmem] * (1 + len(codes) + len(before)),
        out_specs=(pl.BlockSpec(memory_space=pl.ANY), vmem, smem),
        scratch_shapes=[
            VMEM((size, width), jnp.float32),
            VMEM((len(codes), size, LANES), jnp.float32),
            pltpu.SemaphoreType.DMA((4,)),
        ],
        compiler_params=pltpu.CompilerParams(vmem_limit_bytes=8 * 2**20),
        name=name,
    )(coef, base, *codes, *before)


def text_block(block, text, tile, t, halves, row_lse, col_lse, place_ref, coef_ref, grad_ref):
    coef = coef_ref[0, 0]
    r_place, c_place = place_ref[0, 0], place_ref[0, 1]
    half, width = halves[0].shape
    n_col, n_row = row_lse.shape[0], col_lse.shape[0]
    size = block
    col_lse_down = jnp.broadcast_to(col_lse[pl.ds(r_place ^ t, 1), :], (LANES, size)).T
    text_id = c_place * n_row + (r_place ^ t)
    step = 32
    lane_ids = lax.broadcasted_iota(jnp.int32, (step, LANES), 1)
    row_ids = lax.broadcasted_iota(jnp.int32, (step, LANES), 0)

    for which, images in enumerate(halves):

        def one(j, carry):
            at = pl.multiple_of(j * block + which * half, block)
            if tile is None:
                image = images[pl.ds(pl.multiple_of(j * block, block), block), :]
                xs = nt_dot(text[:block, :], image) * coef
            column = c_place ^ (2 * j + which)
            same = jnp.where(r_place * n_col + column == text_id, 1.0, 0.0)
            lse = row_lse[pl.ds(column, 1), :]
            for r in range(0, size, step):
                for lane in range(0, block, LANES):
                    if tile is None:
                        x = xs[r : r + step, lane : lane + LANES]
                    else:
                        x = tile[r : r + step, pl.ds(at + lane, LANES)]
                    e = jnp.exp2(x - lse[:, lane : lane + LANES]) + jnp.exp2(
                        x - col_lse_down[r : r + step, :]
                    )
                    g = 0.5 * e
                    if lane <= r < lane + LANES:
                        g = g - jnp.where(row_ids + (r - lane) == lane_ids, same, 0.0)
                    grad_ref[r : r + step, pl.ds(at + lane, LANES)] = g.astype(jnp.bfloat16)
            return carry

        lax.fori_loop(0, half // block, one, 0, unroll=4)


def image_block(grads, texts, at, block, scale):
    total = None
    for grad, text in zip(grads, texts):
        part = lax.dot_general(
            grad[:, pl.ds(at, block)],
            text[:block, :],
            (((0,), (0,)), ((), ())),
            preferred_element_type=jnp.float32,
        )
        total = part if total is None else total + part
    return scale * total


def text_kernel(order, n_done, kept, block, scale_ref, coef_ref, place_ref, *refs):
    even, odd, row_lse, col_lse, row_extra, col_extra = refs[:6]
    n = len(order)
    texts, rest = refs[6 : 6 + n], refs[6 + n :]
    if kept:
        tile, rest = rest[0], rest[1:]
    done_grads, done_texts, rest = rest[:n_done], rest[n_done : 2 * n_done], rest[2 * n_done :]
    grads, outs, rest = rest[0], rest[1 : 1 + n], rest[1 + n :]
    total, powers = rest[-2:]
    lowest = min(order)
    for i, t in enumerate(order):
        text_block(
            block,
            texts[i],
            tile.at[pl.ds((t - lowest) * block, block)] if kept else None,
            t,
            (even, odd),
            row_lse,
            col_lse,
            place_ref,
            coef_ref,
            grads.at[pl.ds((t - lowest) * block, block)],
        )
    half = even.shape[0]
    scale = scale_ref[0, 0]
    total[...] = scale * (
        jnp.dot(grads[:, :half], even[...], preferred_element_type=jnp.float32)
        + jnp.dot(grads[:, half:], odd[...], preferred_element_type=jnp.float32)
    )
    for i, t in enumerate(order):
        at = (t - lowest) * block
        if t & 1:
            extra_rows = rest[-3]
            put_extra(extra_rows, row_extra)
            encode(outs[i], powers, block, lambda r, at=at: total[at + r : at + r + STEP, :], extra_rows[...])
        else:
            outs[i][:block, :] = total[at : at + block, :]
            put_extra(outs[i].at[block:, :], row_extra)
    if n_done:
        far_ref, near_ref = rest[:2]
        by_text = {t: (grads.at[pl.ds((t - lowest) * block, block)], texts[i]) for i, t in enumerate(order)}

        for images_ref, first in ((far_ref, half), (near_ref, 0)):

            def one(j, carry):
                images_ref[j, :block, :] = image_block(
                    [*done_grads, *[by_text[t][0] for t in order]],
                    [*done_texts, *[by_text[t][1] for t in order]],
                    pl.multiple_of(j * block + first, block),
                    block,
                    scale,
                )
                put_extra(images_ref.at[j, block:, :], col_extra)
                return carry

            lax.fori_loop(0, half // block, one, 0, unroll=4)


def text_grads(scale, coef, place, even, odd, row_lse, col_lse, row_extra, col_extra, texts, tile, order, done):
    half, width = even.shape
    block = row_lse.shape[1]
    n = len(order)
    vmem = pl.BlockSpec(memory_space=VMEM)
    smem = pl.BlockSpec(memory_space=SMEM)
    out_shape = (
        [jax.ShapeDtypeStruct((n * block, 2 * half), jnp.bfloat16)]
        + [
            jax.ShapeDtypeStruct((block + MORE, width), jnp.bfloat16)
            if t & 1
            else jax.ShapeDtypeStruct((block + EXTRA, width), jnp.float32)
            for t in order
        ]
    )
    if done:
        out_shape += [jax.ShapeDtypeStruct((half // block, block + EXTRA, width), jnp.float32)] * 2
    operands = [even, odd, row_lse, col_lse, row_extra, col_extra, *[texts[t] for t in order]]
    operands += tile
    operands += [grad for _, grad in done] + [texts[t] for t, _ in done]
    outs = pl.pallas_call(
        functools.partial(text_kernel, tuple(order), len(done), len(tile), block),
        out_shape=tuple(out_shape),
        in_specs=[smem] * 3 + [vmem] * len(operands),
        out_specs=(vmem,) * len(out_shape),
        scratch_shapes=[
            VMEM((EXTRA, width), jnp.float32),
            VMEM((n * block, width), jnp.float32),
            VMEM((block, LANES), jnp.float32),
        ],
        compiler_params=pltpu.CompilerParams(vmem_limit_bytes=(10 + 2 * n) * 2**20),
        cost_estimate=pl.CostEstimate(
            flops=FLOPS * 4 * n * block * 2 * half * width, bytes_accessed=0, transcendentals=0
        ),
        name=f"text_grads_{n}",
    )(scale, coef, place, *operands)
    parts = {t: outs[1 + i] for i, t in enumerate(order)}
    return outs[0], parts, outs[1 + n :]


def on_device(n_row, n_col, image_embeds, text_embeds, logit_scale):
    block = image_embeds.shape[0]
    r, c = lax.axis_index("row"), lax.axis_index("col")
    place = jnp.stack([r, c]).reshape(1, 2)
    scale = logit_scale.reshape(1, 1)
    coef = scale * LOG2E
    image_half, text_half = cast(image_embeds, text_embeds, 16)
    even, odd, texts, text_last = gather_both(image_half, text_half, n_col, n_row)
    keep = 4 * n_row * n_col * block * block <= 16 * 2**20
    even, odd, *before = stats(
        coef, place, texts, (*even, *odd), (), n_col, n_row, block, keep
    )
    row_parts, col_parts, *tile_last = stats(
        coef, place, [text_last], (even, odd), before[:2], n_col, n_row, block, keep
    )
    texts = [*texts, text_last]
    tile = before[2:]
    row_lse, row_extra, col_lse, col_extra = exchanged(row_parts, col_parts, n_col, n_row)

    held = (scale, coef, place, even, odd, row_lse, col_lse, row_extra, col_extra, texts)
    last = n_row - 1
    last_grad, parts, _ = text_grads(*held, tile_last, [last], [])
    received = swap(parts[last], "row", n_row, 1)
    _, more_parts, (far, near) = text_grads(*held, tile, list(range(last))[::-1], [(last, last_grad)])
    parts |= more_parts
    codes = {q: [] for q in range(0, n_row, 2)}
    codes[last ^ 1].append(received)
    after = [pack_text(parts[last ^ 1], codes[last ^ 1])] if n_row > 2 else [received]
    far = swap(far, "col", n_col, 1)
    odd_parts, far = lax.optimization_barrier(([parts[q] for q in range(1, last, 2)], far))
    for q, part in zip(range(1, last, 2), odd_parts):
        codes[q ^ 1].append(swap(part, "row", n_row, 1))
    for b in range(1, n_row.bit_length() - 1):
        for q in [q for q in codes if q & (1 << b)]:
            code = after[0] if (b, q) == (1, last ^ 1) else pack_text(parts[q], codes[q])
            codes[q ^ (1 << b)].append(swap(code, "row", n_row, 1 << b))
            del codes[q]
    grad_text, text_extra, _ = total_of(coef, parts[0], codes[0], True, [], "grad_text")

    own, others = pack_images(near, far, after)
    others = [swap(code, "col", n_col, 2 * j) for j, code in enumerate(others, 1)]
    first, text_extra = lax.optimization_barrier((others[0], text_extra))
    grad_image, _, grad_scale = total_of(
        coef, added(own, first), others[1:], False, [text_extra], "grad_image"
    )
    return grad_image, grad_text, grad_scale.reshape(())


def solution(mesh):
    images = P(("row", "col"), None)
    texts = P(("col", "row"), None)
    return jax.shard_map(
        functools.partial(on_device, mesh.shape["row"], mesh.shape["col"]),
        mesh=mesh,
        in_specs=(images, texts, P()),
        out_specs=(images, texts, P()),
        check_vma=False,
    )
```

```python
import functools
import math

import jax
import jax.numpy as jnp
from jax import lax
from jax.experimental import pallas as pl
from jax.experimental.pallas import tpu as pltpu
from jax.sharding import PartitionSpec as P

LOG2E = 1.4426950408889634
LN2 = 0.6931471805599453
LANES = 128
VMEM = pltpu.VMEM
SMEM = pltpu.SMEM
FLOPS = 20


def swap(x, axis, n, q):
    return lax.ppermute(x, axis, [(i, i ^ q) for i in range(n)])


def gather_both(image, text, n_col, n_row):
    images = [swap(image, "col", n_col, q) for q in range(2, n_col, 2)]
    texts = [swap(text, "row", n_row, q) for q in range(1, n_row - 1)]
    last = swap(texts[-1], "row", n_row, 1)
    images, texts = lax.optimization_barrier((images, texts))
    odd = [swap(i, "col", n_col, 1) for i in (image, *images)]
    return [image, *images], odd, [text, *texts], last


def nt_dot(a, b):
    return lax.dot_general(a, b, (((1,), (1,)), ((), ())), preferred_element_type=jnp.float32)


def stats_kernel(first, n_text, block, coef_ref, place_ref, *refs):
    texts, refs = refs[:n_text], refs[n_text:]
    coef = coef_ref[0, 0]
    r_place, c_place = place_ref[0, 0], place_ref[0, 1]
    *refs, row_max, col_max, col_sum, col_dot, row_diag = refs
    if first:
        *refs, even, odd, row_ref, col_ref, tile = refs
        halves = (even, odd)
        each = len(refs) // 2
        for i, piece in enumerate(refs):
            at = (i % each) * block
            halves[i // each][at : at + block, :] = piece[...]
        before = None
    else:
        even, odd, *before, row_ref, col_ref, tile = refs
        halves = (even, odd)
    cols, rows = tile.shape
    half = rows // 2
    lead = 0 if first else col_ref.shape[1] - n_text
    col_max[...] = jnp.full(col_max.shape, -jnp.inf, jnp.float32)
    row_diag[...] = jnp.zeros(row_diag.shape, jnp.float32)
    n_col, n_row = row_ref.shape[1], col_ref.shape[1]

    for which, images in enumerate(halves):

        def products(j, carry):
            image = images[pl.ds(pl.multiple_of(j * block, block), block), :]
            at = pl.multiple_of(j * block + which * half, block)
            top = None
            for t in range(n_text):
                part = pl.ds(t * block, block)
                x = nt_dot(texts[t][:block, :], image) * coef
                tile[part, pl.ds(at, block)] = x
                top_t = jnp.max(x, axis=0, keepdims=True)
                top = top_t if top is None else jnp.maximum(top, top_t)
                held = col_max[part, :]
                for lane in range(0, block, LANES):
                    held = jnp.maximum(held, x[:, lane : lane + LANES])
                col_max[part, :] = held
            row_max[0:1, pl.ds(at, block)] = top
            return carry

        lax.fori_loop(0, half // block, products, 0, unroll=4)

    for t in range(n_text):
        among = c_place * n_row + (r_place ^ (lead + t)) - r_place * n_col

        @pl.when((among >= 0) & (among < n_col))
        def _():
            q = c_place ^ among
            at = pl.multiple_of((q // 2) * block + (q % 2) * half, block)
            x = tile[t * block : (t + 1) * block, pl.ds(at, block)]
            down = lax.broadcasted_iota(jnp.int32, x.shape, 0)
            across = lax.broadcasted_iota(jnp.int32, x.shape, 1)
            row_diag[0:1, pl.ds(at, block)] = jnp.sum(
                jnp.where(down == across, x, 0.0), axis=0, keepdims=True
            )

    col_max[...] = jnp.broadcast_to(
        jnp.max(col_max[...], axis=1, keepdims=True), col_max.shape
    )
    sums = []
    for which in range(2):
        lanes = range(which * half, (which + 1) * half, LANES)

        def exponentials(i, acc):
            part = pl.ds(pl.multiple_of(i * 8, 8), 8)
            top = col_max[part, :]
            total = col_sum[part, :] if which else None
            dot = col_dot[part, :] if which else None
            new = [], []
            for n, lane in enumerate(lanes):
                x = tile[part, lane : lane + LANES]
                e = jnp.exp2(x - row_max[0:1, lane : lane + LANES])
                new[0].append(acc[0][n] + e)
                new[1].append(acc[1][n] + e * x)
                e = jnp.exp2(x - top)
                total = e if total is None else total + e
                dot = e * x if dot is None else dot + e * x
            col_sum[part, :] = total
            col_dot[part, :] = dot
            return tuple(new[0]), tuple(new[1])

        zeros = tuple(jnp.zeros((8, LANES), jnp.float32) for _ in lanes)
        sums.append(lax.fori_loop(0, cols // 8, exponentials, (zeros, zeros), unroll=8))

    row_ids = lax.broadcasted_iota(jnp.int32, (n_col, block), 0)
    placed = [jnp.zeros((n_col, block), jnp.float32)] * 4
    for q in range(n_col):
        at = (q // 2) * block
        here = row_ids == (c_place ^ q)
        new = [row_max[0:1, at + (q % 2) * half : at + (q % 2) * half + block]]
        for which in sums[q % 2]:
            new.append(
                jnp.concatenate(
                    [
                        jnp.sum(which[(at + lane) // LANES], axis=0, keepdims=True)
                        for lane in range(0, block, LANES)
                    ],
                    axis=1,
                )
            )
        new.append(row_diag[0:1, at + (q % 2) * half : at + (q % 2) * half + block])
        placed = [jnp.where(here, n, p) for n, p in zip(new, placed)]
    if before:
        placed = merged(placed, [before[0][i] for i in range(4)])
    for i in range(4):
        row_ref[i] = placed[i]
    row_ids = lax.broadcasted_iota(jnp.int32, (n_row, block), 0)
    placed = [before[1][i] if before else jnp.zeros((n_row, block), jnp.float32) for i in range(3)]
    for t in range(n_text):
        part = pl.ds(t * block, block)
        here = row_ids == (r_place ^ (lead + t))
        new = [col_max[part, :].T[0:1, :]]
        for which in (col_sum, col_dot):
            new.append(jnp.sum(which[part, :].T, axis=0, keepdims=True))
        placed = [jnp.where(here, n, p) for n, p in zip(new, placed)]
    for i in range(3):
        col_ref[i] = placed[i]


def stats(coef, place, texts, images, before, n_col, n_row, block, keep):
    width = texts[0].shape[1]
    first = not before
    rows, cols = block * n_col, block * len(texts)
    vmem = pl.BlockSpec(memory_space=VMEM)
    smem = pl.BlockSpec(memory_space=SMEM)
    half = jax.ShapeDtypeStruct((rows // 2, width), jnp.bfloat16)
    out_shape = [half, half] if first else []
    out_shape += [
        jax.ShapeDtypeStruct((4, n_col, block), jnp.float32),
        jax.ShapeDtypeStruct((3, n_row, block), jnp.float32),
    ]
    scratch = [
        VMEM((8, rows), jnp.float32),
        VMEM((cols, LANES), jnp.float32),
        VMEM((cols, LANES), jnp.float32),
        VMEM((cols, LANES), jnp.float32),
        VMEM((8, rows), jnp.float32),
    ]
    if keep:
        out_shape.append(jax.ShapeDtypeStruct((cols, rows), jnp.float32))
    else:
        scratch.insert(0, VMEM((cols, rows), jnp.float32))
    return pl.pallas_call(
        functools.partial(stats_kernel, first, len(texts), block),
        out_shape=tuple(out_shape),
        in_specs=[smem, smem] + [vmem] * (len(texts) + len(images) + len(before)),
        out_specs=(vmem,) * len(out_shape),
        scratch_shapes=scratch,
        compiler_params=pltpu.CompilerParams(
            vmem_limit_bytes=(0 if keep else 4 * rows * cols) + 8 * 2**20
        ),
        cost_estimate=pl.CostEstimate(
            flops=2 * rows * width, bytes_accessed=0, transcendentals=0
        ),
        name="stats" if first else "stats_last",
    )(coef, place, *texts, *images, *before)


def merged(a, b):
    top = jnp.maximum(a[0], b[0])
    wa, wb = jnp.exp2(a[0] - top), jnp.exp2(b[0] - top)
    out = [top] + [a[i] * wa + b[i] * wb for i in (1, 2)]
    return out + [a[i] + b[i] for i in range(3, len(a))]


def by_pairs(blocks, add):
    while len(blocks) > 1:
        blocks = [add(blocks[i], blocks[i + 1]) for i in range(0, len(blocks), 2)]
    return blocks[0]


def lse_and_mean(parts):
    mean = 0.5 * parts[2] / parts[1]
    return parts[0] + jnp.log(parts[1]) * LOG2E, mean - parts[3] if len(parts) > 3 else mean


def exchanged(row_parts, col_parts, n_col, n_row):
    rows, cols = list(row_parts), list(col_parts)
    count = len(cols)
    fill = row_parts.size // col_parts.size + 1
    row_bits = [1 << b for b in range(1, n_col.bit_length() - 1)] + [1]
    col_bits = [1 << b for b in range(n_row.bit_length() - 1)]
    for n, bit in enumerate(row_bits):
        received = swap(jnp.stack(rows), "col", n_col, bit)
        if n < len(col_bits):
            other = swap(jnp.stack(cols * fill), "row", n_row, col_bits[n])
            received, other = lax.optimization_barrier((received, other))
            cols = merged(cols, list(other[:count]))
        rows = merged(rows, list(received))
    return *lse_and_mean(rows), *lse_and_mean(cols)


LEVELS = 32000
LOW = 128
BIAS = 125
EXTRA = 8
MORE = 2 * EXTRA
STEP = 32


def put_extra(out, extra_ref):
    n, width = extra_ref.shape
    rows = min(n, EXTRA)
    out[...] = jnp.zeros(out.shape, out.dtype)
    out[:rows, :width] = sum(extra_ref[i : i + rows, :] for i in range(0, n, rows))


def power(k):
    return jnp.exp2(k).astype(jnp.bfloat16).astype(jnp.float32)


def encode(out, powers, size, slab, extra):
    width = out.shape[1]
    for r in range(0, size, STEP):
        value = slab(r)
        top = jnp.maximum(jnp.max(jnp.abs(value), axis=1, keepdims=True), 1e-30)
        k = jnp.ceil(jnp.log(top) * LOG2E)
        powers[r : r + STEP, :] = jnp.broadcast_to(power(k), (STEP, LANES))
        whole = jnp.floor(jnp.abs(value) * (power(-k) * (LEVELS - 1)) + 0.5) * (1 / LOW)
        high = jnp.floor(whole)
        code = (1.0 + (whole - high)) * jnp.exp2(high - BIAS)
        out[r : r + STEP, :] = jnp.where(value < 0, -code, code).astype(jnp.bfloat16)
    half = width // 2
    first = extra[:, :half].astype(jnp.bfloat16)
    rest = extra[:, :half] - first.astype(jnp.float32)
    second = rest.astype(jnp.bfloat16)
    third = (rest - second.astype(jnp.float32)).astype(jnp.bfloat16)
    fourth = powers[...].T[:EXTRA, :].astype(jnp.bfloat16)
    if size < half:
        fourth = jnp.concatenate([fourth, jnp.zeros((EXTRA, half - size), jnp.bfloat16)], axis=1)
    out[size:, :half] = jnp.concatenate([first, second], axis=0)
    out[size:, half:] = jnp.concatenate([third, fourth], axis=0)


def decode_powers(code, size):
    half = code.shape[1] // 2
    powers = code[size:, half : half + size].astype(jnp.float32)
    return jnp.broadcast_to(powers[EXTRA : EXTRA + 1, :], (LANES, size)).T * (LOW / (LEVELS - 1))


def decode(code, powers, r):
    lanes = []
    for lane in range(0, code.shape[1], LANES):
        c = code[r : r + STEP, lane : lane + LANES].astype(jnp.float32)
        a = jnp.abs(c)
        high = jnp.floor(jnp.log(a) * LOG2E)
        whole = (high + (BIAS - 1)) + a * jnp.exp2(-high)
        lanes.append(jnp.where(c < 0, -whole, whole) * powers[r : r + STEP, :])
    return jnp.concatenate(lanes, axis=1)


def decode_extra(code, size):
    half = code.shape[1] // 2
    left = code[size:, :half].astype(jnp.float32)
    right = code[size:, half:].astype(jnp.float32)
    return left[:EXTRA] + left[EXTRA:] + right[:EXTRA]


def pack_text_kernel(n, base, *refs):
    codes, out, powers, received = refs[:n], *refs[n:]
    size, half = base.shape[0] - EXTRA, base.shape[1] // 2
    more = base[size:, :half]
    for c, code in enumerate(codes):
        received[c] = decode_powers(code, size)
        more = more + decode_extra(code, size)

    def slab(r):
        value = base[r : r + STEP, :]
        for c, code in enumerate(codes):
            value = value + decode(code, received.at[c], r)
        return value

    encode(out, powers, size, slab, more)


def pack_text(base, codes):
    size, width = base.shape[0] - EXTRA, base.shape[1]
    vmem = pl.BlockSpec(memory_space=VMEM)
    return pl.pallas_call(
        functools.partial(pack_text_kernel, len(codes)),
        out_shape=jax.ShapeDtypeStruct((size + MORE, width), jnp.bfloat16),
        in_specs=[vmem] * (1 + len(codes)),
        out_specs=vmem,
        scratch_shapes=[VMEM((size, LANES), jnp.float32), VMEM((len(codes), size, LANES), jnp.float32)],
        compiler_params=pltpu.CompilerParams(vmem_limit_bytes=6 * 2**20),
        cost_estimate=pl.CostEstimate(
            flops=FLOPS * 32 * size * size * width, bytes_accessed=0, transcendentals=0
        ),
        name="pack_text",
    )(base, *codes)


def pack_images_kernel(n, near, far, *refs):
    own, *outs, powers = refs[-n - 1 :]
    size = near.shape[1] - EXTRA
    own[...] = near[0] + far[0]
    for j, out in enumerate(outs, 1):
        encode(
            out,
            powers.at[j - 1],
            size,
            lambda r, j=j: near[j, r : r + STEP, :] + far[j, r : r + STEP, :],
            near[j, size:, :] + far[j, size:, :],
        )


def pack_images(near, far, after):
    n, rows, width = near.shape
    size = rows - EXTRA
    vmem = pl.BlockSpec(memory_space=VMEM)
    code = jax.ShapeDtypeStruct((size + MORE, width), jnp.bfloat16)
    own, *codes = pl.pallas_call(
        functools.partial(pack_images_kernel, n),
        out_shape=(jax.ShapeDtypeStruct((rows, width), jnp.float32),) + (code,) * (n - 1),
        in_specs=[vmem] * 2 + [pl.BlockSpec(memory_space=pl.ANY)] * len(after),
        out_specs=(vmem,) * n,
        scratch_shapes=[VMEM((n - 1, size, LANES), jnp.float32)],
        compiler_params=pltpu.CompilerParams(vmem_limit_bytes=(4 + 2 * n) * 2**20),
        cost_estimate=pl.CostEstimate(
            flops=FLOPS * 8 * n * size * size * width, bytes_accessed=0, transcendentals=0
        ),
        name="pack_images",
    )(near, far, *after)
    return own, codes


def total_kernel(n, in_order, coef_ref, base, *refs):
    codes, before = refs[:n], refs[n:-6]
    out, extra, scalar, value, powers, sems = refs[-6:]
    size, width = base.shape[0] - EXTRA, base.shape[1]
    combine = functools.partial(functools.reduce, jnp.add) if in_order else first_and_pairs
    more = combine([base[size:, : width // 2]] + [decode_extra(code, size) for code in codes])
    more = sum([b[...] for b in before], more)
    extra[...] = more
    if before:
        scalar[0, 0] = jnp.sum(more) / coef_ref[0, 0]
    else:
        scalar[0, 0] = 0.0
    for c, code in enumerate(codes):
        powers[c] = decode_powers(code, size)
    copies = []
    steps = sems.shape[0]
    for i in range(steps):
        part = pl.ds(i * (size // steps), size // steps)
        for r in range(i * (size // steps), (i + 1) * (size // steps), STEP):
            value[r : r + STEP, :] = combine(
                [base[r : r + STEP, :]] + [decode(code, powers.at[c], r) for c, code in enumerate(codes)]
            )
        copies.append(pltpu.make_async_copy(value.at[part], out.at[part], sems.at[i]))
        copies[-1].start()
    for copy in copies:
        copy.wait()


def add_kernel(base, code, out, powers):
    size, half = base.shape[0] - EXTRA, base.shape[1] // 2
    powers[...] = decode_powers(code, size)
    for r in range(0, size, STEP):
        out[r : r + STEP, :] = base[r : r + STEP, :] + decode(code, powers, r)
    out[size:, :half] = base[size:, :half] + decode_extra(code, size)
    out[size:, half:] = jnp.zeros((EXTRA, half), jnp.float32)


def added(base, code):
    vmem = pl.BlockSpec(memory_space=VMEM)
    return pl.pallas_call(
        add_kernel,
        out_shape=jax.ShapeDtypeStruct(base.shape, jnp.float32),
        in_specs=[vmem] * 2,
        out_specs=vmem,
        scratch_shapes=[VMEM((base.shape[0] - EXTRA, LANES), jnp.float32)],
        compiler_params=pltpu.CompilerParams(vmem_limit_bytes=6 * 2**20),
        name="added",
    )(base, code)


def first_and_pairs(blocks):
    if len(blocks) == 1:
        return blocks[0]
    pairs = [blocks[0]] + [blocks[i] + blocks[i + 1] for i in range(1, len(blocks), 2)]
    return by_pairs(pairs, jnp.add)


def total_of(coef, base, codes, in_order, before, name):
    size, width = base.shape[0] - EXTRA, base.shape[1]
    vmem = pl.BlockSpec(memory_space=VMEM)
    smem = pl.BlockSpec(memory_space=SMEM)
    return pl.pallas_call(
        functools.partial(total_kernel, len(codes), in_order),
        out_shape=(
            jax.ShapeDtypeStruct((size, width), jnp.float32),
            jax.ShapeDtypeStruct((EXTRA, width // 2), jnp.float32),
            jax.ShapeDtypeStruct((1, 1), jnp.float32),
        ),
        in_specs=[smem] + [vmem] * (1 + len(codes) + len(before)),
        out_specs=(pl.BlockSpec(memory_space=pl.ANY), vmem, smem),
        scratch_shapes=[
            VMEM((size, width), jnp.float32),
            VMEM((len(codes), size, LANES), jnp.float32),
            pltpu.SemaphoreType.DMA((4,)),
        ],
        compiler_params=pltpu.CompilerParams(vmem_limit_bytes=8 * 2**20),
        name=name,
    )(coef, base, *codes, *before)


def text_block(block, text, tile, t, halves, row_lse, col_lse, place_ref, coef_ref, grad_ref):
    coef = coef_ref[0, 0]
    r_place, c_place = place_ref[0, 0], place_ref[0, 1]
    half, width = halves[0].shape
    n_col, n_row = row_lse.shape[0], col_lse.shape[0]
    size = block
    col_lse_down = jnp.broadcast_to(col_lse[pl.ds(r_place ^ t, 1), :], (LANES, size)).T
    text_id = c_place * n_row + (r_place ^ t)
    step = 32
    lane_ids = lax.broadcasted_iota(jnp.int32, (step, LANES), 1)
    row_ids = lax.broadcasted_iota(jnp.int32, (step, LANES), 0)

    for which, images in enumerate(halves):

        def one(j, carry):
            at = pl.multiple_of(j * block + which * half, block)
            if tile is None:
                image = images[pl.ds(pl.multiple_of(j * block, block), block), :]
                xs = nt_dot(text[:block, :], image) * coef
            column = c_place ^ (2 * j + which)
            same = jnp.where(r_place * n_col + column == text_id, 1.0, 0.0)
            lse = row_lse[pl.ds(column, 1), :]
            for r in range(0, size, step):
                for lane in range(0, block, LANES):
                    if tile is None:
                        x = xs[r : r + step, lane : lane + LANES]
                    else:
                        x = tile[r : r + step, pl.ds(at + lane, LANES)]
                    e = jnp.exp2(x - lse[:, lane : lane + LANES]) + jnp.exp2(
                        x - col_lse_down[r : r + step, :]
                    )
                    g = 0.5 * e
                    if lane <= r < lane + LANES:
                        g = g - jnp.where(row_ids + (r - lane) == lane_ids, same, 0.0)
                    grad_ref[r : r + step, pl.ds(at + lane, LANES)] = g.astype(jnp.bfloat16)
            return carry

        lax.fori_loop(0, half // block, one, 0, unroll=4)


def image_block(grads, texts, at, count, scale, block):
    total = None
    for grad, text in zip(grads, texts):
        part = lax.dot_general(
            grad[:, pl.ds(at, count)],
            text[:block, :],
            (((0,), (0,)), ((), ())),
            preferred_element_type=jnp.float32,
        )
        total = part if total is None else total + part
    return scale * total


def text_kernel(order, n_done, kept, block, scale_ref, coef_ref, place_ref, *refs):
    even, odd, row_lse, col_lse, row_extra, col_extra = refs[:6]
    n = len(order)
    texts, rest = refs[6 : 6 + n], refs[6 + n :]
    if kept:
        tile, rest = rest[0], rest[1:]
    done_grads, done_texts, rest = rest[:n_done], rest[n_done : 2 * n_done], rest[2 * n_done :]
    grads, outs, rest = rest[0], rest[1 : 1 + n], rest[1 + n :]
    total, powers = rest[-2:]
    lowest = min(order)
    for i, t in enumerate(order):
        text_block(
            block,
            texts[i],
            tile.at[pl.ds((t - lowest) * block, block)] if kept else None,
            t,
            (even, odd),
            row_lse,
            col_lse,
            place_ref,
            coef_ref,
            grads.at[pl.ds((t - lowest) * block, block)],
        )
    half = even.shape[0]
    scale = scale_ref[0, 0]
    total[...] = scale * (
        jnp.dot(grads[:, :half], even[...], preferred_element_type=jnp.float32)
        + jnp.dot(grads[:, half:], odd[...], preferred_element_type=jnp.float32)
    )
    for i, t in enumerate(order):
        at = (t - lowest) * block
        if t & 1:
            extra_rows = rest[-3]
            put_extra(extra_rows, row_extra)
            encode(outs[i], powers, block, lambda r, at=at: total[at + r : at + r + STEP, :], extra_rows[...])
        else:
            outs[i][:block, :] = total[at : at + block, :]
            put_extra(outs[i].at[block:, :], row_extra)
    if n_done:
        far_ref, near_ref = rest[:2]
        by_text = {t: (grads.at[pl.ds((t - lowest) * block, block)], texts[i]) for i, t in enumerate(order)}

        for images_ref, first in ((far_ref, half), (near_ref, 0)):

            def one(j, carry):
                pair = image_block(
                    [*done_grads, *[by_text[t][0] for t in order]],
                    [*done_texts, *[by_text[t][1] for t in order]],
                    pl.multiple_of(2 * j * block + first, block),
                    2 * block,
                    scale,
                    block,
                )
                for n in range(2):
                    images_ref[2 * j + n, :block, :] = pair[n * block : (n + 1) * block]
                    put_extra(images_ref.at[2 * j + n, block:, :], col_extra)
                return carry

            lax.fori_loop(0, half // block // 2, one, 0, unroll=2)


def text_grads(scale, coef, place, even, odd, row_lse, col_lse, row_extra, col_extra, texts, tile, order, done):
    half, width = even.shape
    block = row_lse.shape[1]
    n = len(order)
    vmem = pl.BlockSpec(memory_space=VMEM)
    smem = pl.BlockSpec(memory_space=SMEM)
    out_shape = (
        [jax.ShapeDtypeStruct((n * block, 2 * half), jnp.bfloat16)]
        + [
            jax.ShapeDtypeStruct((block + MORE, width), jnp.bfloat16)
            if t & 1
            else jax.ShapeDtypeStruct((block + EXTRA, width), jnp.float32)
            for t in order
        ]
    )
    if done:
        out_shape += [jax.ShapeDtypeStruct((half // block, block + EXTRA, width), jnp.float32)] * 2
    operands = [even, odd, row_lse, col_lse, row_extra, col_extra, *[texts[t] for t in order]]
    operands += tile
    operands += [grad for _, grad in done] + [texts[t] for t, _ in done]
    outs = pl.pallas_call(
        functools.partial(text_kernel, tuple(order), len(done), len(tile), block),
        out_shape=tuple(out_shape),
        in_specs=[smem] * 3 + [vmem] * len(operands),
        out_specs=(vmem,) * len(out_shape),
        scratch_shapes=[
            VMEM((EXTRA, width), jnp.float32),
            VMEM((n * block, width), jnp.float32),
            VMEM((block, LANES), jnp.float32),
        ],
        compiler_params=pltpu.CompilerParams(vmem_limit_bytes=(10 + 2 * n) * 2**20),
        cost_estimate=pl.CostEstimate(
            flops=FLOPS * 4 * n * block * 2 * half * width, bytes_accessed=0, transcendentals=0
        ),
        name=f"text_grads_{n}",
    )(scale, coef, place, *operands)
    parts = {t: outs[1 + i] for i, t in enumerate(order)}
    return outs[0], parts, outs[1 + n :]


def on_device(n_row, n_col, image_embeds, text_embeds, logit_scale):
    block = image_embeds.shape[0]
    r, c = lax.axis_index("row"), lax.axis_index("col")
    place = jnp.stack([r, c]).reshape(1, 2)
    scale = logit_scale.reshape(1, 1)
    coef = scale * LOG2E
    image_half = image_embeds.astype(jnp.bfloat16)
    text_half = jnp.pad(text_embeds.astype(jnp.bfloat16), ((0, 16), (0, 0)))
    even, odd, texts, text_last = gather_both(image_half, text_half, n_col, n_row)
    keep = 4 * n_row * n_col * block * block <= 16 * 2**20
    even, odd, *before = stats(
        coef, place, texts, (*even, *odd), (), n_col, n_row, block, keep
    )
    row_parts, col_parts, *tile_last = stats(
        coef, place, [text_last], (even, odd), before[:2], n_col, n_row, block, keep
    )
    texts = [*texts, text_last]
    tile = before[2:]
    row_lse, row_extra, col_lse, col_extra = exchanged(row_parts, col_parts, n_col, n_row)

    held = (scale, coef, place, even, odd, row_lse, col_lse, row_extra, col_extra, texts)
    last = n_row - 1
    last_grad, parts, _ = text_grads(*held, tile_last, [last], [])
    received = swap(parts[last], "row", n_row, 1)
    _, more_parts, (far, near) = text_grads(*held, tile, list(range(last))[::-1], [(last, last_grad)])
    parts |= more_parts
    codes = {q: [] for q in range(0, n_row, 2)}
    codes[last ^ 1].append(received)
    after = [pack_text(parts[last ^ 1], codes[last ^ 1])] if n_row > 2 else [received]
    far = swap(far, "col", n_col, 1)
    odd_parts, far = lax.optimization_barrier(([parts[q] for q in range(1, last, 2)], far))
    for q, part in zip(range(1, last, 2), odd_parts):
        codes[q ^ 1].append(swap(part, "row", n_row, 1))
    for b in range(1, n_row.bit_length() - 1):
        for q in [q for q in codes if q & (1 << b)]:
            code = after[0] if (b, q) == (1, last ^ 1) else pack_text(parts[q], codes[q])
            codes[q ^ (1 << b)].append(swap(code, "row", n_row, 1 << b))
            del codes[q]
    grad_text, text_extra, _ = total_of(coef, parts[0], codes[0], True, [], "grad_text")

    own, others = pack_images(near, far, after)
    others = [swap(code, "col", n_col, 2 * j) for j, code in enumerate(others, 1)]
    first, text_extra = lax.optimization_barrier((others[0], text_extra))
    grad_image, _, grad_scale = total_of(
        coef, added(own, first), others[1:], False, [text_extra], "grad_image"
    )
    return grad_image, grad_text, grad_scale.reshape(())


def solution(mesh):
    images = P(("row", "col"), None)
    texts = P(("col", "row"), None)
    return jax.shard_map(
        functools.partial(on_device, mesh.shape["row"], mesh.shape["col"]),
        mesh=mesh,
        in_specs=(images, texts, P()),
        out_specs=(images, texts, P()),
        check_vma=False,
    )
```

```python
import functools
import math

import jax
import jax.numpy as jnp
from jax import lax
from jax.experimental import pallas as pl
from jax.experimental.pallas import tpu as pltpu
from jax.sharding import PartitionSpec as P

LOG2E = 1.4426950408889634
LN2 = 0.6931471805599453
LANES = 128
VMEM = pltpu.VMEM
SMEM = pltpu.SMEM
FLOPS = 20


def swap(x, axis, n, q):
    return lax.ppermute(x, axis, [(i, i ^ q) for i in range(n)])


def gather_both(image, text, n_col, n_row):
    images = [swap(image, "col", n_col, q) for q in range(2, n_col, 2)]
    texts = [swap(text, "row", n_row, q) for q in range(1, n_row - 1)]
    last = swap(texts[-1], "row", n_row, 1)
    images, texts = lax.optimization_barrier((images, texts))
    odd = [swap(i, "col", n_col, 1) for i in (image, *images)]
    return [image, *images], odd, [text, *texts], last


def nt_dot(a, b):
    return lax.dot_general(a, b, (((1,), (1,)), ((), ())), preferred_element_type=jnp.float32)


def stats_kernel(first, n_text, block, coef_ref, place_ref, *refs):
    texts, refs = refs[:n_text], refs[n_text:]
    coef = coef_ref[0, 0]
    r_place, c_place = place_ref[0, 0], place_ref[0, 1]
    *refs, row_max, col_max, col_sum, col_dot, row_diag = refs
    if first:
        *refs, even, odd, row_ref, col_ref, tile = refs
        halves = (even, odd)
        each = len(refs) // 2
        for i, piece in enumerate(refs):
            at = (i % each) * block
            halves[i // each][at : at + block, :] = piece[...]
        before = None
    else:
        even, odd, *before, row_ref, col_ref, tile = refs
        halves = (even, odd)
    cols, rows = tile.shape
    half = rows // 2
    lead = 0 if first else col_ref.shape[1] - n_text
    col_max[...] = jnp.full(col_max.shape, -jnp.inf, jnp.float32)
    row_diag[...] = jnp.zeros(row_diag.shape, jnp.float32)
    n_col, n_row = row_ref.shape[1], col_ref.shape[1]

    for which, images in enumerate(halves):

        def products(j, carry):
            image = images[pl.ds(pl.multiple_of(j * block, block), block), :]
            at = pl.multiple_of(j * block + which * half, block)
            top = None
            for t in range(n_text):
                part = pl.ds(t * block, block)
                x = nt_dot(texts[t][:block, :], image) * coef
                tile[part, pl.ds(at, block)] = x
                top_t = jnp.max(x, axis=0, keepdims=True)
                top = top_t if top is None else jnp.maximum(top, top_t)
                held = col_max[part, :]
                for lane in range(0, block, LANES):
                    held = jnp.maximum(held, x[:, lane : lane + LANES])
                col_max[part, :] = held
            row_max[0:1, pl.ds(at, block)] = top
            return carry

        lax.fori_loop(0, half // block, products, 0, unroll=4)

    for t in range(n_text):
        among = c_place * n_row + (r_place ^ (lead + t)) - r_place * n_col

        @pl.when((among >= 0) & (among < n_col))
        def _():
            q = c_place ^ among
            at = pl.multiple_of((q // 2) * block + (q % 2) * half, block)
            x = tile[t * block : (t + 1) * block, pl.ds(at, block)]
            down = lax.broadcasted_iota(jnp.int32, x.shape, 0)
            across = lax.broadcasted_iota(jnp.int32, x.shape, 1)
            row_diag[0:1, pl.ds(at, block)] = jnp.sum(
                jnp.where(down == across, x, 0.0), axis=0, keepdims=True
            )

    col_max[...] = jnp.broadcast_to(
        jnp.max(col_max[...], axis=1, keepdims=True), col_max.shape
    )
    sums = []
    for which in range(2):
        lanes = range(which * half, (which + 1) * half, LANES)

        def exponentials(i, acc):
            part = pl.ds(pl.multiple_of(i * 8, 8), 8)
            top = col_max[part, :]
            total = col_sum[part, :] if which else None
            dot = col_dot[part, :] if which else None
            new = [], []
            for n, lane in enumerate(lanes):
                x = tile[part, lane : lane + LANES]
                e = jnp.exp2(x - row_max[0:1, lane : lane + LANES])
                new[0].append(acc[0][n] + e)
                new[1].append(acc[1][n] + e * x)
                e = jnp.exp2(x - top)
                total = e if total is None else total + e
                dot = e * x if dot is None else dot + e * x
            col_sum[part, :] = total
            col_dot[part, :] = dot
            return tuple(new[0]), tuple(new[1])

        zeros = tuple(jnp.zeros((8, LANES), jnp.float32) for _ in lanes)
        sums.append(lax.fori_loop(0, cols // 8, exponentials, (zeros, zeros), unroll=8))

    row_ids = lax.broadcasted_iota(jnp.int32, (n_col, block), 0)
    placed = [jnp.zeros((n_col, block), jnp.float32)] * 4
    for q in range(n_col):
        at = (q // 2) * block
        here = row_ids == (c_place ^ q)
        new = [row_max[0:1, at + (q % 2) * half : at + (q % 2) * half + block]]
        for which in sums[q % 2]:
            new.append(
                jnp.concatenate(
                    [
                        jnp.sum(which[(at + lane) // LANES], axis=0, keepdims=True)
                        for lane in range(0, block, LANES)
                    ],
                    axis=1,
                )
            )
        new.append(row_diag[0:1, at + (q % 2) * half : at + (q % 2) * half + block])
        placed = [jnp.where(here, n, p) for n, p in zip(new, placed)]
    if before:
        placed = merged(placed, [before[0][i] for i in range(4)])
    for i in range(4):
        row_ref[i] = placed[i]
    row_ids = lax.broadcasted_iota(jnp.int32, (n_row, block), 0)
    placed = [before[1][i] if before else jnp.zeros((n_row, block), jnp.float32) for i in range(3)]
    for t in range(n_text):
        part = pl.ds(t * block, block)
        here = row_ids == (r_place ^ (lead + t))
        new = [col_max[part, :].T[0:1, :]]
        for which in (col_sum, col_dot):
            new.append(jnp.sum(which[part, :].T, axis=0, keepdims=True))
        placed = [jnp.where(here, n, p) for n, p in zip(new, placed)]
    for i in range(3):
        col_ref[i] = placed[i]


def stats(coef, place, texts, images, before, n_col, n_row, block, keep):
    width = texts[0].shape[1]
    first = not before
    rows, cols = block * n_col, block * len(texts)
    vmem = pl.BlockSpec(memory_space=VMEM)
    smem = pl.BlockSpec(memory_space=SMEM)
    half = jax.ShapeDtypeStruct((rows // 2, width), jnp.bfloat16)
    out_shape = [half, half] if first else []
    out_shape += [
        jax.ShapeDtypeStruct((4, n_col, block), jnp.float32),
        jax.ShapeDtypeStruct((3, n_row, block), jnp.float32),
    ]
    scratch = [
        VMEM((8, rows), jnp.float32),
        VMEM((cols, LANES), jnp.float32),
        VMEM((cols, LANES), jnp.float32),
        VMEM((cols, LANES), jnp.float32),
        VMEM((8, rows), jnp.float32),
    ]
    if keep:
        out_shape.append(jax.ShapeDtypeStruct((cols, rows), jnp.float32))
    else:
        scratch.insert(0, VMEM((cols, rows), jnp.float32))
    return pl.pallas_call(
        functools.partial(stats_kernel, first, len(texts), block),
        out_shape=tuple(out_shape),
        in_specs=[smem, smem] + [vmem] * (len(texts) + len(images) + len(before)),
        out_specs=(vmem,) * len(out_shape),
        scratch_shapes=scratch,
        compiler_params=pltpu.CompilerParams(
            vmem_limit_bytes=(0 if keep else 4 * rows * cols) + 8 * 2**20
        ),
        cost_estimate=pl.CostEstimate(
            flops=2 * rows * width, bytes_accessed=0, transcendentals=0
        ),
        name="stats" if first else "stats_last",
    )(coef, place, *texts, *images, *before)


def merged(a, b):
    top = jnp.maximum(a[0], b[0])
    wa, wb = jnp.exp2(a[0] - top), jnp.exp2(b[0] - top)
    out = [top] + [a[i] * wa + b[i] * wb for i in (1, 2)]
    return out + [a[i] + b[i] for i in range(3, len(a))]


def by_pairs(blocks, add):
    while len(blocks) > 1:
        blocks = [add(blocks[i], blocks[i + 1]) for i in range(0, len(blocks), 2)]
    return blocks[0]


def lse_and_mean(parts):
    mean = 0.5 * parts[2] / parts[1]
    return parts[0] + jnp.log(parts[1]) * LOG2E, mean - parts[3] if len(parts) > 3 else mean


def exchanged(row_parts, col_parts, n_col, n_row):
    rows, cols = list(row_parts), list(col_parts)
    count = len(cols)
    fill = row_parts.size // col_parts.size + 1
    row_bits = [1 << b for b in range(1, n_col.bit_length() - 1)] + [1]
    col_bits = [1 << b for b in range(n_row.bit_length() - 1)]
    for n, bit in enumerate(row_bits):
        received = swap(jnp.stack(rows), "col", n_col, bit)
        if n < len(col_bits):
            other = swap(jnp.stack(cols * fill), "row", n_row, col_bits[n])
            received, other = lax.optimization_barrier((received, other))
            cols = merged(cols, list(other[:count]))
        rows = merged(rows, list(received))
    return *lse_and_mean(rows), *lse_and_mean(cols)


LEVELS = 32000
LOW = 128
BIAS = 125
EXTRA = 8
MORE = 2 * EXTRA
STEP = 32


def put_extra(out, extra_ref):
    n, width = extra_ref.shape
    rows = min(n, EXTRA)
    out[...] = jnp.zeros(out.shape, out.dtype)
    out[:rows, :width] = sum(extra_ref[i : i + rows, :] for i in range(0, n, rows))


def power(k):
    return jnp.exp2(k).astype(jnp.bfloat16).astype(jnp.float32)


def encode(out, powers, size, slab, extra):
    width = out.shape[1]
    for r in range(0, size, STEP):
        value = slab(r)
        top = jnp.maximum(jnp.max(jnp.abs(value), axis=1, keepdims=True), 1e-30)
        k = jnp.ceil(jnp.log(top) * LOG2E)
        powers[r : r + STEP, :] = jnp.broadcast_to(power(k), (STEP, LANES))
        whole = jnp.floor(jnp.abs(value) * (power(-k) * (LEVELS - 1)) + 0.5) * (1 / LOW)
        high = jnp.floor(whole)
        code = (1.0 + (whole - high)) * jnp.exp2(high - BIAS)
        out[r : r + STEP, :] = jnp.where(value < 0, -code, code).astype(jnp.bfloat16)
    half = width // 2
    first = extra[:, :half].astype(jnp.bfloat16)
    rest = extra[:, :half] - first.astype(jnp.float32)
    second = rest.astype(jnp.bfloat16)
    third = (rest - second.astype(jnp.float32)).astype(jnp.bfloat16)
    fourth = powers[...].T[:EXTRA, :].astype(jnp.bfloat16)
    if size < half:
        fourth = jnp.concatenate([fourth, jnp.zeros((EXTRA, half - size), jnp.bfloat16)], axis=1)
    out[size:, :half] = jnp.concatenate([first, second], axis=0)
    out[size:, half:] = jnp.concatenate([third, fourth], axis=0)


def decode_powers(code, size):
    half = code.shape[1] // 2
    powers = code[size:, half : half + size].astype(jnp.float32)
    return jnp.broadcast_to(powers[EXTRA : EXTRA + 1, :], (LANES, size)).T * (LOW / (LEVELS - 1))


def decode(code, powers, r):
    lanes = []
    for lane in range(0, code.shape[1], LANES):
        c = code[r : r + STEP, lane : lane + LANES].astype(jnp.float32)
        a = jnp.abs(c)
        high = jnp.floor(jnp.log(a) * LOG2E)
        whole = (high + (BIAS - 1)) + a * jnp.exp2(-high)
        lanes.append(jnp.where(c < 0, -whole, whole) * powers[r : r + STEP, :])
    return jnp.concatenate(lanes, axis=1)


def decode_extra(code, size):
    half = code.shape[1] // 2
    left = code[size:, :half].astype(jnp.float32)
    right = code[size:, half:].astype(jnp.float32)
    return left[:EXTRA] + left[EXTRA:] + right[:EXTRA]


def pack_text_kernel(n, base, *refs):
    codes, out, powers, received = refs[:n], *refs[n:]
    size, half = base.shape[0] - EXTRA, base.shape[1] // 2
    more = base[size:, :half]
    for c, code in enumerate(codes):
        received[c] = decode_powers(code, size)
        more = more + decode_extra(code, size)

    def slab(r):
        value = base[r : r + STEP, :]
        for c, code in enumerate(codes):
            value = value + decode(code, received.at[c], r)
        return value

    encode(out, powers, size, slab, more)


def pack_text(base, codes):
    size, width = base.shape[0] - EXTRA, base.shape[1]
    vmem = pl.BlockSpec(memory_space=VMEM)
    return pl.pallas_call(
        functools.partial(pack_text_kernel, len(codes)),
        out_shape=jax.ShapeDtypeStruct((size + MORE, width), jnp.bfloat16),
        in_specs=[vmem] * (1 + len(codes)),
        out_specs=vmem,
        scratch_shapes=[VMEM((size, LANES), jnp.float32), VMEM((len(codes), size, LANES), jnp.float32)],
        compiler_params=pltpu.CompilerParams(vmem_limit_bytes=6 * 2**20),
        cost_estimate=pl.CostEstimate(
            flops=FLOPS * 32 * size * size * width, bytes_accessed=0, transcendentals=0
        ),
        name="pack_text",
    )(base, *codes)


def pack_images_kernel(n, near, far, *refs):
    own, *outs, powers = refs[-n - 1 :]
    size = near.shape[1] - EXTRA
    own[...] = near[0] + far[0]
    for j, out in enumerate(outs, 1):
        encode(
            out,
            powers.at[j - 1],
            size,
            lambda r, j=j: near[j, r : r + STEP, :] + far[j, r : r + STEP, :],
            near[j, size:, :] + far[j, size:, :],
        )


def pack_images(near, far, after):
    n, rows, width = near.shape
    size = rows - EXTRA
    vmem = pl.BlockSpec(memory_space=VMEM)
    code = jax.ShapeDtypeStruct((size + MORE, width), jnp.bfloat16)
    own, *codes = pl.pallas_call(
        functools.partial(pack_images_kernel, n),
        out_shape=(jax.ShapeDtypeStruct((rows, width), jnp.float32),) + (code,) * (n - 1),
        in_specs=[vmem] * 2 + [pl.BlockSpec(memory_space=pl.ANY)] * len(after),
        out_specs=(vmem,) * n,
        scratch_shapes=[VMEM((n - 1, size, LANES), jnp.float32)],
        compiler_params=pltpu.CompilerParams(vmem_limit_bytes=(4 + 2 * n) * 2**20),
        cost_estimate=pl.CostEstimate(
            flops=FLOPS * 8 * n * size * size * width, bytes_accessed=0, transcendentals=0
        ),
        name="pack_images",
    )(near, far, *after)
    return own, codes


def total_kernel(n, in_order, coef_ref, base, *refs):
    codes, before = refs[:n], refs[n:-6]
    out, extra, scalar, value, powers, sems = refs[-6:]
    size, width = base.shape[0] - EXTRA, base.shape[1]
    combine = functools.partial(functools.reduce, jnp.add) if in_order else first_and_pairs
    for c, code in enumerate(codes):
        powers[c] = decode_powers(code, size)
    copies = []
    steps = sems.shape[0]
    for i in range(steps):
        part = pl.ds(i * (size // steps), size // steps)
        for r in range(i * (size // steps), (i + 1) * (size // steps), STEP):
            value[r : r + STEP, :] = combine(
                [base[r : r + STEP, :]] + [decode(code, powers.at[c], r) for c, code in enumerate(codes)]
            )
        copies.append(pltpu.make_async_copy(value.at[part], out.at[part], sems.at[i]))
        copies[-1].start()
    more = combine([base[size:, : width // 2]] + [decode_extra(code, size) for code in codes])
    more = sum([b[...] for b in before], more)
    extra[...] = more
    scalar[0, 0] = jnp.sum(more) / coef_ref[0, 0]
    for copy in copies:
        copy.wait()


def add_kernel(base, code, out, powers):
    size, half = base.shape[0] - EXTRA, base.shape[1] // 2
    powers[...] = decode_powers(code, size)
    for r in range(0, size, STEP):
        out[r : r + STEP, :] = base[r : r + STEP, :] + decode(code, powers, r)
    out[size:, :half] = base[size:, :half] + decode_extra(code, size)
    out[size:, half:] = jnp.zeros((EXTRA, half), jnp.float32)


def added(base, code):
    vmem = pl.BlockSpec(memory_space=VMEM)
    return pl.pallas_call(
        add_kernel,
        out_shape=jax.ShapeDtypeStruct(base.shape, jnp.float32),
        in_specs=[vmem] * 2,
        out_specs=vmem,
        scratch_shapes=[VMEM((base.shape[0] - EXTRA, LANES), jnp.float32)],
        compiler_params=pltpu.CompilerParams(vmem_limit_bytes=6 * 2**20),
        name="added",
    )(base, code)


def first_and_pairs(blocks):
    if len(blocks) == 1:
        return blocks[0]
    pairs = [blocks[0]] + [blocks[i] + blocks[i + 1] for i in range(1, len(blocks), 2)]
    return by_pairs(pairs, jnp.add)


def total_of(coef, base, codes, in_order, before, name):
    size, width = base.shape[0] - EXTRA, base.shape[1]
    vmem = pl.BlockSpec(memory_space=VMEM)
    smem = pl.BlockSpec(memory_space=SMEM)
    return pl.pallas_call(
        functools.partial(total_kernel, len(codes), in_order),
        out_shape=(
            jax.ShapeDtypeStruct((size, width), jnp.float32),
            jax.ShapeDtypeStruct((EXTRA, width // 2), jnp.float32),
            jax.ShapeDtypeStruct((1, 1), jnp.float32),
        ),
        in_specs=[smem] + [vmem] * (1 + len(codes) + len(before)),
        out_specs=(pl.BlockSpec(memory_space=pl.ANY), vmem, smem),
        scratch_shapes=[
            VMEM((size, width), jnp.float32),
            VMEM((len(codes), size, LANES), jnp.float32),
            pltpu.SemaphoreType.DMA((4,)),
        ],
        compiler_params=pltpu.CompilerParams(vmem_limit_bytes=8 * 2**20),
        name=name,
    )(coef, base, *codes, *before)


def text_block(block, text, tile, t, halves, row_lse, col_lse, place_ref, coef_ref, grad_ref):
    coef = coef_ref[0, 0]
    r_place, c_place = place_ref[0, 0], place_ref[0, 1]
    half, width = halves[0].shape
    n_col, n_row = row_lse.shape[0], col_lse.shape[0]
    size = block
    col_lse_down = jnp.broadcast_to(col_lse[pl.ds(r_place ^ t, 1), :], (LANES, size)).T
    text_id = c_place * n_row + (r_place ^ t)
    step = 32
    lane_ids = lax.broadcasted_iota(jnp.int32, (step, LANES), 1)
    row_ids = lax.broadcasted_iota(jnp.int32, (step, LANES), 0)

    for which, images in enumerate(halves):

        def one(j, carry):
            at = pl.multiple_of(j * block + which * half, block)
            if tile is None:
                image = images[pl.ds(pl.multiple_of(j * block, block), block), :]
                xs = nt_dot(text[:block, :], image) * coef
            column = c_place ^ (2 * j + which)
            same = jnp.where(r_place * n_col + column == text_id, 1.0, 0.0)
            lse = row_lse[pl.ds(column, 1), :]
            for r in range(0, size, step):
                for lane in range(0, block, LANES):
                    if tile is None:
                        x = xs[r : r + step, lane : lane + LANES]
                    else:
                        x = tile[r : r + step, pl.ds(at + lane, LANES)]
                    e = jnp.exp2(x - lse[:, lane : lane + LANES]) + jnp.exp2(
                        x - col_lse_down[r : r + step, :]
                    )
                    g = 0.5 * e
                    if lane <= r < lane + LANES:
                        g = g - jnp.where(row_ids + (r - lane) == lane_ids, same, 0.0)
                    grad_ref[r : r + step, pl.ds(at + lane, LANES)] = g.astype(jnp.bfloat16)
            return carry

        lax.fori_loop(0, half // block, one, 0, unroll=4)


def image_block(grads, texts, at, count, scale, block):
    total = None
    for grad, text in zip(grads, texts):
        part = lax.dot_general(
            grad[:, pl.ds(at, count)],
            text[:block, :],
            (((0,), (0,)), ((), ())),
            preferred_element_type=jnp.float32,
        )
        total = part if total is None else total + part
    return scale * total


def text_kernel(order, n_done, kept, block, scale_ref, coef_ref, place_ref, *refs):
    even, odd, row_lse, col_lse, row_extra, col_extra = refs[:6]
    n = len(order)
    texts, rest = refs[6 : 6 + n], refs[6 + n :]
    if kept:
        tile, rest = rest[0], rest[1:]
    done_grads, done_texts, rest = rest[:n_done], rest[n_done : 2 * n_done], rest[2 * n_done :]
    grads, outs, rest = rest[0], rest[1 : 1 + n], rest[1 + n :]
    total, powers = rest[-2:]
    lowest = min(order)
    for i, t in enumerate(order):
        text_block(
            block,
            texts[i],
            tile.at[pl.ds((t - lowest) * block, block)] if kept else None,
            t,
            (even, odd),
            row_lse,
            col_lse,
            place_ref,
            coef_ref,
            grads.at[pl.ds((t - lowest) * block, block)],
        )
    half = even.shape[0]
    scale = scale_ref[0, 0]
    total[...] = scale * (
        jnp.dot(grads[:, :half], even[...], preferred_element_type=jnp.float32)
        + jnp.dot(grads[:, half:], odd[...], preferred_element_type=jnp.float32)
    )
    for i, t in enumerate(order):
        at = (t - lowest) * block
        if t & 1:
            extra_rows = rest[-3]
            put_extra(extra_rows, row_extra)
            encode(outs[i], powers, block, lambda r, at=at: total[at + r : at + r + STEP, :], extra_rows[...])
        else:
            outs[i][:block, :] = total[at : at + block, :]
            put_extra(outs[i].at[block:, :], row_extra)
    if n_done:
        far_ref, near_ref = rest[:2]
        by_text = {t: (grads.at[pl.ds((t - lowest) * block, block)], texts[i]) for i, t in enumerate(order)}

        for images_ref, first in ((far_ref, half), (near_ref, 0)):

            def one(j, carry):
                for n in range(0, block, LANES):
                    images_ref[j, n : n + LANES, :] = image_block(
                        [*done_grads, *[by_text[t][0] for t in order]],
                        [*done_texts, *[by_text[t][1] for t in order]],
                        pl.multiple_of(j * block + first + n, LANES),
                        LANES,
                        scale,
                        block,
                    )
                put_extra(images_ref.at[j, block:, :], col_extra)
                return carry

            lax.fori_loop(0, half // block, one, 0, unroll=4)


def text_grads(scale, coef, place, even, odd, row_lse, col_lse, row_extra, col_extra, texts, tile, order, done):
    half, width = even.shape
    block = row_lse.shape[1]
    n = len(order)
    vmem = pl.BlockSpec(memory_space=VMEM)
    smem = pl.BlockSpec(memory_space=SMEM)
    out_shape = (
        [jax.ShapeDtypeStruct((n * block, 2 * half), jnp.bfloat16)]
        + [
            jax.ShapeDtypeStruct((block + MORE, width), jnp.bfloat16)
            if t & 1
            else jax.ShapeDtypeStruct((block + EXTRA, width), jnp.float32)
            for t in order
        ]
    )
    if done:
        out_shape += [jax.ShapeDtypeStruct((half // block, block + EXTRA, width), jnp.float32)] * 2
    operands = [even, odd, row_lse, col_lse, row_extra, col_extra, *[texts[t] for t in order]]
    operands += tile
    operands += [grad for _, grad in done] + [texts[t] for t, _ in done]
    outs = pl.pallas_call(
        functools.partial(text_kernel, tuple(order), len(done), len(tile), block),
        out_shape=tuple(out_shape),
        in_specs=[smem] * 3 + [vmem] * len(operands),
        out_specs=(vmem,) * len(out_shape),
        scratch_shapes=[
            VMEM((EXTRA, width), jnp.float32),
            VMEM((n * block, width), jnp.float32),
            VMEM((block, LANES), jnp.float32),
        ],
        compiler_params=pltpu.CompilerParams(vmem_limit_bytes=(10 + 2 * n) * 2**20),
        cost_estimate=pl.CostEstimate(
            flops=FLOPS * 4 * n * block * 2 * half * width, bytes_accessed=0, transcendentals=0
        ),
        name=f"text_grads_{n}",
    )(scale, coef, place, *operands)
    parts = {t: outs[1 + i] for i, t in enumerate(order)}
    return outs[0], parts, outs[1 + n :]


def on_device(n_row, n_col, image_embeds, text_embeds, logit_scale):
    block = image_embeds.shape[0]
    r, c = lax.axis_index("row"), lax.axis_index("col")
    place = jnp.stack([r, c]).reshape(1, 2)
    scale = logit_scale.reshape(1, 1)
    coef = scale * LOG2E
    image_half = image_embeds.astype(jnp.bfloat16)
    text_half = jnp.pad(text_embeds.astype(jnp.bfloat16), ((0, 16), (0, 0)))
    even, odd, texts, text_last = gather_both(image_half, text_half, n_col, n_row)
    keep = 4 * n_row * n_col * block * block <= 16 * 2**20
    even, odd, *before = stats(
        coef, place, texts, (*even, *odd), (), n_col, n_row, block, keep
    )
    row_parts, col_parts, *tile_last = stats(
        coef, place, [text_last], (even, odd), before[:2], n_col, n_row, block, keep
    )
    texts = [*texts, text_last]
    tile = before[2:]
    row_lse, row_extra, col_lse, col_extra = exchanged(row_parts, col_parts, n_col, n_row)

    held = (scale, coef, place, even, odd, row_lse, col_lse, row_extra, col_extra, texts)
    last = n_row - 1
    last_grad, parts, _ = text_grads(*held, tile_last, [last], [])
    received = swap(parts[last], "row", n_row, 1)
    _, more_parts, (far, near) = text_grads(*held, tile, list(range(last))[::-1], [(last, last_grad)])
    parts |= more_parts
    codes = {q: [] for q in range(0, n_row, 2)}
    codes[last ^ 1].append(received)
    after = [pack_text(parts[last ^ 1], codes[last ^ 1])] if n_row > 2 else [received]
    far = swap(far, "col", n_col, 1)
    odd_parts, far = lax.optimization_barrier(([parts[q] for q in range(1, last, 2)], far))
    for q, part in zip(range(1, last, 2), odd_parts):
        codes[q ^ 1].append(swap(part, "row", n_row, 1))
    for b in range(1, n_row.bit_length() - 1):
        for q in [q for q in codes if q & (1 << b)]:
            code = after[0] if (b, q) == (1, last ^ 1) else pack_text(parts[q], codes[q])
            codes[q ^ (1 << b)].append(swap(code, "row", n_row, 1 << b))
            del codes[q]
    grad_text, text_extra, _ = total_of(coef, parts[0], codes[0], True, [], "grad_text")

    own, others = pack_images(near, far, after)
    others = [swap(code, "col", n_col, 2 * j) for j, code in enumerate(others, 1)]
    first, text_extra = lax.optimization_barrier((others[0], text_extra))
    grad_image, _, grad_scale = total_of(
        coef, added(own, first), others[1:], False, [text_extra], "grad_image"
    )
    return grad_image, grad_text, grad_scale.reshape(())


def solution(mesh):
    images = P(("row", "col"), None)
    texts = P(("col", "row"), None)
    return jax.shard_map(
        functools.partial(on_device, mesh.shape["row"], mesh.shape["col"]),
        mesh=mesh,
        in_specs=(images, texts, P()),
        out_specs=(images, texts, P()),
        check_vma=False,
    )
```
